32 devices in a mesh: seq: 8 (over z, x), wide: 4 (over y, core).
Axes of the slice: x: 2, y: 2, z: 4, core: 2. Of those that a mesh axis runs over, the one named last changes fastest.
Arguments:
- hidden_in: bfloat16 [1024, 24, 768], P('wide', 'seq'), may hold values from -9 to 9
- cotangent: bfloat16 [1024, 24, 768], P('wide', 'seq'), may hold values from -6 to 6
- seq_offsets: int32 [24, 8], P('seq'), may hold values from 0 to 896, as said below
- owner_blocks: int32 [8], replicated, may hold values from 1 to 6, 24 in all
- master: float32 [1536, 12288], P('seq', 'wide'), may hold values from -0.72168784 to 0.72168784
- first_moment: float32 [1536, 12288], P('seq', 'wide'), may hold values from -0.00048828125 to 0.00048828125
- second_moment: float32 [1536, 12288], P('seq', 'wide'), may hold values from 1.0592933e-10 to 4.237173e-10
- ln_params: float32 [4, 768], replicated, may hold values from -1 to 2.4
- ln_first: float32 [4, 768], replicated, may hold values from -0.00048828125 to 0.00048828125
- ln_second: float32 [4, 768], replicated, may hold values from 1.0592933e-10 to 4.237173e-10
Outputs:
- mixed: bfloat16 [1024, 24, 768], P('wide', 'seq')
- input_grad: float32 [1024, 24, 768], P('wide', 'seq')
- new_master: float32 [1536, 12288], P('seq', 'wide')
- new_first: float32 [1536, 12288], P('seq', 'wide')
- new_second: float32 [1536, 12288], P('seq', 'wide')
- new_norms: float32 [4, 768], replicated
- norms_first: float32 [4, 768], replicated
- norms_second: float32 [4, 768], replicated
- grad_norm: float32 [], replicated
The draws below stay inside these ranges and needn't reach their ends.
Inputs may be any that keep to these rules, and one draw needn't show every extreme that they name: `seq_offsets`: each pack is cut into whole sequences of 1, 2 or 4 runs of 128 positions, each starting where the previous one ends; every pack holds one sequence of 4 runs; some pack's last run is a sequence of its own. `owner_blocks`: the counts sum to three times the number of indices of seq; some index owns exactly 6 blocks.
All inputs are finite; a program needn't handle non-finite values.
Results may differ from the reference program's by a relative error of at most 0.024.
Values may be sent and summed in bfloat16 or wider, within the bound.
A program may use at most 256 MiB of HBM per device.

```python
import math
import jax
import jax.numpy as jnp
import numpy as np
from jax import lax

D = 768
H = 12
HD = 64
FF = 3072
UNIT = 128
PACK = 1024
NP = 24
CAP = 6
RB = 32
OWN = 1536
CW = 3072
NCOL = 12288
STEP = 10
N_SEQ = 8
N_WIDE = 4


def draw_hidden_in(key, part):
    key = jax.random.fold_in(key, 5)
    base = jnp.clip(jax.random.normal(key, (PACK, NP, D), jnp.float32), -5.0, 5.0)
    column = 0.6 + 1.2 * jnp.arange(D, dtype=jnp.float32) / (D - 1)
    return (base * column).astype(jnp.bfloat16)


def draw_master(key, part):
    key = jax.random.fold_in(key, 7)
    base = jnp.clip(jax.random.normal(key, (OWN, NCOL), jnp.float32), -5.0, 5.0)
    groups = (4 * D + 3 * FF) // CW
    width_e = D // groups
    width_f = FF // groups
    column = jnp.arange(NCOL, dtype=jnp.int32)
    group = (column // CW).astype(jnp.float32)
    inner = column % CW
    rising = 0.7 + 0.6 * group / max(groups - 1, 1)
    root_d = D ** (-0.5)
    scale = jnp.where(inner < 3 * width_e, root_d, jnp.where(inner < 4 * width_e, 4.0 * root_d, jnp.where(inner < 4 * width_e + 2 * width_f, root_d * rising, 2.0 * FF ** (-0.5) * rising)))
    return base * scale[None, :]


def draw_ln_params(key, part):
    key = jax.random.fold_in(key, 9)
    base = jnp.clip(jax.random.normal(key, (4, D), jnp.float32), -3.0, 3.0)
    rising = 0.6 + 1.2 * jnp.arange(D, dtype=jnp.float32) / (D - 1)
    gains = rising[None, :] * (1.0 + 0.1 * base)
    shifts = 0.3 * base
    row = jnp.arange(4, dtype=jnp.int32)[:, None]
    return jnp.where(row % 2 == 0, gains, shifts)


def draw_seq_offsets(key, part):
    key = jax.random.fold_in(key, 11)
    first_key, second_key = jax.random.split(key)
    table = jnp.array(np.array([[0, 0, 0, 0], [0, 0, 2, 2], [0, 0, 2, 3], [0, 1, 1, 3], [0, 1, 2, 2], [0, 1, 2, 3]], dtype=np.int32))
    first_pack = jnp.arange(NP, dtype=jnp.int32) == 0
    pick = jnp.where(first_pack, 5, jax.random.randint(first_key, (NP,), 0, 6))
    other = jnp.take(table, pick, axis=0)
    long_first = jnp.logical_or(jax.random.randint(second_key, (NP,), 0, 2) == 1, first_pack)[:, None]
    zeros = jnp.zeros((NP, 4), jnp.int32)
    front = jnp.where(long_first, zeros, other)
    back = jnp.where(long_first, other + 4, zeros + 4)
    return (jnp.concatenate([front, back], axis=1) * UNIT).astype(jnp.int32)


def block_levels(rng, shape, shards, least, top_value):
    level, own = 1.0, jax.random.fold_in(rng, 6)
    for position, blocks in shards:
        draws = jnp.exp(jax.random.uniform(jax.random.fold_in(own, position), (blocks,), jnp.float32, least / len(shards), top_value / len(shards)))
        level = level * jnp.repeat(draws, shape[position] // blocks).reshape([-1 if axis == position else 1 for axis in range(len(shape))])
    return level


def profile(count, total, bound, skew):
    loads = [(1 << 20) // math.isqrt(rank ** skew) + 1 for rank in range(2, count + 1)]
    rest, given = total - bound - (count - 1), [1] * (count - 1)
    while rest > 0:
        free = [i for i in range(count - 1) if given[i] < bound]
        pool, left = sum([loads[i] for i in free]), rest
        for i in free:
            addition = min(bound - given[i], max(1, left * loads[i] // pool), rest)
            given[i] = given[i] + addition
            rest = rest - addition
    return np.array([bound] + given)


def ragged_sizes(stream_key, count, total, bound, skew):
    if count == 2:
        one = jax.random.randint(stream_key, (), max(1, total - bound), min(bound, total - 1) + 1)
        return jnp.stack([one, total - one])
    tallies = jnp.asarray(profile(count, total, bound, skew), jnp.int32)
    couples = (count - 1) // 2
    giver, receiver = tallies[1:1 + 2 * couples:2], tallies[2:2 + 2 * couples:2]
    margin = jnp.minimum(giver - 1, bound - receiver)
    shifted = jax.random.randint(jax.random.fold_in(stream_key, 1), (couples,), 0, 1 << 20) % (margin + 1)
    tallies = tallies.at[1:1 + 2 * couples:2].set(giver - shifted).at[2:2 + 2 * couples:2].set(receiver + shifted)
    return tallies[jax.random.permutation(jax.random.fold_in(stream_key, 2), count)]


def gaussian(own_key, dims, width, bound, pieces=(), kind=jnp.bfloat16):
    level = block_levels(own_key, dims, pieces, -0.22, 0.18) if pieces else 1.0
    entries = jax.random.normal(own_key, dims, jnp.float32) * width * level
    return jnp.minimum(jnp.maximum(entries, -bound), bound).astype(kind)


def setup_inputs(seed: int = 0) -> dict:
    key_list = jax.random.split(jax.random.key(seed), 11)
    return {
        "hidden_in": draw_hidden_in(jax.random.fold_in(key_list[10], 71), 0),
        "cotangent": gaussian(key_list[1], (PACK, NP, D), 1.0, 6.0, ((0, 4), (1, 8))),
        "seq_offsets": draw_seq_offsets(jax.random.fold_in(key_list[10], 71), 0),
        "owner_blocks": ragged_sizes(key_list[3], N_SEQ, 3 * N_SEQ, CAP, 0).astype(jnp.int32),
        "master": draw_master(jax.random.fold_in(key_list[10], 71), 0),
        "first_moment": gaussian(key_list[5], (OWN, NCOL), (0.11 * (D * (4 * D + 3 * FF) + 4 * D) ** -0.5), 0.00048828125, ((0, 8), (1, 4)), jnp.float32),
        "second_moment": jnp.clip(jnp.exp(math.log(4.237173112375814e-10) - 1.3862944 * jax.random.uniform(key_list[6], (OWN, NCOL), jnp.float32) ** block_levels(key_list[6], (OWN, NCOL), ((0, 8), (1, 4)), -0.2, 0.2)), 1.0592932780939535e-10, 4.237173112375814e-10),
        "ln_params": draw_ln_params(jax.random.fold_in(key_list[10], 71), 0),
        "ln_first": gaussian(key_list[8], (4, D), (0.11 * (D * (4 * D + 3 * FF) + 4 * D) ** -0.5), 0.00048828125, (), jnp.float32),
        "ln_second": jnp.clip(jnp.exp(jax.random.uniform(key_list[9], (4, D), jnp.float32, math.log(1.0592932780939535e-10), math.log(4.237173112375814e-10))), 1.0592932780939535e-10, 4.237173112375814e-10),
    }


@jax.custom_vjp
def low(v):
    return lax.optimization_barrier(v.astype(jnp.bfloat16)).astype(jnp.float32)

@jax.custom_vjp
def low_back(v):
    return v

def low_keep(v):
    return (low(v), None)

def low_pass(kept, grad):
    return (grad,)

def back_keep(v):
    return (v, None)

def back_low(kept, grad):
    return (low(grad),)
low.defvjp(low_keep, low_pass)
low_back.defvjp(back_keep, back_low)
RATE = 0.02
NORM_RATE = 0.6
BETA_ONE = 0.9
BETA_TWO = 0.999
EPSILON = 1e-08
DECAY = 0.01
NORM_EPS = 1e-05
HIGH = lax.Precision.HIGHEST

def matmul(left, right):
    return jnp.dot(left, right, precision=HIGH, preferred_element_type=jnp.float32)

def owner_maps(owner_blocks, rows, cap, block):
    counts = owner_blocks.astype(jnp.int32)
    ends = jnp.cumsum(counts).astype(jnp.int32)
    starts = ends - counts
    slot = jnp.arange(cap * block, dtype=jnp.int32)
    which = slot // block
    source = (starts[:, None] + which[None, :]) * block + (slot % block)[None, :]
    valid = which[None, :] < counts[:, None]
    source = jnp.where(valid, source, 0).reshape(-1).astype(jnp.int32)
    valid = valid.reshape(-1)
    param = jnp.arange(rows, dtype=jnp.int32)
    blocks = param // block
    owner = lax.optimization_barrier(jnp.sum((ends[None, :] <= blocks[:, None]).astype(jnp.int32), axis=1))
    onehot = owner[:, None] == jnp.arange(counts.shape[0], dtype=jnp.int32)[None, :]
    first = lax.optimization_barrier(jnp.sum(jnp.where(onehot, starts[None, :], 0), axis=1))
    target = (owner * (cap * block) + (blocks - first) * block + param % block).astype(jnp.int32)
    return (source, valid, target)

def layer_norm(values, gain, shift):
    center = values - lax.optimization_barrier(jnp.mean(values, axis=-1, keepdims=True))
    variance = lax.optimization_barrier(jnp.mean(center * center, axis=-1, keepdims=True))
    return center * lax.rsqrt(variance + NORM_EPS) * gain + shift

def pack_layer(weights, norms, slopes, tokens, offsets):
    width_e = D // N_WIDE
    width_f = FF // N_WIDE
    heads_local = H // N_WIDE
    scale = HD ** (-0.5)
    starts = jnp.repeat(offsets, UNIT)
    same = starts[:, None] == starts[None, :]
    places = jnp.arange(PACK, dtype=jnp.float32)
    distance = jnp.abs(places[:, None] - places[None, :])
    attn = jnp.zeros((PACK, D), jnp.float32)
    for group in range(N_WIDE):
        part = weights[:, group, :]
        inputs = low_back(tokens)
        queries = low_back(low(matmul(inputs, part[:, :width_e]))).reshape(PACK, heads_local, HD)
        keys_all = low_back(low(matmul(inputs, part[:, width_e:2 * width_e]))).reshape(PACK, heads_local, HD)
        values_all = low_back(low(matmul(inputs, part[:, 2 * width_e:3 * width_e]))).reshape(PACK, heads_local, HD)
        raw = jnp.einsum('qhd,khd->hqk', queries, keys_all, precision=HIGH)
        slope = slopes[group * heads_local:(group + 1) * heads_local]
        scores = low_back(raw) * scale - slope[:, None, None] * distance[None]
        scores = jnp.where(same[None], scores, -1e+30)
        probs = jax.nn.softmax(scores, axis=-1)
        context = jnp.einsum('hqk,khd->qhd', low(probs), values_all, precision=HIGH).reshape(PACK, width_e)
        context = low_back(low(context))
        attn = attn + low(matmul(context, part[:, 3 * width_e:4 * width_e].T))
    attn = low_back(attn)
    normed = layer_norm(tokens + attn, norms[0], norms[1])
    ffn = jnp.zeros((PACK, D), jnp.float32)
    for group in range(N_WIDE):
        part = weights[:, group, :]
        base = 4 * width_e
        inputs = low_back(low(normed))
        gate = low_back(matmul(inputs, part[:, base:base + width_f]))
        up_vals = low_back(matmul(inputs, part[:, base + width_f:base + 2 * width_f]))
        hidden = low(jax.nn.gelu(gate, approximate=False) * up_vals)
        ffn = ffn + low(matmul(hidden, part[:, base + 2 * width_f:base + 3 * width_f].T))
    ffn = low_back(ffn)
    return layer_norm(normed + ffn, norms[2], norms[3])

def forward(weights, norms, tokens, offsets, slopes):

    def one(pair):
        return pack_layer(weights, norms, slopes, pair[0], pair[1])
    result = lax.map(jax.checkpoint(one), (jnp.moveaxis(tokens, 1, 0), offsets))
    return jnp.moveaxis(result, 0, 1)

def adamw(param, grad, first, second, decay, rate):
    first_new = BETA_ONE * first + (1.0 - BETA_ONE) * grad
    second_new = BETA_TWO * second + (1.0 - BETA_TWO) * grad * grad
    first_hat = first_new / (1.0 - BETA_ONE ** STEP)
    second_hat = second_new / (1.0 - BETA_TWO ** STEP)
    param_new = param - rate * (first_hat / (jnp.sqrt(second_hat) + EPSILON) + decay * param)
    return (param_new, first_new, second_new)

def reference(hidden_in, cotangent, seq_offsets, owner_blocks, master, first_moment, second_moment, ln_params, ln_first, ln_second):
    source, valid, target = owner_maps(owner_blocks, D, CAP, RB)
    flat = jnp.take(master, target, axis=0)
    weights = flat.astype(jnp.bfloat16).astype(jnp.float32).reshape(D, N_WIDE, CW)
    slopes = jnp.exp2(-8.0 * (jnp.arange(H).astype(jnp.float32) + 1.0) / H)
    tokens = hidden_in.astype(jnp.float32)

    def layer(weight_arg, norm_arg, token_arg):
        return forward(weight_arg, norm_arg, token_arg, seq_offsets, slopes)
    out, pull = jax.vjp(layer, weights, ln_params, tokens)
    grad_w, grad_ln, grad_x = pull(cotangent.astype(jnp.float32))
    grad_w = grad_w.reshape(D, N_WIDE * CW)
    grad_norm = jnp.sqrt(jnp.sum(grad_w * grad_w) + jnp.sum(grad_ln * grad_ln))
    clip = jnp.minimum(1.0, 1.0 / (grad_norm + 1e-06))
    first_flat = jnp.take(first_moment, target, axis=0)
    second_flat = jnp.take(second_moment, target, axis=0)
    param_new, first_new, second_new = adamw(flat, grad_w * clip, first_flat, second_flat, DECAY, RATE)
    norms_new, norms_first, norms_second = adamw(ln_params, grad_ln * clip, ln_first, ln_second, 0.0, NORM_RATE)

    def padded(array):
        return jnp.where(valid[:, None], jnp.take(array, source, axis=0), 0.0)
    return (out.astype(jnp.bfloat16), grad_x, padded(param_new), padded(first_new), padded(second_new), norms_new, norms_first, norms_second, grad_norm)
```

```python
import jax
import jax.numpy as jnp
from jax import lax
from jax.experimental import pallas as pl
from jax.experimental.pallas import tpu as pltpu
from jax.sharding import PartitionSpec as P

MESH = pl.DeviceIdType.MESH

H = 12
HD = 64
FF = 3072
UNIT = 128
CAP = 6
STEP = 10


RATE = 0.02
NORM_RATE = 0.6
BETA_ONE = 0.9
BETA_TWO = 0.999
EPSILON = 1e-08
DECAY = 0.01
NORM_EPS = 1e-05
ROOT_HALF = 0.7071067811865476
DENSITY_SCALE = 0.3989422804014327
EPS = 1e-05
F32 = jnp.float32
BF16 = jnp.bfloat16
VMEM_LIMIT = 60 * 2**20


def owner_maps(owner_blocks, rows, cap, block):
    ends = jnp.cumsum(owner_blocks)
    starts = ends - owner_blocks
    slot = jnp.arange(cap * block, dtype=jnp.int32)
    which = slot // block
    source = (starts[:, None] + which[None, :]) * block + (slot % block)[None, :]
    valid = which[None, :] < owner_blocks[:, None]
    source = jnp.where(valid, source, 0).reshape(-1)
    valid = valid.reshape(-1)
    param = jnp.arange(rows, dtype=jnp.int32)
    blocks = param // block
    owner = jnp.sum((ends[None, :] <= blocks[:, None]).astype(jnp.int32), axis=1)
    onehot = owner[:, None] == jnp.arange(owner_blocks.shape[0], dtype=jnp.int32)[None, :]
    first = jnp.sum(jnp.where(onehot, starts[None, :], 0), axis=1)
    target = owner * (cap * block) + (blocks - first) * block + param % block
    return (source, valid, target)


def norm_forward(values, gain, shift):
    center = values - jnp.mean(values, axis=-1, keepdims=True)
    variance = jnp.mean(center * center, axis=-1, keepdims=True)
    inverse = lax.rsqrt(variance + NORM_EPS)
    normal = center * inverse
    return (normal * gain + shift, normal, inverse)


def norm_backward(grad, normal, inverse, gain):
    scaled = grad * gain
    result = inverse * (
        scaled
        - jnp.mean(scaled, axis=-1, keepdims=True)
        - normal * jnp.mean(scaled * normal, axis=-1, keepdims=True)
    )
    return (result, jnp.sum(grad * normal, axis=(0, 1)), jnp.sum(grad, axis=(0, 1)))


def adamw(param, grad, first, second, decay, rate):
    first_new = BETA_ONE * first + (1.0 - BETA_ONE) * grad
    second_new = BETA_TWO * second + (1.0 - BETA_TWO) * grad * grad
    first_hat = first_new / (1.0 - BETA_ONE**STEP)
    second_hat = second_new / (1.0 - BETA_TWO**STEP)
    param_new = param - rate * (first_hat / (jnp.sqrt(second_hat) + EPSILON) + decay * param)
    return (param_new, first_new, second_new)


def scores_of(queries, keys_all, same, slope, distance, scale):
    raw = jnp.einsum("qhd,khd->hqk", queries, keys_all, preferred_element_type=jnp.float32)
    scores = raw * scale - slope[:, None, None] * distance[None]
    return jnp.where(same[None], scores, -1e30)


def dot_nn(a, b):
    return lax.dot_general(a, b, (((1,), (0,)), ((), ())), preferred_element_type=F32)


def dot_nt(a, b):
    return lax.dot_general(a, b, (((1,), (1,)), ((), ())), preferred_element_type=F32)


def dot_tn(a, b):
    return lax.dot_general(a, b, (((0,), (0,)), ((), ())), preferred_element_type=F32)


def places():
    wide = lax.axis_index("wide")
    core = lax.rem(wide, 2)
    row = wide // 2
    return wide, core, row, wide + 1 - 2 * core, wide + 2 - 4 * row


def greet(mate, across):
    barrier = pltpu.get_barrier_semaphore()
    for peer in (mate, across):
        pl.semaphore_signal(barrier, inc=1, device_id={"wide": peer}, device_id_type=MESH)
    pl.semaphore_wait(barrier, 2)


def remote(source, target, send, recv, peer):
    return pltpu.make_async_remote_copy(
        src_ref=source,
        dst_ref=target,
        send_sem=send,
        recv_sem=recv,
        device_id={"wide": peer},
        device_id_type=MESH,
    )


class Gather:
    def __init__(self, held, send, recv, share):
        self.held, self.send, self.recv, self.share = held, send, recv, share
        _, self.core, self.row, self.mate, self.across = places()

    def rows(self, core, row):
        return pl.ds(pl.multiple_of((core * 2 + row) * self.share, self.share), self.share)

    def copy(self, pack, leg):
        row = 1 - self.row if leg == 2 else self.row
        block = self.held.at[pack, self.rows(self.core, row)]
        peer = self.mate if leg else self.across
        return remote(block, block, self.send.at[pack, leg], self.recv.at[pack, leg], peer)

    def start(self, pack):
        self.copy(pack, 0).start()
        self.copy(pack, 1).start()

    def finish(self, pack):
        self.copy(pack, 0).wait_recv()
        self.copy(pack, 2).start()
        self.copy(pack, 1).wait_recv()
        self.copy(pack, 2).wait_recv()

    def drain(self, pack):
        for leg in range(3):
            self.copy(pack, leg).wait_send()


class Scatter:
    def __init__(self, part, give, take, cross, reach, own, send, recv, share):
        self.part, self.give, self.take = part, give, take
        self.cross, self.reach, self.own = cross, reach, own
        self.send, self.recv, self.share = send, recv, share
        _, self.core, self.row, self.mate, self.across = places()

    def copy(self, pack, leg):
        source, target = (self.cross, self.reach) if leg else (self.give, self.take)
        peer = self.across if leg else self.mate
        return remote(
            source.at[pack], target.at[pack], self.send.at[pack, leg], self.recv.at[pack, leg], peer
        )

    def half(self, which):
        core = self.core if which else 1 - self.core
        return pl.multiple_of(core * 2 * self.share, 2 * self.share)

    def start(self, pack):
        self.copy(pack, 0).start()

    def middle(self, pack):
        self.copy(pack, 0).wait_recv()
        share = self.share
        far = pl.ds(pl.multiple_of((1 - self.row) * share, share), share)
        near = pl.ds(pl.multiple_of(self.row * share, share), share)
        self.cross[pack] = (self.part[far, :] + self.take[pack, far, :].astype(F32)).astype(BF16)
        self.copy(pack, 1).start()
        self.own[pack] = self.part[near, :] + self.take[pack, near, :].astype(F32)

    def finish(self, pack):
        self.copy(pack, 1).wait_recv()

    def drain(self, pack):
        for leg in range(2):
            self.copy(pack, leg).wait_send()


def scatter_scratch(packs, share, width):
    return [
        pltpu.VMEM((2 * share, width), F32),
        pltpu.VMEM((packs, 2 * share, width), BF16),
        pltpu.VMEM((packs, 2 * share, width), BF16),
        pltpu.VMEM((packs, share, width), BF16),
        pltpu.VMEM((packs, share, width), BF16),
        pltpu.VMEM((packs, share, width), F32),
    ]


def norm_parts(values):
    center = values - jnp.mean(values, axis=-1, keepdims=True)
    inverse = lax.rsqrt(jnp.mean(center * center, axis=-1, keepdims=True) + EPS)
    return center * inverse, inverse


def norm_pull(grad, normal, inverse, gain):
    scaled = grad * gain
    return inverse * (
        scaled
        - jnp.mean(scaled, axis=-1, keepdims=True)
        - normal * jnp.mean(scaled * normal, axis=-1, keepdims=True)
    )


def loop(count, body, unroll=1):
    def step(index, carry):
        body(index)
        return carry

    lax.fori_loop(0, count, step, 0, unroll=unroll)


def tile(index, size):
    return pl.ds(pl.multiple_of(index * size, size), size)


def ffn_kernel(
    r1_ref,
    cot_ref,
    w_ref,
    ln_ref,
    mixed_ref,
    dr1_ref,
    grads_ref,
    lngrad_ref,
    weights,
    held,
    held2,
    gates,
    ups,
    hid,
    dgate,
    dup,
    turned,
    turned2,
    total,
    g_tile,
    u_tile,
    send_a,
    recv_a,
    send_b,
    recv_b,
    send_c,
    recv_c,
    send_d,
    recv_d,
    load_sem,
    store_sem,
    *buffers,
):
    packs, share, width = r1_ref.shape
    rows = 4 * share
    fwd = buffers[:6]
    units = weights.shape[1] // 3
    col = 256
    n_units, n_width = units // col, width // col
    load = pltpu.make_async_copy(w_ref.at[:, pl.ds(w_ref.shape[1] - 3 * units, 3 * units)], weights, load_sem)
    load.start()
    _, core, row, mate, across = places()
    greet(mate, across)
    gather_one = Gather(held, send_a, recv_a, share)
    scatter_one = Scatter(*fwd, send_b, recv_b, share)
    gather_two = Gather(held2, send_c, recv_c, share)
    scatter_two = Scatter(*fwd, send_d, recv_d, share)
    gain1, shift1 = ln_ref[0:1, :], ln_ref[1:2, :]
    gain2, shift2 = ln_ref[2:3, :], ln_ref[3:4, :]
    lngrad_ref[...] = jnp.zeros_like(lngrad_ref)
    chunk = 64

    for pack in range(packs):
        base = pl.multiple_of((core * 2 + row) * share, share)

        def first(index, pack=pack, base=base):
            normal, _ = norm_parts(r1_ref[pack, tile(index, chunk), :])
            held[pack, pl.ds(pl.multiple_of(base + index * chunk, chunk), chunk), :] = (
                normal * gain1 + shift1
            ).astype(BF16)

        loop(share // chunk, first)
        gather_one.start(pack)
    load.wait()

    def forward(pack):
        gather_one.finish(pack)
        for which in range(2):
            base = scatter_one.half(which)
            big = pl.ds(base, 2 * share)

            def ff(index):
                cols = tile(index, col)
                x = held[pack, big, :]
                g_tile[...] = dot_nn(x, weights[:, cols])
                u_tile[...] = dot_nn(x, weights[:, pl.ds(pl.multiple_of(units + index * col, col), col)])

                def act(part):
                    rws = tile(part, 32)
                    gate, up = g_tile[rws, :], u_tile[rws, :]
                    out = pl.ds(pl.multiple_of(base + part * 32, 32), 32)
                    cumulative = 0.5 * (1.0 + lax.erf(gate * ROOT_HALF))
                    hid[out, cols] = (gate * cumulative * up).astype(BF16)
                    gates[pack, out, cols] = gate.astype(BF16)
                    ups[pack, out, cols] = up.astype(BF16)

                loop(2 * share // 32, act, unroll=2)

            loop(n_units, ff)

            def down(index):
                wd = weights[tile(index, col), pl.ds(2 * units, units)]
                value = dot_nt(hid[big, :], wd)
                if which:
                    scatter_one.part[:, tile(index, col)] = value
                else:
                    scatter_one.give[pack, :, tile(index, col)] = value.astype(BF16)

            loop(n_width, down)
            if not which:
                scatter_one.start(pack)
        scatter_one.middle(pack)

    def turn(pack):
        scatter_one.finish(pack)
        gather_two_base = pl.multiple_of((core * 2 + row) * share, share)

        def second(index):
            rws = tile(index, chunk)
            normal, _ = norm_parts(r1_ref[pack, rws, :])
            ffn = scatter_one.own[pack, rws, :] + scatter_one.reach[pack, rws, :].astype(F32)
            normal2, inverse2 = norm_parts(normal * gain1 + shift1 + ffn)
            mixed_ref[pack, rws, :] = (normal2 * gain2 + shift2).astype(BF16)
            grad = cot_ref[pack, rws, :].astype(F32)
            value = norm_pull(grad, normal2, inverse2, gain2)
            dr1_ref[pack, rws, :] = value
            held2[pack, pl.ds(pl.multiple_of(gather_two_base + index * chunk, chunk), chunk), :] = value.astype(BF16)
            lngrad_ref[2:3, :] += jnp.sum(grad * normal2, axis=0, keepdims=True)
            lngrad_ref[3:4, :] += jnp.sum(grad, axis=0, keepdims=True)

        loop(share // chunk, second)
        scatter_one.drain(pack)
        gather_two.start(pack)

    def backward(pack):
        gather_two.finish(pack)
        for which in range(2):
            base = scatter_two.half(which)
            big = pl.ds(base, 2 * share)

            def bf(index):
                cols = tile(index, col)
                g_tile[...] = dot_nn(
                    held2[pack, big, :], weights[:, pl.ds(pl.multiple_of(2 * units + index * col, col), col)]
                )

                def act(part):
                    rws = tile(part, 32)
                    out = pl.ds(pl.multiple_of(base + part * 32, 32), 32)
                    dhid = g_tile[rws, :]
                    gate = gates[pack, out, cols].astype(F32)
                    up = ups[pack, out, cols].astype(F32)
                    cumulative = 0.5 * (1.0 + lax.erf(gate * ROOT_HALF))
                    density = jnp.exp(-0.5 * gate * gate) * DENSITY_SCALE
                    value = gate * cumulative
                    hid[out, cols] = (value * up).astype(BF16)
                    dgate[out, cols] = (dhid * up * (cumulative + gate * density)).astype(BF16)
                    dup[out, cols] = (dhid * value).astype(BF16)

                loop(2 * share // 32, act, unroll=2)

            loop(n_units, bf)

            def back(index):
                rws = tile(index, col)
                value = dot_nt(dgate[big, :], weights[rws, pl.ds(0, units)]) + dot_nt(
                    dup[big, :], weights[rws, pl.ds(units, units)]
                )
                if which:
                    scatter_two.part[:, tile(index, col)] = value
                else:
                    scatter_two.give[pack, :, tile(index, col)] = value.astype(BF16)

            loop(n_width, back)
            if not which:
                scatter_two.start(pack)
        scatter_two.middle(pack)

    def weight_grads(pack):
        def flip(index):
            rws = tile(index, 256)
            turned[:, rws] = held[pack, rws, :].T
            turned2[:, rws] = held2[pack, rws, :].T

        loop(rows // 256, flip)

        def add(index):
            rws = tile(index, col)
            a = turned[rws, :]
            b = turned2[rws, :]
            parts = (dot_nn(a, dgate[...]), dot_nn(a, dup[...]), dot_nn(b, hid[...]))
            for place, value in enumerate(parts):
                cols = pl.ds(place * units, units)
                if pack == 0:
                    total[rws, cols] = value
                else:
                    value = total[rws, cols] + value
                    if pack < packs - 1:
                        total[rws, cols] = value
                    else:
                        gates[place, rws, :] = value.astype(BF16)

        loop(n_width, add)

    def last(pack):
        scatter_two.finish(pack)

        def third(index):
            rws = tile(index, chunk)
            normal, inverse = norm_parts(r1_ref[pack, rws, :])
            grad = dr1_ref[pack, rws, :] + (
                scatter_two.own[pack, rws, :] + scatter_two.reach[pack, rws, :].astype(F32)
            )
            dr1_ref[pack, rws, :] = norm_pull(grad, normal, inverse, gain1)
            lngrad_ref[0:1, :] += jnp.sum(grad * normal, axis=0, keepdims=True)
            lngrad_ref[1:2, :] += jnp.sum(grad, axis=0, keepdims=True)

        loop(share // chunk, third)

    for pack in range(packs):
        forward(pack)
        if pack:
            turn(pack - 1)
    for pack in range(packs):
        backward(pack)
        weight_grads(pack)
        if pack == 0:
            turn(packs - 1)
        else:
            last(pack - 1)
    outs = [
        pltpu.make_async_copy(
            gates.at[place, pl.ds(0, width)],
            grads_ref.at[:, pl.ds(place * units, units)],
            store_sem.at[place],
        )
        for place in range(3)
    ]
    for out in outs:
        out.start()
    last(packs - 1)
    for out in outs:
        out.wait()
    for pack in range(packs):
        gather_one.drain(pack)
        gather_two.drain(pack)
        scatter_two.drain(pack)


def ffn_call(r1, cot, weights, ln_params):
    packs, share, width = r1.shape
    rows = 4 * share
    units = (weights.shape[1] - width) // 3
    vm = pl.BlockSpec(memory_space=pltpu.VMEM)
    hb = pl.BlockSpec(memory_space=pl.ANY)
    dma = pltpu.SemaphoreType.DMA
    return pl.pallas_call(
        ffn_kernel,
        out_shape=(
            jax.ShapeDtypeStruct((packs, share, width), BF16),
            jax.ShapeDtypeStruct((packs, share, width), F32),
            jax.ShapeDtypeStruct((width, 3 * units), BF16),
            jax.ShapeDtypeStruct((8, width), F32),
        ),
        in_specs=[vm, vm, hb, vm],
        out_specs=(vm, vm, hb, vm),
        scratch_shapes=[
            pltpu.VMEM((width, 3 * units), BF16),
            pltpu.VMEM((packs, rows, width), BF16),
            pltpu.VMEM((packs, rows, width), BF16),
            pltpu.VMEM((packs, rows, units), BF16),
            pltpu.VMEM((packs, rows, units), BF16),
            pltpu.VMEM((rows, units), BF16),
            pltpu.VMEM((rows, units), BF16),
            pltpu.VMEM((rows, units), BF16),
            pltpu.VMEM((width, rows), BF16),
            pltpu.VMEM((width, rows), BF16),
            pltpu.VMEM((width, 3 * units), F32),
            pltpu.VMEM((2 * share, 256), F32),
            pltpu.VMEM((2 * share, 256), F32),
            dma((packs, 3)),
            dma((packs, 3)),
            dma((packs, 2)),
            dma((packs, 2)),
            dma((packs, 3)),
            dma((packs, 3)),
            dma((packs, 2)),
            dma((packs, 2)),
            dma(()),
            dma((3,)),
            *scatter_scratch(packs, share, width),
        ],
        compiler_params=pltpu.CompilerParams(
            collective_id=1, has_side_effects=True, vmem_limit_bytes=VMEM_LIMIT
        ),
        name="ffn",
    )(r1, cot, weights, ln_params)


def per_device(
    hidden_in,
    cotangent,
    seq_offsets,
    owner_blocks,
    master,
    first_moment,
    second_moment,
    ln_params,
    ln_first,
    ln_second,
):
    wide_count = lax.axis_size("wide")
    share = hidden_in.shape[0]
    packs = hidden_in.shape[1]
    width = hidden_in.shape[2]
    pack_len = share * wide_count
    slab_rows = master.shape[0]
    block = slab_rows // CAP
    width_e = width // wide_count
    width_f = FF // wide_count
    heads_local = width_e // HD
    scale = HD ** (-0.5)
    source, valid, target = owner_maps(owner_blocks, width, CAP, block)
    gathered = lax.all_gather(master.astype(jnp.bfloat16), "seq", axis=0, tiled=True)
    weights = jnp.take(gathered, target, axis=0)
    w_qkv = weights[:, : 3 * width_e]
    w_out = weights[:, 3 * width_e : 4 * width_e]
    base = 4 * width_e
    w_gate = weights[:, base : base + width_f]
    w_up = weights[:, base + width_f : base + 2 * width_f]
    w_down = weights[:, base + 2 * width_f : base + 3 * width_f]
    head_ids = lax.axis_index("wide") * heads_local + jnp.arange(heads_local, dtype=jnp.int32)
    slope = jnp.exp2(-8.0 * (head_ids.astype(jnp.float32) + 1.0) / H)
    places = jnp.arange(pack_len, dtype=jnp.float32)
    distance = jnp.abs(places[:, None] - places[None, :])
    piece = lax.all_gather(hidden_in, "wide", axis=0, tiled=True)
    tokens_all = piece
    qkv = jnp.einsum("rpd,dc->rpc", piece, w_qkv, preferred_element_type=jnp.float32).astype(
        jnp.bfloat16
    )
    masks = []
    contexts = []
    totals = []
    for index in range(packs):
        starts = jnp.repeat(seq_offsets[index], UNIT)
        same = starts[:, None] == starts[None, :]
        masks.append(same)
        queries = qkv[:, index, :width_e].reshape(pack_len, heads_local, HD)
        keys_all = qkv[:, index, width_e : 2 * width_e].reshape(pack_len, heads_local, HD)
        values_all = qkv[:, index, 2 * width_e :].reshape(pack_len, heads_local, HD)
        scores = scores_of(queries, keys_all, same, slope, distance, scale)
        highest = jnp.max(scores, axis=-1, keepdims=True)
        total = highest + jnp.log(jnp.sum(jnp.exp(scores - highest), axis=-1, keepdims=True))
        probs = jnp.exp(scores - total)
        context = jnp.einsum(
            "hqk,khd->qhd",
            probs.astype(jnp.bfloat16),
            values_all,
            preferred_element_type=jnp.float32,
        )
        contexts.append(context.reshape(pack_len, width_e).astype(jnp.bfloat16))
        totals.append(total)
    context_all = jnp.stack(contexts, axis=1)
    piece = context_all
    attn = lax.psum_scatter(
        jnp.einsum("rpe,de->rpd", piece, w_out, preferred_element_type=jnp.float32).astype(
            jnp.bfloat16
        ),
        "wide",
        scatter_dimension=0,
        tiled=True,
    ).astype(jnp.float32)
    tokens = hidden_in.astype(jnp.float32)
    r1 = jnp.transpose(tokens + attn, (1, 0, 2))
    mixed_p, dr1_p, ffn_grads, ln_rows = ffn_call(
        r1, jnp.transpose(cotangent, (1, 0, 2)), weights, ln_params
    )
    mixed = jnp.transpose(mixed_p, (1, 0, 2))
    grad_one = jnp.transpose(dr1_p, (1, 0, 2))

    def to_owner(grads):
        return jnp.where(valid[:, None], jnp.take(grads, source, axis=0), 0.0)

    ffn_owned = lax.psum_scatter(to_owner(ffn_grads), "seq", scatter_dimension=0, tiled=True)
    piece = lax.all_gather(grad_one.astype(jnp.bfloat16), "wide", axis=0, tiled=True)
    dattn_all = piece
    dcontext = jnp.einsum("rpd,de->rpe", piece, w_out, preferred_element_type=jnp.float32).astype(
        jnp.bfloat16
    )
    grad_out = jnp.einsum("rpd,rpe->de", dattn_all, context_all, preferred_element_type=jnp.float32)
    pieces = []
    for index in range(packs):
        queries = qkv[:, index, :width_e].reshape(pack_len, heads_local, HD)
        keys_all = qkv[:, index, width_e : 2 * width_e].reshape(pack_len, heads_local, HD)
        values_all = qkv[:, index, 2 * width_e :].reshape(pack_len, heads_local, HD)
        scores = scores_of(queries, keys_all, masks[index], slope, distance, scale)
        probs = jnp.exp(scores - totals[index])
        dctx = dcontext[:, index, :].reshape(pack_len, heads_local, HD)
        dprobs = jnp.einsum("qhd,khd->hqk", dctx, values_all, preferred_element_type=jnp.float32)
        dscaled = (
            probs * (dprobs - jnp.sum(probs * dprobs, axis=-1, keepdims=True)) * scale
        ).astype(jnp.bfloat16)
        dqueries = jnp.einsum("hqk,khd->qhd", dscaled, keys_all, preferred_element_type=jnp.float32)
        dkeys = jnp.einsum("hqk,qhd->khd", dscaled, queries, preferred_element_type=jnp.float32)
        dvalues = jnp.einsum(
            "hqk,qhd->khd", probs.astype(jnp.bfloat16), dctx, preferred_element_type=jnp.float32
        )
        pieces.append(
            jnp.concatenate(
                [
                    dqueries.reshape(pack_len, width_e),
                    dkeys.reshape(pack_len, width_e),
                    dvalues.reshape(pack_len, width_e),
                ],
                axis=1,
            ).astype(jnp.bfloat16)
        )
    d_qkv = jnp.stack(pieces, axis=1)
    grad_qkv = jnp.einsum("rpd,rpc->dc", tokens_all, d_qkv, preferred_element_type=jnp.float32)
    piece = d_qkv
    input_grad = grad_one + lax.psum_scatter(
        jnp.einsum("rpc,dc->rpd", piece, w_qkv, preferred_element_type=jnp.float32).astype(
            jnp.bfloat16
        ),
        "wide",
        scatter_dimension=0,
        tiled=True,
    ).astype(jnp.float32)
    attn_grads = jnp.concatenate([grad_qkv, grad_out], axis=1)
    attn_owned = lax.psum_scatter(to_owner(attn_grads), "seq", scatter_dimension=0, tiled=True)
    owned = jnp.concatenate([attn_owned, ffn_owned], axis=1)
    ln_grads = ln_rows[:4]
    squares, ln_total = lax.psum((jnp.sum(owned * owned), ln_grads), ("seq", "wide"))
    grad_norm = jnp.sqrt(squares + jnp.sum(ln_total * ln_total))
    clip = jnp.minimum(1.0, 1.0 / (grad_norm + 1e-06))
    seq_count = owner_blocks.shape[0]
    mine = jnp.arange(seq_count, dtype=jnp.int32) == lax.axis_index("seq")
    own_count = jnp.sum(jnp.where(mine, owner_blocks, 0))
    kept = (jnp.arange(slab_rows, dtype=jnp.int32) // block < own_count)[:, None]
    param_new, first_new, second_new = adamw(
        master, owned * clip, first_moment, second_moment, DECAY, RATE
    )
    norms_new, norms_first, norms_second = adamw(
        ln_params, ln_total * clip, ln_first, ln_second, 0.0, NORM_RATE
    )
    return (
        mixed,
        input_grad,
        jnp.where(kept, param_new, 0.0),
        jnp.where(kept, first_new, 0.0),
        jnp.where(kept, second_new, 0.0),
        norms_new,
        norms_first,
        norms_second,
        grad_norm,
    )


def solution(mesh):
    return jax.shard_map(
        per_device,
        mesh=mesh,
        in_specs=(
            P("wide", "seq", None),
            P("wide", "seq", None),
            P("seq", None),
            P(),
            P("seq", "wide"),
            P("seq", "wide"),
            P("seq", "wide"),
            P(),
            P(),
            P(),
        ),
        out_specs=(
            P("wide", "seq", None),
            P("wide", "seq", None),
            P("seq", "wide"),
            P("seq", "wide"),
            P("seq", "wide"),
            P(),
            P(),
            P(),
            P(),
        ),
        check_vma=False,
    )
```

```python
import jax
import jax.numpy as jnp
from jax import lax
from jax.experimental import pallas as pl
from jax.experimental.pallas import tpu as pltpu
from jax.sharding import PartitionSpec as P

MESH = pl.DeviceIdType.MESH

H = 12
HD = 64
FF = 3072
UNIT = 128
CAP = 6
STEP = 10


RATE = 0.02
NORM_RATE = 0.6
BETA_ONE = 0.9
BETA_TWO = 0.999
EPSILON = 1e-08
DECAY = 0.01
NORM_EPS = 1e-05
ROOT_HALF = 0.7071067811865476
DENSITY_SCALE = 0.3989422804014327
EPS = 1e-05
F32 = jnp.float32
BF16 = jnp.bfloat16
NEG = -1e30
VMEM_LIMIT = 60 * 2**20


def owner_maps(owner_blocks, rows, cap, block):
    ends = jnp.cumsum(owner_blocks)
    starts = ends - owner_blocks
    slot = jnp.arange(cap * block, dtype=jnp.int32)
    which = slot // block
    source = (starts[:, None] + which[None, :]) * block + (slot % block)[None, :]
    valid = which[None, :] < owner_blocks[:, None]
    source = jnp.where(valid, source, 0).reshape(-1)
    valid = valid.reshape(-1)
    param = jnp.arange(rows, dtype=jnp.int32)
    blocks = param // block
    owner = jnp.sum((ends[None, :] <= blocks[:, None]).astype(jnp.int32), axis=1)
    onehot = owner[:, None] == jnp.arange(owner_blocks.shape[0], dtype=jnp.int32)[None, :]
    first = jnp.sum(jnp.where(onehot, starts[None, :], 0), axis=1)
    target = owner * (cap * block) + (blocks - first) * block + param % block
    return (source, valid, target)


def adamw(param, grad, first, second, decay, rate):
    first_new = BETA_ONE * first + (1.0 - BETA_ONE) * grad
    second_new = BETA_TWO * second + (1.0 - BETA_TWO) * grad * grad
    first_hat = first_new / (1.0 - BETA_ONE**STEP)
    second_hat = second_new / (1.0 - BETA_TWO**STEP)
    param_new = param - rate * (first_hat / (jnp.sqrt(second_hat) + EPSILON) + decay * param)
    return (param_new, first_new, second_new)


def dot_nn(a, b):
    return lax.dot_general(a, b, (((1,), (0,)), ((), ())), preferred_element_type=F32)


def dot_nt(a, b):
    return lax.dot_general(a, b, (((1,), (1,)), ((), ())), preferred_element_type=F32)


def dot_tn(a, b):
    return lax.dot_general(a, b, (((0,), (0,)), ((), ())), preferred_element_type=F32)


def places():
    wide = lax.axis_index("wide")
    core = lax.rem(wide, 2)
    row = wide // 2
    return wide, core, row, wide + 1 - 2 * core, wide + 2 - 4 * row


def greet(mate, across):
    barrier = pltpu.get_barrier_semaphore()
    for peer in (mate, across):
        pl.semaphore_signal(barrier, inc=1, device_id={"wide": peer}, device_id_type=MESH)
    pl.semaphore_wait(barrier, 2)


def remote(source, target, send, recv, peer):
    return pltpu.make_async_remote_copy(
        src_ref=source,
        dst_ref=target,
        send_sem=send,
        recv_sem=recv,
        device_id={"wide": peer},
        device_id_type=MESH,
    )


class Gather:
    def __init__(self, held, send, recv, share):
        self.held, self.send, self.recv, self.share = held, send, recv, share
        _, self.core, self.row, self.mate, self.across = places()

    def rows(self, core, row):
        return pl.ds(pl.multiple_of((core * 2 + row) * self.share, self.share), self.share)

    def copy(self, pack, leg):
        row = 1 - self.row if leg == 2 else self.row
        block = self.held.at[pack, self.rows(self.core, row)]
        peer = self.mate if leg else self.across
        return remote(block, block, self.send.at[pack, leg], self.recv.at[pack, leg], peer)

    def start(self, pack):
        self.copy(pack, 0).start()
        self.copy(pack, 1).start()

    def finish(self, pack):
        self.copy(pack, 0).wait_recv()
        self.copy(pack, 2).start()
        self.copy(pack, 1).wait_recv()
        self.copy(pack, 2).wait_recv()

    def drain(self, pack):
        for leg in range(3):
            self.copy(pack, leg).wait_send()


class Scatter:
    def __init__(self, part, give, take, cross, reach, own, send, recv, share):
        self.part, self.give, self.take = part, give, take
        self.cross, self.reach, self.own = cross, reach, own
        self.send, self.recv, self.share = send, recv, share
        _, self.core, self.row, self.mate, self.across = places()

    def copy(self, pack, leg):
        source, target = (self.cross, self.reach) if leg else (self.give, self.take)
        peer = self.across if leg else self.mate
        return remote(
            source.at[pack], target.at[pack], self.send.at[pack, leg], self.recv.at[pack, leg], peer
        )

    def half(self, which):
        core = self.core if which else 1 - self.core
        return pl.multiple_of(core * 2 * self.share, 2 * self.share)

    def start(self, pack):
        self.copy(pack, 0).start()

    def middle(self, pack):
        self.copy(pack, 0).wait_recv()
        share = self.share
        far = pl.ds(pl.multiple_of((1 - self.row) * share, share), share)
        near = pl.ds(pl.multiple_of(self.row * share, share), share)
        self.cross[pack] = (self.part[far, :] + self.take[pack, far, :].astype(F32)).astype(BF16)
        self.copy(pack, 1).start()
        self.own[pack] = self.part[near, :] + self.take[pack, near, :].astype(F32)

    def finish(self, pack):
        self.copy(pack, 1).wait_recv()

    def drain(self, pack):
        for leg in range(2):
            self.copy(pack, leg).wait_send()


def scatter_scratch(packs, share, width):
    return [
        pltpu.VMEM((2 * share, width), F32),
        pltpu.VMEM((packs, 2 * share, width), BF16),
        pltpu.VMEM((packs, 2 * share, width), BF16),
        pltpu.VMEM((packs, share, width), BF16),
        pltpu.VMEM((packs, share, width), BF16),
        pltpu.VMEM((packs, share, width), F32),
    ]


def norm_parts(values):
    center = values - jnp.mean(values, axis=-1, keepdims=True)
    inverse = lax.rsqrt(jnp.mean(center * center, axis=-1, keepdims=True) + EPS)
    return center * inverse, inverse


def norm_pull(grad, normal, inverse, gain):
    scaled = grad * gain
    return inverse * (
        scaled
        - jnp.mean(scaled, axis=-1, keepdims=True)
        - normal * jnp.mean(scaled * normal, axis=-1, keepdims=True)
    )


def loop(count, body, unroll=1):
    def step(index, carry):
        body(index)
        return carry

    lax.fori_loop(0, count, step, 0, unroll=unroll)


def tile(index, size):
    return pl.ds(pl.multiple_of(index * size, size), size)


def ffn_kernel(
    r1_ref,
    cot_ref,
    w_ref,
    ln_ref,
    mixed_ref,
    dr1_ref,
    grads_ref,
    lngrad_ref,
    weights,
    held,
    held2,
    gates,
    ups,
    hid,
    dgate,
    dup,
    turned,
    turned2,
    total,
    g_tile,
    u_tile,
    send_a,
    recv_a,
    send_b,
    recv_b,
    send_c,
    recv_c,
    send_d,
    recv_d,
    load_sem,
    store_sem,
    *buffers,
):
    packs, share, width = r1_ref.shape
    rows = 4 * share
    fwd = buffers[:6]
    units = weights.shape[1] // 3
    col = 256
    n_units, n_width = units // col, width // col
    load = pltpu.make_async_copy(w_ref.at[:, pl.ds(w_ref.shape[1] - 3 * units, 3 * units)], weights, load_sem)
    load.start()
    _, core, row, mate, across = places()
    greet(mate, across)
    gather_one = Gather(held, send_a, recv_a, share)
    scatter_one = Scatter(*fwd, send_b, recv_b, share)
    gather_two = Gather(held2, send_c, recv_c, share)
    scatter_two = Scatter(*fwd, send_d, recv_d, share)
    gain1, shift1 = ln_ref[0:1, :], ln_ref[1:2, :]
    gain2, shift2 = ln_ref[2:3, :], ln_ref[3:4, :]
    lngrad_ref[...] = jnp.zeros_like(lngrad_ref)
    chunk = 64

    for pack in range(packs):
        base = pl.multiple_of((core * 2 + row) * share, share)

        def first(index, pack=pack, base=base):
            normal, _ = norm_parts(r1_ref[pack, tile(index, chunk), :])
            held[pack, pl.ds(pl.multiple_of(base + index * chunk, chunk), chunk), :] = (
                normal * gain1 + shift1
            ).astype(BF16)

        loop(share // chunk, first)
        gather_one.start(pack)
    load.wait()

    def forward(pack):
        gather_one.finish(pack)
        for which in range(2):
            base = scatter_one.half(which)
            big = pl.ds(base, 2 * share)

            def ff(index):
                cols = tile(index, col)
                x = held[pack, big, :]
                g_tile[...] = dot_nn(x, weights[:, cols])
                u_tile[...] = dot_nn(x, weights[:, pl.ds(pl.multiple_of(units + index * col, col), col)])

                def act(part):
                    rws = tile(part, 32)
                    gate, up = g_tile[rws, :], u_tile[rws, :]
                    out = pl.ds(pl.multiple_of(base + part * 32, 32), 32)
                    cumulative = 0.5 * (1.0 + lax.erf(gate * ROOT_HALF))
                    hid[out, cols] = (gate * cumulative * up).astype(BF16)
                    gates[pack, out, cols] = gate.astype(BF16)
                    ups[pack, out, cols] = up.astype(BF16)

                loop(2 * share // 32, act, unroll=2)

            loop(n_units, ff)

            def down(index):
                wd = weights[tile(index, col), pl.ds(2 * units, units)]
                value = dot_nt(hid[big, :], wd)
                if which:
                    scatter_one.part[:, tile(index, col)] = value
                else:
                    scatter_one.give[pack, :, tile(index, col)] = value.astype(BF16)

            loop(n_width, down)
            if not which:
                scatter_one.start(pack)
        scatter_one.middle(pack)

    def turn(pack):
        scatter_one.finish(pack)
        gather_two_base = pl.multiple_of((core * 2 + row) * share, share)

        def second(index):
            rws = tile(index, chunk)
            normal, _ = norm_parts(r1_ref[pack, rws, :])
            ffn = scatter_one.own[pack, rws, :] + scatter_one.reach[pack, rws, :].astype(F32)
            normal2, inverse2 = norm_parts(normal * gain1 + shift1 + ffn)
            mixed_ref[pack, rws, :] = (normal2 * gain2 + shift2).astype(BF16)
            grad = cot_ref[pack, rws, :].astype(F32)
            value = norm_pull(grad, normal2, inverse2, gain2)
            dr1_ref[pack, rws, :] = value
            held2[pack, pl.ds(pl.multiple_of(gather_two_base + index * chunk, chunk), chunk), :] = value.astype(BF16)
            lngrad_ref[2:3, :] += jnp.sum(grad * normal2, axis=0, keepdims=True)
            lngrad_ref[3:4, :] += jnp.sum(grad, axis=0, keepdims=True)

        loop(share // chunk, second)
        scatter_one.drain(pack)
        gather_two.start(pack)

    def backward(pack):
        gather_two.finish(pack)
        for which in range(2):
            base = scatter_two.half(which)
            big = pl.ds(base, 2 * share)

            def bf(index):
                cols = tile(index, col)
                g_tile[...] = dot_nn(
                    held2[pack, big, :], weights[:, pl.ds(pl.multiple_of(2 * units + index * col, col), col)]
                )

                def act(part):
                    rws = tile(part, 32)
                    out = pl.ds(pl.multiple_of(base + part * 32, 32), 32)
                    dhid = g_tile[rws, :]
                    gate = gates[pack, out, cols].astype(F32)
                    up = ups[pack, out, cols].astype(F32)
                    cumulative = 0.5 * (1.0 + lax.erf(gate * ROOT_HALF))
                    density = jnp.exp(-0.5 * gate * gate) * DENSITY_SCALE
                    value = gate * cumulative
                    hid[out, cols] = (value * up).astype(BF16)
                    dgate[out, cols] = (dhid * up * (cumulative + gate * density)).astype(BF16)
                    dup[out, cols] = (dhid * value).astype(BF16)

                loop(2 * share // 32, act, unroll=2)

            loop(n_units, bf)

            def back(index):
                rws = tile(index, col)
                value = dot_nt(dgate[big, :], weights[rws, pl.ds(0, units)]) + dot_nt(
                    dup[big, :], weights[rws, pl.ds(units, units)]
                )
                if which:
                    scatter_two.part[:, tile(index, col)] = value
                else:
                    scatter_two.give[pack, :, tile(index, col)] = value.astype(BF16)

            loop(n_width, back)
            if not which:
                scatter_two.start(pack)
        scatter_two.middle(pack)

    def weight_grads(pack):
        def flip(index):
            rws = tile(index, 256)
            turned[:, rws] = held[pack, rws, :].T
            turned2[:, rws] = held2[pack, rws, :].T

        loop(rows // 256, flip)

        def add(index):
            rws = tile(index, col)
            a = turned[rws, :]
            b = turned2[rws, :]
            parts = (dot_nn(a, dgate[...]), dot_nn(a, dup[...]), dot_nn(b, hid[...]))
            for place, value in enumerate(parts):
                cols = pl.ds(place * units, units)
                if pack == 0:
                    total[rws, cols] = value
                else:
                    value = total[rws, cols] + value
                    if pack < packs - 1:
                        total[rws, cols] = value
                    else:
                        gates[place, rws, :] = value.astype(BF16)

        loop(n_width, add)

    def last(pack):
        scatter_two.finish(pack)

        def third(index):
            rws = tile(index, chunk)
            normal, inverse = norm_parts(r1_ref[pack, rws, :])
            grad = dr1_ref[pack, rws, :] + (
                scatter_two.own[pack, rws, :] + scatter_two.reach[pack, rws, :].astype(F32)
            )
            dr1_ref[pack, rws, :] = norm_pull(grad, normal, inverse, gain1)
            lngrad_ref[0:1, :] += jnp.sum(grad * normal, axis=0, keepdims=True)
            lngrad_ref[1:2, :] += jnp.sum(grad, axis=0, keepdims=True)

        loop(share // chunk, third)

    for pack in range(packs):
        forward(pack)
        if pack:
            turn(pack - 1)
    for pack in range(packs):
        backward(pack)
        weight_grads(pack)
        if pack == 0:
            turn(packs - 1)
        else:
            last(pack - 1)
    outs = [
        pltpu.make_async_copy(
            gates.at[place, pl.ds(0, width)],
            grads_ref.at[:, pl.ds(place * units, units)],
            store_sem.at[place],
        )
        for place in range(3)
    ]
    for out in outs:
        out.start()
    last(packs - 1)
    for out in outs:
        out.wait()
    for pack in range(packs):
        gather_one.drain(pack)
        gather_two.drain(pack)
        scatter_two.drain(pack)


def ffn_call(r1, cot, weights, ln_params):
    packs, share, width = r1.shape
    rows = 4 * share
    units = (weights.shape[1] - width) // 3
    vm = pl.BlockSpec(memory_space=pltpu.VMEM)
    hb = pl.BlockSpec(memory_space=pl.ANY)
    dma = pltpu.SemaphoreType.DMA
    return pl.pallas_call(
        ffn_kernel,
        out_shape=(
            jax.ShapeDtypeStruct((packs, share, width), BF16),
            jax.ShapeDtypeStruct((packs, share, width), F32),
            jax.ShapeDtypeStruct((width, 3 * units), BF16),
            jax.ShapeDtypeStruct((8, width), F32),
        ),
        in_specs=[vm, vm, hb, vm],
        out_specs=(vm, vm, hb, vm),
        scratch_shapes=[
            pltpu.VMEM((width, 3 * units), BF16),
            pltpu.VMEM((packs, rows, width), BF16),
            pltpu.VMEM((packs, rows, width), BF16),
            pltpu.VMEM((packs, rows, units), BF16),
            pltpu.VMEM((packs, rows, units), BF16),
            pltpu.VMEM((rows, units), BF16),
            pltpu.VMEM((rows, units), BF16),
            pltpu.VMEM((rows, units), BF16),
            pltpu.VMEM((width, rows), BF16),
            pltpu.VMEM((width, rows), BF16),
            pltpu.VMEM((width, 3 * units), F32),
            pltpu.VMEM((2 * share, 256), F32),
            pltpu.VMEM((2 * share, 256), F32),
            dma((packs, 3)),
            dma((packs, 3)),
            dma((packs, 2)),
            dma((packs, 2)),
            dma((packs, 3)),
            dma((packs, 3)),
            dma((packs, 2)),
            dma((packs, 2)),
            dma(()),
            dma((3,)),
            *scatter_scratch(packs, share, width),
        ],
        compiler_params=pltpu.CompilerParams(
            collective_id=1, has_side_effects=True, vmem_limit_bytes=VMEM_LIMIT
        ),
        name="ffn",
    )(r1, cot, weights, ln_params)


class Runs:
    def __init__(self, offsets, pack):
        names = [offsets[pack, place] for place in range(8)]
        start = jnp.int32(4)
        for place in range(3, -1, -1):
            start = lax.select(names[place] == names[place + 3], jnp.int32(place), start)
        self.start = start
        self.names = [lax.select(start > place, names[place], names[place + 4]) for place in range(4)]

    def masks(self, index):
        own = self.names[0]
        for place in range(1, 4):
            own = lax.select(index == place, self.names[place], own)
        return [lax.select(own == name, jnp.float32(0.0), jnp.float32(NEG)) for name in self.names]

    def arrange(self, plain, order):
        for place in range(4):
            value = plain[held_run(place), :]
            for start in range(1, 5):
                value = lax.select(self.start == start, plain[held_run(place + start), :], value)
            order(pl.ds(place * UNIT, UNIT), value)
            value = lax.select(self.start > place, plain[held_run(place), :], plain[held_run(place + 4), :])
            order(pl.ds((place + 4) * UNIT, UNIT), value)

    def restore(self, order, plain):
        for run in range(8):
            first = max(0, run - 3)
            value = order[pl.ds((run - first) * UNIT, UNIT), :]
            for start in range(first + 1, min(run, 4) + 1):
                value = lax.select(self.start == start, order[pl.ds((run - start) * UNIT, UNIT), :], value)
            if run < 4:
                value = lax.select(self.start > run, order[pl.ds((run + 4) * UNIT, UNIT), :], value)
            else:
                value = lax.select(self.start <= run - 4, order[pl.ds(run * UNIT, UNIT), :], value)
            plain(held_run(run), value)


def held_run(run):
    half, part = divmod(run, 2)
    return pl.ds(((half % 2) * 2 + half // 2) * 2 * UNIT + part * UNIT, UNIT)


def writer(ref, *at):
    def write(rows, value):
        ref[(*at, rows, slice(None))] = value

    return write


def fill_bias(bias, slopes, wide):
    heads, size, _ = bias.shape

    def fill(index):
        rws = tile(index, UNIT)
        down = lax.broadcasted_iota(jnp.int32, (UNIT, size), 0) + index * UNIT
        along = lax.broadcasted_iota(jnp.int32, (UNIT, size), 1)
        distance = jnp.abs(down - along).astype(F32)
        for head in range(heads):
            bias[head, rws, :] = -slopes[wide * heads + head] * distance

    loop(size // UNIT, fill)


def split_weights(packed, w_qkv, w_out):
    width, each = packed.shape[0], packed.shape[1] // 4
    wide = w_out.shape[1]

    def part(index):
        rws = tile(index, 128)
        zeros = jnp.zeros((128, wide - each), BF16)
        for place in range(4):
            value = jnp.concatenate([packed[rws, pl.ds(place * each, each)], zeros], axis=1)
            if place < 3:
                w_qkv[rws, pl.ds(place * wide, wide)] = value
            else:
                w_out[rws, :] = value

    loop(width // 128, part)


def head_lanes():
    lane = lax.broadcasted_iota(jnp.int32, (1, 128), 1)
    return lane < HD


def attn_kernel(
    offsets_ref,
    slopes_ref,
    x_ref,
    w_ref,
    r1_ref,
    held_ref,
    qkv_ref,
    ctx_ref,
    packed,
    w_qkv,
    w_out,
    bias,
    held,
    plain,
    qkv,
    ctx_order,
    ctx,
    send_a,
    recv_a,
    send_b,
    recv_b,
    load_sem,
    store_sem,
    *buffers,
):
    packs, share, width = x_ref.shape
    rows = 4 * share
    lanes = w_out.shape[1]
    group = rows // 2
    load = pltpu.make_async_copy(w_ref.at[:, pl.ds(0, packed.shape[1])], packed, load_sem)
    load.start()
    wide, core, row, mate, across = places()
    greet(mate, across)
    gather = Gather(held, send_a, recv_a, share)
    scatter = Scatter(*buffers, send_b, recv_b, share)
    base = pl.multiple_of((core * 2 + row) * share, share)
    for pack in range(packs):
        held[pack, pl.ds(base, share), :] = x_ref[pack]
        gather.start(pack)
    fill_bias(bias, slopes_ref, wide)
    load.wait()
    split_weights(packed, w_qkv, w_out)
    low = head_lanes()
    stores = []

    def attend(pack):
        runs = Runs(offsets_ref, pack)
        gather.finish(pack)

        def project(index):
            rws = tile(index, 256)
            plain[rws, :] = dot_nn(held[pack, rws, :], w_qkv[...]).astype(BF16)

        loop(rows // 256, project)
        runs.arrange(plain, writer(qkv, pack))
        for side in range(2):
            keys = pl.ds(side * group, group)

            def chunk(index, side=side, keys=keys, pack=pack):
                rws = pl.ds(pl.multiple_of(side * group + index * UNIT, UNIT), UNIT)
                if side:
                    mask = jnp.concatenate(
                        [jnp.full((1, UNIT), part, F32) for part in runs.masks(index)], axis=1
                    )
                outs = []
                for head in range(3):
                    block = pl.ds(0 if head < 2 else 128, 128)
                    queries = qkv[pack, rws, block]
                    if head < 2:
                        queries = jnp.where(low if head == 0 else ~low, queries, jnp.zeros_like(queries))
                    k_block = pl.ds(lanes + (0 if head < 2 else 128), 128)
                    v_block = pl.ds(2 * lanes + (0 if head < 2 else 128), 128)
                    scores = dot_nt(queries, qkv[pack, keys, k_block]) * HD ** (-0.5)
                    scores = scores + bias[head, tile(index, UNIT), :]
                    if side:
                        scores = scores + mask
                    powers = jnp.exp(scores - jnp.max(scores, axis=-1, keepdims=True))
                    total = jnp.sum(powers, axis=-1, keepdims=True)
                    outs.append(dot_nn(powers.astype(BF16), qkv[pack, keys, v_block]) / total)
                ctx_order[rws, pl.ds(0, 128)] = jnp.where(low, outs[0], outs[1]).astype(BF16)
                ctx_order[rws, pl.ds(128, 128)] = outs[2].astype(BF16)

            loop(4, chunk)
        runs.restore(ctx_order, writer(ctx, pack))
        for which in range(2):
            big = pl.ds(scatter.half(which), 2 * share)

            def out(index, which=which, big=big):
                cols = tile(index, 256)
                value = dot_nt(ctx[pack, big, :], w_out[cols, :])
                if which:
                    scatter.part[:, cols] = value
                else:
                    scatter.give[pack, :, cols] = value.astype(BF16)

            loop(width // 256, out)
            if not which:
                scatter.start(pack)
        scatter.middle(pack)
        for place, (source, target) in enumerate(((held, held_ref), (qkv, qkv_ref), (ctx, ctx_ref))):
            copy = pltpu.make_async_copy(source.at[pack], target.at[pack], store_sem.at[pack, place])
            copy.start()
            stores.append(copy)

    def settle(pack):
        scatter.finish(pack)

        def add(index):
            rws = tile(index, 64)
            attn = scatter.own[pack, rws, :] + scatter.reach[pack, rws, :].astype(F32)
            r1_ref[pack, rws, :] = x_ref[pack, rws, :].astype(F32) + attn

        loop(share // 64, add)

    for pack in range(packs):
        attend(pack)
        if pack:
            settle(pack - 1)
    settle(packs - 1)
    for copy in stores:
        copy.wait()
    for pack in range(packs):
        gather.drain(pack)
        scatter.drain(pack)


def back_kernel(
    offsets_ref,
    slopes_ref,
    dr1_ref,
    w_ref,
    x_ref,
    qkv_ref,
    ctx_ref,
    grad_ref,
    grads_ref,
    packed,
    w_qkv,
    w_out,
    bias,
    held,
    x_all,
    qkv,
    ctx,
    plain,
    dctx,
    dorder,
    dplain,
    sum_k,
    sum_v,
    turned,
    total,
    total_out,
    send_a,
    recv_a,
    send_b,
    recv_b,
    load_sem,
    fetch_sem,
    *buffers,
):
    packs, share, width = dr1_ref.shape
    rows = 4 * share
    lanes = w_out.shape[1]
    group = rows // 2
    load = pltpu.make_async_copy(w_ref.at[:, pl.ds(0, packed.shape[1])], packed, load_sem)
    load.start()
    fetches = []
    for pack in range(packs):
        for place, (source, target) in enumerate(((x_ref, x_all), (qkv_ref, qkv), (ctx_ref, ctx))):
            copy = pltpu.make_async_copy(source.at[pack], target.at[pack], fetch_sem.at[pack, place])
            copy.start()
            fetches.append(copy)
    wide, core, row, mate, across = places()
    greet(mate, across)
    gather = Gather(held, send_a, recv_a, share)
    scatter = Scatter(*buffers, send_b, recv_b, share)
    base = pl.multiple_of((core * 2 + row) * share, share)
    for pack in range(packs):
        held[pack, pl.ds(base, share), :] = dr1_ref[pack].astype(BF16)
        gather.start(pack)
    fill_bias(bias, slopes_ref, wide)
    load.wait()
    split_weights(packed, w_qkv, w_out)
    low = head_lanes()
    scale = HD ** (-0.5)

    def pull(pack):
        runs = Runs(offsets_ref, pack)
        gather.finish(pack)

        def project(index):
            rws = tile(index, 256)
            plain[rws, :] = dot_nn(held[pack, rws, :], w_out[...]).astype(BF16)

        loop(rows // 256, project)
        runs.arrange(plain, writer(dctx))
        for copy in fetches[3 * pack : 3 * pack + 3]:
            copy.wait()
        for side in range(2):
            keys = pl.ds(side * group, group)
            sum_k[...] = jnp.zeros_like(sum_k)
            sum_v[...] = jnp.zeros_like(sum_v)

            def chunk(index, side=side, keys=keys, pack=pack):
                rws = pl.ds(pl.multiple_of(side * group + index * UNIT, UNIT), UNIT)
                masks = runs.masks(index)
                for part in range(2):
                    heads = (0, 1) if part == 0 else (2,)
                    block = pl.ds(part * 128, 128)
                    k_block = pl.ds(lanes + part * 128, 128)
                    v_block = pl.ds(2 * lanes + part * 128, 128)
                    k_all, v_all = qkv[pack, keys, k_block], qkv[pack, keys, v_block]
                    dq = None
                    for head in heads:
                        queries, dout, k_own = qkv[pack, rws, block], dctx[rws, block], k_all
                        if part == 0:
                            keep = low if head == 0 else ~low
                            queries = jnp.where(keep, queries, jnp.zeros_like(queries))
                            dout = jnp.where(keep, dout, jnp.zeros_like(dout))
                            k_own = jnp.where(keep, k_own, jnp.zeros_like(k_own))
                        scores = dot_nt(k_all, queries) * scale + bias[head, :, tile(index, UNIT)]
                        if side:
                            scores = jnp.concatenate(
                                [scores[t * UNIT : (t + 1) * UNIT] + masks[t] for t in range(4)], axis=0
                            )
                        powers = jnp.exp(scores - jnp.max(scores, axis=0, keepdims=True))
                        probs = powers * (1.0 / jnp.sum(powers, axis=0, keepdims=True))
                        dprobs = dot_nt(v_all, dout)
                        delta = jnp.sum(probs * dprobs, axis=0, keepdims=True)
                        dscaled = (probs * (dprobs - delta) * scale).astype(BF16)
                        sum_v[:, block] += dot_nn(probs.astype(BF16), dout)
                        sum_k[:, block] += dot_nn(dscaled, queries)
                        term = dot_tn(dscaled, k_own)
                        dq = term if dq is None else dq + term
                    dorder[rws, block] = dq.astype(BF16)

            loop(4, chunk)
            dorder[keys, pl.ds(lanes, lanes)] = sum_k[...].astype(BF16)
            dorder[keys, pl.ds(2 * lanes, lanes)] = sum_v[...].astype(BF16)
        runs.restore(dorder, writer(dplain))
        for which in range(2):
            big = pl.ds(scatter.half(which), 2 * share)

            def out(index, which=which, big=big):
                cols = tile(index, 256)
                value = dot_nt(dplain[big, :], w_qkv[cols, :])
                if which:
                    scatter.part[:, cols] = value
                else:
                    scatter.give[pack, :, cols] = value.astype(BF16)

            loop(width // 256, out)
            if not which:
                scatter.start(pack)
        scatter.middle(pack)

    def weight_grads(pack):
        for source, result, target in ((x_all, dplain, total), (held, ctx.at[pack], total_out)):

            def flip(index, source=source):
                rws = tile(index, 256)
                turned[:, rws] = source[pack, rws, :].T

            loop(rows // 256, flip)

            def add(index, result=result, target=target):
                rws = tile(index, 256)
                value = dot_nn(turned[rws, :], result[...])
                if pack:
                    value = value + target[rws, :]
                target[rws, :] = value

            loop(width // 256, add)

    def settle(pack):
        scatter.finish(pack)

        def add(index):
            rws = tile(index, 64)
            grad_ref[pack, rws, :] = dr1_ref[pack, rws, :] + (
                scatter.own[pack, rws, :] + scatter.reach[pack, rws, :].astype(F32)
            )

        loop(share // 64, add)

    for pack in range(packs):
        pull(pack)
        weight_grads(pack)
        if pack:
            settle(pack - 1)
    each = width // 4

    def pack_up(index):
        rws = tile(index, 128)
        pieces = [total[rws, pl.ds(place * lanes, each)] for place in range(3)]
        pieces.append(total_out[rws, pl.ds(0, each)])
        grads_ref[rws, :] = jnp.concatenate([piece.astype(BF16) for piece in pieces], axis=1)

    loop(width // 128, pack_up)
    settle(packs - 1)
    for pack in range(packs):
        gather.drain(pack)
        scatter.drain(pack)


def attn_call(x, weights, offsets, slopes):
    packs, share, width = x.shape
    rows = 4 * share
    lanes = 256
    vm = pl.BlockSpec(memory_space=pltpu.VMEM)
    hb = pl.BlockSpec(memory_space=pl.ANY)
    sm = pl.BlockSpec(memory_space=pltpu.SMEM)
    dma = pltpu.SemaphoreType.DMA
    return pl.pallas_call(
        attn_kernel,
        out_shape=(
            jax.ShapeDtypeStruct((packs, share, width), F32),
            jax.ShapeDtypeStruct((packs, rows, width), BF16),
            jax.ShapeDtypeStruct((packs, rows, 3 * lanes), BF16),
            jax.ShapeDtypeStruct((packs, rows, lanes), BF16),
        ),
        in_specs=[sm, sm, vm, hb],
        out_specs=(vm, hb, hb, hb),
        scratch_shapes=[
            pltpu.VMEM((width, width), BF16),
            pltpu.VMEM((width, 3 * lanes), BF16),
            pltpu.VMEM((width, lanes), BF16),
            pltpu.VMEM((3, rows // 2, rows // 2), F32),
            pltpu.VMEM((packs, rows, width), BF16),
            pltpu.VMEM((rows, 3 * lanes), BF16),
            pltpu.VMEM((packs, rows, 3 * lanes), BF16),
            pltpu.VMEM((rows, lanes), BF16),
            pltpu.VMEM((packs, rows, lanes), BF16),
            dma((packs, 3)),
            dma((packs, 3)),
            dma((packs, 2)),
            dma((packs, 2)),
            dma(()),
            dma((packs, 3)),
            *scatter_scratch(packs, share, width),
        ],
        compiler_params=pltpu.CompilerParams(
            collective_id=2, has_side_effects=True, vmem_limit_bytes=VMEM_LIMIT
        ),
        name="attn",
    )(offsets, slopes, x, weights)


def back_call(dr1, weights, x_all, qkv, ctx, offsets, slopes):
    packs, share, width = dr1.shape
    rows = 4 * share
    lanes = 256
    vm = pl.BlockSpec(memory_space=pltpu.VMEM)
    hb = pl.BlockSpec(memory_space=pl.ANY)
    sm = pl.BlockSpec(memory_space=pltpu.SMEM)
    dma = pltpu.SemaphoreType.DMA
    return pl.pallas_call(
        back_kernel,
        out_shape=(
            jax.ShapeDtypeStruct((packs, share, width), F32),
            jax.ShapeDtypeStruct((width, width), BF16),
        ),
        in_specs=[sm, sm, vm, hb, hb, hb, hb],
        out_specs=(vm, vm),
        scratch_shapes=[
            pltpu.VMEM((width, width), BF16),
            pltpu.VMEM((width, 3 * lanes), BF16),
            pltpu.VMEM((width, lanes), BF16),
            pltpu.VMEM((3, rows // 2, rows // 2), F32),
            pltpu.VMEM((packs, rows, width), BF16),
            pltpu.VMEM((packs, rows, width), BF16),
            pltpu.VMEM((packs, rows, 3 * lanes), BF16),
            pltpu.VMEM((packs, rows, lanes), BF16),
            pltpu.VMEM((rows, lanes), BF16),
            pltpu.VMEM((rows, lanes), BF16),
            pltpu.VMEM((rows, 3 * lanes), BF16),
            pltpu.VMEM((rows, 3 * lanes), BF16),
            pltpu.VMEM((rows // 2, lanes), F32),
            pltpu.VMEM((rows // 2, lanes), F32),
            pltpu.VMEM((width, rows), BF16),
            pltpu.VMEM((width, 3 * lanes), F32),
            pltpu.VMEM((width, lanes), F32),
            dma((packs, 3)),
            dma((packs, 3)),
            dma((packs, 2)),
            dma((packs, 2)),
            dma(()),
            dma((packs, 3)),
            *scatter_scratch(packs, share, width),
        ],
        compiler_params=pltpu.CompilerParams(
            collective_id=3, has_side_effects=True, vmem_limit_bytes=VMEM_LIMIT
        ),
        name="back",
    )(offsets, slopes, dr1, weights, x_all, qkv, ctx)


def per_device(
    hidden_in,
    cotangent,
    seq_offsets,
    owner_blocks,
    master,
    first_moment,
    second_moment,
    ln_params,
    ln_first,
    ln_second,
):
    width = hidden_in.shape[2]
    slab_rows = master.shape[0]
    block = slab_rows // CAP
    source, valid, target = owner_maps(owner_blocks, width, CAP, block)
    gathered = lax.all_gather(master.astype(jnp.bfloat16), "seq", axis=0, tiled=True)
    weights = jnp.take(gathered, target, axis=0)
    slopes = jnp.exp2(-8.0 * (jnp.arange(H, dtype=jnp.float32) + 1.0) / H)
    x = jnp.transpose(hidden_in, (1, 0, 2))
    r1, x_all, qkv, ctx = attn_call(x, weights, seq_offsets, slopes)
    mixed_p, dr1_p, ffn_grads, ln_rows = ffn_call(
        r1, jnp.transpose(cotangent, (1, 0, 2)), weights, ln_params
    )
    mixed = jnp.transpose(mixed_p, (1, 0, 2))

    def to_owner(grads):
        return jnp.where(valid[:, None], jnp.take(grads, source, axis=0), 0.0)

    ffn_owned = lax.psum_scatter(to_owner(ffn_grads), "seq", scatter_dimension=0, tiled=True)
    grad_p, attn_grads = back_call(dr1_p, weights, x_all, qkv, ctx, seq_offsets, slopes)
    input_grad = jnp.transpose(grad_p, (1, 0, 2))
    attn_owned = lax.psum_scatter(to_owner(attn_grads), "seq", scatter_dimension=0, tiled=True)
    owned = jnp.concatenate([attn_owned, ffn_owned], axis=1).astype(jnp.float32)
    ln_grads = ln_rows[:4]
    squares, ln_total = lax.psum((jnp.sum(owned * owned), ln_grads), ("seq", "wide"))
    grad_norm = jnp.sqrt(squares + jnp.sum(ln_total * ln_total))
    clip = jnp.minimum(1.0, 1.0 / (grad_norm + 1e-06))
    seq_count = owner_blocks.shape[0]
    mine = jnp.arange(seq_count, dtype=jnp.int32) == lax.axis_index("seq")
    own_count = jnp.sum(jnp.where(mine, owner_blocks, 0))
    kept = (jnp.arange(slab_rows, dtype=jnp.int32) // block < own_count)[:, None]
    param_new, first_new, second_new = adamw(
        master, owned * clip, first_moment, second_moment, DECAY, RATE
    )
    norms_new, norms_first, norms_second = adamw(
        ln_params, ln_total * clip, ln_first, ln_second, 0.0, NORM_RATE
    )
    return (
        mixed,
        input_grad,
        jnp.where(kept, param_new, 0.0),
        jnp.where(kept, first_new, 0.0),
        jnp.where(kept, second_new, 0.0),
        norms_new,
        norms_first,
        norms_second,
        grad_norm,
    )


def solution(mesh):
    return jax.shard_map(
        per_device,
        mesh=mesh,
        in_specs=(
            P("wide", "seq", None),
            P("wide", "seq", None),
            P("seq", None),
            P(),
            P("seq", "wide"),
            P("seq", "wide"),
            P("seq", "wide"),
            P(),
            P(),
            P(),
        ),
        out_specs=(
            P("wide", "seq", None),
            P("wide", "seq", None),
            P("seq", "wide"),
            P("seq", "wide"),
            P("seq", "wide"),
            P(),
            P(),
            P(),
            P(),
        ),
        check_vma=False,
    )
```

```python
import functools

import jax
import jax.numpy as jnp
from jax import lax
from jax.experimental import pallas as pl
from jax.experimental.pallas import tpu as pltpu
from jax.sharding import PartitionSpec as P

MESH = pl.DeviceIdType.MESH

H = 12
HD = 64
FF = 3072
UNIT = 128
CAP = 6
STEP = 10


RATE = 0.02
NORM_RATE = 0.6
BETA_ONE = 0.9
BETA_TWO = 0.999
EPSILON = 1e-08
DECAY = 0.01
NORM_EPS = 1e-05
ROOT_HALF = 0.7071067811865476
DENSITY_SCALE = 0.3989422804014327
EPS = 1e-05
F32 = jnp.float32
BF16 = jnp.bfloat16
NEG = -1e30
VMEM_LIMIT = 60 * 2**20


def owner_maps(owner_blocks, rows, cap, block):
    ends = jnp.cumsum(owner_blocks)
    starts = ends - owner_blocks
    slot = jnp.arange(cap * block, dtype=jnp.int32)
    which = slot // block
    source = (starts[:, None] + which[None, :]) * block + (slot % block)[None, :]
    valid = which[None, :] < owner_blocks[:, None]
    source = jnp.where(valid, source, 0).reshape(-1)
    valid = valid.reshape(-1)
    param = jnp.arange(rows, dtype=jnp.int32)
    blocks = param // block
    owner = jnp.sum((ends[None, :] <= blocks[:, None]).astype(jnp.int32), axis=1)
    onehot = owner[:, None] == jnp.arange(owner_blocks.shape[0], dtype=jnp.int32)[None, :]
    first = jnp.sum(jnp.where(onehot, starts[None, :], 0), axis=1)
    target = owner * (cap * block) + (blocks - first) * block + param % block
    return (source, valid, target)


def adamw(param, grad, first, second, decay, rate):
    first_new = BETA_ONE * first + (1.0 - BETA_ONE) * grad
    second_new = BETA_TWO * second + (1.0 - BETA_TWO) * grad * grad
    first_hat = first_new / (1.0 - BETA_ONE**STEP)
    second_hat = second_new / (1.0 - BETA_TWO**STEP)
    param_new = param - rate * (first_hat / (jnp.sqrt(second_hat) + EPSILON) + decay * param)
    return (param_new, first_new, second_new)


def dot_nn(a, b):
    return lax.dot_general(a, b, (((1,), (0,)), ((), ())), preferred_element_type=F32)


def dot_nt(a, b):
    return lax.dot_general(a, b, (((1,), (1,)), ((), ())), preferred_element_type=F32)


def dot_tn(a, b):
    return lax.dot_general(a, b, (((0,), (0,)), ((), ())), preferred_element_type=F32)


def places():
    wide = lax.axis_index("wide")
    core = lax.rem(wide, 2)
    row = wide // 2
    return wide, core, row, wide + 1 - 2 * core, wide + 2 - 4 * row


def greet(mate, across):
    barrier = pltpu.get_barrier_semaphore()
    for peer in (mate, across):
        pl.semaphore_signal(barrier, inc=1, device_id={"wide": peer}, device_id_type=MESH)
    pl.semaphore_wait(barrier, 2)


def remote(source, target, send, recv, peer, axis="wide"):
    return pltpu.make_async_remote_copy(
        src_ref=source,
        dst_ref=target,
        send_sem=send,
        recv_sem=recv,
        device_id={axis: peer},
        device_id_type=MESH,
    )


class Gather:
    def __init__(self, held, send, recv, share):
        self.held, self.send, self.recv, self.share = held, send, recv, share
        _, self.core, self.row, self.mate, self.across = places()

    def rows(self, core, row):
        return pl.ds(pl.multiple_of((core * 2 + row) * self.share, self.share), self.share)

    def copy(self, pack, leg):
        row = 1 - self.row if leg == 2 else self.row
        block = self.held.at[pack, self.rows(self.core, row)]
        peer = self.mate if leg else self.across
        return remote(block, block, self.send.at[pack, leg], self.recv.at[pack, leg], peer)

    def start(self, pack):
        self.copy(pack, 0).start()
        self.copy(pack, 1).start()

    def finish(self, pack):
        self.copy(pack, 0).wait_recv()
        self.copy(pack, 2).start()
        self.copy(pack, 1).wait_recv()
        self.copy(pack, 2).wait_recv()

    def drain(self, pack):
        for leg in range(3):
            self.copy(pack, leg).wait_send()


class Scatter:
    def __init__(self, part, give, take, cross, reach, own, send, recv, share):
        self.part, self.give, self.take = part, give, take
        self.cross, self.reach, self.own = cross, reach, own
        self.send, self.recv, self.share = send, recv, share
        _, self.core, self.row, self.mate, self.across = places()

    def copy(self, pack, leg):
        source, target = (self.cross, self.reach) if leg else (self.give, self.take)
        peer = self.across if leg else self.mate
        return remote(
            source.at[pack], target.at[pack], self.send.at[pack, leg], self.recv.at[pack, leg], peer
        )

    def half(self, which):
        core = self.core if which else 1 - self.core
        return pl.multiple_of(core * 2 * self.share, 2 * self.share)

    def start(self, pack):
        self.copy(pack, 0).start()

    def middle(self, pack):
        self.copy(pack, 0).wait_recv()
        share = self.share
        far = pl.ds(pl.multiple_of((1 - self.row) * share, share), share)
        near = pl.ds(pl.multiple_of(self.row * share, share), share)
        self.cross[pack] = (self.part[far, :] + self.take[pack, far, :].astype(F32)).astype(BF16)
        self.copy(pack, 1).start()
        self.own[pack] = self.part[near, :] + self.take[pack, near, :].astype(F32)

    def finish(self, pack):
        self.copy(pack, 1).wait_recv()

    def drain(self, pack):
        for leg in range(2):
            self.copy(pack, leg).wait_send()


def scatter_scratch(packs, share, width):
    return [
        pltpu.VMEM((2 * share, width), F32),
        pltpu.VMEM((packs, 2 * share, width), BF16),
        pltpu.VMEM((packs, 2 * share, width), BF16),
        pltpu.VMEM((packs, share, width), BF16),
        pltpu.VMEM((packs, share, width), BF16),
        pltpu.VMEM((packs, share, width), F32),
    ]


def norm_parts(values):
    center = values - jnp.mean(values, axis=-1, keepdims=True)
    inverse = lax.rsqrt(jnp.mean(center * center, axis=-1, keepdims=True) + EPS)
    return center * inverse, inverse


def norm_pull(grad, normal, inverse, gain):
    scaled = grad * gain
    return inverse * (
        scaled
        - jnp.mean(scaled, axis=-1, keepdims=True)
        - normal * jnp.mean(scaled * normal, axis=-1, keepdims=True)
    )


def loop(count, body, unroll=1):
    def step(index, carry):
        body(index)
        return carry

    lax.fori_loop(0, count, step, 0, unroll=unroll)


def tile(index, size):
    return pl.ds(pl.multiple_of(index * size, size), size)


def ffn_kernel(
    r1_ref,
    cot_ref,
    w_ref,
    ln_ref,
    mixed_ref,
    dr1_ref,
    grads_ref,
    lngrad_ref,
    weights,
    held,
    held2,
    gates,
    ups,
    hid,
    dgate,
    dup,
    turned,
    turned2,
    total,
    g_tile,
    u_tile,
    send_a,
    recv_a,
    send_b,
    recv_b,
    send_c,
    recv_c,
    send_d,
    recv_d,
    load_sem,
    store_sem,
    *buffers,
):
    packs, share, width = r1_ref.shape
    rows = 4 * share
    fwd = buffers[:6]
    units = weights.shape[1] // 3
    col = 256
    n_units, n_width = units // col, width // col
    load = pltpu.make_async_copy(w_ref.at[:, pl.ds(w_ref.shape[1] - 3 * units, 3 * units)], weights, load_sem)
    load.start()
    _, core, row, mate, across = places()
    greet(mate, across)
    gather_one = Gather(held, send_a, recv_a, share)
    scatter_one = Scatter(*fwd, send_b, recv_b, share)
    gather_two = Gather(held2, send_c, recv_c, share)
    scatter_two = Scatter(*fwd, send_d, recv_d, share)
    gain1, shift1 = ln_ref[0:1, :], ln_ref[1:2, :]
    gain2, shift2 = ln_ref[2:3, :], ln_ref[3:4, :]
    lngrad_ref[...] = jnp.zeros_like(lngrad_ref)
    chunk = 64

    for pack in range(packs):
        base = pl.multiple_of((core * 2 + row) * share, share)

        def first(index, pack=pack, base=base):
            normal, _ = norm_parts(r1_ref[pack, tile(index, chunk), :])
            held[pack, pl.ds(pl.multiple_of(base + index * chunk, chunk), chunk), :] = (
                normal * gain1 + shift1
            ).astype(BF16)

        loop(share // chunk, first)
        gather_one.start(pack)
    load.wait()

    def forward(pack):
        gather_one.finish(pack)
        for which in range(2):
            base = scatter_one.half(which)
            big = pl.ds(base, 2 * share)

            def ff(index):
                cols = tile(index, col)
                x = held[pack, big, :]
                g_tile[...] = dot_nn(x, weights[:, cols])
                u_tile[...] = dot_nn(x, weights[:, pl.ds(pl.multiple_of(units + index * col, col), col)])

                def act(part):
                    rws = tile(part, 32)
                    gate, up = g_tile[rws, :], u_tile[rws, :]
                    out = pl.ds(pl.multiple_of(base + part * 32, 32), 32)
                    cumulative = 0.5 * (1.0 + lax.erf(gate * ROOT_HALF))
                    hid[out, cols] = (gate * cumulative * up).astype(BF16)
                    gates[pack, out, cols] = gate.astype(BF16)
                    ups[pack, out, cols] = up.astype(BF16)

                loop(2 * share // 32, act, unroll=2)

            loop(n_units, ff)

            def down(index):
                wd = weights[tile(index, col), pl.ds(2 * units, units)]
                value = dot_nt(hid[big, :], wd)
                if which:
                    scatter_one.part[:, tile(index, col)] = value
                else:
                    scatter_one.give[pack, :, tile(index, col)] = value.astype(BF16)

            loop(n_width, down)
            if not which:
                scatter_one.start(pack)
        scatter_one.middle(pack)

    def turn(pack):
        scatter_one.finish(pack)
        gather_two_base = pl.multiple_of((core * 2 + row) * share, share)

        def second(index):
            rws = tile(index, chunk)
            normal, _ = norm_parts(r1_ref[pack, rws, :])
            ffn = scatter_one.own[pack, rws, :] + scatter_one.reach[pack, rws, :].astype(F32)
            normal2, inverse2 = norm_parts(normal * gain1 + shift1 + ffn)
            mixed_ref[pack, rws, :] = (normal2 * gain2 + shift2).astype(BF16)
            grad = cot_ref[pack, rws, :].astype(F32)
            value = norm_pull(grad, normal2, inverse2, gain2)
            dr1_ref[pack, rws, :] = value
            held2[pack, pl.ds(pl.multiple_of(gather_two_base + index * chunk, chunk), chunk), :] = value.astype(BF16)
            lngrad_ref[2:3, :] += jnp.sum(grad * normal2, axis=0, keepdims=True)
            lngrad_ref[3:4, :] += jnp.sum(grad, axis=0, keepdims=True)

        loop(share // chunk, second)
        scatter_one.drain(pack)
        gather_two.start(pack)

    def backward(pack):
        gather_two.finish(pack)
        for which in range(2):
            base = scatter_two.half(which)
            big = pl.ds(base, 2 * share)

            def bf(index):
                cols = tile(index, col)
                g_tile[...] = dot_nn(
                    held2[pack, big, :], weights[:, pl.ds(pl.multiple_of(2 * units + index * col, col), col)]
                )

                def act(part):
                    rws = tile(part, 32)
                    out = pl.ds(pl.multiple_of(base + part * 32, 32), 32)
                    dhid = g_tile[rws, :]
                    gate = gates[pack, out, cols].astype(F32)
                    up = ups[pack, out, cols].astype(F32)
                    cumulative = 0.5 * (1.0 + lax.erf(gate * ROOT_HALF))
                    density = jnp.exp(-0.5 * gate * gate) * DENSITY_SCALE
                    value = gate * cumulative
                    hid[out, cols] = (value * up).astype(BF16)
                    dgate[out, cols] = (dhid * up * (cumulative + gate * density)).astype(BF16)
                    dup[out, cols] = (dhid * value).astype(BF16)

                loop(2 * share // 32, act, unroll=2)

            loop(n_units, bf)

            def back(index):
                rws = tile(index, col)
                value = dot_nt(dgate[big, :], weights[rws, pl.ds(0, units)]) + dot_nt(
                    dup[big, :], weights[rws, pl.ds(units, units)]
                )
                if which:
                    scatter_two.part[:, tile(index, col)] = value
                else:
                    scatter_two.give[pack, :, tile(index, col)] = value.astype(BF16)

            loop(n_width, back)
            if not which:
                scatter_two.start(pack)
        scatter_two.middle(pack)

    def weight_grads(pack):
        def flip(index):
            rws = tile(index, 256)
            turned[:, rws] = held[pack, rws, :].T
            turned2[:, rws] = held2[pack, rws, :].T

        loop(rows // 256, flip)

        def add(index):
            rws = tile(index, col)
            a = turned[rws, :]
            b = turned2[rws, :]
            parts = (dot_nn(a, dgate[...]), dot_nn(a, dup[...]), dot_nn(b, hid[...]))
            for place, value in enumerate(parts):
                cols = pl.ds(place * units, units)
                if pack == 0:
                    total[rws, cols] = value
                else:
                    value = total[rws, cols] + value
                    if pack < packs - 1:
                        total[rws, cols] = value
                    else:
                        gates[place, rws, :] = value.astype(BF16)

        loop(n_width, add)

    def last(pack):
        scatter_two.finish(pack)

        def third(index):
            rws = tile(index, chunk)
            normal, inverse = norm_parts(r1_ref[pack, rws, :])
            grad = dr1_ref[pack, rws, :] + (
                scatter_two.own[pack, rws, :] + scatter_two.reach[pack, rws, :].astype(F32)
            )
            dr1_ref[pack, rws, :] = norm_pull(grad, normal, inverse, gain1)
            lngrad_ref[0:1, :] += jnp.sum(grad * normal, axis=0, keepdims=True)
            lngrad_ref[1:2, :] += jnp.sum(grad, axis=0, keepdims=True)

        loop(share // chunk, third)

    for pack in range(packs):
        forward(pack)
        if pack:
            turn(pack - 1)
    for pack in range(packs):
        backward(pack)
        weight_grads(pack)
        if pack == 0:
            turn(packs - 1)
        else:
            last(pack - 1)
    outs = [
        pltpu.make_async_copy(
            gates.at[place, pl.ds(0, width)],
            grads_ref.at[:, pl.ds(place * units, units)],
            store_sem.at[place],
        )
        for place in range(3)
    ]
    for out in outs:
        out.start()
    last(packs - 1)
    for out in outs:
        out.wait()
    for pack in range(packs):
        gather_one.drain(pack)
        gather_two.drain(pack)
        scatter_two.drain(pack)


def ffn_call(r1, cot, weights, ln_params):
    packs, share, width = r1.shape
    rows = 4 * share
    units = weights.shape[1] // 3
    vm = pl.BlockSpec(memory_space=pltpu.VMEM)
    hb = pl.BlockSpec(memory_space=pl.ANY)
    dma = pltpu.SemaphoreType.DMA
    return pl.pallas_call(
        ffn_kernel,
        out_shape=(
            jax.ShapeDtypeStruct((packs, share, width), BF16),
            jax.ShapeDtypeStruct((packs, share, width), F32),
            jax.ShapeDtypeStruct((width, 3 * units), BF16),
            jax.ShapeDtypeStruct((8, width), F32),
        ),
        in_specs=[vm, vm, hb, vm],
        out_specs=(vm, vm, hb, vm),
        scratch_shapes=[
            pltpu.VMEM((width, 3 * units), BF16),
            pltpu.VMEM((packs, rows, width), BF16),
            pltpu.VMEM((packs, rows, width), BF16),
            pltpu.VMEM((packs, rows, units), BF16),
            pltpu.VMEM((packs, rows, units), BF16),
            pltpu.VMEM((rows, units), BF16),
            pltpu.VMEM((rows, units), BF16),
            pltpu.VMEM((rows, units), BF16),
            pltpu.VMEM((width, rows), BF16),
            pltpu.VMEM((width, rows), BF16),
            pltpu.VMEM((width, 3 * units), F32),
            pltpu.VMEM((2 * share, 256), F32),
            pltpu.VMEM((2 * share, 256), F32),
            dma((packs, 3)),
            dma((packs, 3)),
            dma((packs, 2)),
            dma((packs, 2)),
            dma((packs, 3)),
            dma((packs, 3)),
            dma((packs, 2)),
            dma((packs, 2)),
            dma(()),
            dma((3,)),
            *scatter_scratch(packs, share, width),
        ],
        compiler_params=pltpu.CompilerParams(
            collective_id=1, has_side_effects=True, vmem_limit_bytes=VMEM_LIMIT
        ),
        cost_estimate=pl.CostEstimate(flops=int(70e9), bytes_accessed=4 * 10**7, transcendentals=10**7),
        name="ffn",
    )(r1, cot, weights, ln_params)


class Runs:
    def __init__(self, offsets, pack):
        names = [offsets[pack, place] for place in range(8)]
        start = jnp.int32(4)
        for place in range(3, -1, -1):
            start = lax.select(names[place] == names[place + 3], jnp.int32(place), start)
        self.start = start
        self.names = [lax.select(start > place, names[place], names[place + 4]) for place in range(4)]

    def masks(self, index):
        own = self.names[0]
        for place in range(1, 4):
            own = lax.select(index == place, self.names[place], own)
        return [lax.select(own == name, jnp.float32(0.0), jnp.float32(NEG)) for name in self.names]

    def arrange(self, plain, order):
        for place in range(4):
            value = plain[held_run(place), :]
            for start in range(1, 5):
                value = lax.select(self.start == start, plain[held_run(place + start), :], value)
            order(pl.ds(place * UNIT, UNIT), value)
            value = lax.select(self.start > place, plain[held_run(place), :], plain[held_run(place + 4), :])
            order(pl.ds((place + 4) * UNIT, UNIT), value)

    def restore(self, order, plain):
        for run in range(8):
            first = max(0, run - 3)
            value = order[pl.ds((run - first) * UNIT, UNIT), :]
            for start in range(first + 1, min(run, 4) + 1):
                value = lax.select(self.start == start, order[pl.ds((run - start) * UNIT, UNIT), :], value)
            if run < 4:
                value = lax.select(self.start > run, order[pl.ds((run + 4) * UNIT, UNIT), :], value)
            else:
                value = lax.select(self.start <= run - 4, order[pl.ds(run * UNIT, UNIT), :], value)
            plain(held_run(run), value)


def held_run(run):
    half, part = divmod(run, 2)
    return pl.ds(((half % 2) * 2 + half // 2) * 2 * UNIT + part * UNIT, UNIT)


def writer(ref, *at):
    def write(rows, value):
        ref[(*at, rows, slice(None))] = value

    return write


def fill_bias(bias, slopes, wide):
    heads, size, _ = bias.shape

    def fill(index):
        rws = tile(index, UNIT)
        down = lax.broadcasted_iota(jnp.int32, (UNIT, size), 0) + index * UNIT
        along = lax.broadcasted_iota(jnp.int32, (UNIT, size), 1)
        distance = jnp.abs(down - along).astype(F32)
        for head in range(heads):
            bias[head, rws, :] = -slopes[wide * heads + head] * distance

    loop(size // UNIT, fill)


def split_weights(packed, w_qkv, w_out):
    width, each = packed.shape[0], packed.shape[1] // 4
    wide = w_out.shape[1]

    def part(index):
        rws = tile(index, 128)
        zeros = jnp.zeros((128, wide - each), BF16)
        for place in range(4):
            value = jnp.concatenate([packed[rws, pl.ds(place * each, each)], zeros], axis=1)
            if place < 3:
                w_qkv[rws, pl.ds(place * wide, wide)] = value
            else:
                w_out[rws, :] = value

    loop(width // 128, part)


def head_lanes():
    lane = lax.broadcasted_iota(jnp.int32, (1, 128), 1)
    return lane < HD


def attn_kernel(
    offsets_ref,
    slopes_ref,
    x_ref,
    w_ref,
    r1_ref,
    held_ref,
    qkv_ref,
    ctx_ref,
    packed,
    w_qkv,
    w_out,
    bias,
    held,
    plain,
    qkv,
    ctx_order,
    ctx,
    send_a,
    recv_a,
    send_b,
    recv_b,
    load_sem,
    store_sem,
    *buffers,
):
    packs, share, width = x_ref.shape
    rows = 4 * share
    lanes = w_out.shape[1]
    group = rows // 2
    load = pltpu.make_async_copy(w_ref.at[:, pl.ds(0, packed.shape[1])], packed, load_sem)
    load.start()
    wide, core, row, mate, across = places()
    greet(mate, across)
    gather = Gather(held, send_a, recv_a, share)
    scatter = Scatter(*buffers, send_b, recv_b, share)
    base = pl.multiple_of((core * 2 + row) * share, share)
    for pack in range(packs):
        held[pack, pl.ds(base, share), :] = x_ref[pack]
        gather.start(pack)
    fill_bias(bias, slopes_ref, wide)
    load.wait()
    split_weights(packed, w_qkv, w_out)
    low = head_lanes()
    stores = []

    def attend(pack):
        runs = Runs(offsets_ref, pack)
        gather.finish(pack)

        def project(index):
            rws = tile(index, 256)
            plain[rws, :] = dot_nn(held[pack, rws, :], w_qkv[...]).astype(BF16)

        loop(rows // 256, project)
        runs.arrange(plain, writer(qkv, pack))
        for side in range(2):
            keys = pl.ds(side * group, group)

            def chunk(index, side=side, keys=keys, pack=pack):
                rws = pl.ds(pl.multiple_of(side * group + index * UNIT, UNIT), UNIT)
                if side:
                    mask = jnp.concatenate(
                        [jnp.full((1, UNIT), part, F32) for part in runs.masks(index)], axis=1
                    )
                outs = []
                for head in range(3):
                    block = pl.ds(0 if head < 2 else 128, 128)
                    queries = qkv[pack, rws, block]
                    if head < 2:
                        queries = jnp.where(low if head == 0 else ~low, queries, jnp.zeros_like(queries))
                    k_block = pl.ds(lanes + (0 if head < 2 else 128), 128)
                    v_block = pl.ds(2 * lanes + (0 if head < 2 else 128), 128)
                    scores = dot_nt(queries, qkv[pack, keys, k_block]) * HD ** (-0.5)
                    scores = scores + bias[head, tile(index, UNIT), :]
                    if side:
                        scores = scores + mask
                    powers = jnp.exp(scores - jnp.max(scores, axis=-1, keepdims=True))
                    total = jnp.sum(powers, axis=-1, keepdims=True)
                    outs.append(dot_nn(powers.astype(BF16), qkv[pack, keys, v_block]) / total)
                ctx_order[rws, pl.ds(0, 128)] = jnp.where(low, outs[0], outs[1]).astype(BF16)
                ctx_order[rws, pl.ds(128, 128)] = outs[2].astype(BF16)

            loop(4, chunk)
        runs.restore(ctx_order, writer(ctx, pack))
        for which in range(2):
            big = pl.ds(scatter.half(which), 2 * share)

            def out(index, which=which, big=big):
                cols = tile(index, 256)
                value = dot_nt(ctx[pack, big, :], w_out[cols, :])
                if which:
                    scatter.part[:, cols] = value
                else:
                    scatter.give[pack, :, cols] = value.astype(BF16)

            loop(width // 256, out)
            if not which:
                scatter.start(pack)
        scatter.middle(pack)
        for place, (source, target) in enumerate(((held, held_ref), (qkv, qkv_ref), (ctx, ctx_ref))):
            copy = pltpu.make_async_copy(source.at[pack], target.at[pack], store_sem.at[pack, place])
            copy.start()
            stores.append(copy)

    def settle(pack):
        scatter.finish(pack)

        def add(index):
            rws = tile(index, 64)
            attn = scatter.own[pack, rws, :] + scatter.reach[pack, rws, :].astype(F32)
            r1_ref[pack, rws, :] = x_ref[pack, rws, :].astype(F32) + attn

        loop(share // 64, add)

    for pack in range(packs):
        attend(pack)
        if pack:
            settle(pack - 1)
    settle(packs - 1)
    for copy in stores:
        copy.wait()
    for pack in range(packs):
        gather.drain(pack)
        scatter.drain(pack)


def back_kernel(
    offsets_ref,
    slopes_ref,
    dr1_ref,
    w_ref,
    x_ref,
    qkv_ref,
    ctx_ref,
    grad_ref,
    grads_ref,
    packed,
    w_qkv,
    w_out,
    bias,
    held,
    x_all,
    qkv,
    ctx,
    plain,
    dctx,
    dorder,
    dplain,
    sum_k,
    sum_v,
    turned,
    total,
    total_out,
    send_a,
    recv_a,
    send_b,
    recv_b,
    load_sem,
    fetch_sem,
    *buffers,
):
    packs, share, width = dr1_ref.shape
    rows = 4 * share
    lanes = w_out.shape[1]
    group = rows // 2
    load = pltpu.make_async_copy(w_ref.at[:, pl.ds(0, packed.shape[1])], packed, load_sem)
    load.start()
    fetches = []
    for pack in range(packs):
        for place, (source, target) in enumerate(((x_ref, x_all), (qkv_ref, qkv), (ctx_ref, ctx))):
            copy = pltpu.make_async_copy(source.at[pack], target.at[pack], fetch_sem.at[pack, place])
            copy.start()
            fetches.append(copy)
    wide, core, row, mate, across = places()
    greet(mate, across)
    gather = Gather(held, send_a, recv_a, share)
    scatter = Scatter(*buffers, send_b, recv_b, share)
    base = pl.multiple_of((core * 2 + row) * share, share)
    for pack in range(packs):
        held[pack, pl.ds(base, share), :] = dr1_ref[pack].astype(BF16)
        gather.start(pack)
    fill_bias(bias, slopes_ref, wide)
    load.wait()
    split_weights(packed, w_qkv, w_out)
    low = head_lanes()
    scale = HD ** (-0.5)

    def pull(pack):
        runs = Runs(offsets_ref, pack)
        gather.finish(pack)

        def project(index):
            rws = tile(index, 256)
            plain[rws, :] = dot_nn(held[pack, rws, :], w_out[...]).astype(BF16)

        loop(rows // 256, project)
        runs.arrange(plain, writer(dctx))
        for copy in fetches[3 * pack : 3 * pack + 3]:
            copy.wait()
        for side in range(2):
            keys = pl.ds(side * group, group)
            sum_k[...] = jnp.zeros_like(sum_k)
            sum_v[...] = jnp.zeros_like(sum_v)

            def chunk(index, side=side, keys=keys, pack=pack):
                rws = pl.ds(pl.multiple_of(side * group + index * UNIT, UNIT), UNIT)
                masks = runs.masks(index)
                for part in range(2):
                    heads = (0, 1) if part == 0 else (2,)
                    block = pl.ds(part * 128, 128)
                    k_block = pl.ds(lanes + part * 128, 128)
                    v_block = pl.ds(2 * lanes + part * 128, 128)
                    k_all, v_all = qkv[pack, keys, k_block], qkv[pack, keys, v_block]
                    dq = None
                    for head in heads:
                        queries, dout, k_own = qkv[pack, rws, block], dctx[rws, block], k_all
                        if part == 0:
                            keep = low if head == 0 else ~low
                            queries = jnp.where(keep, queries, jnp.zeros_like(queries))
                            dout = jnp.where(keep, dout, jnp.zeros_like(dout))
                            k_own = jnp.where(keep, k_own, jnp.zeros_like(k_own))
                        scores = dot_nt(k_all, queries) * scale + bias[head, :, tile(index, UNIT)]
                        if side:
                            scores = jnp.concatenate(
                                [scores[t * UNIT : (t + 1) * UNIT] + masks[t] for t in range(4)], axis=0
                            )
                        powers = jnp.exp(scores - jnp.max(scores, axis=0, keepdims=True))
                        probs = powers * (1.0 / jnp.sum(powers, axis=0, keepdims=True))
                        dprobs = dot_nt(v_all, dout)
                        delta = jnp.sum(probs * dprobs, axis=0, keepdims=True)
                        dscaled = (probs * (dprobs - delta) * scale).astype(BF16)
                        sum_v[:, block] += dot_nn(probs.astype(BF16), dout)
                        sum_k[:, block] += dot_nn(dscaled, queries)
                        term = dot_tn(dscaled, k_own)
                        dq = term if dq is None else dq + term
                    dorder[rws, block] = dq.astype(BF16)

            loop(4, chunk)
            dorder[keys, pl.ds(lanes, lanes)] = sum_k[...].astype(BF16)
            dorder[keys, pl.ds(2 * lanes, lanes)] = sum_v[...].astype(BF16)
        runs.restore(dorder, writer(dplain))
        for which in range(2):
            big = pl.ds(scatter.half(which), 2 * share)

            def out(index, which=which, big=big):
                cols = tile(index, 256)
                value = dot_nt(dplain[big, :], w_qkv[cols, :])
                if which:
                    scatter.part[:, cols] = value
                else:
                    scatter.give[pack, :, cols] = value.astype(BF16)

            loop(width // 256, out)
            if not which:
                scatter.start(pack)
        scatter.middle(pack)

    def weight_grads(pack):
        for source, result, target in ((x_all, dplain, total), (held, ctx.at[pack], total_out)):

            def flip(index, source=source):
                rws = tile(index, 256)
                turned[:, rws] = source[pack, rws, :].T

            loop(rows // 256, flip)

            def add(index, result=result, target=target):
                rws = tile(index, 256)
                value = dot_nn(turned[rws, :], result[...])
                if pack:
                    value = value + target[rws, :]
                target[rws, :] = value

            loop(width // 256, add)

    def settle(pack):
        scatter.finish(pack)

        def add(index):
            rws = tile(index, 64)
            grad_ref[pack, rws, :] = dr1_ref[pack, rws, :] + (
                scatter.own[pack, rws, :] + scatter.reach[pack, rws, :].astype(F32)
            )

        loop(share // 64, add)

    for pack in range(packs):
        pull(pack)
        weight_grads(pack)
        if pack:
            settle(pack - 1)
    each = width // 4

    def pack_up(index):
        rws = tile(index, 128)
        pieces = [total[rws, pl.ds(place * lanes, each)] for place in range(3)]
        pieces.append(total_out[rws, pl.ds(0, each)])
        grads_ref[rws, :] = jnp.concatenate([piece.astype(BF16) for piece in pieces], axis=1)

    loop(width // 128, pack_up)
    settle(packs - 1)
    for pack in range(packs):
        gather.drain(pack)
        scatter.drain(pack)


def attn_call(x, weights, offsets, slopes):
    packs, share, width = x.shape
    rows = 4 * share
    lanes = 256
    vm = pl.BlockSpec(memory_space=pltpu.VMEM)
    hb = pl.BlockSpec(memory_space=pl.ANY)
    sm = pl.BlockSpec(memory_space=pltpu.SMEM)
    dma = pltpu.SemaphoreType.DMA
    return pl.pallas_call(
        attn_kernel,
        out_shape=(
            jax.ShapeDtypeStruct((packs, share, width), F32),
            jax.ShapeDtypeStruct((packs, rows, width), BF16),
            jax.ShapeDtypeStruct((packs, rows, 3 * lanes), BF16),
            jax.ShapeDtypeStruct((packs, rows, lanes), BF16),
        ),
        in_specs=[sm, sm, vm, hb],
        out_specs=(vm, hb, hb, hb),
        scratch_shapes=[
            pltpu.VMEM((width, width), BF16),
            pltpu.VMEM((width, 3 * lanes), BF16),
            pltpu.VMEM((width, lanes), BF16),
            pltpu.VMEM((3, rows // 2, rows // 2), F32),
            pltpu.VMEM((packs, rows, width), BF16),
            pltpu.VMEM((rows, 3 * lanes), BF16),
            pltpu.VMEM((packs, rows, 3 * lanes), BF16),
            pltpu.VMEM((rows, lanes), BF16),
            pltpu.VMEM((packs, rows, lanes), BF16),
            dma((packs, 3)),
            dma((packs, 3)),
            dma((packs, 2)),
            dma((packs, 2)),
            dma(()),
            dma((packs, 3)),
            *scatter_scratch(packs, share, width),
        ],
        compiler_params=pltpu.CompilerParams(
            collective_id=2, has_side_effects=True, vmem_limit_bytes=VMEM_LIMIT
        ),
        cost_estimate=pl.CostEstimate(flops=int(14e9), bytes_accessed=4 * 10**7, transcendentals=10**7),
        name="attn",
    )(offsets, slopes, x, weights)


def back_call(dr1, weights, x_all, qkv, ctx, offsets, slopes):
    packs, share, width = dr1.shape
    rows = 4 * share
    lanes = 256
    vm = pl.BlockSpec(memory_space=pltpu.VMEM)
    hb = pl.BlockSpec(memory_space=pl.ANY)
    sm = pl.BlockSpec(memory_space=pltpu.SMEM)
    dma = pltpu.SemaphoreType.DMA
    return pl.pallas_call(
        back_kernel,
        out_shape=(
            jax.ShapeDtypeStruct((packs, share, width), F32),
            jax.ShapeDtypeStruct((width, width), BF16),
        ),
        in_specs=[sm, sm, vm, hb, hb, hb, hb],
        out_specs=(vm, vm),
        scratch_shapes=[
            pltpu.VMEM((width, width), BF16),
            pltpu.VMEM((width, 3 * lanes), BF16),
            pltpu.VMEM((width, lanes), BF16),
            pltpu.VMEM((3, rows // 2, rows // 2), F32),
            pltpu.VMEM((packs, rows, width), BF16),
            pltpu.VMEM((packs, rows, width), BF16),
            pltpu.VMEM((packs, rows, 3 * lanes), BF16),
            pltpu.VMEM((packs, rows, lanes), BF16),
            pltpu.VMEM((rows, lanes), BF16),
            pltpu.VMEM((rows, lanes), BF16),
            pltpu.VMEM((rows, 3 * lanes), BF16),
            pltpu.VMEM((rows, 3 * lanes), BF16),
            pltpu.VMEM((rows // 2, lanes), F32),
            pltpu.VMEM((rows // 2, lanes), F32),
            pltpu.VMEM((width, rows), BF16),
            pltpu.VMEM((width, 3 * lanes), F32),
            pltpu.VMEM((width, lanes), F32),
            dma((packs, 3)),
            dma((packs, 3)),
            dma((packs, 2)),
            dma((packs, 2)),
            dma(()),
            dma((packs, 3)),
            *scatter_scratch(packs, share, width),
        ],
        compiler_params=pltpu.CompilerParams(
            collective_id=3, has_side_effects=True, vmem_limit_bytes=VMEM_LIMIT
        ),
        cost_estimate=pl.CostEstimate(flops=int(40e9), bytes_accessed=4 * 10**7, transcendentals=10**7),
        name="back",
    )(offsets, slopes, dr1, weights, x_all, qkv, ctx)


class OwnerSum:
    def __init__(self, source, sums, beside, along, load, send, recv, chunk):
        self.source, self.sums, self.beside, self.along = source, sums, beside, along
        self.load, self.send, self.recv, self.chunk = load, send, recv, chunk
        seq = lax.axis_index("seq")
        self.line = sums.shape[0]
        self.x = lax.rem(seq, 2)
        self.z = seq // 2

    def chunks(self):
        return self.sums.shape[2] // self.chunk

    def cols(self, index):
        return pl.ds(index * self.chunk, self.chunk)

    def peers(self):
        found = [2 * self.z + 1 - self.x]
        for step in range(1, self.line):
            found.append(2 * lax.rem(self.z + step, self.line) + self.x)
        return found

    def own_load(self):
        return pltpu.make_async_copy(self.source.at[:, self.x], self.sums, self.load)

    def cross(self, index):
        return remote(
            self.source.at[:, 1 - self.x, :, self.cols(index)],
            self.beside.at[index],
            self.send.at[index, 0],
            self.recv.at[index, 0],
            2 * self.z + 1 - self.x,
            "seq",
        )

    def hop(self, index, step):
        other = lax.rem(self.z + step, self.line)
        return remote(
            self.sums.at[other, :, self.cols(index)],
            self.along.at[index, step - 1],
            self.send.at[index, step],
            self.recv.at[index, step],
            2 * other + self.x,
            "seq",
        )

    def start(self):
        self.own_load().start()
        for index in range(self.chunks()):
            self.cross(index).start()

    def add(self, index):
        if index == 0:
            self.own_load().wait()
        self.cross(index).wait_recv()
        cols = self.cols(index)
        for other in range(self.line):

            def part(row, other=other):
                rws = tile(row, 32)
                value = self.sums[other, rws, cols].astype(F32) + self.beside[index, other, rws, :].astype(F32)
                self.sums[other, rws, cols] = value.astype(BF16)

            loop(self.sums.shape[1] // 32, part)
        for step in range(1, self.line):
            self.hop(index, step).start()

    def finish(self, index, target):
        for step in range(1, self.line):
            self.hop(index, step).wait_recv()
        cols = self.cols(index)

        def part(row):
            rws = tile(row, 32)
            value = self.sums[self.z, rws, cols].astype(F32)
            for step in range(1, self.line):
                value = value + self.along[index, step - 1, rws, :].astype(F32)
            target(rws, cols, value)

        loop(self.sums.shape[1] // 32, part)

    def drain(self):
        for index in range(self.chunks()):
            self.cross(index).wait_send()
            for step in range(1, self.line):
                self.hop(index, step).wait_send()


def owner_scratch(line, slab, width, chunk):
    count = width // chunk
    dma = pltpu.SemaphoreType.DMA
    return [
        pltpu.VMEM((line, slab, width), BF16),
        pltpu.VMEM((count, line, slab, chunk), BF16),
        pltpu.VMEM((count, line - 1, slab, chunk), BF16),
        dma(()),
        dma((count, line)),
        dma((count, line)),
    ]


class Total:
    def __init__(self, axis, slots, send, recv):
        self.axis, self.slots, self.send, self.recv = axis, slots, send, recv
        self.count = slots.shape[0]
        self.place = lax.axis_index(axis)

    def copy(self, step):
        mine = self.slots.at[self.place]
        return remote(
            mine, mine, self.send.at[step - 1], self.recv.at[self.place], self.peer(step), self.axis
        )

    def peer(self, step):
        return lax.rem(self.place + step, self.count)

    def start(self, value):
        self.slots[self.place] = value
        for step in range(1, self.count):
            self.copy(step).start()

    def finish(self):
        for step in range(1, self.count):
            other = self.peer(step)
            slot = self.slots.at[other]
            remote(
                slot, slot, self.send.at[step - 1], self.recv.at[other], other, self.axis
            ).wait_recv()
        value = self.slots[0]
        for place in range(1, self.count):
            value = value + self.slots[place]
        return value

    def drain(self):
        for step in range(1, self.count):
            self.copy(step).wait_send()


def total_scratch(count, shape):
    dma = pltpu.SemaphoreType.DMA
    return [pltpu.VMEM((count, *shape), F32), dma((count - 1,)), dma((count,))]


def greet_all(axes):
    barrier = pltpu.get_barrier_semaphore()
    sent = 0
    for axis, count in axes:
        place = lax.axis_index(axis)
        for step in range(1, count):
            peer = lax.rem(place + step, count)
            pl.semaphore_signal(barrier, inc=1, device_id={axis: peer}, device_id_type=MESH)
            sent += 1
    pl.semaphore_wait(barrier, sent)


def close_kernel(
    seq_count,
    wide_count,
    kept_ref,
    grads_ref,
    ffn_ref,
    ln_ref,
    owned_ref,
    ln_out_ref,
    square_ref,
    *scratch,
):
    greet_all((("seq", seq_count), ("wide", wide_count)))
    owners = OwnerSum(grads_ref, *scratch[:6], 256)
    norms = [Total("wide", *scratch[6:9]), Total("seq", *scratch[9:12])]
    squares = [Total("wide", *scratch[12:15]), Total("seq", *scratch[15:18])]
    acc = scratch[18]
    slab = owned_ref.shape[0]
    width = grads_ref.shape[3]
    owners.start()
    norms[0].start(ln_ref[...])
    acc[...] = jnp.zeros_like(acc)

    def keep(rws, value):
        row = lax.broadcasted_iota(jnp.int32, value.shape, 0) + rws.start
        return jnp.where(row < kept_ref[0], value, 0.0)

    def note(value):
        square = value * value
        for place in range(value.shape[1] // 128):
            part = square[:, place * 128 : (place + 1) * 128]
            for row in range(0, value.shape[0], 8):
                acc[...] += part[row : row + 8]

    def put(rws, cols, value):
        value = keep(rws, value)
        owned_ref[rws, cols] = value
        note(value)

    def from_ffn(index):
        rws = tile(index, 8)
        value = keep(rws, ffn_ref[rws, :].astype(F32))
        owned_ref[rws, pl.ds(width, ffn_ref.shape[1])] = value
        note(value)

    for index in range(owners.chunks()):
        owners.add(index)
    norms[1].start(norms[0].finish())
    loop(slab // 8, from_ffn)
    for index in range(owners.chunks()):
        owners.finish(index, put)
    squares[0].start(acc[...])
    squares[1].start(squares[0].finish())
    ln_out_ref[...] = norms[1].finish()
    square_ref[...] = squares[1].finish()
    owners.drain()
    for part in (*norms, *squares):
        part.drain()


def close_call(kept, grads, ffn_owned, ln_rows, seq_count, wide_count):
    slab = ffn_owned.shape[0]
    width = grads.shape[1]
    line = seq_count // 2
    vm = pl.BlockSpec(memory_space=pltpu.VMEM)
    sm = pl.BlockSpec(memory_space=pltpu.SMEM)
    return pl.pallas_call(
        functools.partial(close_kernel, seq_count, wide_count),
        out_shape=(
            jax.ShapeDtypeStruct((slab, width + ffn_owned.shape[1]), F32),
            jax.ShapeDtypeStruct(ln_rows.shape, F32),
            jax.ShapeDtypeStruct((8, 128), F32),
        ),
        in_specs=[sm, pl.BlockSpec(memory_space=pl.ANY), vm, vm],
        out_specs=(vm, vm, vm),
        scratch_shapes=[
            *owner_scratch(line, slab, width, 256),
            *total_scratch(wide_count, ln_rows.shape),
            *total_scratch(seq_count, ln_rows.shape),
            *total_scratch(wide_count, (8, 128)),
            *total_scratch(seq_count, (8, 128)),
            pltpu.VMEM((8, 128), F32),
        ],
        compiler_params=pltpu.CompilerParams(
            collective_id=4, has_side_effects=True, vmem_limit_bytes=VMEM_LIMIT
        ),
        name="close",
    )(kept, grads.reshape(line, 2, slab, width), ffn_owned, ln_rows)


def pick_kernel(block, places_ref, source_ref, target_ref, held, sems, sem):
    count = places_ref.shape[1]

    def copy(index):
        return pltpu.make_async_copy(
            source_ref.at[pl.ds(pl.multiple_of(places_ref[0, index] * block, block), block)],
            held.at[pl.ds(pl.multiple_of(index * block, block), block)],
            sems.at[index],
        )

    loop(count, lambda index: copy(index).start())
    loop(count, lambda index: copy(index).wait())
    out = pltpu.make_async_copy(held, target_ref, sem)
    out.start()
    out.wait()


def spread_kernel(block, places_ref, source_ref, target_ref, held, sems, sem):
    count = places_ref.shape[1]
    load = pltpu.make_async_copy(source_ref, held, sem)
    load.start()
    load.wait()

    def copy(index):
        return pltpu.make_async_copy(
            held.at[pl.ds(pl.multiple_of(index * block, block), block)],
            target_ref.at[pl.ds(pl.multiple_of(places_ref[1, index] * block, block), block)],
            sems.at[index],
        )

    loop(count, lambda index: copy(index).start())
    loop(count, lambda index: copy(index).wait())


def move_blocks(kernel, source, places, rows, block):
    hb = pl.BlockSpec(memory_space=pl.ANY)
    count = places.shape[1]
    return pl.pallas_call(
        functools.partial(kernel, block),
        out_shape=jax.ShapeDtypeStruct((rows, source.shape[1]), source.dtype),
        in_specs=[pl.BlockSpec(memory_space=pltpu.SMEM), hb],
        out_specs=hb,
        scratch_shapes=[
            pltpu.VMEM((count * block, source.shape[1]), source.dtype),
            pltpu.SemaphoreType.DMA((count,)),
            pltpu.SemaphoreType.DMA(()),
        ],
        compiler_params=pltpu.CompilerParams(vmem_limit_bytes=VMEM_LIMIT),
        name="move",
    )(places, source)


def per_device(
    hidden_in,
    cotangent,
    seq_offsets,
    owner_blocks,
    master,
    first_moment,
    second_moment,
    ln_params,
    ln_first,
    ln_second,
):
    width = hidden_in.shape[2]
    slab_rows = master.shape[0]
    block = slab_rows // CAP
    source, valid, target = owner_maps(owner_blocks, width, CAP, block)
    low = master.astype(jnp.bfloat16)
    first = lax.all_gather(low[:, :width], "seq", axis=0, tiled=True)
    rest = lax.all_gather(low[:, width:], "seq", axis=0, tiled=True)
    gathered_rows = slab_rows * lax.axis_size("seq")
    count = width // block
    fits = block % 16 == 0
    slots = target[::block] // block
    both = jnp.stack([slots, slots])

    def to_order(array):
        if fits:
            return move_blocks(pick_kernel, array, both, width, block)
        return jnp.take(array, target, axis=0)

    def to_owner(grads):
        if fits:
            return move_blocks(spread_kernel, grads, both, gathered_rows, block)
        return jnp.take(grads, source, axis=0)

    weights = to_order(first)
    w_ffn = to_order(rest)
    slopes = jnp.exp2(-8.0 * (jnp.arange(H, dtype=jnp.float32) + 1.0) / H)
    x = jnp.transpose(hidden_in, (1, 0, 2))
    r1, x_all, qkv, ctx = attn_call(x, weights, seq_offsets, slopes)
    mixed_p, dr1_p, ffn_grads, ln_rows = ffn_call(
        r1, jnp.transpose(cotangent, (1, 0, 2)), w_ffn, ln_params
    )
    mixed = jnp.transpose(mixed_p, (1, 0, 2))

    ffn_padded, dr1_p = lax.optimization_barrier((to_owner(ffn_grads), dr1_p))
    ffn_owned = lax.psum_scatter(ffn_padded, "seq", scatter_dimension=0, tiled=True)
    grad_p, attn_grads = back_call(dr1_p, weights, x_all, qkv, ctx, seq_offsets, slopes)
    input_grad = jnp.transpose(grad_p, (1, 0, 2))
    attn_padded = to_owner(attn_grads)
    seq_count = lax.axis_size("seq")
    mine = jnp.arange(seq_count, dtype=jnp.int32) == lax.axis_index("seq")
    own_rows = jnp.sum(jnp.where(mine, owner_blocks, 0)) * block
    kept = (jnp.arange(slab_rows, dtype=jnp.int32) < own_rows)[:, None]
    if fits and seq_count == 8:
        owned, ln_total, parts = close_call(
            own_rows[None], attn_padded, ffn_owned, ln_rows, seq_count, lax.axis_size("wide")
        )
        squares, ln_total = jnp.sum(parts), ln_total[:4]
    else:
        attn_owned = lax.psum_scatter(attn_padded, "seq", scatter_dimension=0, tiled=True)
        owned = jnp.concatenate([attn_owned, ffn_owned], axis=1).astype(jnp.float32)
        owned = jnp.where(kept, owned, 0.0)
        squares, ln_total = lax.psum((jnp.sum(owned * owned), ln_rows[:4]), ("seq", "wide"))
    grad_norm = jnp.sqrt(squares + jnp.sum(ln_total * ln_total))
    clip = jnp.minimum(1.0, 1.0 / (grad_norm + 1e-06))
    param_new, first_new, second_new = adamw(
        master, owned * clip, first_moment, second_moment, DECAY, RATE
    )
    norms_new, norms_first, norms_second = adamw(
        ln_params, ln_total * clip, ln_first, ln_second, 0.0, NORM_RATE
    )
    return (
        mixed,
        input_grad,
        jnp.where(kept, param_new, 0.0),
        jnp.where(kept, first_new, 0.0),
        jnp.where(kept, second_new, 0.0),
        norms_new,
        norms_first,
        norms_second,
        grad_norm,
    )


def solution(mesh):
    return jax.shard_map(
        per_device,
        mesh=mesh,
        in_specs=(
            P("wide", "seq", None),
            P("wide", "seq", None),
            P("seq", None),
            P(),
            P("seq", "wide"),
            P("seq", "wide"),
            P("seq", "wide"),
            P(),
            P(),
            P(),
        ),
        out_specs=(
            P("wide", "seq", None),
            P("wide", "seq", None),
            P("seq", "wide"),
            P("seq", "wide"),
            P("seq", "wide"),
            P(),
            P(),
            P(),
            P(),
        ),
        check_vma=False,
    )
```

```python
import functools

import jax
import jax.numpy as jnp
from jax import lax
from jax.experimental import pallas as pl
from jax.experimental.pallas import tpu as pltpu
from jax.sharding import PartitionSpec as P

MESH = pl.DeviceIdType.MESH

H = 12
HD = 64
FF = 3072
UNIT = 128
CAP = 6
STEP = 10


RATE = 0.02
NORM_RATE = 0.6
BETA_ONE = 0.9
BETA_TWO = 0.999
EPSILON = 1e-08
DECAY = 0.01
NORM_EPS = 1e-05
ROOT_HALF = 0.7071067811865476
DENSITY_SCALE = 0.3989422804014327
EPS = 1e-05
F32 = jnp.float32
BF16 = jnp.bfloat16
NEG = -1e30
OWNER_CHUNKS = 6
PAIRS = 4
SINGLES = 2
VMEM_LIMIT = 60 * 2**20


def owner_maps(owner_blocks, rows, cap, block):
    ends = jnp.cumsum(owner_blocks)
    starts = ends - owner_blocks
    slot = jnp.arange(cap * block, dtype=jnp.int32)
    which = slot // block
    source = (starts[:, None] + which[None, :]) * block + (slot % block)[None, :]
    valid = which[None, :] < owner_blocks[:, None]
    source = jnp.where(valid, source, 0).reshape(-1)
    valid = valid.reshape(-1)
    param = jnp.arange(rows, dtype=jnp.int32)
    blocks = param // block
    owner = jnp.sum((ends[None, :] <= blocks[:, None]).astype(jnp.int32), axis=1)
    onehot = owner[:, None] == jnp.arange(owner_blocks.shape[0], dtype=jnp.int32)[None, :]
    first = jnp.sum(jnp.where(onehot, starts[None, :], 0), axis=1)
    target = owner * (cap * block) + (blocks - first) * block + param % block
    return (source, valid, target)


def adamw(param, grad, first, second, decay, rate):
    first_new = BETA_ONE * first + (1.0 - BETA_ONE) * grad
    second_new = BETA_TWO * second + (1.0 - BETA_TWO) * grad * grad
    first_hat = first_new / (1.0 - BETA_ONE**STEP)
    second_hat = second_new / (1.0 - BETA_TWO**STEP)
    param_new = param - rate * (first_hat / (jnp.sqrt(second_hat) + EPSILON) + decay * param)
    return (param_new, first_new, second_new)


def dot_nn(a, b):
    return lax.dot_general(a, b, (((1,), (0,)), ((), ())), preferred_element_type=F32)


def dot_nt(a, b):
    return lax.dot_general(a, b, (((1,), (1,)), ((), ())), preferred_element_type=F32)


def dot_tn(a, b):
    return lax.dot_general(a, b, (((0,), (0,)), ((), ())), preferred_element_type=F32)


def places():
    wide = lax.axis_index("wide")
    core = lax.rem(wide, 2)
    row = wide // 2
    return wide, core, row, wide + 1 - 2 * core, wide + 2 - 4 * row


def greet(mate, across):
    barrier = pltpu.get_barrier_semaphore()
    for peer in (mate, across):
        pl.semaphore_signal(barrier, inc=1, device_id={"wide": peer}, device_id_type=MESH)
    pl.semaphore_wait(barrier, 2)


def remote(source, target, send, recv, peer, axis="wide"):
    return pltpu.make_async_remote_copy(
        src_ref=source,
        dst_ref=target,
        send_sem=send,
        recv_sem=recv,
        device_id={axis: peer},
        device_id_type=MESH,
    )


class Gather:
    def __init__(self, held, send, recv, share):
        self.held, self.send, self.recv, self.share = held, send, recv, share
        _, self.core, self.row, self.mate, self.across = places()

    def rows(self, core, row):
        return pl.ds(pl.multiple_of((core * 2 + row) * self.share, self.share), self.share)

    def copy(self, pack, leg):
        row = 1 - self.row if leg == 2 else self.row
        block = self.held.at[pack, self.rows(self.core, row)]
        peer = self.mate if leg else self.across
        return remote(block, block, self.send.at[pack, leg], self.recv.at[pack, leg], peer)

    def start(self, pack):
        self.copy(pack, 0).start()
        self.copy(pack, 1).start()

    def finish(self, pack):
        self.copy(pack, 0).wait_recv()
        self.copy(pack, 2).start()
        self.copy(pack, 1).wait_recv()
        self.copy(pack, 2).wait_recv()

    def drain(self, pack):
        for leg in range(3):
            self.copy(pack, leg).wait_send()


class Scatter:
    def __init__(self, part, give, take, cross, reach, own, send, recv, share):
        self.part, self.give, self.take = part, give, take
        self.cross, self.reach, self.own = cross, reach, own
        self.send, self.recv, self.share = send, recv, share
        _, self.core, self.row, self.mate, self.across = places()

    def copy(self, pack, leg):
        source, target = (self.cross, self.reach) if leg else (self.give, self.take)
        peer = self.across if leg else self.mate
        return remote(
            source.at[pack], target.at[pack], self.send.at[pack, leg], self.recv.at[pack, leg], peer
        )

    def half(self, which):
        core = self.core if which else 1 - self.core
        return pl.multiple_of(core * 2 * self.share, 2 * self.share)

    def start(self, pack):
        self.copy(pack, 0).start()

    def middle(self, pack):
        self.copy(pack, 0).wait_recv()
        share = self.share
        far = pl.ds(pl.multiple_of((1 - self.row) * share, share), share)
        near = pl.ds(pl.multiple_of(self.row * share, share), share)
        self.cross[pack] = (self.part[far, :] + self.take[pack, far, :].astype(F32)).astype(BF16)
        self.copy(pack, 1).start()
        self.own[pack] = self.part[near, :] + self.take[pack, near, :].astype(F32)

    def finish(self, pack):
        self.copy(pack, 1).wait_recv()

    def drain(self, pack):
        for leg in range(2):
            self.copy(pack, leg).wait_send()


def scatter_scratch(packs, share, width):
    return [
        pltpu.VMEM((2 * share, width), F32),
        pltpu.VMEM((packs, 2 * share, width), BF16),
        pltpu.VMEM((packs, 2 * share, width), BF16),
        pltpu.VMEM((packs, share, width), BF16),
        pltpu.VMEM((packs, share, width), BF16),
        pltpu.VMEM((packs, share, width), F32),
    ]


def norm_parts(values):
    center = values - jnp.mean(values, axis=-1, keepdims=True)
    inverse = lax.rsqrt(jnp.mean(center * center, axis=-1, keepdims=True) + EPS)
    return center * inverse, inverse


def norm_pull(grad, normal, inverse, gain):
    scaled = grad * gain
    return inverse * (
        scaled
        - jnp.mean(scaled, axis=-1, keepdims=True)
        - normal * jnp.mean(scaled * normal, axis=-1, keepdims=True)
    )


def loop(count, body, unroll=1):
    def step(index, carry):
        body(index)
        return carry

    lax.fori_loop(0, count, step, 0, unroll=unroll)


def tile(index, size):
    return pl.ds(pl.multiple_of(index * size, size), size)


def ffn_kernel(
    r1_ref,
    cot_ref,
    w_ref,
    ln_ref,
    mixed_ref,
    dr1_ref,
    grads_ref,
    lngrad_ref,
    weights,
    held,
    held2,
    gates,
    ups,
    hid,
    dgate,
    dup,
    turned,
    turned2,
    total,
    g_tile,
    u_tile,
    send_a,
    recv_a,
    send_b,
    recv_b,
    send_c,
    recv_c,
    send_d,
    recv_d,
    load_sem,
    store_sem,
    *buffers,
):
    packs, share, width = r1_ref.shape
    rows = 4 * share
    fwd = buffers[:6]
    units = weights.shape[1] // 3
    col = 256
    n_units, n_width = units // col, width // col
    load = pltpu.make_async_copy(w_ref.at[:, pl.ds(w_ref.shape[1] - 3 * units, 3 * units)], weights, load_sem)
    load.start()
    _, core, row, mate, across = places()
    greet(mate, across)
    gather_one = Gather(held, send_a, recv_a, share)
    scatter_one = Scatter(*fwd, send_b, recv_b, share)
    gather_two = Gather(held2, send_c, recv_c, share)
    scatter_two = Scatter(*fwd, send_d, recv_d, share)
    gain1, shift1 = ln_ref[0:1, :], ln_ref[1:2, :]
    gain2, shift2 = ln_ref[2:3, :], ln_ref[3:4, :]
    lngrad_ref[...] = jnp.zeros_like(lngrad_ref)
    chunk = 64

    for pack in range(packs):
        base = pl.multiple_of((core * 2 + row) * share, share)

        def first(index, pack=pack, base=base):
            normal, _ = norm_parts(r1_ref[pack, tile(index, chunk), :])
            held[pack, pl.ds(pl.multiple_of(base + index * chunk, chunk), chunk), :] = (
                normal * gain1 + shift1
            ).astype(BF16)

        loop(share // chunk, first)
        gather_one.start(pack)
    load.wait()

    def forward(pack):
        gather_one.finish(pack)
        for which in range(2):
            base = scatter_one.half(which)
            big = pl.ds(base, 2 * share)

            def ff(index):
                cols = tile(index, col)
                x = held[pack, big, :]
                g_tile[...] = dot_nn(x, weights[:, cols])
                u_tile[...] = dot_nn(x, weights[:, pl.ds(pl.multiple_of(units + index * col, col), col)])

                def act(part):
                    rws = tile(part, 32)
                    gate, up = g_tile[rws, :], u_tile[rws, :]
                    out = pl.ds(pl.multiple_of(base + part * 32, 32), 32)
                    cumulative = 0.5 * (1.0 + lax.erf(gate * ROOT_HALF))
                    hid[out, cols] = (gate * cumulative * up).astype(BF16)
                    gates[pack, out, cols] = gate.astype(BF16)
                    ups[pack, out, cols] = up.astype(BF16)

                loop(2 * share // 32, act, unroll=2)

            loop(n_units, ff)

            def down(index):
                wd = weights[tile(index, col), pl.ds(2 * units, units)]
                value = dot_nt(hid[big, :], wd)
                if which:
                    scatter_one.part[:, tile(index, col)] = value
                else:
                    scatter_one.give[pack, :, tile(index, col)] = value.astype(BF16)

            loop(n_width, down)
            if not which:
                scatter_one.start(pack)
        scatter_one.middle(pack)

    def turn(pack):
        scatter_one.finish(pack)
        gather_two_base = pl.multiple_of((core * 2 + row) * share, share)

        def second(index):
            rws = tile(index, chunk)
            normal, _ = norm_parts(r1_ref[pack, rws, :])
            ffn = scatter_one.own[pack, rws, :] + scatter_one.reach[pack, rws, :].astype(F32)
            normal2, inverse2 = norm_parts(normal * gain1 + shift1 + ffn)
            mixed_ref[pack, rws, :] = (normal2 * gain2 + shift2).astype(BF16)
            grad = cot_ref[pack, rws, :].astype(F32)
            value = norm_pull(grad, normal2, inverse2, gain2)
            dr1_ref[pack, rws, :] = value
            held2[pack, pl.ds(pl.multiple_of(gather_two_base + index * chunk, chunk), chunk), :] = value.astype(BF16)
            lngrad_ref[2:3, :] += jnp.sum(grad * normal2, axis=0, keepdims=True)
            lngrad_ref[3:4, :] += jnp.sum(grad, axis=0, keepdims=True)

        loop(share // chunk, second)
        scatter_one.drain(pack)
        gather_two.start(pack)

    def backward(pack):
        gather_two.finish(pack)
        for which in range(2):
            base = scatter_two.half(which)
            big = pl.ds(base, 2 * share)

            def bf(index):
                cols = tile(index, col)
                g_tile[...] = dot_nn(
                    held2[pack, big, :], weights[:, pl.ds(pl.multiple_of(2 * units + index * col, col), col)]
                )

                def act(part):
                    rws = tile(part, 32)
                    out = pl.ds(pl.multiple_of(base + part * 32, 32), 32)
                    dhid = g_tile[rws, :]
                    gate = gates[pack, out, cols].astype(F32)
                    up = ups[pack, out, cols].astype(F32)
                    cumulative = 0.5 * (1.0 + lax.erf(gate * ROOT_HALF))
                    density = jnp.exp(-0.5 * gate * gate) * DENSITY_SCALE
                    value = gate * cumulative
                    hid[out, cols] = (value * up).astype(BF16)
                    dgate[out, cols] = (dhid * up * (cumulative + gate * density)).astype(BF16)
                    dup[out, cols] = (dhid * value).astype(BF16)

                loop(2 * share // 32, act, unroll=2)

            loop(n_units, bf)

            def back(index):
                rws = tile(index, col)
                value = dot_nt(dgate[big, :], weights[rws, pl.ds(0, units)]) + dot_nt(
                    dup[big, :], weights[rws, pl.ds(units, units)]
                )
                if which:
                    scatter_two.part[:, tile(index, col)] = value
                else:
                    scatter_two.give[pack, :, tile(index, col)] = value.astype(BF16)

            loop(n_width, back)
            if not which:
                scatter_two.start(pack)
        scatter_two.middle(pack)

    def weight_grads(pack):
        def flip(index):
            rws = tile(index, 256)
            turned[:, rws] = held[pack, rws, :].T
            turned2[:, rws] = held2[pack, rws, :].T

        loop(rows // 256, flip)

        def add(index):
            rws = tile(index, col)
            a = turned[rws, :]
            b = turned2[rws, :]
            parts = (dot_nn(a, dgate[...]), dot_nn(a, dup[...]), dot_nn(b, hid[...]))
            for place, value in enumerate(parts):
                cols = pl.ds(place * units, units)
                if pack == 0:
                    total[rws, cols] = value
                else:
                    value = total[rws, cols] + value
                    if pack < packs - 1:
                        total[rws, cols] = value
                    else:
                        gates[place, rws, :] = value.astype(BF16)

        loop(n_width, add)

    def last(pack):
        scatter_two.finish(pack)

        def third(index):
            rws = tile(index, chunk)
            normal, inverse = norm_parts(r1_ref[pack, rws, :])
            grad = dr1_ref[pack, rws, :] + (
                scatter_two.own[pack, rws, :] + scatter_two.reach[pack, rws, :].astype(F32)
            )
            dr1_ref[pack, rws, :] = norm_pull(grad, normal, inverse, gain1)
            lngrad_ref[0:1, :] += jnp.sum(grad * normal, axis=0, keepdims=True)
            lngrad_ref[1:2, :] += jnp.sum(grad, axis=0, keepdims=True)

        loop(share // chunk, third)

    for pack in range(packs):
        forward(pack)
        if pack:
            turn(pack - 1)
    for pack in range(packs):
        backward(pack)
        weight_grads(pack)
        if pack == 0:
            turn(packs - 1)
        else:
            last(pack - 1)
    outs = [
        pltpu.make_async_copy(
            gates.at[place, pl.ds(0, width)],
            grads_ref.at[:, pl.ds(place * units, units)],
            store_sem.at[place],
        )
        for place in range(3)
    ]
    for out in outs:
        out.start()
    last(packs - 1)
    for out in outs:
        out.wait()
    for pack in range(packs):
        gather_one.drain(pack)
        gather_two.drain(pack)
        scatter_two.drain(pack)


def ffn_call(r1, cot, weights, ln_params):
    packs, share, width = r1.shape
    rows = 4 * share
    units = weights.shape[1] // 3
    vm = pl.BlockSpec(memory_space=pltpu.VMEM)
    hb = pl.BlockSpec(memory_space=pl.ANY)
    dma = pltpu.SemaphoreType.DMA
    return pl.pallas_call(
        ffn_kernel,
        out_shape=(
            jax.ShapeDtypeStruct((packs, share, width), BF16),
            jax.ShapeDtypeStruct((packs, share, width), F32),
            jax.ShapeDtypeStruct((width, 3 * units), BF16),
            jax.ShapeDtypeStruct((8, width), F32),
        ),
        in_specs=[vm, vm, hb, vm],
        out_specs=(vm, vm, hb, vm),
        scratch_shapes=[
            pltpu.VMEM((width, 3 * units), BF16),
            pltpu.VMEM((packs, rows, width), BF16),
            pltpu.VMEM((packs, rows, width), BF16),
            pltpu.VMEM((packs, rows, units), BF16),
            pltpu.VMEM((packs, rows, units), BF16),
            pltpu.VMEM((rows, units), BF16),
            pltpu.VMEM((rows, units), BF16),
            pltpu.VMEM((rows, units), BF16),
            pltpu.VMEM((width, rows), BF16),
            pltpu.VMEM((width, rows), BF16),
            pltpu.VMEM((width, 3 * units), F32),
            pltpu.VMEM((2 * share, 256), F32),
            pltpu.VMEM((2 * share, 256), F32),
            dma((packs, 3)),
            dma((packs, 3)),
            dma((packs, 2)),
            dma((packs, 2)),
            dma((packs, 3)),
            dma((packs, 3)),
            dma((packs, 2)),
            dma((packs, 2)),
            dma(()),
            dma((3,)),
            *scatter_scratch(packs, share, width),
        ],
        compiler_params=pltpu.CompilerParams(
            collective_id=1, has_side_effects=True, vmem_limit_bytes=VMEM_LIMIT
        ),
        cost_estimate=pl.CostEstimate(flops=int(70e9), bytes_accessed=4 * 10**7, transcendentals=10**7),
        name="ffn",
    )(r1, cot, weights, ln_params)


class Runs:
    def __init__(self, offsets, pack):
        names = [offsets[pack, place] for place in range(8)]
        start = jnp.int32(4)
        for place in range(3, -1, -1):
            start = lax.select(names[place] == names[place + 3], jnp.int32(place), start)
        self.start = start
        self.names = [lax.select(start > place, names[place], names[place + 4]) for place in range(4)]

    def masks(self, index):
        own = self.names[0]
        for place in range(1, 4):
            own = lax.select(index == place, self.names[place], own)
        return [lax.select(own == name, jnp.float32(0.0), jnp.float32(NEG)) for name in self.names]

    def arrange(self, plain, order):
        for place in range(4):
            value = plain[held_run(place), :]
            for start in range(1, 5):
                value = lax.select(self.start == start, plain[held_run(place + start), :], value)
            order(pl.ds(place * UNIT, UNIT), value)
            value = lax.select(self.start > place, plain[held_run(place), :], plain[held_run(place + 4), :])
            order(pl.ds((place + 4) * UNIT, UNIT), value)

    def restore(self, order, plain):
        for run in range(8):
            first = max(0, run - 3)
            value = order[pl.ds((run - first) * UNIT, UNIT), :]
            for start in range(first + 1, min(run, 4) + 1):
                value = lax.select(self.start == start, order[pl.ds((run - start) * UNIT, UNIT), :], value)
            if run < 4:
                value = lax.select(self.start > run, order[pl.ds((run + 4) * UNIT, UNIT), :], value)
            else:
                value = lax.select(self.start <= run - 4, order[pl.ds(run * UNIT, UNIT), :], value)
            plain(held_run(run), value)


def held_run(run):
    half, part = divmod(run, 2)
    return pl.ds(((half % 2) * 2 + half // 2) * 2 * UNIT + part * UNIT, UNIT)


def writer(ref, *at):
    def write(rows, value):
        ref[(*at, rows, slice(None))] = value

    return write


def fill_bias(bias, slopes, wide):
    heads, size, _ = bias.shape

    def fill(index):
        rws = tile(index, UNIT)
        down = lax.broadcasted_iota(jnp.int32, (UNIT, size), 0) + index * UNIT
        along = lax.broadcasted_iota(jnp.int32, (UNIT, size), 1)
        distance = jnp.abs(down - along).astype(F32)
        for head in range(heads):
            bias[head, rws, :] = -slopes[wide * heads + head] * distance

    loop(size // UNIT, fill)


def split_weights(packed, w_qkv, w_out):
    width, each = packed.shape[0], packed.shape[1] // 4
    wide = w_out.shape[1]

    def part(index):
        rws = tile(index, 128)
        zeros = jnp.zeros((128, wide - each), BF16)
        for place in range(4):
            value = jnp.concatenate([packed[rws, pl.ds(place * each, each)], zeros], axis=1)
            if place < 3:
                w_qkv[rws, pl.ds(place * wide, wide)] = value
            else:
                w_out[rws, :] = value

    loop(width // 128, part)


def mask_row(runs, index):
    return jnp.concatenate([jnp.full((1, UNIT), part, F32) for part in runs.masks(index)], axis=1)


def split_heads(value, low):
    none = jnp.zeros_like(value)
    return jnp.concatenate([jnp.where(low, value, none), jnp.where(low, none, value)], axis=0)


def head_lanes():
    lane = lax.broadcasted_iota(jnp.int32, (1, 128), 1)
    return lane < HD


def attn_kernel(
    gathering,
    offsets_ref,
    slopes_ref,
    slots_ref,
    x_ref,
    w_ref,
    r1_ref,
    held_ref,
    qkv_ref,
    ctx_ref,
    w_qkv_ref,
    w_out_ref,
    packed,
    w_qkv,
    w_out,
    bias,
    held,
    plain,
    qkv,
    ctx_order,
    ctx,
    send_a,
    recv_a,
    send_b,
    recv_b,
    load_sem,
    store_sem,
    *buffers,
):
    packs, share, width = x_ref.shape
    rows = 4 * share
    lanes = w_out.shape[1]
    group = rows // 2
    wide, core, row, mate, across = places()
    if gathering:
        slabs, slab, send_w, recv_w, *buffers = buffers
        load = pltpu.make_async_copy(w_ref.at[:, pl.ds(0, slab.shape[1])], slab, load_sem)
        load.start()
        owners = OwnerGather(slabs, send_w, recv_w, slab.shape[0], send_w.shape[2])
        greet_all((("seq", 2 * owners.line), ("wide", 4)))
        load.wait()
        slabs[owners.mine(), :] = slab[...].astype(BF16)
        owners.start()
    else:
        load = pltpu.make_async_copy(w_ref.at[:, pl.ds(0, packed.shape[1])], packed, load_sem)
        load.start()
        greet(mate, across)
    gather = Gather(held, send_a, recv_a, share)
    scatter = Scatter(*buffers, send_b, recv_b, share)
    base = pl.multiple_of((core * 2 + row) * share, share)
    for pack in range(packs):
        held[pack, pl.ds(base, share), :] = x_ref[pack]
        gather.start(pack)
    fill_bias(bias, slopes_ref, wide)
    if gathering:
        owners.pass_on()
        owners.finish()
        order_slabs(slots_ref, slabs, packed, 2 * owners.line)
    else:
        load.wait()
    split_weights(packed, w_qkv, w_out)
    low = head_lanes()
    scale = jnp.asarray(HD ** (-0.5), BF16)
    stores = [
        pltpu.make_async_copy(w_qkv, w_qkv_ref, store_sem.at[packs, 0]),
        pltpu.make_async_copy(w_out, w_out_ref, store_sem.at[packs, 1]),
    ]
    for copy in stores:
        copy.start()

    def attend(pack):
        runs = Runs(offsets_ref, pack)
        gather.finish(pack)

        def project(index):
            rws = tile(index, 256)
            value = dot_nn(held[pack, rws, :], w_qkv[...])
            plain[rws, pl.ds(0, lanes)] = (value[:, :lanes].astype(BF16) * scale).astype(BF16)
            plain[rws, pl.ds(lanes, 2 * lanes)] = value[:, lanes:].astype(BF16)

        loop(rows // 256, project)
        runs.arrange(plain, writer(qkv, pack))
        for side in range(2):
            keys = pl.ds(side * group, group)

            def weigh(part, queries, offset, side=side, keys=keys, pack=pack):
                scores = dot_nt(queries, qkv[pack, keys, pl.ds(lanes + part * 128, 128)]) + offset
                powers = jnp.exp(scores - jnp.max(scores, axis=-1, keepdims=True))
                total = jnp.sum(powers, axis=-1, keepdims=True)
                return dot_nn(powers.astype(BF16), qkv[pack, keys, pl.ds(2 * lanes + part * 128, 128)]) / total

            def pair(index, side=side, pack=pack):
                rws = pl.ds(pl.multiple_of(side * group + index * UNIT, UNIT), UNIT)
                offset = jnp.concatenate([bias[head, tile(index, UNIT), :] for head in range(2)], axis=0)
                if side:
                    offset = offset + mask_row(runs, index)
                out = weigh(0, split_heads(qkv[pack, rws, pl.ds(0, 128)], low), offset)
                ctx_order[rws, pl.ds(0, 128)] = jnp.where(low, out[:UNIT], out[UNIT:]).astype(BF16)

            def single(index, side=side, pack=pack):
                rws = pl.ds(pl.multiple_of(side * group + index * 2 * UNIT, 2 * UNIT), 2 * UNIT)
                offset = bias[2, tile(index, 2 * UNIT), :]
                if side:
                    offset = jnp.concatenate(
                        [
                            offset[half * UNIT : (half + 1) * UNIT] + mask_row(runs, 2 * index + half)
                            for half in range(2)
                        ],
                        axis=0,
                    )
                out = weigh(1, qkv[pack, rws, pl.ds(128, 128)], offset)
                ctx_order[rws, pl.ds(128, 128)] = out.astype(BF16)

            loop(4, pair, unroll=PAIRS)
            loop(2, single, unroll=SINGLES)
        runs.restore(ctx_order, writer(ctx, pack))
        for which in range(2):
            big = pl.ds(scatter.half(which), 2 * share)

            def out(index, which=which, big=big):
                cols = tile(index, 256)
                value = dot_nt(ctx[pack, big, :], w_out[cols, :])
                if which:
                    scatter.part[:, cols] = value
                else:
                    scatter.give[pack, :, cols] = value.astype(BF16)

            loop(width // 256, out)
            if not which:
                scatter.start(pack)
        scatter.middle(pack)
        for place, (source, target) in enumerate(((held, held_ref), (qkv, qkv_ref), (ctx, ctx_ref))):
            copy = pltpu.make_async_copy(source.at[pack], target.at[pack], store_sem.at[pack, place])
            copy.start()
            stores.append(copy)

    def settle(pack):
        scatter.finish(pack)

        def add(index):
            rws = tile(index, 64)
            attn = scatter.own[pack, rws, :] + scatter.reach[pack, rws, :].astype(F32)
            r1_ref[pack, rws, :] = x_ref[pack, rws, :].astype(F32) + attn

        loop(share // 64, add)

    for pack in range(packs):
        attend(pack)
        if pack:
            settle(pack - 1)
    settle(packs - 1)
    for copy in stores:
        copy.wait()
    for pack in range(packs):
        gather.drain(pack)
        scatter.drain(pack)
    if gathering:
        owners.drain()


def back_kernel(
    summing,
    offsets_ref,
    slopes_ref,
    dr1_ref,
    w_qkv_ref,
    w_out_ref,
    x_ref,
    qkv_ref,
    ctx_ref,
    *rest,
):
    padded_ref, rest = (rest[0], rest[1:]) if summing else (None, rest)
    grad_ref, grads_ref, *rest = rest
    owned_ref, rest = (rest[0], rest[1:]) if summing else (None, rest)
    (
        w_qkv,
        w_out,
        bias,
        held,
        x_all,
        qkv,
        ctx,
        plain,
        dctx,
        dorder,
        dplain,
        sum_k,
        sum_v,
        turned,
        total,
        total_out,
        send_a,
        recv_a,
        send_b,
        recv_b,
        load_sem,
        fetch_sem,
        *buffers,
    ) = rest
    if summing:
        owners = OwnerSum(padded_ref, *buffers[6:], owned_ref.shape[1] // OWNER_CHUNKS)
    packs, share, width = dr1_ref.shape
    rows = 4 * share
    lanes = w_out.shape[1]
    group = rows // 2
    loads = [
        pltpu.make_async_copy(source, target, load_sem.at[place])
        for place, (source, target) in enumerate(((w_qkv_ref, w_qkv), (w_out_ref, w_out)))
    ]
    for copy in loads:
        copy.start()
    fetches = []
    for pack in range(packs):
        for place, (source, target) in enumerate(((x_ref, x_all), (qkv_ref, qkv), (ctx_ref, ctx))):
            copy = pltpu.make_async_copy(source.at[pack], target.at[pack], fetch_sem.at[pack, place])
            copy.start()
            fetches.append(copy)
    wide, core, row, mate, across = places()
    if summing:
        greet_all((("seq", 2 * owners.line), ("wide", 4)))
    else:
        greet(mate, across)
    gather = Gather(held, send_a, recv_a, share)
    scatter = Scatter(*buffers[:6], send_b, recv_b, share)
    base = pl.multiple_of((core * 2 + row) * share, share)
    for pack in range(packs):
        held[pack, pl.ds(base, share), :] = dr1_ref[pack].astype(BF16)
        gather.start(pack)
    if summing:
        owners.start()
    fill_bias(bias, slopes_ref, wide)
    for copy in loads:
        copy.wait()
    low = head_lanes()
    scale = HD ** (-0.5)

    def pull(pack):
        runs = Runs(offsets_ref, pack)
        gather.finish(pack)

        def project(index):
            rws = tile(index, 256)
            plain[rws, :] = dot_nn(held[pack, rws, :], w_out[...]).astype(BF16)

        loop(rows // 256, project)
        runs.arrange(plain, writer(dctx))
        for copy in fetches[3 * pack : 3 * pack + 3]:
            copy.wait()
        for side in range(2):
            keys = pl.ds(side * group, group)
            sum_k[...] = jnp.zeros_like(sum_k)
            sum_v[...] = jnp.zeros_like(sum_v)

            def masked(offset, index):
                return jnp.concatenate(
                    [offset[t * UNIT : (t + 1) * UNIT] + value for t, value in enumerate(runs.masks(index))],
                    axis=0,
                )

            def pull_back(part, queries, dout, offset, keys=keys, pack=pack):
                block = pl.ds(part * 128, 128)
                k_all = qkv[pack, keys, pl.ds(lanes + part * 128, 128)]
                v_all = qkv[pack, keys, pl.ds(2 * lanes + part * 128, 128)]
                scores = dot_nt(k_all, queries) + offset
                powers = jnp.exp(scores - jnp.max(scores, axis=0, keepdims=True))
                probs = powers * (1.0 / jnp.sum(powers, axis=0, keepdims=True))
                dprobs = dot_nt(v_all, dout)
                delta = jnp.sum(probs * dprobs, axis=0, keepdims=True)
                dscores = (probs * (dprobs - delta)).astype(BF16)
                sum_v[:, block] += dot_nn(probs.astype(BF16), dout)
                sum_k[:, block] += dot_nn(dscores, queries)
                return dot_tn(dscores, k_all) * scale

            def pair(index, side=side, pack=pack):
                rws = pl.ds(pl.multiple_of(side * group + index * UNIT, UNIT), UNIT)
                block = pl.ds(0, 128)
                offsets = [bias[head, :, tile(index, UNIT)] for head in range(2)]
                if side:
                    offsets = [masked(offset, index) for offset in offsets]
                dq = pull_back(
                    0,
                    split_heads(qkv[pack, rws, block], low),
                    split_heads(dctx[rws, block], low),
                    jnp.concatenate(offsets, axis=1),
                )
                dorder[rws, block] = jnp.where(low, dq[:UNIT], dq[UNIT:]).astype(BF16)

            def single(index, side=side, pack=pack):
                rws = pl.ds(pl.multiple_of(side * group + index * 2 * UNIT, 2 * UNIT), 2 * UNIT)
                block = pl.ds(128, 128)
                offset = bias[2, :, tile(index, 2 * UNIT)]
                if side:
                    offset = jnp.concatenate(
                        [
                            masked(offset[:, half * UNIT : (half + 1) * UNIT], 2 * index + half)
                            for half in range(2)
                        ],
                        axis=1,
                    )
                dorder[rws, block] = pull_back(1, qkv[pack, rws, block], dctx[rws, block], offset).astype(BF16)

            loop(4, pair, unroll=PAIRS)
            loop(2, single, unroll=SINGLES)
            if summing:
                owners.add(2 * pack + side)
            dorder[keys, pl.ds(lanes, lanes)] = sum_k[...].astype(BF16)
            dorder[keys, pl.ds(2 * lanes, lanes)] = sum_v[...].astype(BF16)
        runs.restore(dorder, writer(dplain))
        for which in range(2):
            big = pl.ds(scatter.half(which), 2 * share)

            def out(index, which=which, big=big):
                cols = tile(index, 256)
                value = dot_nt(dplain[big, :], w_qkv[cols, :])
                if which:
                    scatter.part[:, cols] = value
                else:
                    scatter.give[pack, :, cols] = value.astype(BF16)

            loop(width // 256, out)
            if not which:
                scatter.start(pack)
        scatter.middle(pack)

    def weight_grads(pack):
        for source, result, target in ((x_all, dplain, total), (held, ctx.at[pack], total_out)):

            def flip(index, source=source):
                rws = tile(index, 256)
                turned[:, rws] = source[pack, rws, :].T

            loop(rows // 256, flip)

            def add(index, result=result, target=target):
                rws = tile(index, 256)
                value = dot_nn(turned[rws, :], result[...])
                if pack:
                    value = value + target[rws, :]
                target[rws, :] = value

            loop(width // 256, add)

    def settle(pack):
        scatter.finish(pack)

        def add(index):
            rws = tile(index, 64)
            grad_ref[pack, rws, :] = dr1_ref[pack, rws, :] + (
                scatter.own[pack, rws, :] + scatter.reach[pack, rws, :].astype(F32)
            )

        loop(share // 64, add)

    for pack in range(packs):
        pull(pack)
        weight_grads(pack)
        if pack:
            settle(pack - 1)
    each = width // 4

    def pack_up(index):
        rws = tile(index, 128)
        pieces = [total[rws, pl.ds(place * lanes, each)] for place in range(3)]
        pieces.append(total_out[rws, pl.ds(0, each)])
        grads_ref[rws, :] = jnp.concatenate([piece.astype(BF16) for piece in pieces], axis=1)

    loop(width // 128, pack_up)
    settle(packs - 1)

    def put(rws, cols, value):
        owned_ref[rws, cols] = value.astype(BF16)

    if summing:
        for index in range(OWNER_CHUNKS):
            owners.finish(index, put)
        owners.drain()
    for pack in range(packs):
        gather.drain(pack)
        scatter.drain(pack)


def attn_call(x, weights, slots, offsets, slopes, seq_count):
    packs, share, width = x.shape
    rows = 4 * share
    lanes = 256
    vm = pl.BlockSpec(memory_space=pltpu.VMEM)
    hb = pl.BlockSpec(memory_space=pl.ANY)
    sm = pl.BlockSpec(memory_space=pltpu.SMEM)
    dma = pltpu.SemaphoreType.DMA
    more = []
    if seq_count:
        parts, slab = 2, weights.shape[0]
        more = [
            pltpu.VMEM((seq_count * slab, width), BF16),
            pltpu.VMEM((slab, width), F32),
            dma((2, seq_count // 2, parts)),
            dma((2, seq_count // 2, parts)),
        ]
    return pl.pallas_call(
        functools.partial(attn_kernel, bool(seq_count)),
        out_shape=(
            jax.ShapeDtypeStruct((packs, share, width), F32),
            jax.ShapeDtypeStruct((packs, rows, width), BF16),
            jax.ShapeDtypeStruct((packs, rows, 3 * lanes), BF16),
            jax.ShapeDtypeStruct((packs, rows, lanes), BF16),
            jax.ShapeDtypeStruct((width, 3 * lanes), BF16),
            jax.ShapeDtypeStruct((width, lanes), BF16),
        ),
        in_specs=[sm, sm, sm, vm, hb],
        out_specs=(vm, hb, hb, hb, hb, hb),
        scratch_shapes=[
            pltpu.VMEM((width, width), BF16),
            pltpu.VMEM((width, 3 * lanes), BF16),
            pltpu.VMEM((width, lanes), BF16),
            pltpu.VMEM((3, rows // 2, rows // 2), F32),
            pltpu.VMEM((packs, rows, width), BF16),
            pltpu.VMEM((rows, 3 * lanes), BF16),
            pltpu.VMEM((packs, rows, 3 * lanes), BF16),
            pltpu.VMEM((rows, lanes), BF16),
            pltpu.VMEM((packs, rows, lanes), BF16),
            dma((packs, 3)),
            dma((packs, 3)),
            dma((packs, 2)),
            dma((packs, 2)),
            dma(()),
            dma((packs + 1, 3)),
            *more,
            *scatter_scratch(packs, share, width),
        ],
        compiler_params=pltpu.CompilerParams(
            collective_id=2, has_side_effects=True, vmem_limit_bytes=VMEM_LIMIT
        ),
        cost_estimate=pl.CostEstimate(flops=int(14e9), bytes_accessed=4 * 10**7, transcendentals=10**7),
        name="attn",
    )(offsets, slopes, slots, x, weights)


def back_call(dr1, w_qkv, w_out, x_all, qkv, ctx, padded, offsets, slopes, seq_count):
    packs, share, width = dr1.shape
    rows = 4 * share
    lanes = 256
    summing = padded is not None
    more_in, more_out, more_scratch = [], [], []
    if summing:
        slab, cols, line = padded.shape[0] // seq_count, padded.shape[1], seq_count // 2
        more_in = [padded.reshape(line, 2, slab, cols)]
        more_out = [jax.ShapeDtypeStruct((slab, cols), BF16)]
        more_scratch = owner_scratch(line, slab, cols, cols // OWNER_CHUNKS)
    vm = pl.BlockSpec(memory_space=pltpu.VMEM)
    hb = pl.BlockSpec(memory_space=pl.ANY)
    sm = pl.BlockSpec(memory_space=pltpu.SMEM)
    dma = pltpu.SemaphoreType.DMA
    return pl.pallas_call(
        functools.partial(back_kernel, summing),
        out_shape=(
            jax.ShapeDtypeStruct((packs, share, width), F32),
            jax.ShapeDtypeStruct((width, width), BF16),
            *more_out,
        ),
        in_specs=[sm, sm, vm, hb, hb, hb, hb, hb] + [hb] * len(more_in),
        out_specs=(vm, vm, *[vm] * len(more_out)),
        scratch_shapes=[
            pltpu.VMEM((width, 3 * lanes), BF16),
            pltpu.VMEM((width, lanes), BF16),
            pltpu.VMEM((3, rows // 2, rows // 2), F32),
            pltpu.VMEM((packs, rows, width), BF16),
            pltpu.VMEM((packs, rows, width), BF16),
            pltpu.VMEM((packs, rows, 3 * lanes), BF16),
            pltpu.VMEM((packs, rows, lanes), BF16),
            pltpu.VMEM((rows, lanes), BF16),
            pltpu.VMEM((rows, lanes), BF16),
            pltpu.VMEM((rows, 3 * lanes), BF16),
            pltpu.VMEM((rows, 3 * lanes), BF16),
            pltpu.VMEM((rows // 2, lanes), F32),
            pltpu.VMEM((rows // 2, lanes), F32),
            pltpu.VMEM((width, rows), BF16),
            pltpu.VMEM((width, 3 * lanes), F32),
            pltpu.VMEM((width, lanes), F32),
            dma((packs, 3)),
            dma((packs, 3)),
            dma((packs, 2)),
            dma((packs, 2)),
            dma((2,)),
            dma((packs, 3)),
            *scatter_scratch(packs, share, width),
            *more_scratch,
        ],
        compiler_params=pltpu.CompilerParams(
            collective_id=3, has_side_effects=True, vmem_limit_bytes=VMEM_LIMIT
        ),
        cost_estimate=pl.CostEstimate(flops=int(40e9), bytes_accessed=4 * 10**7, transcendentals=10**7),
        name="back",
    )(offsets, slopes, dr1, w_qkv, w_out, x_all, qkv, ctx, *more_in)


class OwnerGather:
    def __init__(self, held, send, recv, slab, parts):
        self.held, self.send, self.recv, self.slab, self.parts = held, send, recv, slab, parts
        seq = lax.axis_index("seq")
        self.line = held.shape[0] // slab // 2
        self.x = lax.rem(seq, 2)
        self.z = seq // 2

    def block(self, owner, part):
        size = self.held.shape[1] // self.parts
        rows = pl.ds(pl.multiple_of(owner * self.slab, self.slab), self.slab)
        return self.held.at[rows, pl.ds(part * size, size)]

    def mine(self):
        return pl.ds(pl.multiple_of((2 * self.z + self.x) * self.slab, self.slab), self.slab)

    def source(self, step):
        return lax.rem(self.z + self.line - step, self.line)

    def hop(self, step, part):
        block = self.block(2 * self.z + self.x, part)
        peer = 2 * lax.rem(self.z + step, self.line) + self.x
        return remote(block, block, self.send.at[0, step, part], self.recv.at[0, step, part], peer, "seq")

    def landed(self, step, part):
        block = self.block(2 * self.source(step) + self.x, part)
        peer = 2 * self.z + 1 - self.x
        return remote(block, block, self.send.at[0, step, part], self.recv.at[0, step, part], peer, "seq")

    def cross(self, step, part, x):
        block = self.block(2 * self.source(step) + x, part)
        peer = 2 * self.z + 1 - self.x
        return remote(block, block, self.send.at[1, step, part], self.recv.at[1, step, part], peer, "seq")

    def start(self):
        for part in range(self.parts):
            self.cross(0, part, self.x).start()
        for step in range(1, self.line):
            for part in range(self.parts):
                self.hop(step, part).start()

    def pass_on(self):
        for step in range(1, self.line):
            for part in range(self.parts):
                self.landed(step, part).wait_recv()
                self.cross(step, part, self.x).start()

    def finish(self):
        for step in range(self.line):
            for part in range(self.parts):
                self.cross(step, part, 1 - self.x).wait_recv()

    def drain(self):
        for step in range(self.line):
            for part in range(self.parts):
                self.cross(step, part, self.x).wait_send()
                if step:
                    self.hop(step, part).wait_send()


def order_slabs(slots, slabs, packed, owners):
    blocks, rows, slab = slots.shape[0], packed.shape[0], slabs.shape[0] // owners
    block, step = rows // blocks, 8
    for first in range(0, blocks, step):
        last = first + step - 1
        low = first // CAP
        high = max(o for o in range(owners) if max(o, blocks - CAP * (owners - o)) <= last)
        count = (high - low + 1) * slab
        lines = []
        for place in range(first, first + step):
            down = lax.broadcasted_iota(jnp.int32, (block, count), 0)
            along = lax.broadcasted_iota(jnp.int32, (block, count), 1)
            hit = along - down == slots[place] * block - low * slab
            lines.append(jnp.where(hit, 1.0, 0.0).astype(BF16))
        value = dot_nn(jnp.concatenate(lines, axis=0), slabs[pl.ds(low * slab, count), :])
        packed[pl.ds(first * block, step * block), :] = value.astype(BF16)


class OwnerSum:
    def __init__(self, source, sums, beside, along, load, send, recv, chunk):
        self.source, self.sums, self.beside, self.along = source, sums, beside, along
        self.load, self.send, self.recv, self.chunk = load, send, recv, chunk
        seq = lax.axis_index("seq")
        self.line = sums.shape[0]
        self.x = lax.rem(seq, 2)
        self.z = seq // 2

    def chunks(self):
        return self.sums.shape[2] // self.chunk

    def cols(self, index):
        return pl.ds(index * self.chunk, self.chunk)

    def peers(self):
        found = [2 * self.z + 1 - self.x]
        for step in range(1, self.line):
            found.append(2 * lax.rem(self.z + step, self.line) + self.x)
        return found

    def own_load(self):
        return pltpu.make_async_copy(self.source.at[:, self.x], self.sums, self.load)

    def cross(self, index):
        return remote(
            self.source.at[:, 1 - self.x, :, self.cols(index)],
            self.beside.at[index],
            self.send.at[index, 0],
            self.recv.at[index, 0],
            2 * self.z + 1 - self.x,
            "seq",
        )

    def hop(self, index, step):
        other = lax.rem(self.z + step, self.line)
        return remote(
            self.sums.at[other, :, self.cols(index)],
            self.along.at[index, step - 1],
            self.send.at[index, step],
            self.recv.at[index, step],
            2 * other + self.x,
            "seq",
        )

    def start(self):
        self.own_load().start()
        for index in range(self.chunks()):
            self.cross(index).start()

    def add(self, index):
        if index == 0:
            self.own_load().wait()
        self.cross(index).wait_recv()
        cols = self.cols(index)
        for other in range(self.line):

            def part(row, other=other):
                rws = tile(row, 32)
                value = self.sums[other, rws, cols].astype(F32) + self.beside[index, other, rws, :].astype(F32)
                self.sums[other, rws, cols] = value.astype(BF16)

            loop(self.sums.shape[1] // 32, part)
        for step in range(1, self.line):
            self.hop(index, step).start()

    def finish(self, index, target):
        for step in range(1, self.line):
            self.hop(index, step).wait_recv()
        cols = self.cols(index)

        def part(row):
            rws = tile(row, 32)
            value = self.sums[self.z, rws, cols].astype(F32)
            for step in range(1, self.line):
                value = value + self.along[index, step - 1, rws, :].astype(F32)
            target(rws, cols, value)

        loop(self.sums.shape[1] // 32, part)

    def drain(self):
        for index in range(self.chunks()):
            self.cross(index).wait_send()
            for step in range(1, self.line):
                self.hop(index, step).wait_send()


def owner_scratch(line, slab, width, chunk):
    count = width // chunk
    dma = pltpu.SemaphoreType.DMA
    return [
        pltpu.VMEM((line, slab, width), BF16),
        pltpu.VMEM((count, line, slab, chunk), BF16),
        pltpu.VMEM((count, line - 1, slab, chunk), BF16),
        dma(()),
        dma((count, line)),
        dma((count, line)),
    ]


class Total:
    def __init__(self, axis, slots, send, recv):
        self.axis, self.slots, self.send, self.recv = axis, slots, send, recv
        self.count = slots.shape[0]
        self.place = lax.axis_index(axis)

    def copy(self, step):
        mine = self.slots.at[self.place]
        return remote(
            mine, mine, self.send.at[step - 1], self.recv.at[self.place], self.peer(step), self.axis
        )

    def peer(self, step):
        return lax.rem(self.place + step, self.count)

    def start(self, value):
        self.slots[self.place] = value
        for step in range(1, self.count):
            self.copy(step).start()

    def finish(self):
        for step in range(1, self.count):
            other = self.peer(step)
            slot = self.slots.at[other]
            remote(
                slot, slot, self.send.at[step - 1], self.recv.at[other], other, self.axis
            ).wait_recv()
        value = self.slots[0]
        for place in range(1, self.count):
            value = value + self.slots[place]
        return value

    def drain(self):
        for step in range(1, self.count):
            self.copy(step).wait_send()


def total_scratch(count, shape):
    dma = pltpu.SemaphoreType.DMA
    return [pltpu.VMEM((count, *shape), F32), dma((count - 1,)), dma((count,))]


def greet_all(axes):
    barrier = pltpu.get_barrier_semaphore()
    sent = 0
    for axis, count in axes:
        place = lax.axis_index(axis)
        for step in range(1, count):
            peer = lax.rem(place + step, count)
            pl.semaphore_signal(barrier, inc=1, device_id={axis: peer}, device_id_type=MESH)
            sent += 1
    pl.semaphore_wait(barrier, sent)


def close_kernel(
    seq_count,
    wide_count,
    kept_ref,
    grads_ref,
    ffn_ref,
    ln_ref,
    owned_ref,
    ln_out_ref,
    square_ref,
    *scratch,
):
    greet_all((("seq", seq_count), ("wide", wide_count)))
    owners = OwnerSum(grads_ref, *scratch[:6], 256)
    norms = [Total("wide", *scratch[6:9]), Total("seq", *scratch[9:12])]
    squares = [Total("wide", *scratch[12:15]), Total("seq", *scratch[15:18])]
    acc = scratch[18]
    slab = owned_ref.shape[0]
    width = grads_ref.shape[3]
    owners.start()
    norms[0].start(ln_ref[...])
    acc[...] = jnp.zeros_like(acc)

    def keep(rws, value):
        row = lax.broadcasted_iota(jnp.int32, value.shape, 0) + rws.start
        return jnp.where(row < kept_ref[0], value, 0.0)

    def note(value):
        square = value * value
        for place in range(value.shape[1] // 128):
            part = square[:, place * 128 : (place + 1) * 128]
            for row in range(0, value.shape[0], 8):
                acc[...] += part[row : row + 8]

    def put(rws, cols, value):
        value = keep(rws, value)
        owned_ref[rws, cols] = value
        note(value)

    def from_ffn(index):
        rws = tile(index, 8)
        value = keep(rws, ffn_ref[rws, :].astype(F32))
        owned_ref[rws, pl.ds(width, ffn_ref.shape[1])] = value
        note(value)

    for index in range(owners.chunks()):
        owners.add(index)
    norms[1].start(norms[0].finish())
    loop(slab // 8, from_ffn)
    for index in range(owners.chunks()):
        owners.finish(index, put)
    squares[0].start(acc[...])
    squares[1].start(squares[0].finish())
    ln_out_ref[...] = norms[1].finish()
    square_ref[...] = squares[1].finish()
    owners.drain()
    for part in (*norms, *squares):
        part.drain()


def close_call(kept, grads, ffn_owned, ln_rows, seq_count, wide_count):
    slab = ffn_owned.shape[0]
    width = grads.shape[1]
    line = seq_count // 2
    vm = pl.BlockSpec(memory_space=pltpu.VMEM)
    sm = pl.BlockSpec(memory_space=pltpu.SMEM)
    return pl.pallas_call(
        functools.partial(close_kernel, seq_count, wide_count),
        out_shape=(
            jax.ShapeDtypeStruct((slab, width + ffn_owned.shape[1]), F32),
            jax.ShapeDtypeStruct(ln_rows.shape, F32),
            jax.ShapeDtypeStruct((8, 128), F32),
        ),
        in_specs=[sm, pl.BlockSpec(memory_space=pl.ANY), vm, vm],
        out_specs=(vm, vm, vm),
        scratch_shapes=[
            *owner_scratch(line, slab, width, 256),
            *total_scratch(wide_count, ln_rows.shape),
            *total_scratch(seq_count, ln_rows.shape),
            *total_scratch(wide_count, (8, 128)),
            *total_scratch(seq_count, (8, 128)),
            pltpu.VMEM((8, 128), F32),
        ],
        compiler_params=pltpu.CompilerParams(
            collective_id=4, has_side_effects=True, vmem_limit_bytes=VMEM_LIMIT
        ),
        name="close",
    )(kept, grads.reshape(line, 2, slab, width), ffn_owned, ln_rows)


def pick_kernel(block, places_ref, source_ref, target_ref, held, sems, sem):
    count = places_ref.shape[1]

    def copy(index):
        return pltpu.make_async_copy(
            source_ref.at[pl.ds(pl.multiple_of(places_ref[0, index] * block, block), block)],
            held.at[pl.ds(pl.multiple_of(index * block, block), block)],
            sems.at[index],
        )

    loop(count, lambda index: copy(index).start())
    loop(count, lambda index: copy(index).wait())
    out = pltpu.make_async_copy(held, target_ref, sem)
    out.start()
    out.wait()


def spread_kernel(block, places_ref, source_ref, target_ref, held, sems, sem):
    count = places_ref.shape[1]
    load = pltpu.make_async_copy(source_ref, held, sem)
    load.start()
    load.wait()

    def copy(index):
        return pltpu.make_async_copy(
            held.at[pl.ds(pl.multiple_of(index * block, block), block)],
            target_ref.at[pl.ds(pl.multiple_of(places_ref[1, index] * block, block), block)],
            sems.at[index],
        )

    loop(count, lambda index: copy(index).start())
    loop(count, lambda index: copy(index).wait())


def move_blocks(kernel, source, places, rows, block):
    hb = pl.BlockSpec(memory_space=pl.ANY)
    count = places.shape[1]
    return pl.pallas_call(
        functools.partial(kernel, block),
        out_shape=jax.ShapeDtypeStruct((rows, source.shape[1]), source.dtype),
        in_specs=[pl.BlockSpec(memory_space=pltpu.SMEM), hb],
        out_specs=hb,
        scratch_shapes=[
            pltpu.VMEM((count * block, source.shape[1]), source.dtype),
            pltpu.SemaphoreType.DMA((count,)),
            pltpu.SemaphoreType.DMA(()),
        ],
        compiler_params=pltpu.CompilerParams(vmem_limit_bytes=VMEM_LIMIT),
        name="move",
    )(places, source)


def per_device(
    hidden_in,
    cotangent,
    seq_offsets,
    owner_blocks,
    master,
    first_moment,
    second_moment,
    ln_params,
    ln_first,
    ln_second,
):
    width = hidden_in.shape[2]
    slab_rows = master.shape[0]
    block = slab_rows // CAP
    source, valid, target = owner_maps(owner_blocks, width, CAP, block)
    low = master.astype(jnp.bfloat16)
    rest = lax.all_gather(low[:, width:], "seq", axis=0, tiled=True)
    gathered_rows = slab_rows * lax.axis_size("seq")
    count = width // block
    fits = block % 16 == 0
    slots = target[::block] // block
    both = jnp.stack([slots, slots])

    def to_order(array):
        if fits:
            return move_blocks(pick_kernel, array, both, width, block)
        return jnp.take(array, target, axis=0)

    def to_owner(grads):
        if fits:
            return move_blocks(spread_kernel, grads, both, gathered_rows, block)
        return jnp.take(grads, source, axis=0)

    seq_count = lax.axis_size("seq")
    own_kernels = fits and seq_count == 8
    if own_kernels:
        weights = master
    else:
        weights = to_order(lax.all_gather(low[:, :width], "seq", axis=0, tiled=True))
    w_ffn = to_order(rest)
    slopes = jnp.exp2(-8.0 * (jnp.arange(H, dtype=jnp.float32) + 1.0) / H)
    x = jnp.transpose(hidden_in, (1, 0, 2))
    r1, x_all, qkv, ctx, w_qkv, w_out = attn_call(
        x, weights, slots, seq_offsets, slopes, seq_count if own_kernels else 0
    )
    mixed_p, dr1_p, ffn_grads, ln_rows = ffn_call(
        r1, jnp.transpose(cotangent, (1, 0, 2)), w_ffn, ln_params
    )
    mixed = jnp.transpose(mixed_p, (1, 0, 2))

    ffn_padded = to_owner(ffn_grads)
    grad_p, attn_grads, *more = back_call(
        dr1_p, w_qkv, w_out, x_all, qkv, ctx, ffn_padded if own_kernels else None, seq_offsets, slopes, seq_count
    )
    input_grad = jnp.transpose(grad_p, (1, 0, 2))
    attn_padded = to_owner(attn_grads)
    mine = jnp.arange(seq_count, dtype=jnp.int32) == lax.axis_index("seq")
    own_rows = jnp.sum(jnp.where(mine, owner_blocks, 0)) * block
    kept = (jnp.arange(slab_rows, dtype=jnp.int32) < own_rows)[:, None]
    if own_kernels:
        owned, ln_total, parts = close_call(
            own_rows[None], attn_padded, more[0], ln_rows, seq_count, lax.axis_size("wide")
        )
        squares, ln_total = jnp.sum(parts), ln_total[:4]
    else:
        ffn_owned = lax.psum_scatter(ffn_padded, "seq", scatter_dimension=0, tiled=True)
        attn_owned = lax.psum_scatter(attn_padded, "seq", scatter_dimension=0, tiled=True)
        owned = jnp.concatenate([attn_owned, ffn_owned], axis=1).astype(jnp.float32)
        owned = jnp.where(kept, owned, 0.0)
        squares, ln_total = lax.psum((jnp.sum(owned * owned), ln_rows[:4]), ("seq", "wide"))
    grad_norm = jnp.sqrt(squares + jnp.sum(ln_total * ln_total))
    clip = jnp.minimum(1.0, 1.0 / (grad_norm + 1e-06))
    param_new, first_new, second_new = adamw(
        master, owned * clip, first_moment, second_moment, DECAY, RATE
    )
    norms_new, norms_first, norms_second = adamw(
        ln_params, ln_total * clip, ln_first, ln_second, 0.0, NORM_RATE
    )
    return (
        mixed,
        input_grad,
        jnp.where(kept, param_new, 0.0),
        jnp.where(kept, first_new, 0.0),
        jnp.where(kept, second_new, 0.0),
        norms_new,
        norms_first,
        norms_second,
        grad_norm,
    )


def solution(mesh):
    return jax.shard_map(
        per_device,
        mesh=mesh,
        in_specs=(
            P("wide", "seq", None),
            P("wide", "seq", None),
            P("seq", None),
            P(),
            P("seq", "wide"),
            P("seq", "wide"),
            P("seq", "wide"),
            P(),
            P(),
            P(),
        ),
        out_specs=(
            P("wide", "seq", None),
            P("wide", "seq", None),
            P("seq", "wide"),
            P("seq", "wide"),
            P("seq", "wide"),
            P(),
            P(),
            P(),
            P(),
        ),
        check_vma=False,
    )
```

```python
import functools

import jax
import jax.numpy as jnp
from jax import lax
from jax.experimental import pallas as pl
from jax.experimental.pallas import tpu as pltpu
from jax.sharding import PartitionSpec as P

MESH = pl.DeviceIdType.MESH

H = 12
HD = 64
FF = 3072
UNIT = 128
CAP = 6
STEP = 10


RATE = 0.02
NORM_RATE = 0.6
BETA_ONE = 0.9
BETA_TWO = 0.999
EPSILON = 1e-08
DECAY = 0.01
NORM_EPS = 1e-05
ROOT_HALF = 0.7071067811865476
DENSITY_SCALE = 0.3989422804014327
EPS = 1e-05
F32 = jnp.float32
BF16 = jnp.bfloat16
NEG = -1e30
PAIRS = 4
SINGLES = 2
VMEM_LIMIT = 60 * 2**20


def owner_maps(owner_blocks, rows, cap, block):
    ends = jnp.cumsum(owner_blocks)
    starts = ends - owner_blocks
    slot = jnp.arange(cap * block, dtype=jnp.int32)
    which = slot // block
    source = (starts[:, None] + which[None, :]) * block + (slot % block)[None, :]
    valid = which[None, :] < owner_blocks[:, None]
    source = jnp.where(valid, source, 0).reshape(-1)
    valid = valid.reshape(-1)
    param = jnp.arange(rows, dtype=jnp.int32)
    blocks = param // block
    owner = jnp.sum((ends[None, :] <= blocks[:, None]).astype(jnp.int32), axis=1)
    onehot = owner[:, None] == jnp.arange(owner_blocks.shape[0], dtype=jnp.int32)[None, :]
    first = jnp.sum(jnp.where(onehot, starts[None, :], 0), axis=1)
    target = owner * (cap * block) + (blocks - first) * block + param % block
    return (source, valid, target)


def adamw(param, grad, first, second, decay, rate):
    first_new = BETA_ONE * first + (1.0 - BETA_ONE) * grad
    second_new = BETA_TWO * second + (1.0 - BETA_TWO) * grad * grad
    first_hat = first_new / (1.0 - BETA_ONE**STEP)
    second_hat = second_new / (1.0 - BETA_TWO**STEP)
    param_new = param - rate * (first_hat / (jnp.sqrt(second_hat) + EPSILON) + decay * param)
    return (param_new, first_new, second_new)


def dot_nn(a, b):
    return lax.dot_general(a, b, (((1,), (0,)), ((), ())), preferred_element_type=F32)


def dot_nt(a, b):
    return lax.dot_general(a, b, (((1,), (1,)), ((), ())), preferred_element_type=F32)


def dot_tn(a, b):
    return lax.dot_general(a, b, (((0,), (0,)), ((), ())), preferred_element_type=F32)


def places():
    wide = lax.axis_index("wide")
    core = lax.rem(wide, 2)
    row = wide // 2
    return wide, core, row, wide + 1 - 2 * core, wide + 2 - 4 * row


def greet(mate, across):
    barrier = pltpu.get_barrier_semaphore()
    for peer in (mate, across):
        pl.semaphore_signal(barrier, inc=1, device_id={"wide": peer}, device_id_type=MESH)
    pl.semaphore_wait(barrier, 2)


def remote(source, target, send, recv, peer, axis="wide"):
    return pltpu.make_async_remote_copy(
        src_ref=source,
        dst_ref=target,
        send_sem=send,
        recv_sem=recv,
        device_id={axis: peer},
        device_id_type=MESH,
    )


class Gather:
    def __init__(self, held, send, recv, share):
        self.held, self.send, self.recv, self.share = held, send, recv, share
        _, self.core, self.row, self.mate, self.across = places()

    def rows(self, core, row):
        return pl.ds(pl.multiple_of((core * 2 + row) * self.share, self.share), self.share)

    def copy(self, pack, leg):
        row = 1 - self.row if leg == 2 else self.row
        block = self.held.at[pack, self.rows(self.core, row)]
        peer = self.mate if leg else self.across
        return remote(block, block, self.send.at[pack, leg], self.recv.at[pack, leg], peer)

    def start(self, pack):
        self.copy(pack, 0).start()
        self.copy(pack, 1).start()

    def finish(self, pack):
        self.copy(pack, 0).wait_recv()
        self.copy(pack, 2).start()
        self.copy(pack, 1).wait_recv()
        self.copy(pack, 2).wait_recv()

    def drain(self, pack):
        for leg in range(3):
            self.copy(pack, leg).wait_send()


class Scatter:
    def __init__(self, part, give, take, cross, reach, own, send, recv, share):
        self.part, self.give, self.take = part, give, take
        self.cross, self.reach, self.own = cross, reach, own
        self.send, self.recv, self.share = send, recv, share
        _, self.core, self.row, self.mate, self.across = places()

    def copy(self, pack, leg):
        source, target = (self.cross, self.reach) if leg else (self.give, self.take)
        peer = self.across if leg else self.mate
        return remote(
            source.at[pack], target.at[pack], self.send.at[pack, leg], self.recv.at[pack, leg], peer
        )

    def half(self, which):
        core = self.core if which else 1 - self.core
        return pl.multiple_of(core * 2 * self.share, 2 * self.share)

    def start(self, pack):
        self.copy(pack, 0).start()

    def middle(self, pack):
        self.copy(pack, 0).wait_recv()
        share = self.share
        far = pl.ds(pl.multiple_of((1 - self.row) * share, share), share)
        near = pl.ds(pl.multiple_of(self.row * share, share), share)
        self.cross[pack] = (self.part[far, :] + self.take[pack, far, :].astype(F32)).astype(BF16)
        self.copy(pack, 1).start()
        self.own[pack] = self.part[near, :] + self.take[pack, near, :].astype(F32)

    def finish(self, pack):
        self.copy(pack, 1).wait_recv()

    def drain(self, pack):
        for leg in range(2):
            self.copy(pack, leg).wait_send()


def scatter_scratch(packs, share, width):
    return [
        pltpu.VMEM((2 * share, width), F32),
        pltpu.VMEM((packs, 2 * share, width), BF16),
        pltpu.VMEM((packs, 2 * share, width), BF16),
        pltpu.VMEM((packs, share, width), BF16),
        pltpu.VMEM((packs, share, width), BF16),
        pltpu.VMEM((packs, share, width), F32),
    ]


def norm_parts(values):
    center = values - jnp.mean(values, axis=-1, keepdims=True)
    inverse = lax.rsqrt(jnp.mean(center * center, axis=-1, keepdims=True) + EPS)
    return center * inverse, inverse


def norm_pull(grad, normal, inverse, gain):
    scaled = grad * gain
    return inverse * (
        scaled
        - jnp.mean(scaled, axis=-1, keepdims=True)
        - normal * jnp.mean(scaled * normal, axis=-1, keepdims=True)
    )


def loop(count, body, unroll=1):
    def step(index, carry):
        body(index)
        return carry

    lax.fori_loop(0, count, step, 0, unroll=unroll)


def tile(index, size):
    return pl.ds(pl.multiple_of(index * size, size), size)


def ffn_kernel(
    r1_ref,
    cot_ref,
    w_ref,
    ln_ref,
    mixed_ref,
    dr1_ref,
    grads_ref,
    lngrad_ref,
    weights,
    held,
    held2,
    gates,
    ups,
    hid,
    dgate,
    dup,
    turned,
    turned2,
    total,
    g_tile,
    u_tile,
    send_a,
    recv_a,
    send_b,
    recv_b,
    send_c,
    recv_c,
    send_d,
    recv_d,
    load_sem,
    store_sem,
    *buffers,
):
    packs, share, width = r1_ref.shape
    rows = 4 * share
    fwd = buffers[:6]
    units = weights.shape[1] // 3
    col = 256
    n_units, n_width = units // col, width // col
    load = pltpu.make_async_copy(w_ref.at[:, pl.ds(w_ref.shape[1] - 3 * units, 3 * units)], weights, load_sem)
    load.start()
    _, core, row, mate, across = places()
    greet(mate, across)
    gather_one = Gather(held, send_a, recv_a, share)
    scatter_one = Scatter(*fwd, send_b, recv_b, share)
    gather_two = Gather(held2, send_c, recv_c, share)
    scatter_two = Scatter(*fwd, send_d, recv_d, share)
    gain1, shift1 = ln_ref[0:1, :], ln_ref[1:2, :]
    gain2, shift2 = ln_ref[2:3, :], ln_ref[3:4, :]
    lngrad_ref[...] = jnp.zeros_like(lngrad_ref)
    chunk = 64

    for pack in range(packs):
        base = pl.multiple_of((core * 2 + row) * share, share)

        def first(index, pack=pack, base=base):
            normal, _ = norm_parts(r1_ref[pack, tile(index, chunk), :])
            held[pack, pl.ds(pl.multiple_of(base + index * chunk, chunk), chunk), :] = (
                normal * gain1 + shift1
            ).astype(BF16)

        loop(share // chunk, first)
        gather_one.start(pack)
    load.wait()

    def forward(pack):
        gather_one.finish(pack)
        for which in range(2):
            base = scatter_one.half(which)
            big = pl.ds(base, 2 * share)

            def ff(index):
                cols = tile(index, col)
                x = held[pack, big, :]
                g_tile[...] = dot_nn(x, weights[:, cols])
                u_tile[...] = dot_nn(x, weights[:, pl.ds(pl.multiple_of(units + index * col, col), col)])

                def act(part):
                    rws = tile(part, 32)
                    gate, up = g_tile[rws, :], u_tile[rws, :]
                    out = pl.ds(pl.multiple_of(base + part * 32, 32), 32)
                    cumulative = 0.5 * (1.0 + lax.erf(gate * ROOT_HALF))
                    hid[out, cols] = (gate * cumulative * up).astype(BF16)
                    gates[pack, out, cols] = gate.astype(BF16)
                    ups[pack, out, cols] = up.astype(BF16)

                loop(2 * share // 32, act, unroll=2)

            loop(n_units, ff)

            def down(index):
                wd = weights[tile(index, col), pl.ds(2 * units, units)]
                value = dot_nt(hid[big, :], wd)
                if which:
                    scatter_one.part[:, tile(index, col)] = value
                else:
                    scatter_one.give[pack, :, tile(index, col)] = value.astype(BF16)

            loop(n_width, down)
            if not which:
                scatter_one.start(pack)
        scatter_one.middle(pack)

    def turn(pack):
        scatter_one.finish(pack)
        gather_two_base = pl.multiple_of((core * 2 + row) * share, share)

        def second(index):
            rws = tile(index, chunk)
            normal, _ = norm_parts(r1_ref[pack, rws, :])
            ffn = scatter_one.own[pack, rws, :] + scatter_one.reach[pack, rws, :].astype(F32)
            normal2, inverse2 = norm_parts(normal * gain1 + shift1 + ffn)
            mixed_ref[pack, rws, :] = (normal2 * gain2 + shift2).astype(BF16)
            grad = cot_ref[pack, rws, :].astype(F32)
            value = norm_pull(grad, normal2, inverse2, gain2)
            dr1_ref[pack, rws, :] = value
            held2[pack, pl.ds(pl.multiple_of(gather_two_base + index * chunk, chunk), chunk), :] = value.astype(BF16)
            lngrad_ref[2:3, :] += jnp.sum(grad * normal2, axis=0, keepdims=True)
            lngrad_ref[3:4, :] += jnp.sum(grad, axis=0, keepdims=True)

        loop(share // chunk, second)
        scatter_one.drain(pack)
        gather_two.start(pack)

    def backward(pack):
        gather_two.finish(pack)
        for which in range(2):
            base = scatter_two.half(which)
            big = pl.ds(base, 2 * share)

            def bf(index):
                cols = tile(index, col)
                g_tile[...] = dot_nn(
                    held2[pack, big, :], weights[:, pl.ds(pl.multiple_of(2 * units + index * col, col), col)]
                )

                def act(part):
                    rws = tile(part, 32)
                    out = pl.ds(pl.multiple_of(base + part * 32, 32), 32)
                    dhid = g_tile[rws, :]
                    gate = gates[pack, out, cols].astype(F32)
                    up = ups[pack, out, cols].astype(F32)
                    cumulative = 0.5 * (1.0 + lax.erf(gate * ROOT_HALF))
                    density = jnp.exp(-0.5 * gate * gate) * DENSITY_SCALE
                    value = gate * cumulative
                    hid[out, cols] = (value * up).astype(BF16)
                    dgate[out, cols] = (dhid * up * (cumulative + gate * density)).astype(BF16)
                    dup[out, cols] = (dhid * value).astype(BF16)

                loop(2 * share // 32, act, unroll=2)

            loop(n_units, bf)

            def back(index):
                rws = tile(index, col)
                value = dot_nt(dgate[big, :], weights[rws, pl.ds(0, units)]) + dot_nt(
                    dup[big, :], weights[rws, pl.ds(units, units)]
                )
                if which:
                    scatter_two.part[:, tile(index, col)] = value
                else:
                    scatter_two.give[pack, :, tile(index, col)] = value.astype(BF16)

            loop(n_width, back)
            if not which:
                scatter_two.start(pack)
        scatter_two.middle(pack)

    def weight_grads(pack):
        def flip(index):
            rws = tile(index, 256)
            turned[:, rws] = held[pack, rws, :].T
            turned2[:, rws] = held2[pack, rws, :].T

        loop(rows // 256, flip)

        def add(index):
            rws = tile(index, col)
            a = turned[rws, :]
            b = turned2[rws, :]
            parts = (dot_nn(a, dgate[...]), dot_nn(a, dup[...]), dot_nn(b, hid[...]))
            for place, value in enumerate(parts):
                cols = pl.ds(place * units, units)
                if pack == 0:
                    total[rws, cols] = value
                else:
                    value = total[rws, cols] + value
                    if pack < packs - 1:
                        total[rws, cols] = value
                    else:
                        gates[place, rws, :] = value.astype(BF16)

        loop(n_width, add)

    def last(pack):
        scatter_two.finish(pack)

        def third(index):
            rws = tile(index, chunk)
            normal, inverse = norm_parts(r1_ref[pack, rws, :])
            grad = dr1_ref[pack, rws, :] + (
                scatter_two.own[pack, rws, :] + scatter_two.reach[pack, rws, :].astype(F32)
            )
            dr1_ref[pack, rws, :] = norm_pull(grad, normal, inverse, gain1)
            lngrad_ref[0:1, :] += jnp.sum(grad * normal, axis=0, keepdims=True)
            lngrad_ref[1:2, :] += jnp.sum(grad, axis=0, keepdims=True)

        loop(share // chunk, third)

    for pack in range(packs):
        forward(pack)
        if pack:
            turn(pack - 1)
    for pack in range(packs):
        backward(pack)
        weight_grads(pack)
        if pack == 0:
            turn(packs - 1)
        else:
            last(pack - 1)
    outs = [
        pltpu.make_async_copy(
            gates.at[place, pl.ds(0, width)],
            grads_ref.at[:, pl.ds(place * units, units)],
            store_sem.at[place],
        )
        for place in range(3)
    ]
    for out in outs:
        out.start()
    last(packs - 1)
    for out in outs:
        out.wait()
    for pack in range(packs):
        gather_one.drain(pack)
        gather_two.drain(pack)
        scatter_two.drain(pack)


def ffn_call(r1, cot, weights, ln_params):
    packs, share, width = r1.shape
    rows = 4 * share
    units = weights.shape[1] // 3
    vm = pl.BlockSpec(memory_space=pltpu.VMEM)
    hb = pl.BlockSpec(memory_space=pl.ANY)
    dma = pltpu.SemaphoreType.DMA
    return pl.pallas_call(
        ffn_kernel,
        out_shape=(
            jax.ShapeDtypeStruct((packs, share, width), BF16),
            jax.ShapeDtypeStruct((packs, share, width), F32),
            jax.ShapeDtypeStruct((width, 3 * units), BF16),
            jax.ShapeDtypeStruct((8, width), F32),
        ),
        in_specs=[vm, vm, hb, vm],
        out_specs=(vm, vm, hb, vm),
        scratch_shapes=[
            pltpu.VMEM((width, 3 * units), BF16),
            pltpu.VMEM((packs, rows, width), BF16),
            pltpu.VMEM((packs, rows, width), BF16),
            pltpu.VMEM((packs, rows, units), BF16),
            pltpu.VMEM((packs, rows, units), BF16),
            pltpu.VMEM((rows, units), BF16),
            pltpu.VMEM((rows, units), BF16),
            pltpu.VMEM((rows, units), BF16),
            pltpu.VMEM((width, rows), BF16),
            pltpu.VMEM((width, rows), BF16),
            pltpu.VMEM((width, 3 * units), F32),
            pltpu.VMEM((2 * share, 256), F32),
            pltpu.VMEM((2 * share, 256), F32),
            dma((packs, 3)),
            dma((packs, 3)),
            dma((packs, 2)),
            dma((packs, 2)),
            dma((packs, 3)),
            dma((packs, 3)),
            dma((packs, 2)),
            dma((packs, 2)),
            dma(()),
            dma((3,)),
            *scatter_scratch(packs, share, width),
        ],
        compiler_params=pltpu.CompilerParams(
            collective_id=1, has_side_effects=True, vmem_limit_bytes=VMEM_LIMIT
        ),
        cost_estimate=pl.CostEstimate(flops=int(70e9), bytes_accessed=4 * 10**7, transcendentals=10**7),
        name="ffn",
    )(r1, cot, weights, ln_params)


class Runs:
    def __init__(self, offsets, pack):
        names = [offsets[pack, place] for place in range(8)]
        start = jnp.int32(4)
        for place in range(3, -1, -1):
            start = lax.select(names[place] == names[place + 3], jnp.int32(place), start)
        self.start = start
        self.names = [lax.select(start > place, names[place], names[place + 4]) for place in range(4)]

    def masks(self, index):
        own = self.names[0]
        for place in range(1, 4):
            own = lax.select(index == place, self.names[place], own)
        return [lax.select(own == name, jnp.float32(0.0), jnp.float32(NEG)) for name in self.names]

    def arrange(self, plain, order):
        for place in range(4):
            value = plain[held_run(place), :]
            for start in range(1, 5):
                value = lax.select(self.start == start, plain[held_run(place + start), :], value)
            order(pl.ds(place * UNIT, UNIT), value)
            value = lax.select(self.start > place, plain[held_run(place), :], plain[held_run(place + 4), :])
            order(pl.ds((place + 4) * UNIT, UNIT), value)

    def restore(self, order, plain):
        for run in range(8):
            first = max(0, run - 3)
            value = order[pl.ds((run - first) * UNIT, UNIT), :]
            for start in range(first + 1, min(run, 4) + 1):
                value = lax.select(self.start == start, order[pl.ds((run - start) * UNIT, UNIT), :], value)
            if run < 4:
                value = lax.select(self.start > run, order[pl.ds((run + 4) * UNIT, UNIT), :], value)
            else:
                value = lax.select(self.start <= run - 4, order[pl.ds(run * UNIT, UNIT), :], value)
            plain(held_run(run), value)


def held_run(run):
    half, part = divmod(run, 2)
    return pl.ds(((half % 2) * 2 + half // 2) * 2 * UNIT + part * UNIT, UNIT)


def writer(ref, *at):
    def write(rows, value):
        ref[(*at, rows, slice(None))] = value

    return write


def fill_bias(bias, slopes, wide):
    heads, size, _ = bias.shape

    def fill(index):
        rws = tile(index, UNIT)
        down = lax.broadcasted_iota(jnp.int32, (UNIT, size), 0) + index * UNIT
        along = lax.broadcasted_iota(jnp.int32, (UNIT, size), 1)
        distance = jnp.abs(down - along).astype(F32)
        for head in range(heads):
            bias[head, rws, :] = -slopes[wide * heads + head] * distance

    loop(size // UNIT, fill)


def split_weights(packed, w_qkv, w_out):
    width, each = packed.shape[0], packed.shape[1] // 4
    wide = w_out.shape[1]

    def part(index):
        rws = tile(index, 128)
        zeros = jnp.zeros((128, wide - each), BF16)
        for place in range(4):
            value = jnp.concatenate([packed[rws, pl.ds(place * each, each)], zeros], axis=1)
            if place < 3:
                w_qkv[rws, pl.ds(place * wide, wide)] = value
            else:
                w_out[rws, :] = value

    loop(width // 128, part)


def mask_row(runs, index):
    return jnp.concatenate([jnp.full((1, UNIT), part, F32) for part in runs.masks(index)], axis=1)


def split_heads(value, low):
    none = jnp.zeros_like(value)
    return jnp.concatenate([jnp.where(low, value, none), jnp.where(low, none, value)], axis=0)


def head_lanes():
    lane = lax.broadcasted_iota(jnp.int32, (1, 128), 1)
    return lane < HD


def attn_kernel(
    gathering,
    offsets_ref,
    slopes_ref,
    slots_ref,
    x_ref,
    w_ref,
    r1_ref,
    held_ref,
    qkv_ref,
    ctx_ref,
    w_qkv_ref,
    w_out_ref,
    *rest,
):
    w_ffn_ref, rest = (rest[0], rest[1:]) if gathering else (None, rest)
    (
        packed,
        w_qkv,
        w_out,
        bias,
        held,
        plain,
        qkv,
        ctx_order,
        ctx,
        send_a,
        recv_a,
        send_b,
        recv_b,
        load_sem,
        store_sem,
        *buffers,
    ) = rest
    packs, share, width = x_ref.shape
    rows = 4 * share
    lanes = w_out.shape[1]
    group = rows // 2
    wide, core, row, mate, across = places()
    if gathering:
        slab, near, near_send, near_recv, far, far_send, far_recv, ordered, *buffers = buffers
        load = pltpu.make_async_copy(w_ref, slab, load_sem)
        load.start()
        owners = OwnerGather(near, near_send, near_recv, slab.shape[0])
        others = OwnerGather(far, far_send, far_recv, slab.shape[0])
        holders = near.shape[1] // slab.shape[0]
        greet_all((("seq", holders), ("wide", 4)))
        load.wait()
        cut = near.shape[2]
        for part in range(owners.groups):
            value = slab[:, part * cut : (part + 1) * cut]
            near[part, owners.rows(owners.seq), :] = value.astype(BF16)
        owners.start()
        cut = far.shape[2]
        for part in range(others.groups):
            value = slab[:, width + part * cut : width + (part + 1) * cut]
            far[part, others.rows(others.seq), :] = value.astype(BF16)
    else:
        load = pltpu.make_async_copy(w_ref.at[:, pl.ds(0, packed.shape[1])], packed, load_sem)
        load.start()
        greet(mate, across)
    gather = Gather(held, send_a, recv_a, share)
    scatter = Scatter(*buffers, send_b, recv_b, share)
    base = pl.multiple_of((core * 2 + row) * share, share)
    for pack in range(packs):
        held[pack, pl.ds(base, share), :] = x_ref[pack]
        gather.start(pack)
    fill_bias(bias, slopes_ref, wide)
    stores = []
    todo = []

    def pump(count):
        for _ in range(min(count, len(todo))):
            todo.pop(0)()

    if gathering:
        for step in owners.steps():
            step()
        others.start()
        todo = others.steps()
        cut = near.shape[2]
        for part in range(owners.groups):
            owners.finish(part)
            order_slabs(slots_ref, near, part, packed, pl.ds(part * cut, cut), holders)

        def settled(part):
            others.finish(part)
            cut = far.shape[2]
            cols = pl.ds(part * cut, cut)
            order_slabs(slots_ref, far, part, ordered, cols, holders)
            copy = pltpu.make_async_copy(
                ordered.at[:, cols], w_ffn_ref.at[:, cols], store_sem.at[packs + 1, part]
            )
            copy.start()
            stores.append(copy)

        todo += [functools.partial(settled, part) for part in range(others.groups)]
    else:
        load.wait()
    split_weights(packed, w_qkv, w_out)
    low = head_lanes()
    scale = jnp.asarray(HD ** (-0.5), BF16)
    for place, (source, target) in enumerate(((w_qkv, w_qkv_ref), (w_out, w_out_ref))):
        copy = pltpu.make_async_copy(source, target, store_sem.at[packs, place])
        copy.start()
        stores.append(copy)

    def attend(pack):
        runs = Runs(offsets_ref, pack)
        gather.finish(pack)

        def project(index):
            rws = tile(index, 256)
            value = dot_nn(held[pack, rws, :], w_qkv[...])
            plain[rws, pl.ds(0, lanes)] = (value[:, :lanes].astype(BF16) * scale).astype(BF16)
            plain[rws, pl.ds(lanes, 2 * lanes)] = value[:, lanes:].astype(BF16)

        loop(rows // 256, project)
        runs.arrange(plain, writer(qkv, pack))
        for side in range(2):
            keys = pl.ds(side * group, group)

            def weigh(part, queries, offset, side=side, keys=keys, pack=pack):
                scores = dot_nt(queries, qkv[pack, keys, pl.ds(lanes + part * 128, 128)]) + offset
                powers = jnp.exp(scores - jnp.max(scores, axis=-1, keepdims=True))
                total = jnp.sum(powers, axis=-1, keepdims=True)
                return dot_nn(powers.astype(BF16), qkv[pack, keys, pl.ds(2 * lanes + part * 128, 128)]) / total

            def pair(index, side=side, pack=pack):
                rws = pl.ds(pl.multiple_of(side * group + index * UNIT, UNIT), UNIT)
                offset = jnp.concatenate([bias[head, tile(index, UNIT), :] for head in range(2)], axis=0)
                if side:
                    offset = offset + mask_row(runs, index)
                out = weigh(0, split_heads(qkv[pack, rws, pl.ds(0, 128)], low), offset)
                ctx_order[rws, pl.ds(0, 128)] = jnp.where(low, out[:UNIT], out[UNIT:]).astype(BF16)

            def single(index, side=side, pack=pack):
                rws = pl.ds(pl.multiple_of(side * group + index * 2 * UNIT, 2 * UNIT), 2 * UNIT)
                offset = bias[2, tile(index, 2 * UNIT), :]
                if side:
                    offset = jnp.concatenate(
                        [
                            offset[half * UNIT : (half + 1) * UNIT] + mask_row(runs, 2 * index + half)
                            for half in range(2)
                        ],
                        axis=0,
                    )
                out = weigh(1, qkv[pack, rws, pl.ds(128, 128)], offset)
                ctx_order[rws, pl.ds(128, 128)] = out.astype(BF16)

            loop(4, pair, unroll=PAIRS)
            loop(2, single, unroll=SINGLES)
            pump(1 if pack else 0)
        runs.restore(ctx_order, writer(ctx, pack))
        for which in range(2):
            big = pl.ds(scatter.half(which), 2 * share)

            def out(index, which=which, big=big):
                cols = tile(index, 256)
                value = dot_nt(ctx[pack, big, :], w_out[cols, :])
                if which:
                    scatter.part[:, cols] = value
                else:
                    scatter.give[pack, :, cols] = value.astype(BF16)

            loop(width // 256, out)
            if not which:
                scatter.start(pack)
        scatter.middle(pack)
        pump(2)
        for place, (source, target) in enumerate(((held, held_ref), (qkv, qkv_ref), (ctx, ctx_ref))):
            copy = pltpu.make_async_copy(source.at[pack], target.at[pack], store_sem.at[pack, place])
            copy.start()
            stores.append(copy)

    def settle(pack):
        scatter.finish(pack)

        def add(index):
            rws = tile(index, 64)
            attn = scatter.own[pack, rws, :] + scatter.reach[pack, rws, :].astype(F32)
            r1_ref[pack, rws, :] = x_ref[pack, rws, :].astype(F32) + attn

        loop(share // 64, add)

    for pack in range(packs):
        attend(pack)
        if pack:
            settle(pack - 1)
    settle(packs - 1)
    pump(len(todo))
    for copy in stores:
        copy.wait()
    for pack in range(packs):
        gather.drain(pack)
        scatter.drain(pack)
    if gathering:
        owners.drain()
        others.drain()


def back_kernel(
    summing,
    offsets_ref,
    slopes_ref,
    dr1_ref,
    w_qkv_ref,
    w_out_ref,
    x_ref,
    qkv_ref,
    ctx_ref,
    *rest,
):
    padded_ref, rest = (rest[0], rest[1:]) if summing else (None, rest)
    grad_ref, grads_ref, *rest = rest
    owned_ref, rest = (rest[0], rest[1:]) if summing else (None, rest)
    (
        w_qkv,
        w_out,
        bias,
        held,
        x_all,
        qkv,
        ctx,
        plain,
        dctx,
        dorder,
        dplain,
        sum_k,
        sum_v,
        turned,
        total,
        total_out,
        send_a,
        recv_a,
        send_b,
        recv_b,
        load_sem,
        fetch_sem,
        *buffers,
    ) = rest
    if summing:
        owners = OwnerSum(padded_ref, *buffers[6:])

        def put(rws, cols, value):
            owned_ref[rws, cols] = value.astype(BF16)

        todo = owners.steps(put)
    else:
        todo = []

    def pump(count):
        for _ in range(min(count, len(todo))):
            todo.pop(0)()

    packs, share, width = dr1_ref.shape
    rows = 4 * share
    lanes = w_out.shape[1]
    group = rows // 2
    loads = [
        pltpu.make_async_copy(source, target, load_sem.at[place])
        for place, (source, target) in enumerate(((w_qkv_ref, w_qkv), (w_out_ref, w_out)))
    ]
    for copy in loads:
        copy.start()
    fetches = []
    for pack in range(packs):
        for place, (source, target) in enumerate(((x_ref, x_all), (qkv_ref, qkv), (ctx_ref, ctx))):
            copy = pltpu.make_async_copy(source.at[pack], target.at[pack], fetch_sem.at[pack, place])
            copy.start()
            fetches.append(copy)
    wide, core, row, mate, across = places()
    if summing:
        greet_all((("seq", padded_ref.shape[0]), ("wide", 4)))
    else:
        greet(mate, across)
    gather = Gather(held, send_a, recv_a, share)
    scatter = Scatter(*buffers[:6], send_b, recv_b, share)
    base = pl.multiple_of((core * 2 + row) * share, share)
    for pack in range(packs):
        held[pack, pl.ds(base, share), :] = dr1_ref[pack].astype(BF16)
        gather.start(pack)
    if summing:
        owners.start()
    fill_bias(bias, slopes_ref, wide)
    for copy in loads:
        copy.wait()
    low = head_lanes()
    scale = HD ** (-0.5)

    def pull(pack):
        runs = Runs(offsets_ref, pack)
        gather.finish(pack)

        def project(index):
            rws = tile(index, 256)
            plain[rws, :] = dot_nn(held[pack, rws, :], w_out[...]).astype(BF16)

        loop(rows // 256, project)
        runs.arrange(plain, writer(dctx))
        for copy in fetches[3 * pack : 3 * pack + 3]:
            copy.wait()
        for side in range(2):
            keys = pl.ds(side * group, group)
            sum_k[...] = jnp.zeros_like(sum_k)
            sum_v[...] = jnp.zeros_like(sum_v)

            def masked(offset, index):
                return jnp.concatenate(
                    [offset[t * UNIT : (t + 1) * UNIT] + value for t, value in enumerate(runs.masks(index))],
                    axis=0,
                )

            def pull_back(part, queries, dout, offset, keys=keys, pack=pack):
                block = pl.ds(part * 128, 128)
                k_all = qkv[pack, keys, pl.ds(lanes + part * 128, 128)]
                v_all = qkv[pack, keys, pl.ds(2 * lanes + part * 128, 128)]
                scores = dot_nt(k_all, queries) + offset
                powers = jnp.exp(scores - jnp.max(scores, axis=0, keepdims=True))
                probs = powers * (1.0 / jnp.sum(powers, axis=0, keepdims=True))
                dprobs = dot_nt(v_all, dout)
                delta = jnp.sum(probs * dprobs, axis=0, keepdims=True)
                dscores = (probs * (dprobs - delta)).astype(BF16)
                sum_v[:, block] += dot_nn(probs.astype(BF16), dout)
                sum_k[:, block] += dot_nn(dscores, queries)
                return dot_tn(dscores, k_all) * scale

            def pair(index, side=side, pack=pack):
                rws = pl.ds(pl.multiple_of(side * group + index * UNIT, UNIT), UNIT)
                block = pl.ds(0, 128)
                offsets = [bias[head, :, tile(index, UNIT)] for head in range(2)]
                if side:
                    offsets = [masked(offset, index) for offset in offsets]
                dq = pull_back(
                    0,
                    split_heads(qkv[pack, rws, block], low),
                    split_heads(dctx[rws, block], low),
                    jnp.concatenate(offsets, axis=1),
                )
                dorder[rws, block] = jnp.where(low, dq[:UNIT], dq[UNIT:]).astype(BF16)

            def single(index, side=side, pack=pack):
                rws = pl.ds(pl.multiple_of(side * group + index * 2 * UNIT, 2 * UNIT), 2 * UNIT)
                block = pl.ds(128, 128)
                offset = bias[2, :, tile(index, 2 * UNIT)]
                if side:
                    offset = jnp.concatenate(
                        [
                            masked(offset[:, half * UNIT : (half + 1) * UNIT], 2 * index + half)
                            for half in range(2)
                        ],
                        axis=1,
                    )
                dorder[rws, block] = pull_back(1, qkv[pack, rws, block], dctx[rws, block], offset).astype(BF16)

            loop(4, pair, unroll=PAIRS)
            loop(2, single, unroll=SINGLES)
            pump(((4, 2), (1, 1), (1, 1))[pack][side])
            dorder[keys, pl.ds(lanes, lanes)] = sum_k[...].astype(BF16)
            dorder[keys, pl.ds(2 * lanes, lanes)] = sum_v[...].astype(BF16)
        runs.restore(dorder, writer(dplain))
        for which in range(2):
            big = pl.ds(scatter.half(which), 2 * share)

            def out(index, which=which, big=big):
                cols = tile(index, 256)
                value = dot_nt(dplain[big, :], w_qkv[cols, :])
                if which:
                    scatter.part[:, cols] = value
                else:
                    scatter.give[pack, :, cols] = value.astype(BF16)

            loop(width // 256, out)
            if not which:
                scatter.start(pack)
        scatter.middle(pack)
        pump((2, 1, 1)[pack])

    def weight_grads(pack):
        for source, result, target in ((x_all, dplain, total), (held, ctx.at[pack], total_out)):

            def flip(index, source=source):
                rws = tile(index, 256)
                turned[:, rws] = source[pack, rws, :].T

            loop(rows // 256, flip)

            def add(index, result=result, target=target):
                rws = tile(index, 256)
                value = dot_nn(turned[rws, :], result[...])
                if pack:
                    value = value + target[rws, :]
                target[rws, :] = value

            loop(width // 256, add)

    def settle(pack):
        scatter.finish(pack)

        def add(index):
            rws = tile(index, 64)
            grad_ref[pack, rws, :] = dr1_ref[pack, rws, :] + (
                scatter.own[pack, rws, :] + scatter.reach[pack, rws, :].astype(F32)
            )

        loop(share // 64, add)

    for pack in range(packs):
        pull(pack)
        weight_grads(pack)
        pump((2, 1, 0)[pack])
        if pack:
            settle(pack - 1)
    each = width // 4

    def pack_up(index):
        rws = tile(index, 128)
        pieces = [total[rws, pl.ds(place * lanes, each)] for place in range(3)]
        pieces.append(total_out[rws, pl.ds(0, each)])
        grads_ref[rws, :] = jnp.concatenate([piece.astype(BF16) for piece in pieces], axis=1)

    loop(width // 128, pack_up)
    settle(packs - 1)

    pump(len(todo))
    if summing:
        owners.drain()
    for pack in range(packs):
        gather.drain(pack)
        scatter.drain(pack)


def attn_call(x, weights, slots, offsets, slopes, seq_count):
    packs, share, width = x.shape
    rows = 4 * share
    lanes = 256
    vm = pl.BlockSpec(memory_space=pltpu.VMEM)
    hb = pl.BlockSpec(memory_space=pl.ANY)
    sm = pl.BlockSpec(memory_space=pltpu.SMEM)
    dma = pltpu.SemaphoreType.DMA
    more, more_out = [], []
    if seq_count:
        slab, units = weights.shape[0], weights.shape[1] - width
        groups = len(GATHER_ORDERS)
        more = [
            pltpu.VMEM(weights.shape, F32),
            *gather_scratch(seq_count * slab, width, groups),
            *gather_scratch(seq_count * slab, units, groups),
            pltpu.VMEM((width, units), BF16),
        ]
        more_out = [jax.ShapeDtypeStruct((width, units), BF16)]
    return pl.pallas_call(
        functools.partial(attn_kernel, bool(seq_count)),
        out_shape=(
            jax.ShapeDtypeStruct((packs, share, width), F32),
            jax.ShapeDtypeStruct((packs, rows, width), BF16),
            jax.ShapeDtypeStruct((packs, rows, 3 * lanes), BF16),
            jax.ShapeDtypeStruct((packs, rows, lanes), BF16),
            jax.ShapeDtypeStruct((width, 3 * lanes), BF16),
            jax.ShapeDtypeStruct((width, lanes), BF16),
            *more_out,
        ),
        in_specs=[sm, sm, sm, vm, hb],
        out_specs=(vm, *[hb] * (5 + len(more_out))),
        scratch_shapes=[
            pltpu.VMEM((width, width), BF16),
            pltpu.VMEM((width, 3 * lanes), BF16),
            pltpu.VMEM((width, lanes), BF16),
            pltpu.VMEM((3, rows // 2, rows // 2), F32),
            pltpu.VMEM((packs, rows, width), BF16),
            pltpu.VMEM((rows, 3 * lanes), BF16),
            pltpu.VMEM((packs, rows, 3 * lanes), BF16),
            pltpu.VMEM((rows, lanes), BF16),
            pltpu.VMEM((packs, rows, lanes), BF16),
            dma((packs, 3)),
            dma((packs, 3)),
            dma((packs, 2)),
            dma((packs, 2)),
            dma(()),
            dma((packs + 2, 3)),
            *more,
            *scatter_scratch(packs, share, width),
        ],
        compiler_params=pltpu.CompilerParams(
            collective_id=2, has_side_effects=True, vmem_limit_bytes=VMEM_LIMIT
        ),
        cost_estimate=pl.CostEstimate(flops=int(14e9), bytes_accessed=4 * 10**7, transcendentals=10**7),
        name="attn",
    )(offsets, slopes, slots, x, weights)


def back_call(dr1, w_qkv, w_out, x_all, qkv, ctx, padded, offsets, slopes, seq_count):
    packs, share, width = dr1.shape
    rows = 4 * share
    lanes = 256
    summing = padded is not None
    more_in, more_out, more_scratch = [], [], []
    if summing:
        slab, cols = padded.shape[0] // seq_count, padded.shape[1]
        more_in = [padded.reshape(seq_count, slab, cols)]
        more_out = [jax.ShapeDtypeStruct((slab, cols), BF16)]
        more_scratch = owner_scratch(slab, cols, len(SUM_ORDERS))
    vm = pl.BlockSpec(memory_space=pltpu.VMEM)
    hb = pl.BlockSpec(memory_space=pl.ANY)
    sm = pl.BlockSpec(memory_space=pltpu.SMEM)
    dma = pltpu.SemaphoreType.DMA
    return pl.pallas_call(
        functools.partial(back_kernel, summing),
        out_shape=(
            jax.ShapeDtypeStruct((packs, share, width), F32),
            jax.ShapeDtypeStruct((width, width), BF16),
            *more_out,
        ),
        in_specs=[sm, sm, vm, hb, hb, hb, hb, hb] + [hb] * len(more_in),
        out_specs=(vm, vm, *[vm] * len(more_out)),
        scratch_shapes=[
            pltpu.VMEM((width, 3 * lanes), BF16),
            pltpu.VMEM((width, lanes), BF16),
            pltpu.VMEM((3, rows // 2, rows // 2), F32),
            pltpu.VMEM((packs, rows, width), BF16),
            pltpu.VMEM((packs, rows, width), BF16),
            pltpu.VMEM((packs, rows, 3 * lanes), BF16),
            pltpu.VMEM((packs, rows, lanes), BF16),
            pltpu.VMEM((rows, lanes), BF16),
            pltpu.VMEM((rows, lanes), BF16),
            pltpu.VMEM((rows, 3 * lanes), BF16),
            pltpu.VMEM((rows, 3 * lanes), BF16),
            pltpu.VMEM((rows // 2, lanes), F32),
            pltpu.VMEM((rows // 2, lanes), F32),
            pltpu.VMEM((width, rows), BF16),
            pltpu.VMEM((width, 3 * lanes), F32),
            pltpu.VMEM((width, lanes), F32),
            dma((packs, 3)),
            dma((packs, 3)),
            dma((packs, 2)),
            dma((packs, 2)),
            dma((2,)),
            dma((packs, 3)),
            *scatter_scratch(packs, share, width),
            *more_scratch,
        ],
        compiler_params=pltpu.CompilerParams(
            collective_id=3, has_side_effects=True, vmem_limit_bytes=VMEM_LIMIT
        ),
        cost_estimate=pl.CostEstimate(flops=int(40e9), bytes_accessed=4 * 10**7, transcendentals=10**7),
        name="back",
    )(offsets, slopes, dr1, w_qkv, w_out, x_all, qkv, ctx, *more_in)


def flip_bits(place, *bits):
    for bit in bits:
        place = place + bit - 2 * bit * lax.rem(place // bit, 2)
    return place


GATHER_ORDERS = ((4, 2, 1), (4, 2, 1), (4, 1, 2))
SUM_ORDERS = ((1, 2, 4), (1, 2, 4), (2, 1, 4))


class OwnerGather:
    PEERS = (0, 1, 2, 1, 2, 2, 2)
    SLABS = ((), (), (), (0,), (0,), (1,), (0, 1))

    def __init__(self, held, send, recv, slab):
        self.held, self.send, self.recv, self.slab = held, send, recv, slab
        self.groups = held.shape[0]
        self.seq = lax.axis_index("seq")

    def rows(self, owner):
        return pl.ds(pl.multiple_of(owner * self.slab, self.slab), self.slab)

    def copy(self, group, leg, incoming=False):
        order = GATHER_ORDERS[group]
        bits = [order[place] for place in self.SLABS[leg]]
        if incoming:
            bits.append(order[self.PEERS[leg]])
        block = self.held.at[group, self.rows(flip_bits(self.seq, *bits))]
        peer = flip_bits(self.seq, order[self.PEERS[leg]])
        return remote(block, block, self.send.at[group, leg], self.recv.at[group, leg], peer, "seq")

    def start(self):
        for group in range(self.groups):
            for leg in range(3):
                self.copy(group, leg).start()

    def steps(self):
        found = []
        for first, *rest in ((0, 3, 4), (1, 5), (3, 6)):
            for group in range(self.groups):

                def step(group=group, first=first, rest=rest):
                    self.copy(group, first, True).wait_recv()
                    for leg in rest:
                        self.copy(group, leg).start()

                found.append(step)
        return found

    def finish(self, group):
        for leg in (2, 4, 5, 6):
            self.copy(group, leg, True).wait_recv()

    def drain(self):
        for group in range(self.groups):
            for leg in range(7):
                self.copy(group, leg).wait_send()


def gather_scratch(rows, cols, groups):
    dma = pltpu.SemaphoreType.DMA
    return [pltpu.VMEM((groups, rows, cols // groups), BF16), dma((groups, 7)), dma((groups, 7))]


def order_slabs(slots, slabs, group, target, cols, owners):
    blocks, rows, slab = slots.shape[0], target.shape[0], slabs.shape[1] // owners
    block, step = rows // blocks, 8
    for first in range(0, blocks, step):
        last = first + step - 1
        low = first // CAP
        high = max(o for o in range(owners) if max(o, blocks - CAP * (owners - o)) <= last)
        count = (high - low + 1) * slab
        lines = []
        for place in range(first, first + step):
            down = lax.broadcasted_iota(jnp.int32, (block, count), 0)
            along = lax.broadcasted_iota(jnp.int32, (block, count), 1)
            hit = along - down == slots[place] * block - low * slab
            lines.append(jnp.where(hit, 1.0, 0.0).astype(BF16))
        lines = jnp.concatenate(lines, axis=0)
        for part in range(0, cols.size, 256):
            value = dot_nn(lines, slabs[group, pl.ds(low * slab, count), pl.ds(part, 256)])
            target[pl.ds(first * block, step * block), pl.ds(cols.start + part, 256)] = value.astype(BF16)


class OwnerSum:
    KEPT = ((1, 2), (1,), (2,), ())

    def __init__(self, source, own, first, second, third, load, send, recv):
        self.source, self.own, self.first, self.second, self.third = source, own, first, second, third
        self.load, self.send, self.recv = load, send, recv
        self.groups, self.slab, self.size = own.shape[0], own.shape[2], own.shape[3]
        self.seq = lax.axis_index("seq")

    def block(self, group, step, *more):
        order = SUM_ORDERS[group]
        owner = flip_bits(self.seq, *[order[place] for place in self.KEPT[step]], *more)
        return self.source.at[owner, :, pl.ds(group * self.size, self.size)]

    def fetch(self, group, step):
        return pltpu.make_async_copy(
            self.block(group, step), self.own.at[group, step], self.load.at[group, step]
        )

    def copy(self, group, leg):
        order = SUM_ORDERS[group]
        if leg < 4:
            source, target, bit = self.block(group, leg, order[0]), self.first.at[group, leg], order[0]
        elif leg < 6:
            source, target, bit = self.own.at[group, leg - 4], self.second.at[group, leg - 4], order[1]
        else:
            source, target, bit = self.own.at[group, 2], self.third.at[group], order[2]
        return remote(
            source, target, self.send.at[group, leg], self.recv.at[group, leg], flip_bits(self.seq, bit), "seq"
        )

    def start(self):
        for group in range(self.groups):
            for step in range(4):
                self.copy(group, step).start()
                self.fetch(group, step).start()

    def into(self, group, step, *others):
        def part(row):
            rws = tile(row, 32)
            value = self.own[group, step, rws, :].astype(F32)
            for other in others:
                value = value + other[rws, :].astype(F32)
            self.own[group, step, rws, :] = value.astype(BF16)

        loop(self.slab // 32, part)

    def add(self, group, step):
        self.fetch(group, step).wait()
        self.copy(group, step).wait_recv()
        if step < 2:
            self.into(group, step, self.first.at[group, step])
            self.copy(group, 4 + step).start()

    def pair(self, group):
        self.copy(group, 4).wait_recv()
        self.into(group, 2, self.first.at[group, 2], self.second.at[group, 0])
        self.copy(group, 6).start()

    def finish(self, group, target):
        self.copy(group, 5).wait_recv()
        self.copy(group, 6).wait_recv()

        def part(row):
            rws = tile(row, 32)
            value = self.own[group, 3, rws, :].astype(F32)
            for other in (self.first.at[group, 3], self.second.at[group, 1], self.third.at[group]):
                value = value + other[rws, :].astype(F32)
            target(rws, pl.ds(group * self.size, self.size), value)

        loop(self.slab // 32, part)

    def steps(self, target):
        found = []
        for step in range(4):
            found.append(functools.partial(self.add, 0, step))
            found.append(functools.partial(self.add, 2, step))
        for step in range(2):
            found.append(functools.partial(self.add, 1, step))
        found.append(functools.partial(self.pair, 0))
        for step in range(2, 4):
            found.append(functools.partial(self.add, 1, step))
        found.append(functools.partial(self.finish, 0, target))
        for group in (1, 2):
            found.append(functools.partial(self.pair, group))
        for group in (1, 2):
            found.append(functools.partial(self.finish, group, target))
        return found

    def drain(self):
        for group in range(self.groups):
            for leg in range(7):
                self.copy(group, leg).wait_send()


def owner_scratch(slab, width, groups):
    dma = pltpu.SemaphoreType.DMA
    size = width // groups
    return [
        pltpu.VMEM((groups, 4, slab, size), BF16),
        pltpu.VMEM((groups, 4, slab, size), BF16),
        pltpu.VMEM((groups, 2, slab, size), BF16),
        pltpu.VMEM((groups, slab, size), BF16),
        dma((groups, 4)),
        dma((groups, 7)),
        dma((groups, 7)),
    ]


class Total:
    def __init__(self, axis, slots, send, recv):
        self.axis, self.slots, self.send, self.recv = axis, slots, send, recv
        self.count = slots.shape[0]
        self.place = lax.axis_index(axis)

    def copy(self, step):
        mine = self.slots.at[self.place]
        return remote(
            mine, mine, self.send.at[step - 1], self.recv.at[self.place], self.peer(step), self.axis
        )

    def peer(self, step):
        return lax.rem(self.place + step, self.count)

    def start(self, value):
        self.slots[self.place] = value
        for step in range(1, self.count):
            self.copy(step).start()

    def finish(self):
        for step in range(1, self.count):
            other = self.peer(step)
            slot = self.slots.at[other]
            remote(
                slot, slot, self.send.at[step - 1], self.recv.at[other], other, self.axis
            ).wait_recv()
        value = self.slots[0]
        for place in range(1, self.count):
            value = value + self.slots[place]
        return value

    def drain(self):
        for step in range(1, self.count):
            self.copy(step).wait_send()


def total_scratch(count, shape):
    dma = pltpu.SemaphoreType.DMA
    return [pltpu.VMEM((count, *shape), F32), dma((count - 1,)), dma((count,))]


def greet_all(axes):
    barrier = pltpu.get_barrier_semaphore()
    sent = 0
    for axis, count in axes:
        place = lax.axis_index(axis)
        for step in range(1, count):
            peer = lax.rem(place + step, count)
            pl.semaphore_signal(barrier, inc=1, device_id={axis: peer}, device_id_type=MESH)
            sent += 1
    pl.semaphore_wait(barrier, sent)


def close_kernel(
    seq_count,
    wide_count,
    kept_ref,
    grads_ref,
    ffn_ref,
    ln_ref,
    owned_ref,
    ln_out_ref,
    square_ref,
    *scratch,
):
    greet_all((("seq", seq_count), ("wide", wide_count)))
    sums, scratch = scratch[:7], scratch[7:]
    owners = OwnerSum(grads_ref, *sums)
    norms = [Total("wide", *scratch[0:3]), Total("seq", *scratch[3:6])]
    squares = [Total("wide", *scratch[6:9]), Total("seq", *scratch[9:12])]
    acc = scratch[12]
    slab = owned_ref.shape[0]
    width = grads_ref.shape[2]
    owners.start()
    norms[0].start(ln_ref[...])
    acc[...] = jnp.zeros_like(acc)

    def keep(rws, value):
        row = lax.broadcasted_iota(jnp.int32, value.shape, 0) + rws.start
        return jnp.where(row < kept_ref[0], value, 0.0)

    def note(value):
        square = value * value
        rows = sum(square[row : row + 8] for row in range(0, value.shape[0], 8))
        acc[...] += sum(rows[:, place : place + 128] for place in range(0, value.shape[1], 128))

    def put(rws, cols, value):
        value = keep(rws, value)
        owned_ref[rws, cols] = value
        note(value)

    def from_ffn(index):
        rws = tile(index, 16)
        value = keep(rws, ffn_ref[rws, :].astype(F32))
        owned_ref[rws, pl.ds(width, ffn_ref.shape[1])] = value
        note(value)

    steps = owners.steps(put)
    for step in steps[:8]:
        step()
    norms[1].start(norms[0].finish())
    for step in steps[8:14]:
        step()
    loop(slab // 16, from_ffn)
    for step in steps[14:]:
        step()
    squares[0].start(acc[...])
    squares[1].start(squares[0].finish())
    ln_out_ref[...] = norms[1].finish()
    square_ref[...] = squares[1].finish()
    owners.drain()
    for part in (*norms, *squares):
        part.drain()


def close_call(kept, grads, ffn_owned, ln_rows, seq_count, wide_count):
    slab = ffn_owned.shape[0]
    width = grads.shape[1]
    vm = pl.BlockSpec(memory_space=pltpu.VMEM)
    sm = pl.BlockSpec(memory_space=pltpu.SMEM)
    return pl.pallas_call(
        functools.partial(close_kernel, seq_count, wide_count),
        out_shape=(
            jax.ShapeDtypeStruct((slab, width + ffn_owned.shape[1]), F32),
            jax.ShapeDtypeStruct(ln_rows.shape, F32),
            jax.ShapeDtypeStruct((8, 128), F32),
        ),
        in_specs=[sm, pl.BlockSpec(memory_space=pl.ANY), vm, vm],
        out_specs=(vm, vm, vm),
        scratch_shapes=[
            *owner_scratch(slab, width, len(SUM_ORDERS)),
            *total_scratch(wide_count, ln_rows.shape),
            *total_scratch(seq_count, ln_rows.shape),
            *total_scratch(wide_count, (8, 128)),
            *total_scratch(seq_count, (8, 128)),
            pltpu.VMEM((8, 128), F32),
        ],
        compiler_params=pltpu.CompilerParams(
            collective_id=4, has_side_effects=True, vmem_limit_bytes=VMEM_LIMIT
        ),
        name="close",
    )(kept, grads.reshape(seq_count, slab, width), ffn_owned, ln_rows)


def pick_kernel(block, places_ref, source_ref, target_ref, held, sems, sem):
    count = places_ref.shape[1]

    def copy(index):
        return pltpu.make_async_copy(
            source_ref.at[pl.ds(pl.multiple_of(places_ref[0, index] * block, block), block)],
            held.at[pl.ds(pl.multiple_of(index * block, block), block)],
            sems.at[index],
        )

    loop(count, lambda index: copy(index).start())
    loop(count, lambda index: copy(index).wait())
    out = pltpu.make_async_copy(held, target_ref, sem)
    out.start()
    out.wait()


def spread_kernel(block, places_ref, source_ref, target_ref, held, sems, sem):
    count = places_ref.shape[1]
    load = pltpu.make_async_copy(source_ref, held, sem)
    load.start()
    load.wait()

    def copy(index):
        return pltpu.make_async_copy(
            held.at[pl.ds(pl.multiple_of(index * block, block), block)],
            target_ref.at[pl.ds(pl.multiple_of(places_ref[1, index] * block, block), block)],
            sems.at[index],
        )

    loop(count, lambda index: copy(index).start())
    loop(count, lambda index: copy(index).wait())


def move_blocks(kernel, source, places, rows, block):
    hb = pl.BlockSpec(memory_space=pl.ANY)
    count = places.shape[1]
    return pl.pallas_call(
        functools.partial(kernel, block),
        out_shape=jax.ShapeDtypeStruct((rows, source.shape[1]), source.dtype),
        in_specs=[pl.BlockSpec(memory_space=pltpu.SMEM), hb],
        out_specs=hb,
        scratch_shapes=[
            pltpu.VMEM((count * block, source.shape[1]), source.dtype),
            pltpu.SemaphoreType.DMA((count,)),
            pltpu.SemaphoreType.DMA(()),
        ],
        compiler_params=pltpu.CompilerParams(vmem_limit_bytes=VMEM_LIMIT),
        name="move",
    )(places, source)


def per_device(
    hidden_in,
    cotangent,
    seq_offsets,
    owner_blocks,
    master,
    first_moment,
    second_moment,
    ln_params,
    ln_first,
    ln_second,
):
    width = hidden_in.shape[2]
    slab_rows = master.shape[0]
    block = slab_rows // CAP
    source, valid, target = owner_maps(owner_blocks, width, CAP, block)
    gathered_rows = slab_rows * lax.axis_size("seq")
    count = width // block
    fits = block % 16 == 0
    slots = target[::block] // block
    both = jnp.stack([slots, slots])

    def to_order(array):
        if fits:
            return move_blocks(pick_kernel, array, both, width, block)
        return jnp.take(array, target, axis=0)

    def to_owner(grads):
        if fits:
            return move_blocks(spread_kernel, grads, both, gathered_rows, block)
        return jnp.take(grads, source, axis=0)

    seq_count = lax.axis_size("seq")
    own_kernels = fits and seq_count == 8
    if own_kernels:
        weights = master
    else:
        low = master.astype(jnp.bfloat16)
        weights, w_ffn = (
            to_order(lax.all_gather(part, "seq", axis=0, tiled=True)) for part in (low[:, :width], low[:, width:])
        )
    slopes = jnp.exp2(-8.0 * (jnp.arange(H, dtype=jnp.float32) + 1.0) / H)
    x = jnp.transpose(hidden_in, (1, 0, 2))
    r1, x_all, qkv, ctx, w_qkv, w_out, *more = attn_call(
        x, weights, slots, seq_offsets, slopes, seq_count if own_kernels else 0
    )
    w_ffn = more[0] if own_kernels else w_ffn
    mixed_p, dr1_p, ffn_grads, ln_rows = ffn_call(
        r1, jnp.transpose(cotangent, (1, 0, 2)), w_ffn, ln_params
    )
    mixed = jnp.transpose(mixed_p, (1, 0, 2))

    ffn_padded = to_owner(ffn_grads)
    grad_p, attn_grads, *more = back_call(
        dr1_p, w_qkv, w_out, x_all, qkv, ctx, ffn_padded if own_kernels else None, seq_offsets, slopes, seq_count
    )
    input_grad = jnp.transpose(grad_p, (1, 0, 2))
    attn_padded = to_owner(attn_grads)
    mine = jnp.arange(seq_count, dtype=jnp.int32) == lax.axis_index("seq")
    own_rows = jnp.sum(jnp.where(mine, owner_blocks, 0)) * block
    kept = (jnp.arange(slab_rows, dtype=jnp.int32) < own_rows)[:, None]
    if own_kernels:
        owned, ln_total, parts = close_call(
            own_rows[None], attn_padded, more[0], ln_rows, seq_count, lax.axis_size("wide")
        )
        squares, ln_total = jnp.sum(parts), ln_total[:4]
    else:
        ffn_owned = lax.psum_scatter(ffn_padded, "seq", scatter_dimension=0, tiled=True)
        attn_owned = lax.psum_scatter(attn_padded, "seq", scatter_dimension=0, tiled=True)
        owned = jnp.concatenate([attn_owned, ffn_owned], axis=1).astype(jnp.float32)
        owned = jnp.where(kept, owned, 0.0)
        squares, ln_total = lax.psum((jnp.sum(owned * owned), ln_rows[:4]), ("seq", "wide"))
    grad_norm = jnp.sqrt(squares + jnp.sum(ln_total * ln_total))
    clip = jnp.minimum(1.0, 1.0 / (grad_norm + 1e-06))
    param_new, first_new, second_new = adamw(
        master, owned * clip, first_moment, second_moment, DECAY, RATE
    )
    norms_new, norms_first, norms_second = adamw(
        ln_params, ln_total * clip, ln_first, ln_second, 0.0, NORM_RATE
    )
    return (
        mixed,
        input_grad,
        jnp.where(kept, param_new, 0.0),
        jnp.where(kept, first_new, 0.0),
        jnp.where(kept, second_new, 0.0),
        norms_new,
        norms_first,
        norms_second,
        grad_norm,
    )


def solution(mesh):
    return jax.shard_map(
        per_device,
        mesh=mesh,
        in_specs=(
            P("wide", "seq", None),
            P("wide", "seq", None),
            P("seq", None),
            P(),
            P("seq", "wide"),
            P("seq", "wide"),
            P("seq", "wide"),
            P(),
            P(),
            P(),
        ),
        out_specs=(
            P("wide", "seq", None),
            P("wide", "seq", None),
            P("seq", "wide"),
            P("seq", "wide"),
            P("seq", "wide"),
            P(),
            P(),
            P(),
            P(),
        ),
        check_vma=False,
    )
```

```python
import functools

import jax
import jax.numpy as jnp
from jax import lax
from jax.experimental import pallas as pl
from jax.experimental.pallas import tpu as pltpu
from jax.sharding import PartitionSpec as P

MESH = pl.DeviceIdType.MESH

H = 12
HD = 64
FF = 3072
UNIT = 128
CAP = 6
STEP = 10


RATE = 0.02
NORM_RATE = 0.6
BETA_ONE = 0.9
BETA_TWO = 0.999
EPSILON = 1e-08
DECAY = 0.01
NORM_EPS = 1e-05
ROOT_HALF = 0.7071067811865476
DENSITY_SCALE = 0.3989422804014327
EPS = 1e-05
F32 = jnp.float32
BF16 = jnp.bfloat16
NEG = -1e30
PAIRS = 4
SINGLES = 2
ROWS = 16
VMEM_LIMIT = 60 * 2**20


def owner_maps(owner_blocks, rows, cap, block):
    ends = jnp.cumsum(owner_blocks)
    starts = ends - owner_blocks
    slot = jnp.arange(cap * block, dtype=jnp.int32)
    which = slot // block
    source = (starts[:, None] + which[None, :]) * block + (slot % block)[None, :]
    valid = which[None, :] < owner_blocks[:, None]
    source = jnp.where(valid, source, 0).reshape(-1)
    valid = valid.reshape(-1)
    param = jnp.arange(rows, dtype=jnp.int32)
    blocks = param // block
    owner = jnp.sum((ends[None, :] <= blocks[:, None]).astype(jnp.int32), axis=1)
    onehot = owner[:, None] == jnp.arange(owner_blocks.shape[0], dtype=jnp.int32)[None, :]
    first = jnp.sum(jnp.where(onehot, starts[None, :], 0), axis=1)
    target = owner * (cap * block) + (blocks - first) * block + param % block
    return (source, valid, target)


def adamw(param, grad, first, second, decay, rate):
    first_new = BETA_ONE * first + (1.0 - BETA_ONE) * grad
    second_new = BETA_TWO * second + (1.0 - BETA_TWO) * grad * grad
    first_hat = first_new / (1.0 - BETA_ONE**STEP)
    second_hat = second_new / (1.0 - BETA_TWO**STEP)
    param_new = param - rate * (first_hat / (jnp.sqrt(second_hat) + EPSILON) + decay * param)
    return (param_new, first_new, second_new)


def dot_nn(a, b):
    return lax.dot_general(a, b, (((1,), (0,)), ((), ())), preferred_element_type=F32)


def dot_nt(a, b):
    return lax.dot_general(a, b, (((1,), (1,)), ((), ())), preferred_element_type=F32)


def dot_tn(a, b):
    return lax.dot_general(a, b, (((0,), (0,)), ((), ())), preferred_element_type=F32)


def places():
    wide = lax.axis_index("wide")
    core = lax.rem(wide, 2)
    row = wide // 2
    return wide, core, row, wide + 1 - 2 * core, wide + 2 - 4 * row


def greet(mate, across):
    barrier = pltpu.get_barrier_semaphore()
    for peer in (mate, across):
        pl.semaphore_signal(barrier, inc=1, device_id={"wide": peer}, device_id_type=MESH)
    pl.semaphore_wait(barrier, 2)


def remote(source, target, send, recv, peer, axis="wide"):
    return pltpu.make_async_remote_copy(
        src_ref=source,
        dst_ref=target,
        send_sem=send,
        recv_sem=recv,
        device_id={axis: peer},
        device_id_type=MESH,
    )


class Gather:
    def __init__(self, held, send, recv, share):
        self.held, self.send, self.recv, self.share = held, send, recv, share
        _, self.core, self.row, self.mate, self.across = places()

    def rows(self, core, row):
        return pl.ds(pl.multiple_of((core * 2 + row) * self.share, self.share), self.share)

    def copy(self, pack, leg):
        row = 1 - self.row if leg == 2 else self.row
        block = self.held.at[pack, self.rows(self.core, row)]
        peer = self.mate if leg else self.across
        return remote(block, block, self.send.at[pack, leg], self.recv.at[pack, leg], peer)

    def start(self, pack):
        self.copy(pack, 0).start()
        self.copy(pack, 1).start()

    def finish(self, pack):
        self.copy(pack, 0).wait_recv()
        self.copy(pack, 2).start()
        self.copy(pack, 1).wait_recv()
        self.copy(pack, 2).wait_recv()

    def drain(self, pack):
        for leg in range(3):
            self.copy(pack, leg).wait_send()


class Scatter:
    def __init__(self, part, give, take, cross, reach, own, send, recv, share):
        self.part, self.give, self.take = part, give, take
        self.cross, self.reach, self.own = cross, reach, own
        self.send, self.recv, self.share = send, recv, share
        _, self.core, self.row, self.mate, self.across = places()

    def copy(self, pack, leg):
        source, target = (self.cross, self.reach) if leg else (self.give, self.take)
        peer = self.across if leg else self.mate
        return remote(
            source.at[pack], target.at[pack], self.send.at[pack, leg], self.recv.at[pack, leg], peer
        )

    def half(self, which):
        core = self.core if which else 1 - self.core
        return pl.multiple_of(core * 2 * self.share, 2 * self.share)

    def start(self, pack):
        self.copy(pack, 0).start()

    def middle(self, pack):
        self.copy(pack, 0).wait_recv()
        share = self.share
        far = pl.ds(pl.multiple_of((1 - self.row) * share, share), share)
        near = pl.ds(pl.multiple_of(self.row * share, share), share)
        self.cross[pack] = (self.part[far, :] + self.take[pack, far, :].astype(F32)).astype(BF16)
        self.copy(pack, 1).start()
        self.own[pack] = self.part[near, :] + self.take[pack, near, :].astype(F32)

    def finish(self, pack):
        self.copy(pack, 1).wait_recv()

    def drain(self, pack):
        for leg in range(2):
            self.copy(pack, leg).wait_send()


def scatter_scratch(packs, share, width):
    return [
        pltpu.VMEM((2 * share, width), F32),
        pltpu.VMEM((packs, 2 * share, width), BF16),
        pltpu.VMEM((packs, 2 * share, width), BF16),
        pltpu.VMEM((packs, share, width), BF16),
        pltpu.VMEM((packs, share, width), BF16),
        pltpu.VMEM((packs, share, width), F32),
    ]


def norm_parts(values):
    center = values - jnp.mean(values, axis=-1, keepdims=True)
    inverse = lax.rsqrt(jnp.mean(center * center, axis=-1, keepdims=True) + EPS)
    return center * inverse, inverse


def norm_pull(grad, normal, inverse, gain):
    scaled = grad * gain
    return inverse * (
        scaled
        - jnp.mean(scaled, axis=-1, keepdims=True)
        - normal * jnp.mean(scaled * normal, axis=-1, keepdims=True)
    )


def loop(count, body, unroll=1):
    def step(index, carry):
        body(index)
        return carry

    lax.fori_loop(0, count, step, 0, unroll=unroll)


def tile(index, size):
    return pl.ds(pl.multiple_of(index * size, size), size)


def ffn_kernel(
    r1_ref,
    cot_ref,
    held_ref,
    w_ref,
    ln_ref,
    mixed_ref,
    dr1_ref,
    grads_ref,
    lngrad_ref,
    weights,
    held,
    held2,
    gates,
    ups,
    hid,
    dgate,
    dup,
    turned,
    turned2,
    total,
    g_tile,
    u_tile,
    send_a,
    recv_a,
    send_b,
    recv_b,
    send_c,
    recv_c,
    send_d,
    recv_d,
    load_sem,
    store_sem,
    *buffers,
):
    packs, share, width = r1_ref.shape
    rows = 4 * share
    fwd = buffers[:6]
    units = weights.shape[1] // 3
    col = 256
    n_width = width // col
    loads = [pltpu.make_async_copy(w_ref, weights, load_sem.at[packs - 1])]
    for pack in range(packs - 1):
        loads.append(pltpu.make_async_copy(held_ref.at[pack], held.at[pack], load_sem.at[pack]))
    for load in loads:
        load.start()
    _, core, row, mate, across = places()
    greet(mate, across)
    gather_one = Gather(held, send_a, recv_a, share)
    scatter_one = Scatter(*fwd, send_b, recv_b, share)
    gather_two = Gather(held2, send_c, recv_c, share)
    scatter_two = Scatter(*fwd, send_d, recv_d, share)
    gain1, shift1 = ln_ref[0:1, :], ln_ref[1:2, :]
    gain2, shift2 = ln_ref[2:3, :], ln_ref[3:4, :]
    lngrad_ref[...] = jnp.zeros_like(lngrad_ref)
    chunk = 32

    base = pl.multiple_of((core * 2 + row) * share, share)

    def first(index):
        normal, _ = norm_parts(r1_ref[packs - 1, tile(index, chunk), :])
        held[packs - 1, pl.ds(pl.multiple_of(base + index * chunk, chunk), chunk), :] = (
            normal * gain1 + shift1
        ).astype(BF16)

    loop(share // chunk, first, unroll=4)
    gather_one.start(packs - 1)
    loads[0].wait()

    def widen(pack):
        def ff(index):
            first = pl.multiple_of(index * share, share)
            x = held[pack, pl.ds(first, share), :]
            g_tile[...] = dot_nn(x, weights[:, pl.ds(0, units)])
            u_tile[...] = dot_nn(x, weights[:, pl.ds(units, units)])

            def act(part):
                rws = tile(part, ROWS)
                gate, up = g_tile[rws, :], u_tile[rws, :]
                out = pl.ds(pl.multiple_of(first + part * ROWS, ROWS), ROWS)
                cumulative = 0.5 * (1.0 + lax.erf(gate * ROOT_HALF))
                hid[out, :] = (gate * cumulative * up).astype(BF16)
                gates[pack, out, :] = gate.astype(BF16)
                ups[pack, out, :] = up.astype(BF16)

            loop(share // ROWS, act, unroll=2)

        loop(4, ff)

    def narrow(pack):
        for which in range(2):
            base = scatter_one.half(which)

            def down(index, base=base, which=which):
                rws = pl.ds(pl.multiple_of(base + index * share, share), share)
                value = dot_nt(hid[rws, :], weights[:, pl.ds(2 * units, units)])
                if which:
                    scatter_one.part[tile(index, share), :] = value
                else:
                    scatter_one.give[pack, tile(index, share), :] = value.astype(BF16)

            loop(2, down)
            if not which:
                scatter_one.start(pack)
        scatter_one.middle(pack)

    def turn(pack):
        scatter_one.finish(pack)
        gather_two_base = pl.multiple_of((core * 2 + row) * share, share)

        def second(index):
            rws = tile(index, chunk)
            normal, _ = norm_parts(r1_ref[pack, rws, :])
            ffn = scatter_one.own[pack, rws, :] + scatter_one.reach[pack, rws, :].astype(F32)
            normal2, inverse2 = norm_parts(normal * gain1 + shift1 + ffn)
            mixed_ref[pack, rws, :] = (normal2 * gain2 + shift2).astype(BF16)
            grad = cot_ref[pack, rws, :].astype(F32)
            value = norm_pull(grad, normal2, inverse2, gain2)
            dr1_ref[pack, rws, :] = value
            held2[pack, pl.ds(pl.multiple_of(gather_two_base + index * chunk, chunk), chunk), :] = value.astype(BF16)
            lngrad_ref[2:3, :] += jnp.sum(grad * normal2, axis=0, keepdims=True)
            lngrad_ref[3:4, :] += jnp.sum(grad, axis=0, keepdims=True)

        loop(share // chunk, second, unroll=4)
        scatter_one.drain(pack)
        gather_two.start(pack)

    def backward(pack):
        gather_two.finish(pack)
        for which in range(2):
            base = scatter_two.half(which)

            def bf(index, base=base):
                first = pl.multiple_of(base + index * share, share)
                g_tile[...] = dot_nn(held2[pack, pl.ds(first, share), :], weights[:, pl.ds(2 * units, units)])

                def act(part):
                    rws = tile(part, ROWS)
                    out = pl.ds(pl.multiple_of(first + part * ROWS, ROWS), ROWS)
                    dhid = g_tile[rws, :]
                    gate = gates[pack, out, :].astype(F32)
                    up = ups[pack, out, :].astype(F32)
                    cumulative = 0.5 * (1.0 + lax.erf(gate * ROOT_HALF))
                    density = jnp.exp(-0.5 * gate * gate) * DENSITY_SCALE
                    value = gate * cumulative
                    hid[out, :] = (value * up).astype(BF16)
                    dgate[out, :] = (dhid * up * (cumulative + gate * density)).astype(BF16)
                    dup[out, :] = (dhid * value).astype(BF16)

                loop(share // ROWS, act, unroll=2)

            loop(2, bf)

            def back(index, base=base, which=which):
                rws = pl.ds(pl.multiple_of(base + index * share, share), share)
                value = dot_nt(dgate[rws, :], weights[:, pl.ds(0, units)]) + dot_nt(
                    dup[rws, :], weights[:, pl.ds(units, units)]
                )
                if which:
                    scatter_two.part[tile(index, share), :] = value
                else:
                    scatter_two.give[pack, tile(index, share), :] = value.astype(BF16)

            loop(2, back)
            if not which:
                scatter_two.start(pack)
        scatter_two.middle(pack)

    def weight_grads(pack):
        def flip(index):
            rws = tile(index, 256)
            turned[:, rws] = held[pack, rws, :].T
            turned2[:, rws] = held2[pack, rws, :].T

        loop(rows // 256, flip)

        def add(index):
            rws = tile(index, col)
            a = turned[rws, :]
            b = turned2[rws, :]
            parts = (dot_nn(a, dgate[...]), dot_nn(a, dup[...]), dot_nn(b, hid[...]))
            for place, value in enumerate(parts):
                cols = pl.ds(place * units, units)
                if pack == 0:
                    total[rws, cols] = value
                else:
                    value = total[rws, cols] + value
                    if pack < packs - 1:
                        total[rws, cols] = value
                    else:
                        gates[place, rws, :] = value.astype(BF16)

        loop(n_width, add)

    def last(pack):
        scatter_two.finish(pack)

        def third(index):
            rws = tile(index, chunk)
            normal, inverse = norm_parts(r1_ref[pack, rws, :])
            grad = dr1_ref[pack, rws, :] + (
                scatter_two.own[pack, rws, :] + scatter_two.reach[pack, rws, :].astype(F32)
            )
            dr1_ref[pack, rws, :] = norm_pull(grad, normal, inverse, gain1)
            lngrad_ref[0:1, :] += jnp.sum(grad * normal, axis=0, keepdims=True)
            lngrad_ref[1:2, :] += jnp.sum(grad, axis=0, keepdims=True)

        loop(share // chunk, third, unroll=4)

    for pack in range(packs):
        if pack < packs - 1:
            loads[pack + 1].wait()
        else:
            gather_one.finish(pack)
        widen(pack)
        narrow(pack)
        if pack:
            turn(pack - 1)
    for pack in range(packs):
        backward(pack)
        weight_grads(pack)
        if pack == 0:
            turn(packs - 1)
        else:
            last(pack - 1)
    outs = [
        pltpu.make_async_copy(
            gates.at[place, pl.ds(0, width)],
            grads_ref.at[:, pl.ds(place * units, units)],
            store_sem.at[place],
        )
        for place in range(3)
    ]
    for out in outs:
        out.start()
    last(packs - 1)
    for out in outs:
        out.wait()
    gather_one.drain(packs - 1)
    for pack in range(packs):
        gather_two.drain(pack)
        scatter_two.drain(pack)


def ffn_call(r1, cot, held, weights, ln_params):
    packs, share, width = r1.shape
    rows = 4 * share
    units = weights.shape[1] // 3
    vm = pl.BlockSpec(memory_space=pltpu.VMEM)
    hb = pl.BlockSpec(memory_space=pl.ANY)
    dma = pltpu.SemaphoreType.DMA
    return pl.pallas_call(
        ffn_kernel,
        out_shape=(
            jax.ShapeDtypeStruct((packs, share, width), BF16),
            jax.ShapeDtypeStruct((packs, share, width), F32),
            jax.ShapeDtypeStruct((width, 3 * units), BF16),
            jax.ShapeDtypeStruct((8, width), F32),
        ),
        in_specs=[vm, vm, hb, hb, vm],
        out_specs=(vm, vm, hb, vm),
        scratch_shapes=[
            pltpu.VMEM((width, 3 * units), BF16),
            pltpu.VMEM((packs, rows, width), BF16),
            pltpu.VMEM((packs, rows, width), BF16),
            pltpu.VMEM((packs, rows, units), BF16),
            pltpu.VMEM((packs, rows, units), BF16),
            pltpu.VMEM((rows, units), BF16),
            pltpu.VMEM((rows, units), BF16),
            pltpu.VMEM((rows, units), BF16),
            pltpu.VMEM((width, rows), BF16),
            pltpu.VMEM((width, rows), BF16),
            pltpu.VMEM((width, 3 * units), F32),
            pltpu.VMEM((share, units), F32),
            pltpu.VMEM((share, units), F32),
            dma((packs, 3)),
            dma((packs, 3)),
            dma((packs, 2)),
            dma((packs, 2)),
            dma((packs, 3)),
            dma((packs, 3)),
            dma((packs, 2)),
            dma((packs, 2)),
            dma((packs,)),
            dma((3,)),
            *scatter_scratch(packs, share, width),
        ],
        compiler_params=pltpu.CompilerParams(
            collective_id=1, has_side_effects=True, vmem_limit_bytes=VMEM_LIMIT
        ),
        cost_estimate=pl.CostEstimate(flops=int(70e9), bytes_accessed=4 * 10**7, transcendentals=10**7),
        name="ffn",
    )(r1, cot, held, weights, ln_params)


class Runs:
    def __init__(self, offsets, pack):
        names = [offsets[pack, place] for place in range(8)]
        start = jnp.int32(4)
        for place in range(3, -1, -1):
            start = lax.select(names[place] == names[place + 3], jnp.int32(place), start)
        self.start = start
        self.names = [lax.select(start > place, names[place], names[place + 4]) for place in range(4)]

    def masks(self, index):
        own = self.names[0]
        for place in range(1, 4):
            own = lax.select(index == place, self.names[place], own)
        return [lax.select(own == name, jnp.float32(0.0), jnp.float32(NEG)) for name in self.names]

    def arrange(self, plain, order):
        for place in range(4):
            value = plain[held_run(place), :]
            for start in range(1, 5):
                value = lax.select(self.start == start, plain[held_run(place + start), :], value)
            order(pl.ds(place * UNIT, UNIT), value)
            value = lax.select(self.start > place, plain[held_run(place), :], plain[held_run(place + 4), :])
            order(pl.ds((place + 4) * UNIT, UNIT), value)

    def restore(self, order, plain):
        for run in range(8):
            first = max(0, run - 3)
            value = order[pl.ds((run - first) * UNIT, UNIT), :]
            for start in range(first + 1, min(run, 4) + 1):
                value = lax.select(self.start == start, order[pl.ds((run - start) * UNIT, UNIT), :], value)
            if run < 4:
                value = lax.select(self.start > run, order[pl.ds((run + 4) * UNIT, UNIT), :], value)
            else:
                value = lax.select(self.start <= run - 4, order[pl.ds(run * UNIT, UNIT), :], value)
            plain(held_run(run), value)


def held_run(run):
    half, part = divmod(run, 2)
    return pl.ds(((half % 2) * 2 + half // 2) * 2 * UNIT + part * UNIT, UNIT)


def writer(ref, *at):
    def write(rows, value):
        ref[(*at, rows, slice(None))] = value

    return write


def fill_bias(bias, slopes, wide):
    heads, size, _ = bias.shape

    def fill(index):
        rws = tile(index, UNIT)
        down = lax.broadcasted_iota(jnp.int32, (UNIT, size), 0) + index * UNIT
        along = lax.broadcasted_iota(jnp.int32, (UNIT, size), 1)
        distance = jnp.abs(down - along).astype(F32)
        for head in range(heads):
            bias[head, rws, :] = -slopes[wide * heads + head] * distance

    loop(size // UNIT, fill)


def split_weights(packed, w_qkv, w_out):
    width, each = packed.shape[0], packed.shape[1] // 4
    wide = w_out.shape[1]

    def part(index):
        rws = tile(index, 128)
        zeros = jnp.zeros((128, wide - each), BF16)
        for place in range(4):
            value = jnp.concatenate([packed[rws, pl.ds(place * each, each)], zeros], axis=1)
            if place < 3:
                w_qkv[rws, pl.ds(place * wide, wide)] = value
            else:
                w_out[rws, :] = value

    loop(width // 128, part)


def mask_row(runs, index):
    return jnp.concatenate([jnp.full((1, UNIT), part, F32) for part in runs.masks(index)], axis=1)


def split_heads(value, low):
    none = jnp.zeros_like(value)
    return jnp.concatenate([jnp.where(low, value, none), jnp.where(low, none, value)], axis=0)


def head_lanes():
    lane = lax.broadcasted_iota(jnp.int32, (1, 128), 1)
    return lane < HD


def attn_kernel(
    gathering,
    offsets_ref,
    slopes_ref,
    slots_ref,
    x_ref,
    w_ref,
    ln_ref,
    r1_ref,
    normed_ref,
    held_ref,
    qkv_ref,
    ctx_ref,
    w_qkv_ref,
    w_out_ref,
    *rest,
):
    w_ffn_ref, rest = (rest[0], rest[1:]) if gathering else (None, rest)
    (
        packed,
        w_qkv,
        w_out,
        bias,
        held,
        normed,
        plain,
        qkv,
        ctx_order,
        ctx,
        send_a,
        recv_a,
        send_b,
        recv_b,
        send_c,
        recv_c,
        load_sem,
        store_sem,
        *buffers,
    ) = rest
    packs, share, width = x_ref.shape
    rows = 4 * share
    lanes = w_out.shape[1]
    group = rows // 2
    wide, core, row, mate, across = places()
    if gathering:
        slab, near, near_send, near_recv, far, far_send, far_recv, ordered, *buffers = buffers
        load = pltpu.make_async_copy(w_ref, slab, load_sem)
        load.start()
        owners = OwnerGather(near, near_send, near_recv, slab.shape[0])
        others = OwnerGather(far, far_send, far_recv, slab.shape[0])
        holders = near.shape[1] // slab.shape[0]
        greet_all((("seq", holders), ("wide", 4)))
        load.wait()
        cut = near.shape[2]
        for part in range(owners.groups):
            value = slab[:, part * cut : (part + 1) * cut]
            near[part, owners.rows(owners.seq), :] = value.astype(BF16)
        owners.start()
        cut = far.shape[2]
        for part in range(others.groups):
            value = slab[:, width + part * cut : width + (part + 1) * cut]
            far[part, others.rows(others.seq), :] = value.astype(BF16)
    else:
        load = pltpu.make_async_copy(w_ref.at[:, pl.ds(0, packed.shape[1])], packed, load_sem)
        load.start()
        greet(mate, across)
    gather = Gather(held, send_a, recv_a, share)
    scatter = Scatter(*buffers, send_b, recv_b, share)
    spread = Gather(normed, send_c, recv_c, share)
    gain, shift = ln_ref[0:1, :], ln_ref[1:2, :]
    base = pl.multiple_of((core * 2 + row) * share, share)
    for pack in range(packs):
        held[pack, pl.ds(base, share), :] = x_ref[pack]
        gather.start(pack)
    fill_bias(bias, slopes_ref, wide)
    stores = []
    todo = []

    def pump(count):
        for _ in range(min(count, len(todo))):
            todo.pop(0)()

    if gathering:
        for step in owners.steps():
            step()
        others.start()
        todo = others.steps()
        cut = near.shape[2]
        for part in range(owners.groups):
            owners.finish(part)
            order_slabs(slots_ref, near, part, packed, pl.ds(part * cut, cut), holders)

        def settled(part):
            others.finish(part)
            cut = far.shape[2]
            cols = pl.ds(part * cut, cut)
            order_slabs(slots_ref, far, part, ordered, cols, holders)
            copy = pltpu.make_async_copy(
                ordered.at[:, cols], w_ffn_ref.at[:, cols], store_sem.at[packs + 1, part]
            )
            copy.start()
            stores.append(copy)

        todo += [functools.partial(settled, part) for part in range(others.groups)]
    else:
        load.wait()
    split_weights(packed, w_qkv, w_out)
    low = head_lanes()
    scale = jnp.asarray(HD ** (-0.5), BF16)
    for place, (source, target) in enumerate(((w_qkv, w_qkv_ref), (w_out, w_out_ref))):
        copy = pltpu.make_async_copy(source, target, store_sem.at[packs, place])
        copy.start()
        stores.append(copy)

    def attend(pack):
        runs = Runs(offsets_ref, pack)
        gather.finish(pack)

        def project(index):
            rws = tile(index, 256)
            value = dot_nn(held[pack, rws, :], w_qkv[...])
            plain[rws, pl.ds(0, lanes)] = (value[:, :lanes].astype(BF16) * scale).astype(BF16)
            plain[rws, pl.ds(lanes, 2 * lanes)] = value[:, lanes:].astype(BF16)

        loop(rows // 256, project)
        runs.arrange(plain, writer(qkv, pack))
        for side in range(2):
            keys = pl.ds(side * group, group)

            def weigh(part, queries, offset, side=side, keys=keys, pack=pack):
                scores = dot_nt(queries, qkv[pack, keys, pl.ds(lanes + part * 128, 128)]) + offset
                powers = jnp.exp(scores - jnp.max(scores, axis=-1, keepdims=True))
                total = jnp.sum(powers, axis=-1, keepdims=True)
                return dot_nn(powers.astype(BF16), qkv[pack, keys, pl.ds(2 * lanes + part * 128, 128)]) / total

            def pair(index, side=side, pack=pack):
                rws = pl.ds(pl.multiple_of(side * group + index * UNIT, UNIT), UNIT)
                offset = jnp.concatenate([bias[head, tile(index, UNIT), :] for head in range(2)], axis=0)
                if side:
                    offset = offset + mask_row(runs, index)
                out = weigh(0, split_heads(qkv[pack, rws, pl.ds(0, 128)], low), offset)
                ctx_order[rws, pl.ds(0, 128)] = jnp.where(low, out[:UNIT], out[UNIT:]).astype(BF16)

            def single(index, side=side, pack=pack):
                rws = pl.ds(pl.multiple_of(side * group + index * 2 * UNIT, 2 * UNIT), 2 * UNIT)
                offset = bias[2, tile(index, 2 * UNIT), :]
                if side:
                    offset = jnp.concatenate(
                        [
                            offset[half * UNIT : (half + 1) * UNIT] + mask_row(runs, 2 * index + half)
                            for half in range(2)
                        ],
                        axis=0,
                    )
                out = weigh(1, qkv[pack, rws, pl.ds(128, 128)], offset)
                ctx_order[rws, pl.ds(128, 128)] = out.astype(BF16)

            loop(4, pair, unroll=PAIRS)
            loop(2, single, unroll=SINGLES)
            pump(1 if pack else 0)
        runs.restore(ctx_order, writer(ctx, pack))
        for which in range(2):
            big = pl.ds(scatter.half(which), 2 * share)

            def out(index, which=which, big=big):
                cols = tile(index, 256)
                value = dot_nt(ctx[pack, big, :], w_out[cols, :])
                if which:
                    scatter.part[:, cols] = value
                else:
                    scatter.give[pack, :, cols] = value.astype(BF16)

            loop(width // 256, out)
            if not which:
                scatter.start(pack)
        scatter.middle(pack)
        pump(2)
        for place, (source, target) in enumerate(((held, held_ref), (qkv, qkv_ref), (ctx, ctx_ref))):
            copy = pltpu.make_async_copy(source.at[pack], target.at[pack], store_sem.at[pack, place])
            copy.start()
            stores.append(copy)

    def settle(pack):
        scatter.finish(pack)

        last = pack == packs - 1

        def add(index):
            rws = tile(index, 32)
            attn = scatter.own[pack, rws, :] + scatter.reach[pack, rws, :].astype(F32)
            value = x_ref[pack, rws, :].astype(F32) + attn
            r1_ref[pack, rws, :] = value
            if not last:
                normal, _ = norm_parts(value)
                out = pl.ds(pl.multiple_of(base + index * 32, 32), 32)
                normed[pack, out, :] = (normal * gain + shift).astype(BF16)

        loop(share // 32, add, unroll=4)
        if not last:
            spread.start(pack)

    def hand_on(pack):
        spread.finish(pack)
        copy = pltpu.make_async_copy(normed.at[pack], normed_ref.at[pack], store_sem.at[packs + 2, pack])
        copy.start()
        stores.append(copy)

    for pack in range(packs):
        attend(pack)
        if pack:
            settle(pack - 1)
        if pack > 1:
            hand_on(pack - 2)
    settle(packs - 1)
    pump(len(todo))
    hand_on(packs - 2)
    for copy in stores:
        copy.wait()
    for pack in range(packs):
        gather.drain(pack)
        scatter.drain(pack)
        if pack < packs - 1:
            spread.drain(pack)
    if gathering:
        owners.drain()
        others.drain()


def back_kernel(
    summing,
    offsets_ref,
    slopes_ref,
    dr1_ref,
    w_qkv_ref,
    w_out_ref,
    x_ref,
    qkv_ref,
    ctx_ref,
    *rest,
):
    padded_ref, rest = (rest[0], rest[1:]) if summing else (None, rest)
    grad_ref, grads_ref, *rest = rest
    owned_ref, rest = (rest[0], rest[1:]) if summing else (None, rest)
    (
        w_qkv,
        w_out,
        bias,
        held,
        x_all,
        qkv,
        ctx,
        plain,
        dctx,
        dorder,
        dplain,
        sum_k,
        sum_v,
        turned,
        total,
        total_out,
        send_a,
        recv_a,
        send_b,
        recv_b,
        load_sem,
        fetch_sem,
        *buffers,
    ) = rest
    if summing:
        owners = OwnerSum(padded_ref, *buffers[6:])

        def put(rws, cols, value):
            owned_ref[rws, cols] = value.astype(BF16)

        todo = owners.steps(put)
    else:
        todo = []

    def pump(count):
        for _ in range(min(count, len(todo))):
            todo.pop(0)()

    packs, share, width = dr1_ref.shape
    rows = 4 * share
    lanes = w_out.shape[1]
    group = rows // 2
    loads = [
        pltpu.make_async_copy(source, target, load_sem.at[place])
        for place, (source, target) in enumerate(((w_qkv_ref, w_qkv), (w_out_ref, w_out)))
    ]
    for copy in loads:
        copy.start()
    fetches = []
    for pack in range(packs):
        for place, (source, target) in enumerate(((x_ref, x_all), (qkv_ref, qkv), (ctx_ref, ctx))):
            copy = pltpu.make_async_copy(source.at[pack], target.at[pack], fetch_sem.at[pack, place])
            copy.start()
            fetches.append(copy)
    wide, core, row, mate, across = places()
    if summing:
        greet_all((("seq", padded_ref.shape[0]), ("wide", 4)))
    else:
        greet(mate, across)
    gather = Gather(held, send_a, recv_a, share)
    scatter = Scatter(*buffers[:6], send_b, recv_b, share)
    base = pl.multiple_of((core * 2 + row) * share, share)
    for pack in range(packs):
        held[pack, pl.ds(base, share), :] = dr1_ref[pack].astype(BF16)
        gather.start(pack)
    if summing:
        owners.start(0, 2)
    fill_bias(bias, slopes_ref, wide)
    for copy in loads:
        copy.wait()
    low = head_lanes()
    scale = HD ** (-0.5)

    def pull(pack):
        runs = Runs(offsets_ref, pack)
        gather.finish(pack)

        def project(index):
            rws = tile(index, 256)
            plain[rws, :] = dot_nn(held[pack, rws, :], w_out[...]).astype(BF16)

        loop(rows // 256, project)
        runs.arrange(plain, writer(dctx))
        for copy in fetches[3 * pack : 3 * pack + 3]:
            copy.wait()
        for side in range(2):
            keys = pl.ds(side * group, group)
            sum_k[...] = jnp.zeros_like(sum_k)
            sum_v[...] = jnp.zeros_like(sum_v)

            def masked(offset, index):
                return jnp.concatenate(
                    [offset[t * UNIT : (t + 1) * UNIT] + value for t, value in enumerate(runs.masks(index))],
                    axis=0,
                )

            def pull_back(part, queries, dout, offset, keys=keys, pack=pack):
                block = pl.ds(part * 128, 128)
                k_all = qkv[pack, keys, pl.ds(lanes + part * 128, 128)]
                v_all = qkv[pack, keys, pl.ds(2 * lanes + part * 128, 128)]
                scores = dot_nt(k_all, queries) + offset
                powers = jnp.exp(scores - jnp.max(scores, axis=0, keepdims=True))
                probs = powers * (1.0 / jnp.sum(powers, axis=0, keepdims=True))
                dprobs = dot_nt(v_all, dout)
                delta = jnp.sum(probs * dprobs, axis=0, keepdims=True)
                dscores = (probs * (dprobs - delta)).astype(BF16)
                sum_v[:, block] += dot_nn(probs.astype(BF16), dout)
                sum_k[:, block] += dot_nn(dscores, queries)
                return dot_tn(dscores, k_all) * scale

            def pair(index, side=side, pack=pack):
                rws = pl.ds(pl.multiple_of(side * group + index * UNIT, UNIT), UNIT)
                block = pl.ds(0, 128)
                offsets = [bias[head, :, tile(index, UNIT)] for head in range(2)]
                if side:
                    offsets = [masked(offset, index) for offset in offsets]
                dq = pull_back(
                    0,
                    split_heads(qkv[pack, rws, block], low),
                    split_heads(dctx[rws, block], low),
                    jnp.concatenate(offsets, axis=1),
                )
                dorder[rws, block] = jnp.where(low, dq[:UNIT], dq[UNIT:]).astype(BF16)

            def single(index, side=side, pack=pack):
                rws = pl.ds(pl.multiple_of(side * group + index * 2 * UNIT, 2 * UNIT), 2 * UNIT)
                block = pl.ds(128, 128)
                offset = bias[2, :, tile(index, 2 * UNIT)]
                if side:
                    offset = jnp.concatenate(
                        [
                            masked(offset[:, half * UNIT : (half + 1) * UNIT], 2 * index + half)
                            for half in range(2)
                        ],
                        axis=1,
                    )
                dorder[rws, block] = pull_back(1, qkv[pack, rws, block], dctx[rws, block], offset).astype(BF16)

            loop(4, pair, unroll=PAIRS)
            loop(2, single, unroll=SINGLES)
            pump(((4, 2), (1, 0), (2, 2))[pack][side])
            dorder[keys, pl.ds(lanes, lanes)] = sum_k[...].astype(BF16)
            dorder[keys, pl.ds(2 * lanes, lanes)] = sum_v[...].astype(BF16)
        runs.restore(dorder, writer(dplain))
        for which in range(2):
            big = pl.ds(scatter.half(which), 2 * share)

            def out(index, which=which, big=big):
                cols = tile(index, 256)
                value = dot_nt(dplain[big, :], w_qkv[cols, :])
                if which:
                    scatter.part[:, cols] = value
                else:
                    scatter.give[pack, :, cols] = value.astype(BF16)

            loop(width // 256, out)
            if not which:
                scatter.start(pack)
        scatter.middle(pack)
        pump((2, 1, 1)[pack])

    def weight_grads(pack):
        for source, result, target in ((x_all, dplain, total), (held, ctx.at[pack], total_out)):

            def flip(index, source=source):
                rws = tile(index, 256)
                turned[:, rws] = source[pack, rws, :].T

            loop(rows // 256, flip)

            def add(index, result=result, target=target):
                rws = tile(index, 256)
                value = dot_nn(turned[rws, :], result[...])
                if pack:
                    value = value + target[rws, :]
                target[rws, :] = value

            loop(width // 256, add)

    def settle(pack):
        scatter.finish(pack)

        def add(index):
            rws = tile(index, 64)
            grad_ref[pack, rws, :] = dr1_ref[pack, rws, :] + (
                scatter.own[pack, rws, :] + scatter.reach[pack, rws, :].astype(F32)
            )

        loop(share // 64, add)

    for pack in range(packs):
        pull(pack)
        weight_grads(pack)
        pump((1, 0, 1)[pack])
        if pack:
            settle(pack - 1)
    each = width // 4

    def pack_up(index):
        rws = tile(index, 128)
        pieces = [total[rws, pl.ds(place * lanes, each)] for place in range(3)]
        pieces.append(total_out[rws, pl.ds(0, each)])
        grads_ref[rws, :] = jnp.concatenate([piece.astype(BF16) for piece in pieces], axis=1)

    loop(width // 128, pack_up)
    settle(packs - 1)

    pump(len(todo))
    if summing:
        owners.drain()
    for pack in range(packs):
        gather.drain(pack)
        scatter.drain(pack)


def attn_call(x, weights, ln_params, slots, offsets, slopes, seq_count):
    packs, share, width = x.shape
    rows = 4 * share
    lanes = 256
    vm = pl.BlockSpec(memory_space=pltpu.VMEM)
    hb = pl.BlockSpec(memory_space=pl.ANY)
    sm = pl.BlockSpec(memory_space=pltpu.SMEM)
    dma = pltpu.SemaphoreType.DMA
    more, more_out = [], []
    if seq_count:
        slab, units = weights.shape[0], weights.shape[1] - width
        groups = len(GATHER_ORDERS)
        more = [
            pltpu.VMEM(weights.shape, F32),
            *gather_scratch(seq_count * slab, width, groups),
            *gather_scratch(seq_count * slab, units, groups),
            pltpu.VMEM((width, units), BF16),
        ]
        more_out = [jax.ShapeDtypeStruct((width, units), BF16)]
    return pl.pallas_call(
        functools.partial(attn_kernel, bool(seq_count)),
        out_shape=(
            jax.ShapeDtypeStruct((packs, share, width), F32),
            jax.ShapeDtypeStruct((packs - 1, rows, width), BF16),
            jax.ShapeDtypeStruct((packs, rows, width), BF16),
            jax.ShapeDtypeStruct((packs, rows, 3 * lanes), BF16),
            jax.ShapeDtypeStruct((packs, rows, lanes), BF16),
            jax.ShapeDtypeStruct((width, 3 * lanes), BF16),
            jax.ShapeDtypeStruct((width, lanes), BF16),
            *more_out,
        ),
        in_specs=[sm, sm, sm, vm, hb, vm],
        out_specs=(vm, *[hb] * (6 + len(more_out))),
        scratch_shapes=[
            pltpu.VMEM((width, width), BF16),
            pltpu.VMEM((width, 3 * lanes), BF16),
            pltpu.VMEM((width, lanes), BF16),
            pltpu.VMEM((3, rows // 2, rows // 2), F32),
            pltpu.VMEM((packs, rows, width), BF16),
            pltpu.VMEM((packs - 1, rows, width), BF16),
            pltpu.VMEM((rows, 3 * lanes), BF16),
            pltpu.VMEM((packs, rows, 3 * lanes), BF16),
            pltpu.VMEM((rows, lanes), BF16),
            pltpu.VMEM((packs, rows, lanes), BF16),
            dma((packs, 3)),
            dma((packs, 3)),
            dma((packs, 2)),
            dma((packs, 2)),
            dma((packs, 3)),
            dma((packs, 3)),
            dma(()),
            dma((packs + 3, 3)),
            *more,
            *scatter_scratch(packs, share, width),
        ],
        compiler_params=pltpu.CompilerParams(
            collective_id=2, has_side_effects=True, vmem_limit_bytes=VMEM_LIMIT
        ),
        cost_estimate=pl.CostEstimate(flops=int(14e9), bytes_accessed=4 * 10**7, transcendentals=10**7),
        name="attn",
    )(offsets, slopes, slots, x, weights, ln_params)


def back_call(dr1, w_qkv, w_out, x_all, qkv, ctx, padded, offsets, slopes, seq_count):
    packs, share, width = dr1.shape
    rows = 4 * share
    lanes = 256
    summing = padded is not None
    more_in, more_out, more_scratch = [], [], []
    if summing:
        slab, cols = padded.shape[0] // seq_count, padded.shape[1]
        more_in = [padded.reshape(seq_count, slab, cols)]
        more_out = [jax.ShapeDtypeStruct((slab, cols), BF16)]
        more_scratch = owner_scratch(slab, cols, len(SUM_ORDERS))
    vm = pl.BlockSpec(memory_space=pltpu.VMEM)
    hb = pl.BlockSpec(memory_space=pl.ANY)
    sm = pl.BlockSpec(memory_space=pltpu.SMEM)
    dma = pltpu.SemaphoreType.DMA
    return pl.pallas_call(
        functools.partial(back_kernel, summing),
        out_shape=(
            jax.ShapeDtypeStruct((packs, share, width), F32),
            jax.ShapeDtypeStruct((width, width), BF16),
            *more_out,
        ),
        in_specs=[sm, sm, vm, hb, hb, hb, hb, hb] + [hb] * len(more_in),
        out_specs=(vm, vm, *[vm] * len(more_out)),
        scratch_shapes=[
            pltpu.VMEM((width, 3 * lanes), BF16),
            pltpu.VMEM((width, lanes), BF16),
            pltpu.VMEM((3, rows // 2, rows // 2), F32),
            pltpu.VMEM((packs, rows, width), BF16),
            pltpu.VMEM((packs, rows, width), BF16),
            pltpu.VMEM((packs, rows, 3 * lanes), BF16),
            pltpu.VMEM((packs, rows, lanes), BF16),
            pltpu.VMEM((rows, lanes), BF16),
            pltpu.VMEM((rows, lanes), BF16),
            pltpu.VMEM((rows, 3 * lanes), BF16),
            pltpu.VMEM((rows, 3 * lanes), BF16),
            pltpu.VMEM((rows // 2, lanes), F32),
            pltpu.VMEM((rows // 2, lanes), F32),
            pltpu.VMEM((width, rows), BF16),
            pltpu.VMEM((width, 3 * lanes), F32),
            pltpu.VMEM((width, lanes), F32),
            dma((packs, 3)),
            dma((packs, 3)),
            dma((packs, 2)),
            dma((packs, 2)),
            dma((2,)),
            dma((packs, 3)),
            *scatter_scratch(packs, share, width),
            *more_scratch,
        ],
        compiler_params=pltpu.CompilerParams(
            collective_id=3, has_side_effects=True, vmem_limit_bytes=VMEM_LIMIT
        ),
        cost_estimate=pl.CostEstimate(flops=int(40e9), bytes_accessed=4 * 10**7, transcendentals=10**7),
        name="back",
    )(offsets, slopes, dr1, w_qkv, w_out, x_all, qkv, ctx, *more_in)


def flip_bits(place, *bits):
    for bit in bits:
        place = place + bit - 2 * bit * lax.rem(place // bit, 2)
    return place


GATHER_ORDERS = ((4, 2, 1), (4, 2, 1), (4, 1, 2))
SUM_ORDERS = ((1, 2, 4), (1, 2, 4), (2, 1, 4))


class OwnerGather:
    PEERS = (0, 1, 2, 1, 2, 2, 2)
    SLABS = ((), (), (), (0,), (0,), (1,), (0, 1))

    def __init__(self, held, send, recv, slab):
        self.held, self.send, self.recv, self.slab = held, send, recv, slab
        self.groups = held.shape[0]
        self.seq = lax.axis_index("seq")

    def rows(self, owner):
        return pl.ds(pl.multiple_of(owner * self.slab, self.slab), self.slab)

    def copy(self, group, leg, incoming=False):
        order = GATHER_ORDERS[group]
        bits = [order[place] for place in self.SLABS[leg]]
        if incoming:
            bits.append(order[self.PEERS[leg]])
        block = self.held.at[group, self.rows(flip_bits(self.seq, *bits))]
        peer = flip_bits(self.seq, order[self.PEERS[leg]])
        return remote(block, block, self.send.at[group, leg], self.recv.at[group, leg], peer, "seq")

    def start(self):
        for group in range(self.groups):
            for leg in range(3):
                self.copy(group, leg).start()

    def steps(self):
        found = []
        for first, *rest in ((0, 3, 4), (1, 5), (3, 6)):
            for group in range(self.groups):

                def step(group=group, first=first, rest=rest):
                    self.copy(group, first, True).wait_recv()
                    for leg in rest:
                        self.copy(group, leg).start()

                found.append(step)
        return found

    def finish(self, group):
        for leg in (2, 4, 5, 6):
            self.copy(group, leg, True).wait_recv()

    def drain(self):
        for group in range(self.groups):
            for leg in range(7):
                self.copy(group, leg).wait_send()


def gather_scratch(rows, cols, groups):
    dma = pltpu.SemaphoreType.DMA
    return [pltpu.VMEM((groups, rows, cols // groups), BF16), dma((groups, 7)), dma((groups, 7))]


def order_slabs(slots, slabs, group, target, cols, owners):
    blocks, rows, slab = slots.shape[0], target.shape[0], slabs.shape[1] // owners
    block, step = rows // blocks, 8
    for first in range(0, blocks, step):
        last = first + step - 1
        low = first // CAP
        high = max(o for o in range(owners) if max(o, blocks - CAP * (owners - o)) <= last)
        count = (high - low + 1) * slab
        lines = []
        for place in range(first, first + step):
            down = lax.broadcasted_iota(jnp.int32, (block, count), 0)
            along = lax.broadcasted_iota(jnp.int32, (block, count), 1)
            hit = along - down == slots[place] * block - low * slab
            lines.append(jnp.where(hit, 1.0, 0.0).astype(BF16))
        lines = jnp.concatenate(lines, axis=0)
        for part in range(0, cols.size, 256):
            value = dot_nn(lines, slabs[group, pl.ds(low * slab, count), pl.ds(part, 256)])
            target[pl.ds(first * block, step * block), pl.ds(cols.start + part, 256)] = value.astype(BF16)


class OwnerSum:
    KEPT = ((1, 2), (1,), (2,), ())

    def __init__(self, source, own, first, second, third, load, send, recv):
        self.source, self.own, self.first, self.second, self.third = source, own, first, second, third
        self.load, self.send, self.recv = load, send, recv
        self.groups, self.slab, self.size = own.shape[0], own.shape[2], own.shape[3]
        self.seq = lax.axis_index("seq")

    def block(self, group, step, *more):
        order = SUM_ORDERS[group]
        owner = flip_bits(self.seq, *[order[place] for place in self.KEPT[step]], *more)
        return self.source.at[owner, :, pl.ds(group * self.size, self.size)]

    def fetch(self, group, step):
        return pltpu.make_async_copy(
            self.block(group, step), self.own.at[group, step], self.load.at[group, step]
        )

    def copy(self, group, leg):
        order = SUM_ORDERS[group]
        if leg < 4:
            source, target, bit = self.block(group, leg, order[0]), self.first.at[group, leg], order[0]
        elif leg < 6:
            source, target, bit = self.own.at[group, leg - 4], self.second.at[group, leg - 4], order[1]
        else:
            source, target, bit = self.own.at[group, 2], self.third.at[group], order[2]
        return remote(
            source, target, self.send.at[group, leg], self.recv.at[group, leg], flip_bits(self.seq, bit), "seq"
        )

    def start(self, *groups):
        for group in groups:
            for step in range(4):
                self.copy(group, step).start()
                self.fetch(group, step).start()

    def into(self, group, step, *others):
        def part(row):
            rws = tile(row, 32)
            value = self.own[group, step, rws, :].astype(F32)
            for other in others:
                value = value + other[rws, :].astype(F32)
            self.own[group, step, rws, :] = value.astype(BF16)

        loop(self.slab // 32, part)

    def add(self, group, step):
        self.fetch(group, step).wait()
        self.copy(group, step).wait_recv()
        if step < 2:
            self.into(group, step, self.first.at[group, step])
            self.copy(group, 4 + step).start()
        if group == 2 and step == 1:
            self.start(1)

    def pair(self, group):
        self.copy(group, 4).wait_recv()
        self.into(group, 2, self.first.at[group, 2], self.second.at[group, 0])
        self.copy(group, 6).start()

    def finish(self, group, target):
        self.copy(group, 5).wait_recv()
        self.copy(group, 6).wait_recv()

        def part(row):
            rws = tile(row, 32)
            value = self.own[group, 3, rws, :].astype(F32)
            for other in (self.first.at[group, 3], self.second.at[group, 1], self.third.at[group]):
                value = value + other[rws, :].astype(F32)
            target(rws, pl.ds(group * self.size, self.size), value)

        loop(self.slab // 32, part)

    def steps(self, target):
        add, pair, finish = self.add, self.pair, self.finish
        found = [functools.partial(add, group, step) for step in range(4) for group in (0, 2)]
        found += [functools.partial(pair, 0), functools.partial(pair, 2)]
        found += [functools.partial(add, 1, 0), functools.partial(add, 1, 1)]
        found += [functools.partial(finish, 0, target), functools.partial(finish, 2, target)]
        found += [functools.partial(add, 1, 2), functools.partial(pair, 1), functools.partial(add, 1, 3)]
        found.append(functools.partial(finish, 1, target))
        return found

    def drain(self):
        for group in range(self.groups):
            for leg in range(7):
                self.copy(group, leg).wait_send()


def owner_scratch(slab, width, groups):
    dma = pltpu.SemaphoreType.DMA
    size = width // groups
    return [
        pltpu.VMEM((groups, 4, slab, size), BF16),
        pltpu.VMEM((groups, 4, slab, size), BF16),
        pltpu.VMEM((groups, 2, slab, size), BF16),
        pltpu.VMEM((groups, slab, size), BF16),
        dma((groups, 4)),
        dma((groups, 7)),
        dma((groups, 7)),
    ]


class Total:
    def __init__(self, axis, slots, send, recv):
        self.axis, self.slots, self.send, self.recv = axis, slots, send, recv
        self.count = slots.shape[0]
        self.place = lax.axis_index(axis)

    def copy(self, step):
        mine = self.slots.at[self.place]
        return remote(
            mine, mine, self.send.at[step - 1], self.recv.at[self.place], self.peer(step), self.axis
        )

    def peer(self, step):
        return lax.rem(self.place + step, self.count)

    def start(self, value):
        self.slots[self.place] = value
        for step in range(1, self.count):
            self.copy(step).start()

    def finish(self):
        for step in range(1, self.count):
            other = self.peer(step)
            slot = self.slots.at[other]
            remote(
                slot, slot, self.send.at[step - 1], self.recv.at[other], other, self.axis
            ).wait_recv()
        value = self.slots[0]
        for place in range(1, self.count):
            value = value + self.slots[place]
        return value

    def drain(self):
        for step in range(1, self.count):
            self.copy(step).wait_send()


def total_scratch(count, shape):
    dma = pltpu.SemaphoreType.DMA
    return [pltpu.VMEM((count, *shape), F32), dma((count - 1,)), dma((count,))]


def greet_all(axes):
    barrier = pltpu.get_barrier_semaphore()
    sent = 0
    for axis, count in axes:
        place = lax.axis_index(axis)
        for step in range(1, count):
            peer = lax.rem(place + step, count)
            pl.semaphore_signal(barrier, inc=1, device_id={axis: peer}, device_id_type=MESH)
            sent += 1
    pl.semaphore_wait(barrier, sent)


def close_kernel(
    seq_count,
    wide_count,
    kept_ref,
    grads_ref,
    ffn_ref,
    ln_ref,
    owned_ref,
    ln_out_ref,
    square_ref,
    *scratch,
):
    greet_all((("seq", seq_count), ("wide", wide_count)))
    sums, scratch = scratch[:7], scratch[7:]
    owners = OwnerSum(grads_ref, *sums)
    norms = [Total("wide", *scratch[0:3]), Total("seq", *scratch[3:6])]
    squares = [Total("wide", *scratch[6:9]), Total("seq", *scratch[9:12])]
    acc = scratch[12]
    slab = owned_ref.shape[0]
    width = grads_ref.shape[2]
    owners.start(0, 2)
    norms[0].start(ln_ref[...])
    acc[...] = jnp.zeros_like(acc)

    def keep(rws, value):
        row = lax.broadcasted_iota(jnp.int32, value.shape, 0) + rws.start
        return jnp.where(row < kept_ref[0], value, 0.0)

    def note(value):
        square = value * value
        rows = sum(square[row : row + 8] for row in range(0, value.shape[0], 8))
        acc[...] += sum(rows[:, place : place + 128] for place in range(0, value.shape[1], 128))

    def put(rws, cols, value):
        value = keep(rws, value)
        owned_ref[rws, cols] = value
        note(value)

    def from_ffn(index):
        rws = tile(index, 16)
        value = keep(rws, ffn_ref[rws, :].astype(F32))
        owned_ref[rws, pl.ds(width, ffn_ref.shape[1])] = value
        note(value)

    steps = owners.steps(put)
    for step in steps[:10]:
        step()
    norms[1].start(norms[0].finish())
    for step in steps[10:14]:
        step()
    loop(slab // 16, from_ffn)
    for step in steps[14:]:
        step()
    squares[0].start(acc[...])
    squares[1].start(squares[0].finish())
    ln_out_ref[...] = norms[1].finish()
    square_ref[...] = squares[1].finish()
    owners.drain()
    for part in (*norms, *squares):
        part.drain()


def close_call(kept, grads, ffn_owned, ln_rows, seq_count, wide_count):
    slab = ffn_owned.shape[0]
    width = grads.shape[1]
    vm = pl.BlockSpec(memory_space=pltpu.VMEM)
    sm = pl.BlockSpec(memory_space=pltpu.SMEM)
    return pl.pallas_call(
        functools.partial(close_kernel, seq_count, wide_count),
        out_shape=(
            jax.ShapeDtypeStruct((slab, width + ffn_owned.shape[1]), F32),
            jax.ShapeDtypeStruct(ln_rows.shape, F32),
            jax.ShapeDtypeStruct((8, 128), F32),
        ),
        in_specs=[sm, pl.BlockSpec(memory_space=pl.ANY), vm, vm],
        out_specs=(vm, vm, vm),
        scratch_shapes=[
            *owner_scratch(slab, width, len(SUM_ORDERS)),
            *total_scratch(wide_count, ln_rows.shape),
            *total_scratch(seq_count, ln_rows.shape),
            *total_scratch(wide_count, (8, 128)),
            *total_scratch(seq_count, (8, 128)),
            pltpu.VMEM((8, 128), F32),
        ],
        compiler_params=pltpu.CompilerParams(
            collective_id=4, has_side_effects=True, vmem_limit_bytes=VMEM_LIMIT
        ),
        name="close",
    )(kept, grads.reshape(seq_count, slab, width), ffn_owned, ln_rows)


def pick_kernel(block, places_ref, source_ref, target_ref, held, sems, sem):
    count = places_ref.shape[1]

    def copy(index):
        return pltpu.make_async_copy(
            source_ref.at[pl.ds(pl.multiple_of(places_ref[0, index] * block, block), block)],
            held.at[pl.ds(pl.multiple_of(index * block, block), block)],
            sems.at[index],
        )

    loop(count, lambda index: copy(index).start())
    loop(count, lambda index: copy(index).wait())
    out = pltpu.make_async_copy(held, target_ref, sem)
    out.start()
    out.wait()


def spread_kernel(block, places_ref, source_ref, target_ref, held, sems, sem):
    count = places_ref.shape[1]
    load = pltpu.make_async_copy(source_ref, held, sem)
    load.start()
    load.wait()

    def copy(index):
        return pltpu.make_async_copy(
            held.at[pl.ds(pl.multiple_of(index * block, block), block)],
            target_ref.at[pl.ds(pl.multiple_of(places_ref[1, index] * block, block), block)],
            sems.at[index],
        )

    loop(count, lambda index: copy(index).start())
    loop(count, lambda index: copy(index).wait())


def move_blocks(kernel, source, places, rows, block):
    hb = pl.BlockSpec(memory_space=pl.ANY)
    count = places.shape[1]
    return pl.pallas_call(
        functools.partial(kernel, block),
        out_shape=jax.ShapeDtypeStruct((rows, source.shape[1]), source.dtype),
        in_specs=[pl.BlockSpec(memory_space=pltpu.SMEM), hb],
        out_specs=hb,
        scratch_shapes=[
            pltpu.VMEM((count * block, source.shape[1]), source.dtype),
            pltpu.SemaphoreType.DMA((count,)),
            pltpu.SemaphoreType.DMA(()),
        ],
        compiler_params=pltpu.CompilerParams(vmem_limit_bytes=VMEM_LIMIT),
        name="move",
    )(places, source)


def per_device(
    hidden_in,
    cotangent,
    seq_offsets,
    owner_blocks,
    master,
    first_moment,
    second_moment,
    ln_params,
    ln_first,
    ln_second,
):
    width = hidden_in.shape[2]
    slab_rows = master.shape[0]
    block = slab_rows // CAP
    source, valid, target = owner_maps(owner_blocks, width, CAP, block)
    gathered_rows = slab_rows * lax.axis_size("seq")
    count = width // block
    fits = block % 16 == 0
    slots = target[::block] // block
    both = jnp.stack([slots, slots])

    def to_order(array):
        if fits:
            return move_blocks(pick_kernel, array, both, width, block)
        return jnp.take(array, target, axis=0)

    def to_owner(grads):
        if fits:
            return move_blocks(spread_kernel, grads, both, gathered_rows, block)
        return jnp.take(grads, source, axis=0)

    seq_count = lax.axis_size("seq")
    own_kernels = fits and seq_count == 8
    if own_kernels:
        weights = master
    else:
        low = master.astype(jnp.bfloat16)
        weights, w_ffn = (
            to_order(lax.all_gather(part, "seq", axis=0, tiled=True)) for part in (low[:, :width], low[:, width:])
        )
    slopes = jnp.exp2(-8.0 * (jnp.arange(H, dtype=jnp.float32) + 1.0) / H)
    x = jnp.transpose(hidden_in, (1, 0, 2))
    r1, normed, x_all, qkv, ctx, w_qkv, w_out, *more = attn_call(
        x, weights, ln_params, slots, seq_offsets, slopes, seq_count if own_kernels else 0
    )
    w_ffn = more[0] if own_kernels else w_ffn
    mixed_p, dr1_p, ffn_grads, ln_rows = ffn_call(
        r1, jnp.transpose(cotangent, (1, 0, 2)), normed, w_ffn, ln_params
    )
    mixed = jnp.transpose(mixed_p, (1, 0, 2))

    ffn_padded = to_owner(ffn_grads)
    grad_p, attn_grads, *more = back_call(
        dr1_p, w_qkv, w_out, x_all, qkv, ctx, ffn_padded if own_kernels else None, seq_offsets, slopes, seq_count
    )
    input_grad = jnp.transpose(grad_p, (1, 0, 2))
    attn_padded = to_owner(attn_grads)
    mine = jnp.arange(seq_count, dtype=jnp.int32) == lax.axis_index("seq")
    own_rows = jnp.sum(jnp.where(mine, owner_blocks, 0)) * block
    kept = (jnp.arange(slab_rows, dtype=jnp.int32) < own_rows)[:, None]
    if own_kernels:
        owned, ln_total, parts = close_call(
            own_rows[None], attn_padded, more[0], ln_rows, seq_count, lax.axis_size("wide")
        )
        squares, ln_total = jnp.sum(parts), ln_total[:4]
    else:
        ffn_owned = lax.psum_scatter(ffn_padded, "seq", scatter_dimension=0, tiled=True)
        attn_owned = lax.psum_scatter(attn_padded, "seq", scatter_dimension=0, tiled=True)
        owned = jnp.concatenate([attn_owned, ffn_owned], axis=1).astype(jnp.float32)
        owned = jnp.where(kept, owned, 0.0)
        squares, ln_total = lax.psum((jnp.sum(owned * owned), ln_rows[:4]), ("seq", "wide"))
    grad_norm = jnp.sqrt(squares + jnp.sum(ln_total * ln_total))
    clip = jnp.minimum(1.0, 1.0 / (grad_norm + 1e-06))
    param_new, first_new, second_new = adamw(
        master, owned * clip, first_moment, second_moment, DECAY, RATE
    )
    norms_new, norms_first, norms_second = adamw(
        ln_params, ln_total * clip, ln_first, ln_second, 0.0, NORM_RATE
    )
    return (
        mixed,
        input_grad,
        jnp.where(kept, param_new, 0.0),
        jnp.where(kept, first_new, 0.0),
        jnp.where(kept, second_new, 0.0),
        norms_new,
        norms_first,
        norms_second,
        grad_norm,
    )


def solution(mesh):
    return jax.shard_map(
        per_device,
        mesh=mesh,
        in_specs=(
            P("wide", "seq", None),
            P("wide", "seq", None),
            P("seq", None),
            P(),
            P("seq", "wide"),
            P("seq", "wide"),
            P("seq", "wide"),
            P(),
            P(),
            P(),
        ),
        out_specs=(
            P("wide", "seq", None),
            P("wide", "seq", None),
            P("seq", "wide"),
            P("seq", "wide"),
            P("seq", "wide"),
            P(),
            P(),
            P(),
            P(),
        ),
        check_vma=False,
    )
```

```python
import functools

import jax
import jax.numpy as jnp
from jax import lax
from jax.experimental import pallas as pl
from jax.experimental.pallas import tpu as pltpu
from jax.sharding import PartitionSpec as P

MESH = pl.DeviceIdType.MESH

H = 12
HD = 64
FF = 3072
UNIT = 128
CAP = 6
STEP = 10


RATE = 0.02
NORM_RATE = 0.6
BETA_ONE = 0.9
BETA_TWO = 0.999
EPSILON = 1e-08
DECAY = 0.01
NORM_EPS = 1e-05
ROOT_HALF = 0.7071067811865476
DENSITY_SCALE = 0.3989422804014327
EPS = 1e-05
F32 = jnp.float32
BF16 = jnp.bfloat16
NEG = -1e30
PAIRS = 4
SINGLES = 2
ROWS = 16
VMEM_LIMIT = 60 * 2**20


def owner_maps(owner_blocks, rows, cap, block):
    ends = jnp.cumsum(owner_blocks)
    starts = ends - owner_blocks
    slot = jnp.arange(cap * block, dtype=jnp.int32)
    which = slot // block
    source = (starts[:, None] + which[None, :]) * block + (slot % block)[None, :]
    valid = which[None, :] < owner_blocks[:, None]
    source = jnp.where(valid, source, 0).reshape(-1)
    valid = valid.reshape(-1)
    param = jnp.arange(rows, dtype=jnp.int32)
    blocks = param // block
    owner = jnp.sum((ends[None, :] <= blocks[:, None]).astype(jnp.int32), axis=1)
    onehot = owner[:, None] == jnp.arange(owner_blocks.shape[0], dtype=jnp.int32)[None, :]
    first = jnp.sum(jnp.where(onehot, starts[None, :], 0), axis=1)
    target = owner * (cap * block) + (blocks - first) * block + param % block
    return (source, valid, target)


def adamw(param, grad, first, second, decay, rate):
    first_new = BETA_ONE * first + (1.0 - BETA_ONE) * grad
    second_new = BETA_TWO * second + (1.0 - BETA_TWO) * grad * grad
    first_hat = first_new / (1.0 - BETA_ONE**STEP)
    second_hat = second_new / (1.0 - BETA_TWO**STEP)
    param_new = param - rate * (first_hat / (jnp.sqrt(second_hat) + EPSILON) + decay * param)
    return (param_new, first_new, second_new)


def dot_nn(a, b):
    return lax.dot_general(a, b, (((1,), (0,)), ((), ())), preferred_element_type=F32)


def dot_nt(a, b):
    return lax.dot_general(a, b, (((1,), (1,)), ((), ())), preferred_element_type=F32)


def dot_tn(a, b):
    return lax.dot_general(a, b, (((0,), (0,)), ((), ())), preferred_element_type=F32)


def places():
    wide = lax.axis_index("wide")
    core = lax.rem(wide, 2)
    row = wide // 2
    return wide, core, row, wide + 1 - 2 * core, wide + 2 - 4 * row


def greet(mate, across):
    barrier = pltpu.get_barrier_semaphore()
    for peer in (mate, across):
        pl.semaphore_signal(barrier, inc=1, device_id={"wide": peer}, device_id_type=MESH)
    pl.semaphore_wait(barrier, 2)


def remote(source, target, send, recv, peer, axis="wide"):
    return pltpu.make_async_remote_copy(
        src_ref=source,
        dst_ref=target,
        send_sem=send,
        recv_sem=recv,
        device_id={axis: peer},
        device_id_type=MESH,
    )


class Gather:
    def __init__(self, held, send, recv, share):
        self.held, self.send, self.recv, self.share = held, send, recv, share
        _, self.core, self.row, self.mate, self.across = places()

    def rows(self, core, row):
        return pl.ds(pl.multiple_of((core * 2 + row) * self.share, self.share), self.share)

    def copy(self, pack, leg):
        row = 1 - self.row if leg == 2 else self.row
        block = self.held.at[pack, self.rows(self.core, row)]
        peer = self.mate if leg else self.across
        return remote(block, block, self.send.at[pack, leg], self.recv.at[pack, leg], peer)

    def start(self, pack):
        self.copy(pack, 0).start()
        self.copy(pack, 1).start()

    def finish(self, pack):
        self.copy(pack, 0).wait_recv()
        self.copy(pack, 2).start()
        self.copy(pack, 1).wait_recv()
        self.copy(pack, 2).wait_recv()

    def drain(self, pack):
        for leg in range(3):
            self.copy(pack, leg).wait_send()


class Scatter:
    def __init__(self, part, give, take, cross, reach, own, send, recv, share):
        self.part, self.give, self.take = part, give, take
        self.cross, self.reach, self.own = cross, reach, own
        self.send, self.recv, self.share = send, recv, share
        _, self.core, self.row, self.mate, self.across = places()

    def copy(self, pack, leg):
        source, target = (self.cross, self.reach) if leg else (self.give, self.take)
        peer = self.across if leg else self.mate
        return remote(
            source.at[pack], target.at[pack], self.send.at[pack, leg], self.recv.at[pack, leg], peer
        )

    def half(self, which):
        core = self.core if which else 1 - self.core
        return pl.multiple_of(core * 2 * self.share, 2 * self.share)

    def start(self, pack):
        self.copy(pack, 0).start()

    def middle(self, pack):
        self.copy(pack, 0).wait_recv()
        share = self.share
        far = pl.ds(pl.multiple_of((1 - self.row) * share, share), share)
        near = pl.ds(pl.multiple_of(self.row * share, share), share)
        self.cross[pack] = (self.part[far, :] + self.take[pack, far, :].astype(F32)).astype(BF16)
        self.copy(pack, 1).start()
        self.own[pack] = self.part[near, :] + self.take[pack, near, :].astype(F32)

    def finish(self, pack):
        self.copy(pack, 1).wait_recv()

    def drain(self, pack):
        for leg in range(2):
            self.copy(pack, leg).wait_send()


def scatter_scratch(packs, share, width):
    return [
        pltpu.VMEM((2 * share, width), F32),
        pltpu.VMEM((packs, 2 * share, width), BF16),
        pltpu.VMEM((packs, 2 * share, width), BF16),
        pltpu.VMEM((packs, share, width), BF16),
        pltpu.VMEM((packs, share, width), BF16),
        pltpu.VMEM((packs, share, width), F32),
    ]


def norm_parts(values):
    center = values - jnp.mean(values, axis=-1, keepdims=True)
    inverse = lax.rsqrt(jnp.mean(center * center, axis=-1, keepdims=True) + EPS)
    return center * inverse, inverse


def norm_pull(grad, normal, inverse, gain):
    scaled = grad * gain
    return inverse * (
        scaled
        - jnp.mean(scaled, axis=-1, keepdims=True)
        - normal * jnp.mean(scaled * normal, axis=-1, keepdims=True)
    )


def loop(count, body, unroll=1):
    def step(index, carry):
        body(index)
        return carry

    lax.fori_loop(0, count, step, 0, unroll=unroll)


def tile(index, size):
    return pl.ds(pl.multiple_of(index * size, size), size)


def ffn_kernel(
    r1_ref,
    cot_ref,
    held_ref,
    w_ref,
    ln_ref,
    mixed_ref,
    dr1_ref,
    grads_ref,
    lngrad_ref,
    weights,
    held,
    held2,
    gates,
    ups,
    hid,
    dgate,
    dup,
    turned,
    turned2,
    total,
    g_tile,
    u_tile,
    send_a,
    recv_a,
    send_b,
    recv_b,
    send_c,
    recv_c,
    send_d,
    recv_d,
    load_sem,
    store_sem,
    *buffers,
):
    packs, share, width = r1_ref.shape
    rows = 4 * share
    fwd = buffers[:6]
    units = weights.shape[1] // 3
    col = 256
    n_width = width // col
    loads = [pltpu.make_async_copy(w_ref, weights, load_sem.at[packs - 1])]
    for pack in range(packs - 1):
        loads.append(pltpu.make_async_copy(held_ref.at[pack], held.at[pack], load_sem.at[pack]))
    for load in loads:
        load.start()
    _, core, row, mate, across = places()
    greet(mate, across)
    gather_one = Gather(held, send_a, recv_a, share)
    scatter_one = Scatter(*fwd, send_b, recv_b, share)
    gather_two = Gather(held2, send_c, recv_c, share)
    scatter_two = Scatter(*fwd, send_d, recv_d, share)
    gain1, shift1 = ln_ref[0:1, :], ln_ref[1:2, :]
    gain2, shift2 = ln_ref[2:3, :], ln_ref[3:4, :]
    lngrad_ref[...] = jnp.zeros_like(lngrad_ref)
    chunk = 32

    base = pl.multiple_of((core * 2 + row) * share, share)

    def first(index):
        normal, _ = norm_parts(r1_ref[packs - 1, tile(index, chunk), :])
        held[packs - 1, pl.ds(pl.multiple_of(base + index * chunk, chunk), chunk), :] = (
            normal * gain1 + shift1
        ).astype(BF16)

    loop(share // chunk, first, unroll=4)
    gather_one.start(packs - 1)
    loads[0].wait()

    def widen(pack):
        def ff(index):
            first = pl.multiple_of(index * share, share)
            x = held[pack, pl.ds(first, share), :]
            g_tile[...] = dot_nn(x, weights[:, pl.ds(0, units)])
            u_tile[...] = dot_nn(x, weights[:, pl.ds(units, units)])

            def act(part):
                rws = tile(part, ROWS)
                gate, up = g_tile[rws, :], u_tile[rws, :]
                out = pl.ds(pl.multiple_of(first + part * ROWS, ROWS), ROWS)
                cumulative = 0.5 * (1.0 + lax.erf(gate * ROOT_HALF))
                hid[out, :] = (gate * cumulative * up).astype(BF16)
                gates[pack, out, :] = gate.astype(BF16)
                ups[pack, out, :] = up.astype(BF16)

            loop(share // ROWS, act, unroll=2)

        loop(4, ff)

    def narrow(pack):
        for which in range(2):
            base = scatter_one.half(which)

            def down(index, base=base, which=which):
                rws = pl.ds(pl.multiple_of(base + index * share, share), share)
                value = dot_nt(hid[rws, :], weights[:, pl.ds(2 * units, units)])
                if which:
                    scatter_one.part[tile(index, share), :] = value
                else:
                    scatter_one.give[pack, tile(index, share), :] = value.astype(BF16)

            loop(2, down)
            if not which:
                scatter_one.start(pack)
        scatter_one.middle(pack)

    def turn(pack):
        scatter_one.finish(pack)
        gather_two_base = pl.multiple_of((core * 2 + row) * share, share)

        def second(index):
            rws = tile(index, chunk)
            normal, _ = norm_parts(r1_ref[pack, rws, :])
            ffn = scatter_one.own[pack, rws, :] + scatter_one.reach[pack, rws, :].astype(F32)
            normal2, inverse2 = norm_parts(normal * gain1 + shift1 + ffn)
            mixed_ref[pack, rws, :] = (normal2 * gain2 + shift2).astype(BF16)
            grad = cot_ref[pack, rws, :].astype(F32)
            value = norm_pull(grad, normal2, inverse2, gain2)
            dr1_ref[pack, rws, :] = value
            held2[pack, pl.ds(pl.multiple_of(gather_two_base + index * chunk, chunk), chunk), :] = value.astype(BF16)
            lngrad_ref[2:3, :] += jnp.sum(grad * normal2, axis=0, keepdims=True)
            lngrad_ref[3:4, :] += jnp.sum(grad, axis=0, keepdims=True)

        loop(share // chunk, second, unroll=4)
        scatter_one.drain(pack)
        gather_two.start(pack)

    def backward(pack):
        gather_two.finish(pack)
        for which in range(2):
            base = scatter_two.half(which)

            def bf(index, base=base):
                first = pl.multiple_of(base + index * share, share)
                g_tile[...] = dot_nn(held2[pack, pl.ds(first, share), :], weights[:, pl.ds(2 * units, units)])

                def act(part):
                    rws = tile(part, ROWS)
                    out = pl.ds(pl.multiple_of(first + part * ROWS, ROWS), ROWS)
                    dhid = g_tile[rws, :]
                    gate = gates[pack, out, :].astype(F32)
                    up = ups[pack, out, :].astype(F32)
                    cumulative = 0.5 * (1.0 + lax.erf(gate * ROOT_HALF))
                    density = jnp.exp(-0.5 * gate * gate) * DENSITY_SCALE
                    value = gate * cumulative
                    hid[out, :] = (value * up).astype(BF16)
                    dgate[out, :] = (dhid * up * (cumulative + gate * density)).astype(BF16)
                    dup[out, :] = (dhid * value).astype(BF16)

                loop(share // ROWS, act, unroll=2)

            loop(2, bf)

            def back(index, base=base, which=which):
                rws = pl.ds(pl.multiple_of(base + index * share, share), share)
                value = dot_nt(dgate[rws, :], weights[:, pl.ds(0, units)]) + dot_nt(
                    dup[rws, :], weights[:, pl.ds(units, units)]
                )
                if which:
                    scatter_two.part[tile(index, share), :] = value
                else:
                    scatter_two.give[pack, tile(index, share), :] = value.astype(BF16)

            loop(2, back)
            if not which:
                scatter_two.start(pack)
        scatter_two.middle(pack)

    def weight_grads(pack):
        def flip(index):
            rws = tile(index, 256)
            turned[:, rws] = held[pack, rws, :].T
            turned2[:, rws] = held2[pack, rws, :].T

        loop(rows // 256, flip)

        def add(index):
            rws = tile(index, col)
            a = turned[rws, :]
            b = turned2[rws, :]
            parts = (dot_nn(a, dgate[...]), dot_nn(a, dup[...]), dot_nn(b, hid[...]))
            for place, value in enumerate(parts):
                cols = pl.ds(place * units, units)
                if pack == 0:
                    total[rws, cols] = value
                else:
                    value = total[rws, cols] + value
                    if pack < packs - 1:
                        total[rws, cols] = value
                    else:
                        gates[place, rws, :] = value.astype(BF16)

        loop(n_width, add)

    def last(pack):
        scatter_two.finish(pack)

        def third(index):
            rws = tile(index, chunk)
            normal, inverse = norm_parts(r1_ref[pack, rws, :])
            grad = dr1_ref[pack, rws, :] + (
                scatter_two.own[pack, rws, :] + scatter_two.reach[pack, rws, :].astype(F32)
            )
            dr1_ref[pack, rws, :] = norm_pull(grad, normal, inverse, gain1)
            lngrad_ref[0:1, :] += jnp.sum(grad * normal, axis=0, keepdims=True)
            lngrad_ref[1:2, :] += jnp.sum(grad, axis=0, keepdims=True)

        loop(share // chunk, third, unroll=4)

    for pack in range(packs):
        if pack < packs - 1:
            loads[pack + 1].wait()
        else:
            gather_one.finish(pack)
        widen(pack)
        narrow(pack)
        if pack:
            turn(pack - 1)
    for pack in range(packs):
        backward(pack)
        weight_grads(pack)
        if pack == 0:
            turn(packs - 1)
        else:
            last(pack - 1)
    outs = [
        pltpu.make_async_copy(
            gates.at[place, pl.ds(0, width)],
            grads_ref.at[:, pl.ds(place * units, units)],
            store_sem.at[place],
        )
        for place in range(3)
    ]
    for out in outs:
        out.start()
    last(packs - 1)
    for out in outs:
        out.wait()
    gather_one.drain(packs - 1)
    for pack in range(packs):
        gather_two.drain(pack)
        scatter_two.drain(pack)


def ffn_call(r1, cot, held, weights, ln_params):
    packs, share, width = r1.shape
    rows = 4 * share
    units = weights.shape[1] // 3
    vm = pl.BlockSpec(memory_space=pltpu.VMEM)
    hb = pl.BlockSpec(memory_space=pl.ANY)
    dma = pltpu.SemaphoreType.DMA
    return pl.pallas_call(
        ffn_kernel,
        out_shape=(
            jax.ShapeDtypeStruct((packs, share, width), BF16),
            jax.ShapeDtypeStruct((packs, share, width), F32),
            jax.ShapeDtypeStruct((width, 3 * units), BF16),
            jax.ShapeDtypeStruct((8, width), F32),
        ),
        in_specs=[vm, vm, hb, hb, vm],
        out_specs=(vm, vm, hb, vm),
        scratch_shapes=[
            pltpu.VMEM((width, 3 * units), BF16),
            pltpu.VMEM((packs, rows, width), BF16),
            pltpu.VMEM((packs, rows, width), BF16),
            pltpu.VMEM((packs, rows, units), BF16),
            pltpu.VMEM((packs, rows, units), BF16),
            pltpu.VMEM((rows, units), BF16),
            pltpu.VMEM((rows, units), BF16),
            pltpu.VMEM((rows, units), BF16),
            pltpu.VMEM((width, rows), BF16),
            pltpu.VMEM((width, rows), BF16),
            pltpu.VMEM((width, 3 * units), F32),
            pltpu.VMEM((share, units), F32),
            pltpu.VMEM((share, units), F32),
            dma((packs, 3)),
            dma((packs, 3)),
            dma((packs, 2)),
            dma((packs, 2)),
            dma((packs, 3)),
            dma((packs, 3)),
            dma((packs, 2)),
            dma((packs, 2)),
            dma((packs,)),
            dma((3,)),
            *scatter_scratch(packs, share, width),
        ],
        compiler_params=pltpu.CompilerParams(
            collective_id=1, has_side_effects=True, vmem_limit_bytes=VMEM_LIMIT
        ),
        cost_estimate=pl.CostEstimate(flops=int(70e9), bytes_accessed=4 * 10**7, transcendentals=10**7),
        name="ffn",
    )(r1, cot, held, weights, ln_params)


class Runs:
    def __init__(self, offsets, pack):
        names = [offsets[pack, place] for place in range(8)]
        start = jnp.int32(4)
        for place in range(3, -1, -1):
            start = lax.select(names[place] == names[place + 3], jnp.int32(place), start)
        self.start = start
        self.names = [lax.select(start > place, names[place], names[place + 4]) for place in range(4)]

    def masks(self, index):
        own = self.names[0]
        for place in range(1, 4):
            own = lax.select(index == place, self.names[place], own)
        return [lax.select(own == name, jnp.float32(0.0), jnp.float32(NEG)) for name in self.names]

    def arrange(self, plain, order):
        for place in range(4):
            value = plain[held_run(place), :]
            for start in range(1, 5):
                value = lax.select(self.start == start, plain[held_run(place + start), :], value)
            order(pl.ds(place * UNIT, UNIT), value)
            value = lax.select(self.start > place, plain[held_run(place), :], plain[held_run(place + 4), :])
            order(pl.ds((place + 4) * UNIT, UNIT), value)

    def restore(self, order, plain):
        for run in range(8):
            first = max(0, run - 3)
            value = order[pl.ds((run - first) * UNIT, UNIT), :]
            for start in range(first + 1, min(run, 4) + 1):
                value = lax.select(self.start == start, order[pl.ds((run - start) * UNIT, UNIT), :], value)
            if run < 4:
                value = lax.select(self.start > run, order[pl.ds((run + 4) * UNIT, UNIT), :], value)
            else:
                value = lax.select(self.start <= run - 4, order[pl.ds(run * UNIT, UNIT), :], value)
            plain(held_run(run), value)


def held_run(run):
    half, part = divmod(run, 2)
    return pl.ds(((half % 2) * 2 + half // 2) * 2 * UNIT + part * UNIT, UNIT)


def writer(ref, *at):
    def write(rows, value):
        ref[(*at, rows, slice(None))] = value

    return write


def fill_bias(bias, slopes, wide):
    heads, size, _ = bias.shape

    def fill(index):
        rws = tile(index, UNIT)
        down = lax.broadcasted_iota(jnp.int32, (UNIT, size), 0) + index * UNIT
        along = lax.broadcasted_iota(jnp.int32, (UNIT, size), 1)
        distance = jnp.abs(down - along).astype(F32)
        for head in range(heads):
            bias[head, rws, :] = -slopes[wide * heads + head] * distance

    loop(size // UNIT, fill)


def split_weights(packed, w_qkv, w_out):
    width, each = packed.shape[0], packed.shape[1] // 4
    wide = w_out.shape[1]

    def part(index):
        rws = tile(index, 128)
        zeros = jnp.zeros((128, wide - each), BF16)
        for place in range(4):
            value = jnp.concatenate([packed[rws, pl.ds(place * each, each)], zeros], axis=1)
            if place < 3:
                w_qkv[rws, pl.ds(place * wide, wide)] = value
            else:
                w_out[rws, :] = value

    loop(width // 128, part)


def mask_row(runs, index):
    return jnp.concatenate([jnp.full((1, UNIT), part, F32) for part in runs.masks(index)], axis=1)


def split_heads(value, low):
    none = jnp.zeros_like(value)
    return jnp.concatenate([jnp.where(low, value, none), jnp.where(low, none, value)], axis=0)


def head_lanes():
    lane = lax.broadcasted_iota(jnp.int32, (1, 128), 1)
    return lane < HD


def attn_kernel(
    gathering,
    offsets_ref,
    slopes_ref,
    slots_ref,
    x_ref,
    w_ref,
    ln_ref,
    r1_ref,
    normed_ref,
    held_ref,
    qkv_ref,
    ctx_ref,
    w_qkv_ref,
    w_out_ref,
    *rest,
):
    w_ffn_ref, rest = (rest[0], rest[1:]) if gathering else (None, rest)
    (
        packed,
        w_qkv,
        w_out,
        bias,
        held,
        normed,
        plain,
        qkv,
        ctx_order,
        ctx,
        send_a,
        recv_a,
        send_b,
        recv_b,
        send_c,
        recv_c,
        load_sem,
        store_sem,
        *buffers,
    ) = rest
    packs, share, width = x_ref.shape
    rows = 4 * share
    lanes = w_out.shape[1]
    group = rows // 2
    wide, core, row, mate, across = places()
    if gathering:
        slab, near, near_send, near_recv, far, far_send, far_recv, ordered, *buffers = buffers
        load = pltpu.make_async_copy(w_ref, slab, load_sem)
        load.start()
        owners = OwnerGather(near, near_send, near_recv, slab.shape[0])
        others = OwnerGather(far, far_send, far_recv, slab.shape[0])
        holders = near.shape[1] // slab.shape[0]
        greet_all((("seq", holders), ("wide", 4)))
        load.wait()
        cut = near.shape[2]
        for part in range(owners.groups):
            value = slab[:, part * cut : (part + 1) * cut]
            near[part, owners.rows(owners.seq), :] = value.astype(BF16)
        owners.start()
        cut = far.shape[2]
        for part in range(others.groups):
            value = slab[:, width + part * cut : width + (part + 1) * cut]
            far[part, others.rows(others.seq), :] = value.astype(BF16)
    else:
        load = pltpu.make_async_copy(w_ref.at[:, pl.ds(0, packed.shape[1])], packed, load_sem)
        load.start()
        greet(mate, across)
    gather = Gather(held, send_a, recv_a, share)
    scatter = Scatter(*buffers, send_b, recv_b, share)
    spread = Gather(normed, send_c, recv_c, share)
    gain, shift = ln_ref[0:1, :], ln_ref[1:2, :]
    base = pl.multiple_of((core * 2 + row) * share, share)
    for pack in range(packs):
        held[pack, pl.ds(base, share), :] = x_ref[pack]
        gather.start(pack)
    fill_bias(bias, slopes_ref, wide)
    stores = []
    todo = []

    def pump(count):
        for _ in range(min(count, len(todo))):
            todo.pop(0)()

    if gathering:
        for step in owners.steps():
            step()
        others.start()
        todo = others.steps()
        cut = near.shape[2]
        for part in range(owners.groups):
            owners.finish(part)
            order_slabs(slots_ref, near, part, packed, pl.ds(part * cut, cut), holders)

        def settled(part):
            others.finish(part)
            cut = far.shape[2]
            cols = pl.ds(part * cut, cut)
            order_slabs(slots_ref, far, part, ordered, cols, holders)
            copy = pltpu.make_async_copy(
                ordered.at[:, cols], w_ffn_ref.at[:, cols], store_sem.at[packs + 1, part]
            )
            copy.start()
            stores.append(copy)

        todo += [functools.partial(settled, part) for part in range(others.groups)]
    else:
        load.wait()
    split_weights(packed, w_qkv, w_out)
    low = head_lanes()
    scale = jnp.asarray(HD ** (-0.5), BF16)
    for place, (source, target) in enumerate(((w_qkv, w_qkv_ref), (w_out, w_out_ref))):
        copy = pltpu.make_async_copy(source, target, store_sem.at[packs, place])
        copy.start()
        stores.append(copy)

    def attend(pack):
        runs = Runs(offsets_ref, pack)
        gather.finish(pack)

        def project(index):
            rws = tile(index, 256)
            value = dot_nn(held[pack, rws, :], w_qkv[...])
            plain[rws, pl.ds(0, lanes)] = (value[:, :lanes].astype(BF16) * scale).astype(BF16)
            plain[rws, pl.ds(lanes, 2 * lanes)] = value[:, lanes:].astype(BF16)

        loop(rows // 256, project)
        runs.arrange(plain, writer(qkv, pack))
        for side in range(2):
            keys = pl.ds(side * group, group)

            def weigh(part, queries, offset, side=side, keys=keys, pack=pack):
                scores = dot_nt(queries, qkv[pack, keys, pl.ds(lanes + part * 128, 128)]) + offset
                powers = jnp.exp(scores - jnp.max(scores, axis=-1, keepdims=True))
                total = jnp.sum(powers, axis=-1, keepdims=True)
                return dot_nn(powers.astype(BF16), qkv[pack, keys, pl.ds(2 * lanes + part * 128, 128)]) / total

            def pair(index, side=side, pack=pack):
                rws = pl.ds(pl.multiple_of(side * group + index * UNIT, UNIT), UNIT)
                offset = jnp.concatenate([bias[head, tile(index, UNIT), :] for head in range(2)], axis=0)
                if side:
                    offset = offset + mask_row(runs, index)
                out = weigh(0, split_heads(qkv[pack, rws, pl.ds(0, 128)], low), offset)
                ctx_order[rws, pl.ds(0, 128)] = jnp.where(low, out[:UNIT], out[UNIT:]).astype(BF16)

            def single(index, side=side, pack=pack):
                rws = pl.ds(pl.multiple_of(side * group + index * 2 * UNIT, 2 * UNIT), 2 * UNIT)
                offset = bias[2, tile(index, 2 * UNIT), :]
                if side:
                    offset = jnp.concatenate(
                        [
                            offset[half * UNIT : (half + 1) * UNIT] + mask_row(runs, 2 * index + half)
                            for half in range(2)
                        ],
                        axis=0,
                    )
                out = weigh(1, qkv[pack, rws, pl.ds(128, 128)], offset)
                ctx_order[rws, pl.ds(128, 128)] = out.astype(BF16)

            loop(4, pair, unroll=PAIRS)
            loop(2, single, unroll=SINGLES)
            pump(1 if pack else 0)
        runs.restore(ctx_order, writer(ctx, pack))
        for which in range(2):
            big = pl.ds(scatter.half(which), 2 * share)

            def out(index, which=which, big=big):
                cols = tile(index, 256)
                value = dot_nt(ctx[pack, big, :], w_out[cols, :])
                if which:
                    scatter.part[:, cols] = value
                else:
                    scatter.give[pack, :, cols] = value.astype(BF16)

            loop(width // 256, out)
            if not which:
                scatter.start(pack)
        scatter.middle(pack)
        pump(2)
        for place, (source, target) in enumerate(((held, held_ref), (qkv, qkv_ref), (ctx, ctx_ref))):
            copy = pltpu.make_async_copy(source.at[pack], target.at[pack], store_sem.at[pack, place])
            copy.start()
            stores.append(copy)

    def settle(pack):
        scatter.finish(pack)

        last = pack == packs - 1

        def add(index):
            rws = tile(index, 32)
            attn = scatter.own[pack, rws, :] + scatter.reach[pack, rws, :].astype(F32)
            value = x_ref[pack, rws, :].astype(F32) + attn
            r1_ref[pack, rws, :] = value
            if not last:
                normal, _ = norm_parts(value)
                out = pl.ds(pl.multiple_of(base + index * 32, 32), 32)
                normed[pack, out, :] = (normal * gain + shift).astype(BF16)

        loop(share // 32, add, unroll=4)
        if not last:
            spread.start(pack)

    def hand_on(pack):
        spread.finish(pack)
        copy = pltpu.make_async_copy(normed.at[pack], normed_ref.at[pack], store_sem.at[packs + 2, pack])
        copy.start()
        stores.append(copy)

    for pack in range(packs):
        attend(pack)
        if pack:
            settle(pack - 1)
        if pack > 1:
            hand_on(pack - 2)
    settle(packs - 1)
    pump(len(todo))
    hand_on(packs - 2)
    for copy in stores:
        copy.wait()
    for pack in range(packs):
        gather.drain(pack)
        scatter.drain(pack)
        if pack < packs - 1:
            spread.drain(pack)
    if gathering:
        owners.drain()
        others.drain()


def back_kernel(
    summing,
    offsets_ref,
    slopes_ref,
    dr1_ref,
    w_qkv_ref,
    w_out_ref,
    x_ref,
    qkv_ref,
    ctx_ref,
    *rest,
):
    padded_ref, rest = (rest[0], rest[1:]) if summing else (None, rest)
    grad_ref, grads_ref, *rest = rest
    owned_ref, rest = (rest[0], rest[1:]) if summing else (None, rest)
    (
        w_qkv,
        w_out,
        bias,
        held,
        x_all,
        qkv,
        ctx,
        plain,
        dctx,
        dorder,
        dplain,
        sum_k,
        sum_v,
        turned,
        total,
        total_out,
        send_a,
        recv_a,
        send_b,
        recv_b,
        load_sem,
        fetch_sem,
        *buffers,
    ) = rest
    if summing:
        owners = OwnerSum(padded_ref, *buffers[6:])

        def put(rws, cols, value):
            owned_ref[rws, cols] = value.astype(BF16)

        todo = owners.steps(put)
    else:
        todo = []

    def pump(count):
        for _ in range(min(count, len(todo))):
            todo.pop(0)()

    packs, share, width = dr1_ref.shape
    rows = 4 * share
    lanes = w_out.shape[1]
    group = rows // 2
    loads = [
        pltpu.make_async_copy(source, target, load_sem.at[place])
        for place, (source, target) in enumerate(((w_qkv_ref, w_qkv), (w_out_ref, w_out)))
    ]
    for copy in loads:
        copy.start()
    fetches = []
    for pack in range(packs):
        for place, (source, target) in enumerate(((x_ref, x_all), (qkv_ref, qkv), (ctx_ref, ctx))):
            copy = pltpu.make_async_copy(source.at[pack], target.at[pack], fetch_sem.at[pack, place])
            copy.start()
            fetches.append(copy)
    wide, core, row, mate, across = places()
    if summing:
        greet_all((("seq", padded_ref.shape[0]), ("wide", 4)))
    else:
        greet(mate, across)
    gather = Gather(held, send_a, recv_a, share)
    scatter = Scatter(*buffers[:6], send_b, recv_b, share)
    base = pl.multiple_of((core * 2 + row) * share, share)
    for pack in range(packs):
        held[pack, pl.ds(base, share), :] = dr1_ref[pack].astype(BF16)
        gather.start(pack)
    if summing:
        owners.start(0, 2)
    fill_bias(bias, slopes_ref, wide)
    for copy in loads:
        copy.wait()
    low = head_lanes()
    scale = HD ** (-0.5)

    def pull(pack):
        runs = Runs(offsets_ref, pack)
        gather.finish(pack)

        def project(index):
            rws = tile(index, 256)
            plain[rws, :] = dot_nn(held[pack, rws, :], w_out[...]).astype(BF16)

        loop(rows // 256, project)
        runs.arrange(plain, writer(dctx))
        for copy in fetches[3 * pack : 3 * pack + 3]:
            copy.wait()
        for side in range(2):
            keys = pl.ds(side * group, group)
            sum_k[...] = jnp.zeros_like(sum_k)
            sum_v[...] = jnp.zeros_like(sum_v)

            def masked(offset, index):
                return jnp.concatenate(
                    [offset[t * UNIT : (t + 1) * UNIT] + value for t, value in enumerate(runs.masks(index))],
                    axis=0,
                )

            def pull_back(part, queries, dout, offset, keys=keys, pack=pack):
                block = pl.ds(part * 128, 128)
                k_all = qkv[pack, keys, pl.ds(lanes + part * 128, 128)]
                v_all = qkv[pack, keys, pl.ds(2 * lanes + part * 128, 128)]
                scores = dot_nt(k_all, queries) + offset
                powers = jnp.exp(scores - jnp.max(scores, axis=0, keepdims=True))
                probs = powers * (1.0 / jnp.sum(powers, axis=0, keepdims=True))
                dprobs = dot_nt(v_all, dout)
                delta = jnp.sum(probs * dprobs, axis=0, keepdims=True)
                dscores = (probs * (dprobs - delta)).astype(BF16)
                sum_v[:, block] += dot_nn(probs.astype(BF16), dout)
                sum_k[:, block] += dot_nn(dscores, queries)
                return dot_tn(dscores, k_all) * scale

            def pair(index, side=side, pack=pack):
                rws = pl.ds(pl.multiple_of(side * group + index * UNIT, UNIT), UNIT)
                block = pl.ds(0, 128)
                offsets = [bias[head, :, tile(index, UNIT)] for head in range(2)]
                if side:
                    offsets = [masked(offset, index) for offset in offsets]
                dq = pull_back(
                    0,
                    split_heads(qkv[pack, rws, block], low),
                    split_heads(dctx[rws, block], low),
                    jnp.concatenate(offsets, axis=1),
                )
                dorder[rws, block] = jnp.where(low, dq[:UNIT], dq[UNIT:]).astype(BF16)

            def single(index, side=side, pack=pack):
                rws = pl.ds(pl.multiple_of(side * group + index * 2 * UNIT, 2 * UNIT), 2 * UNIT)
                block = pl.ds(128, 128)
                offset = bias[2, :, tile(index, 2 * UNIT)]
                if side:
                    offset = jnp.concatenate(
                        [
                            masked(offset[:, half * UNIT : (half + 1) * UNIT], 2 * index + half)
                            for half in range(2)
                        ],
                        axis=1,
                    )
                dorder[rws, block] = pull_back(1, qkv[pack, rws, block], dctx[rws, block], offset).astype(BF16)

            loop(4, pair, unroll=PAIRS)
            loop(2, single, unroll=SINGLES)
            pump(((4, 2), (1, 0), (2, 2))[pack][side])
            dorder[keys, pl.ds(lanes, lanes)] = sum_k[...].astype(BF16)
            dorder[keys, pl.ds(2 * lanes, lanes)] = sum_v[...].astype(BF16)
        runs.restore(dorder, writer(dplain))
        for which in range(2):
            big = pl.ds(scatter.half(which), 2 * share)

            def out(index, which=which, big=big):
                cols = tile(index, 256)
                value = dot_nt(dplain[big, :], w_qkv[cols, :])
                if which:
                    scatter.part[:, cols] = value
                else:
                    scatter.give[pack, :, cols] = value.astype(BF16)

            loop(width // 256, out)
            if not which:
                scatter.start(pack)
        scatter.middle(pack)
        pump((2, 1, 1)[pack])

    def weight_grads(pack):
        for source, result, target in ((x_all, dplain, total), (held, ctx.at[pack], total_out)):

            def flip(index, source=source):
                rws = tile(index, 256)
                turned[:, rws] = source[pack, rws, :].T

            loop(rows // 256, flip)

            def add(index, result=result, target=target):
                rws = tile(index, 256)
                value = dot_nn(turned[rws, :], result[...])
                if pack:
                    value = value + target[rws, :]
                target[rws, :] = value

            loop(width // 256, add)

    def settle(pack):
        scatter.finish(pack)

        def add(index):
            rws = tile(index, 64)
            grad_ref[pack, rws, :] = dr1_ref[pack, rws, :] + (
                scatter.own[pack, rws, :] + scatter.reach[pack, rws, :].astype(F32)
            )

        loop(share // 64, add)

    for pack in range(packs):
        pull(pack)
        weight_grads(pack)
        pump((1, 0, 1)[pack])
        if pack:
            settle(pack - 1)
    each = width // 4

    def pack_up(index):
        rws = tile(index, 128)
        pieces = [total[rws, pl.ds(place * lanes, each)] for place in range(3)]
        pieces.append(total_out[rws, pl.ds(0, each)])
        grads_ref[rws, :] = jnp.concatenate([piece.astype(BF16) for piece in pieces], axis=1)

    loop(width // 128, pack_up)
    settle(packs - 1)

    pump(len(todo))
    if summing:
        owners.drain()
    for pack in range(packs):
        gather.drain(pack)
        scatter.drain(pack)


def attn_call(x, weights, ln_params, slots, offsets, slopes, seq_count):
    packs, share, width = x.shape
    rows = 4 * share
    lanes = 256
    vm = pl.BlockSpec(memory_space=pltpu.VMEM)
    hb = pl.BlockSpec(memory_space=pl.ANY)
    sm = pl.BlockSpec(memory_space=pltpu.SMEM)
    dma = pltpu.SemaphoreType.DMA
    more, more_out = [], []
    if seq_count:
        slab, units = weights.shape[0], weights.shape[1] - width
        groups = len(GATHER_ORDERS)
        more = [
            pltpu.VMEM(weights.shape, F32),
            *gather_scratch(seq_count * slab, width, groups),
            *gather_scratch(seq_count * slab, units, groups),
            pltpu.VMEM((width, units), BF16),
        ]
        more_out = [jax.ShapeDtypeStruct((width, units), BF16)]
    return pl.pallas_call(
        functools.partial(attn_kernel, bool(seq_count)),
        out_shape=(
            jax.ShapeDtypeStruct((packs, share, width), F32),
            jax.ShapeDtypeStruct((packs - 1, rows, width), BF16),
            jax.ShapeDtypeStruct((packs, rows, width), BF16),
            jax.ShapeDtypeStruct((packs, rows, 3 * lanes), BF16),
            jax.ShapeDtypeStruct((packs, rows, lanes), BF16),
            jax.ShapeDtypeStruct((width, 3 * lanes), BF16),
            jax.ShapeDtypeStruct((width, lanes), BF16),
            *more_out,
        ),
        in_specs=[sm, sm, sm, vm, hb, vm],
        out_specs=(vm, *[hb] * (6 + len(more_out))),
        scratch_shapes=[
            pltpu.VMEM((width, width), BF16),
            pltpu.VMEM((width, 3 * lanes), BF16),
            pltpu.VMEM((width, lanes), BF16),
            pltpu.VMEM((3, rows // 2, rows // 2), F32),
            pltpu.VMEM((packs, rows, width), BF16),
            pltpu.VMEM((packs - 1, rows, width), BF16),
            pltpu.VMEM((rows, 3 * lanes), BF16),
            pltpu.VMEM((packs, rows, 3 * lanes), BF16),
            pltpu.VMEM((rows, lanes), BF16),
            pltpu.VMEM((packs, rows, lanes), BF16),
            dma((packs, 3)),
            dma((packs, 3)),
            dma((packs, 2)),
            dma((packs, 2)),
            dma((packs, 3)),
            dma((packs, 3)),
            dma(()),
            dma((packs + 3, 3)),
            *more,
            *scatter_scratch(packs, share, width),
        ],
        compiler_params=pltpu.CompilerParams(
            collective_id=2, has_side_effects=True, vmem_limit_bytes=VMEM_LIMIT
        ),
        cost_estimate=pl.CostEstimate(flops=int(14e9), bytes_accessed=4 * 10**7, transcendentals=10**7),
        name="attn",
    )(offsets, slopes, slots, x, weights, ln_params)


def back_call(dr1, w_qkv, w_out, x_all, qkv, ctx, padded, offsets, slopes, seq_count):
    packs, share, width = dr1.shape
    rows = 4 * share
    lanes = 256
    summing = padded is not None
    more_in, more_out, more_scratch = [], [], []
    if summing:
        slab, cols = padded.shape[0] // seq_count, padded.shape[1]
        more_in = [padded.reshape(seq_count, slab, cols)]
        more_out = [jax.ShapeDtypeStruct((slab, cols), BF16)]
        more_scratch = owner_scratch(slab, cols, len(SUM_ORDERS))
    vm = pl.BlockSpec(memory_space=pltpu.VMEM)
    hb = pl.BlockSpec(memory_space=pl.ANY)
    sm = pl.BlockSpec(memory_space=pltpu.SMEM)
    dma = pltpu.SemaphoreType.DMA
    return pl.pallas_call(
        functools.partial(back_kernel, summing),
        out_shape=(
            jax.ShapeDtypeStruct((packs, share, width), F32),
            jax.ShapeDtypeStruct((width, width), BF16),
            *more_out,
        ),
        in_specs=[sm, sm, vm, hb, hb, hb, hb, hb] + [hb] * len(more_in),
        out_specs=(vm, vm, *[vm] * len(more_out)),
        scratch_shapes=[
            pltpu.VMEM((width, 3 * lanes), BF16),
            pltpu.VMEM((width, lanes), BF16),
            pltpu.VMEM((3, rows // 2, rows // 2), F32),
            pltpu.VMEM((packs, rows, width), BF16),
            pltpu.VMEM((packs, rows, width), BF16),
            pltpu.VMEM((packs, rows, 3 * lanes), BF16),
            pltpu.VMEM((packs, rows, lanes), BF16),
            pltpu.VMEM((rows, lanes), BF16),
            pltpu.VMEM((rows, lanes), BF16),
            pltpu.VMEM((rows, 3 * lanes), BF16),
            pltpu.VMEM((rows, 3 * lanes), BF16),
            pltpu.VMEM((rows // 2, lanes), F32),
            pltpu.VMEM((rows // 2, lanes), F32),
            pltpu.VMEM((width, rows), BF16),
            pltpu.VMEM((width, 3 * lanes), F32),
            pltpu.VMEM((width, lanes), F32),
            dma((packs, 3)),
            dma((packs, 3)),
            dma((packs, 2)),
            dma((packs, 2)),
            dma((2,)),
            dma((packs, 3)),
            *scatter_scratch(packs, share, width),
            *more_scratch,
        ],
        compiler_params=pltpu.CompilerParams(
            collective_id=3, has_side_effects=True, vmem_limit_bytes=VMEM_LIMIT
        ),
        cost_estimate=pl.CostEstimate(flops=int(40e9), bytes_accessed=4 * 10**7, transcendentals=10**7),
        name="back",
    )(offsets, slopes, dr1, w_qkv, w_out, x_all, qkv, ctx, *more_in)


def flip_bits(place, *bits):
    for bit in bits:
        place = place + bit - 2 * bit * lax.rem(place // bit, 2)
    return place


GATHER_ORDERS = ((4, 2, 1), (4, 2, 1), (4, 1, 2))
SUM_ORDERS = ((1, 2, 4), (1, 2, 4), (2, 1, 4))


class OwnerGather:
    PEERS = (0, 1, 2, 1, 2, 2, 2)
    SLABS = ((), (), (), (0,), (0,), (1,), (0, 1))

    def __init__(self, held, send, recv, slab):
        self.held, self.send, self.recv, self.slab = held, send, recv, slab
        self.groups = held.shape[0]
        self.seq = lax.axis_index("seq")

    def rows(self, owner):
        return pl.ds(pl.multiple_of(owner * self.slab, self.slab), self.slab)

    def copy(self, group, leg, incoming=False):
        order = GATHER_ORDERS[group]
        bits = [order[place] for place in self.SLABS[leg]]
        if incoming:
            bits.append(order[self.PEERS[leg]])
        block = self.held.at[group, self.rows(flip_bits(self.seq, *bits))]
        peer = flip_bits(self.seq, order[self.PEERS[leg]])
        return remote(block, block, self.send.at[group, leg], self.recv.at[group, leg], peer, "seq")

    def start(self):
        for group in range(self.groups):
            for leg in range(3):
                self.copy(group, leg).start()

    def steps(self):
        found = []
        for first, *rest in ((0, 3, 4), (1, 5), (3, 6)):
            for group in range(self.groups):

                def step(group=group, first=first, rest=rest):
                    self.copy(group, first, True).wait_recv()
                    for leg in rest:
                        self.copy(group, leg).start()

                found.append(step)
        return found

    def finish(self, group):
        for leg in (2, 4, 5, 6):
            self.copy(group, leg, True).wait_recv()

    def drain(self):
        for group in range(self.groups):
            for leg in range(7):
                self.copy(group, leg).wait_send()


def gather_scratch(rows, cols, groups):
    dma = pltpu.SemaphoreType.DMA
    return [pltpu.VMEM((groups, rows, cols // groups), BF16), dma((groups, 7)), dma((groups, 7))]


def order_slabs(slots, slabs, group, target, cols, owners):
    blocks, rows, slab = slots.shape[0], target.shape[0], slabs.shape[1] // owners
    block, step = rows // blocks, 8
    for first in range(0, blocks, step):
        last = first + step - 1
        low = first // CAP
        high = max(o for o in range(owners) if max(o, blocks - CAP * (owners - o)) <= last)
        count = (high - low + 1) * slab
        lines = []
        for place in range(first, first + step):
            down = lax.broadcasted_iota(jnp.int32, (block, count), 0)
            along = lax.broadcasted_iota(jnp.int32, (block, count), 1)
            hit = along - down == slots[place] * block - low * slab
            lines.append(jnp.where(hit, 1.0, 0.0).astype(BF16))
        lines = jnp.concatenate(lines, axis=0)
        for part in range(0, cols.size, 256):
            value = dot_nn(lines, slabs[group, pl.ds(low * slab, count), pl.ds(part, 256)])
            target[pl.ds(first * block, step * block), pl.ds(cols.start + part, 256)] = value.astype(BF16)


class OwnerSum:
    KEPT = ((1, 2), (1,), (2,), ())

    def __init__(self, source, own, first, second, third, load, send, recv):
        self.source, self.own, self.first, self.second, self.third = source, own, first, second, third
        self.load, self.send, self.recv = load, send, recv
        self.groups, self.slab, self.size = own.shape[0], own.shape[2], own.shape[3]
        self.seq = lax.axis_index("seq")

    def block(self, group, step, *more):
        order = SUM_ORDERS[group]
        owner = flip_bits(self.seq, *[order[place] for place in self.KEPT[step]], *more)
        return self.source.at[owner, :, pl.ds(group * self.size, self.size)]

    def fetch(self, group, step):
        return pltpu.make_async_copy(
            self.block(group, step), self.own.at[group, step], self.load.at[group, step]
        )

    def copy(self, group, leg):
        order = SUM_ORDERS[group]
        if leg < 4:
            source, target, bit = self.block(group, leg, order[0]), self.first.at[group, leg], order[0]
        elif leg < 6:
            source, target, bit = self.own.at[group, leg - 4], self.second.at[group, leg - 4], order[1]
        else:
            source, target, bit = self.own.at[group, 2], self.third.at[group], order[2]
        return remote(
            source, target, self.send.at[group, leg], self.recv.at[group, leg], flip_bits(self.seq, bit), "seq"
        )

    def start(self, *groups):
        for group in groups:
            for step in range(4):
                self.copy(group, step).start()
                self.fetch(group, step).start()

    def into(self, group, step, *others):
        def part(row):
            rws = tile(row, 32)
            value = self.own[group, step, rws, :].astype(F32)
            for other in others:
                value = value + other[rws, :].astype(F32)
            self.own[group, step, rws, :] = value.astype(BF16)

        loop(self.slab // 32, part)

    def add(self, group, step):
        self.fetch(group, step).wait()
        self.copy(group, step).wait_recv()
        if step < 2:
            self.into(group, step, self.first.at[group, step])
            self.copy(group, 4 + step).start()
        if group == 2 and step == 1:
            self.start(1)

    def pair(self, group):
        self.copy(group, 4).wait_recv()
        self.into(group, 2, self.first.at[group, 2], self.second.at[group, 0])
        self.copy(group, 6).start()

    def finish(self, group, target):
        self.copy(group, 5).wait_recv()
        self.copy(group, 6).wait_recv()

        def part(row):
            rws = tile(row, 32)
            value = self.own[group, 3, rws, :].astype(F32)
            for other in (self.first.at[group, 3], self.second.at[group, 1], self.third.at[group]):
                value = value + other[rws, :].astype(F32)
            target(rws, pl.ds(group * self.size, self.size), value)

        loop(self.slab // 32, part)

    def steps(self, target):
        add, pair, finish = self.add, self.pair, self.finish
        found = [functools.partial(add, group, step) for step in range(4) for group in (0, 2)]
        found += [functools.partial(pair, 0), functools.partial(pair, 2)]
        found += [functools.partial(add, 1, 0), functools.partial(add, 1, 1)]
        found += [functools.partial(finish, 0, target), functools.partial(finish, 2, target)]
        found += [functools.partial(add, 1, 2), functools.partial(pair, 1), functools.partial(add, 1, 3)]
        found.append(functools.partial(finish, 1, target))
        return found

    def drain(self):
        for group in range(self.groups):
            for leg in range(7):
                self.copy(group, leg).wait_send()


def owner_scratch(slab, width, groups):
    dma = pltpu.SemaphoreType.DMA
    size = width // groups
    return [
        pltpu.VMEM((groups, 4, slab, size), BF16),
        pltpu.VMEM((groups, 4, slab, size), BF16),
        pltpu.VMEM((groups, 2, slab, size), BF16),
        pltpu.VMEM((groups, slab, size), BF16),
        dma((groups, 4)),
        dma((groups, 7)),
        dma((groups, 7)),
    ]


class Total:
    def __init__(self, axis, slots, send, recv):
        self.axis, self.slots, self.send, self.recv = axis, slots, send, recv
        self.count = slots.shape[0]
        self.place = lax.axis_index(axis)

    def copy(self, step):
        mine = self.slots.at[self.place]
        return remote(
            mine, mine, self.send.at[step - 1], self.recv.at[self.place], self.peer(step), self.axis
        )

    def peer(self, step):
        return lax.rem(self.place + step, self.count)

    def start(self, value):
        self.slots[self.place] = value
        for step in range(1, self.count):
            self.copy(step).start()

    def finish(self):
        for step in range(1, self.count):
            other = self.peer(step)
            slot = self.slots.at[other]
            remote(
                slot, slot, self.send.at[step - 1], self.recv.at[other], other, self.axis
            ).wait_recv()
        value = self.slots[0]
        for place in range(1, self.count):
            value = value + self.slots[place]
        return value

    def drain(self):
        for step in range(1, self.count):
            self.copy(step).wait_send()


def total_scratch(count, shape):
    dma = pltpu.SemaphoreType.DMA
    return [pltpu.VMEM((count, *shape), F32), dma((count - 1,)), dma((count,))]


def greet_all(axes):
    barrier = pltpu.get_barrier_semaphore()
    sent = 0
    for axis, count in axes:
        place = lax.axis_index(axis)
        for step in range(1, count):
            peer = lax.rem(place + step, count)
            pl.semaphore_signal(barrier, inc=1, device_id={axis: peer}, device_id_type=MESH)
            sent += 1
    pl.semaphore_wait(barrier, sent)


def close_kernel(
    seq_count,
    wide_count,
    kept_ref,
    grads_ref,
    ffn_ref,
    ln_ref,
    owned_ref,
    ln_out_ref,
    square_ref,
    *scratch,
):
    greet_all((("seq", seq_count), ("wide", wide_count)))
    sums, scratch = scratch[:7], scratch[7:]
    owners = OwnerSum(grads_ref, *sums)
    norms = [Total("wide", *scratch[0:3]), Total("seq", *scratch[3:6])]
    squares = [Total("wide", *scratch[6:9]), Total("seq", *scratch[9:12])]
    acc = scratch[12]
    slab = owned_ref.shape[0]
    width = grads_ref.shape[2]
    owners.start(0, 2)
    norms[0].start(ln_ref[...])
    acc[...] = jnp.zeros_like(acc)

    def keep(rws, value):
        row = lax.broadcasted_iota(jnp.int32, value.shape, 0) + rws.start
        return jnp.where(row < kept_ref[0], value, 0.0)

    def note(value):
        square = value * value
        rows = sum(square[row : row + 8] for row in range(0, value.shape[0], 8))
        acc[...] += sum(rows[:, place : place + 128] for place in range(0, value.shape[1], 128))

    def put(rws, cols, value):
        value = keep(rws, value)
        owned_ref[rws, cols] = value
        note(value)

    def from_ffn(index):
        rws = tile(index, 16)
        value = keep(rws, ffn_ref[rws, :].astype(F32))
        owned_ref[rws, pl.ds(width, ffn_ref.shape[1])] = value
        note(value)

    steps = owners.steps(put)
    for step in steps[:10]:
        step()
    norms[1].start(norms[0].finish())
    for step in steps[10:14]:
        step()
    loop(slab // 16, from_ffn)
    for step in steps[14:]:
        step()
    squares[0].start(acc[...])
    squares[1].start(squares[0].finish())
    ln_out_ref[...] = norms[1].finish()
    square_ref[...] = squares[1].finish()
    owners.drain()
    for part in (*norms, *squares):
        part.drain()


def close_call(kept, grads, ffn_owned, ln_rows, seq_count, wide_count):
    slab = ffn_owned.shape[0]
    width = grads.shape[1]
    vm = pl.BlockSpec(memory_space=pltpu.VMEM)
    sm = pl.BlockSpec(memory_space=pltpu.SMEM)
    return pl.pallas_call(
        functools.partial(close_kernel, seq_count, wide_count),
        out_shape=(
            jax.ShapeDtypeStruct((slab, width + ffn_owned.shape[1]), F32),
            jax.ShapeDtypeStruct(ln_rows.shape, F32),
            jax.ShapeDtypeStruct((8, 128), F32),
        ),
        in_specs=[sm, pl.BlockSpec(memory_space=pl.ANY), vm, vm],
        out_specs=(vm, vm, vm),
        scratch_shapes=[
            *owner_scratch(slab, width, len(SUM_ORDERS)),
            *total_scratch(wide_count, ln_rows.shape),
            *total_scratch(seq_count, ln_rows.shape),
            *total_scratch(wide_count, (8, 128)),
            *total_scratch(seq_count, (8, 128)),
            pltpu.VMEM((8, 128), F32),
        ],
        compiler_params=pltpu.CompilerParams(
            collective_id=4, has_side_effects=True, vmem_limit_bytes=VMEM_LIMIT
        ),
        name="close",
    )(kept, grads.reshape(seq_count, slab, width), ffn_owned, ln_rows)


def adam_kernel(
    own_ref,
    owned_ref,
    master_ref,
    first_ref,
    second_ref,
    parts_ref,
    total_ref,
    params_ref,
    ln_first_ref,
    ln_second_ref,
    new_master_ref,
    new_first_ref,
    new_second_ref,
    norms_ref,
    norms_first_ref,
    norms_second_ref,
    norm_ref,
):
    rows = params_ref.shape[0]
    total = total_ref[0:rows, :]
    squares = jnp.sum(parts_ref[...], axis=(0, 1), keepdims=True)
    norm = jnp.sqrt(squares + jnp.sum(total * total, axis=(0, 1), keepdims=True))
    clip = jnp.minimum(1.0, 1.0 / (norm + 1e-06))
    norm_ref[...] = norm
    step = pl.program_id(0)
    size = owned_ref.shape[0]

    @pl.when(step == 0)
    def _():
        new = adamw(
            params_ref[...], total * clip, ln_first_ref[...], ln_second_ref[...], 0.0, NORM_RATE
        )
        for target, value in zip((norms_ref, norms_first_ref, norms_second_ref), new):
            target[...] = value

    def part(index):
        rws = tile(index, 8)
        new = adamw(
            master_ref[rws, :], owned_ref[rws, :] * clip, first_ref[rws, :], second_ref[rws, :], DECAY, RATE
        )
        row = lax.broadcasted_iota(jnp.int32, (8, owned_ref.shape[1]), 0) + step * size + index * 8
        for target, value in zip((new_master_ref, new_first_ref, new_second_ref), new):
            target[rws, :] = jnp.where(row < own_ref[0], value, 0.0)

    loop(size // 8, part)


def adam_call(own_rows, owned, master, first, second, parts, total, params, ln_first, ln_second):
    slab, cols = master.shape
    size = slab // 6
    big = pl.BlockSpec((size, cols), lambda step: (step, 0))
    small = lambda array: pl.BlockSpec(array.shape, lambda step: (0, 0))
    like = lambda array: jax.ShapeDtypeStruct(array.shape, F32)
    return pl.pallas_call(
        adam_kernel,
        grid=(6,),
        out_shape=(
            like(master),
            like(master),
            like(master),
            like(params),
            like(params),
            like(params),
            jax.ShapeDtypeStruct((1, 1), F32),
        ),
        in_specs=[
            pl.BlockSpec(memory_space=pltpu.SMEM),
            big,
            big,
            big,
            big,
            small(parts),
            small(total),
            small(params),
            small(params),
            small(params),
        ],
        out_specs=(
            big,
            big,
            big,
            small(params),
            small(params),
            small(params),
            pl.BlockSpec((1, 1), lambda step: (0, 0)),
        ),
        compiler_params=pltpu.CompilerParams(vmem_limit_bytes=VMEM_LIMIT),
        name="adam",
    )(own_rows, owned, master, first, second, parts, total, params, ln_first, ln_second)


def pick_kernel(block, places_ref, source_ref, target_ref, held, sems, sem):
    count = places_ref.shape[1]

    def copy(index):
        return pltpu.make_async_copy(
            source_ref.at[pl.ds(pl.multiple_of(places_ref[0, index] * block, block), block)],
            held.at[pl.ds(pl.multiple_of(index * block, block), block)],
            sems.at[index],
        )

    loop(count, lambda index: copy(index).start())
    loop(count, lambda index: copy(index).wait())
    out = pltpu.make_async_copy(held, target_ref, sem)
    out.start()
    out.wait()


def spread_kernel(block, places_ref, source_ref, target_ref, held, sems, sem):
    count = places_ref.shape[1]
    load = pltpu.make_async_copy(source_ref, held, sem)
    load.start()
    load.wait()

    def copy(index):
        return pltpu.make_async_copy(
            held.at[pl.ds(pl.multiple_of(index * block, block), block)],
            target_ref.at[pl.ds(pl.multiple_of(places_ref[1, index] * block, block), block)],
            sems.at[index],
        )

    loop(count, lambda index: copy(index).start())
    loop(count, lambda index: copy(index).wait())


def move_blocks(kernel, source, places, rows, block):
    hb = pl.BlockSpec(memory_space=pl.ANY)
    count = places.shape[1]
    return pl.pallas_call(
        functools.partial(kernel, block),
        out_shape=jax.ShapeDtypeStruct((rows, source.shape[1]), source.dtype),
        in_specs=[pl.BlockSpec(memory_space=pltpu.SMEM), hb],
        out_specs=hb,
        scratch_shapes=[
            pltpu.VMEM((count * block, source.shape[1]), source.dtype),
            pltpu.SemaphoreType.DMA((count,)),
            pltpu.SemaphoreType.DMA(()),
        ],
        compiler_params=pltpu.CompilerParams(vmem_limit_bytes=VMEM_LIMIT),
        name="move",
    )(places, source)


def per_device(
    hidden_in,
    cotangent,
    seq_offsets,
    owner_blocks,
    master,
    first_moment,
    second_moment,
    ln_params,
    ln_first,
    ln_second,
):
    width = hidden_in.shape[2]
    slab_rows = master.shape[0]
    block = slab_rows // CAP
    source, valid, target = owner_maps(owner_blocks, width, CAP, block)
    gathered_rows = slab_rows * lax.axis_size("seq")
    count = width // block
    fits = block % 16 == 0
    slots = target[::block] // block
    both = jnp.stack([slots, slots])

    def to_order(array):
        if fits:
            return move_blocks(pick_kernel, array, both, width, block)
        return jnp.take(array, target, axis=0)

    def to_owner(grads):
        if fits:
            return move_blocks(spread_kernel, grads, both, gathered_rows, block)
        return jnp.take(grads, source, axis=0)

    seq_count = lax.axis_size("seq")
    own_kernels = fits and seq_count == 8
    if own_kernels:
        weights = master
    else:
        low = master.astype(jnp.bfloat16)
        weights, w_ffn = (
            to_order(lax.all_gather(part, "seq", axis=0, tiled=True)) for part in (low[:, :width], low[:, width:])
        )
    slopes = jnp.exp2(-8.0 * (jnp.arange(H, dtype=jnp.float32) + 1.0) / H)
    x = jnp.transpose(hidden_in, (1, 0, 2))
    r1, normed, x_all, qkv, ctx, w_qkv, w_out, *more = attn_call(
        x, weights, ln_params, slots, seq_offsets, slopes, seq_count if own_kernels else 0
    )
    w_ffn = more[0] if own_kernels else w_ffn
    mixed_p, dr1_p, ffn_grads, ln_rows = ffn_call(
        r1, jnp.transpose(cotangent, (1, 0, 2)), normed, w_ffn, ln_params
    )
    mixed = jnp.transpose(mixed_p, (1, 0, 2))

    ffn_padded = to_owner(ffn_grads)
    grad_p, attn_grads, *more = back_call(
        dr1_p, w_qkv, w_out, x_all, qkv, ctx, ffn_padded if own_kernels else None, seq_offsets, slopes, seq_count
    )
    input_grad = jnp.transpose(grad_p, (1, 0, 2))
    attn_padded = to_owner(attn_grads)
    mine = jnp.arange(seq_count, dtype=jnp.int32) == lax.axis_index("seq")
    own_rows = jnp.sum(jnp.where(mine, owner_blocks, 0)) * block
    kept = (jnp.arange(slab_rows, dtype=jnp.int32) < own_rows)[:, None]
    if own_kernels:
        owned, ln_total, parts = close_call(
            own_rows[None], attn_padded, more[0], ln_rows, seq_count, lax.axis_size("wide")
        )
        *updated, grad_norm = adam_call(
            own_rows[None],
            owned,
            master,
            first_moment,
            second_moment,
            parts,
            ln_total,
            ln_params,
            ln_first,
            ln_second,
        )
        return (mixed, input_grad, *updated, grad_norm[0, 0])
    ffn_owned = lax.psum_scatter(ffn_padded, "seq", scatter_dimension=0, tiled=True)
    attn_owned = lax.psum_scatter(attn_padded, "seq", scatter_dimension=0, tiled=True)
    owned = jnp.concatenate([attn_owned, ffn_owned], axis=1).astype(jnp.float32)
    owned = jnp.where(kept, owned, 0.0)
    squares, ln_total = lax.psum((jnp.sum(owned * owned), ln_rows[:4]), ("seq", "wide"))
    grad_norm = jnp.sqrt(squares + jnp.sum(ln_total * ln_total))
    clip = jnp.minimum(1.0, 1.0 / (grad_norm + 1e-06))
    param_new, first_new, second_new = adamw(
        master, owned * clip, first_moment, second_moment, DECAY, RATE
    )
    norms_new, norms_first, norms_second = adamw(
        ln_params, ln_total * clip, ln_first, ln_second, 0.0, NORM_RATE
    )
    return (
        mixed,
        input_grad,
        jnp.where(kept, param_new, 0.0),
        jnp.where(kept, first_new, 0.0),
        jnp.where(kept, second_new, 0.0),
        norms_new,
        norms_first,
        norms_second,
        grad_norm,
    )


def solution(mesh):
    return jax.shard_map(
        per_device,
        mesh=mesh,
        in_specs=(
            P("wide", "seq", None),
            P("wide", "seq", None),
            P("seq", None),
            P(),
            P("seq", "wide"),
            P("seq", "wide"),
            P("seq", "wide"),
            P(),
            P(),
            P(),
        ),
        out_specs=(
            P("wide", "seq", None),
            P("wide", "seq", None),
            P("seq", "wide"),
            P("seq", "wide"),
            P("seq", "wide"),
            P(),
            P(),
            P(),
            P(),
        ),
        check_vma=False,
    )
```

```python
import functools

import jax
import jax.numpy as jnp
from jax import lax
from jax.experimental import pallas as pl
from jax.experimental.pallas import tpu as pltpu
from jax.sharding import PartitionSpec as P

MESH = pl.DeviceIdType.MESH

H = 12
HD = 64
FF = 3072
UNIT = 128
CAP = 6
STEP = 10


RATE = 0.02
NORM_RATE = 0.6
BETA_ONE = 0.9
BETA_TWO = 0.999
EPSILON = 1e-08
DECAY = 0.01
NORM_EPS = 1e-05
ROOT_HALF = 0.7071067811865476
DENSITY_SCALE = 0.3989422804014327
EPS = 1e-05
F32 = jnp.float32
BF16 = jnp.bfloat16
NEG = -1e30
PAIRS = 4
SINGLES = 2
ROWS = 16
VMEM_LIMIT = 60 * 2**20


def owner_maps(owner_blocks, rows, cap, block):
    ends = jnp.cumsum(owner_blocks)
    starts = ends - owner_blocks
    slot = jnp.arange(cap * block, dtype=jnp.int32)
    which = slot // block
    source = (starts[:, None] + which[None, :]) * block + (slot % block)[None, :]
    valid = which[None, :] < owner_blocks[:, None]
    source = jnp.where(valid, source, 0).reshape(-1)
    valid = valid.reshape(-1)
    param = jnp.arange(rows, dtype=jnp.int32)
    blocks = param // block
    owner = jnp.sum((ends[None, :] <= blocks[:, None]).astype(jnp.int32), axis=1)
    onehot = owner[:, None] == jnp.arange(owner_blocks.shape[0], dtype=jnp.int32)[None, :]
    first = jnp.sum(jnp.where(onehot, starts[None, :], 0), axis=1)
    target = owner * (cap * block) + (blocks - first) * block + param % block
    return (source, valid, target)


def adamw(param, grad, first, second, decay, rate):
    first_new = BETA_ONE * first + (1.0 - BETA_ONE) * grad
    second_new = BETA_TWO * second + (1.0 - BETA_TWO) * grad * grad
    first_hat = first_new / (1.0 - BETA_ONE**STEP)
    second_hat = second_new / (1.0 - BETA_TWO**STEP)
    param_new = param - rate * (first_hat / (jnp.sqrt(second_hat) + EPSILON) + decay * param)
    return (param_new, first_new, second_new)


def dot_nn(a, b):
    return lax.dot_general(a, b, (((1,), (0,)), ((), ())), preferred_element_type=F32)


def dot_nt(a, b):
    return lax.dot_general(a, b, (((1,), (1,)), ((), ())), preferred_element_type=F32)


def dot_tn(a, b):
    return lax.dot_general(a, b, (((0,), (0,)), ((), ())), preferred_element_type=F32)


def places():
    wide = lax.axis_index("wide")
    core = lax.rem(wide, 2)
    row = wide // 2
    return wide, core, row, wide + 1 - 2 * core, wide + 2 - 4 * row


def greet(mate, across):
    barrier = pltpu.get_barrier_semaphore()
    for peer in (mate, across):
        pl.semaphore_signal(barrier, inc=1, device_id={"wide": peer}, device_id_type=MESH)
    pl.semaphore_wait(barrier, 2)


def remote(source, target, send, recv, peer, axis="wide"):
    return pltpu.make_async_remote_copy(
        src_ref=source,
        dst_ref=target,
        send_sem=send,
        recv_sem=recv,
        device_id={axis: peer},
        device_id_type=MESH,
    )


class Gather:
    def __init__(self, held, send, recv, share):
        self.held, self.send, self.recv, self.share = held, send, recv, share
        _, self.core, self.row, self.mate, self.across = places()

    def rows(self, core, row):
        return pl.ds(pl.multiple_of((core * 2 + row) * self.share, self.share), self.share)

    def copy(self, pack, leg):
        row = 1 - self.row if leg == 2 else self.row
        block = self.held.at[pack, self.rows(self.core, row)]
        peer = self.mate if leg else self.across
        return remote(block, block, self.send.at[pack, leg], self.recv.at[pack, leg], peer)

    def start(self, pack):
        self.copy(pack, 0).start()
        self.copy(pack, 1).start()

    def finish(self, pack):
        self.copy(pack, 0).wait_recv()
        self.copy(pack, 2).start()
        self.copy(pack, 1).wait_recv()
        self.copy(pack, 2).wait_recv()

    def drain(self, pack):
        for leg in range(3):
            self.copy(pack, leg).wait_send()


class Scatter:
    def __init__(self, part, give, take, cross, reach, own, send, recv, share):
        self.part, self.give, self.take = part, give, take
        self.cross, self.reach, self.own = cross, reach, own
        self.send, self.recv, self.share = send, recv, share
        _, self.core, self.row, self.mate, self.across = places()

    def copy(self, pack, leg):
        source, target = (self.cross, self.reach) if leg else (self.give, self.take)
        peer = self.across if leg else self.mate
        return remote(
            source.at[pack], target.at[pack], self.send.at[pack, leg], self.recv.at[pack, leg], peer
        )

    def half(self, which):
        core = self.core if which else 1 - self.core
        return pl.multiple_of(core * 2 * self.share, 2 * self.share)

    def start(self, pack):
        self.copy(pack, 0).start()

    def middle(self, pack):
        self.copy(pack, 0).wait_recv()
        share = self.share
        far = pl.ds(pl.multiple_of((1 - self.row) * share, share), share)
        near = pl.ds(pl.multiple_of(self.row * share, share), share)
        self.cross[pack] = (self.part[far, :] + self.take[pack, far, :].astype(F32)).astype(BF16)
        self.copy(pack, 1).start()
        self.own[pack] = self.part[near, :] + self.take[pack, near, :].astype(F32)

    def finish(self, pack):
        self.copy(pack, 1).wait_recv()

    def drain(self, pack):
        for leg in range(2):
            self.copy(pack, leg).wait_send()


def scatter_scratch(packs, share, width):
    return [
        pltpu.VMEM((2 * share, width), F32),
        pltpu.VMEM((packs, 2 * share, width), BF16),
        pltpu.VMEM((packs, 2 * share, width), BF16),
        pltpu.VMEM((packs, share, width), BF16),
        pltpu.VMEM((packs, share, width), BF16),
        pltpu.VMEM((packs, share, width), F32),
    ]


def norm_parts(values):
    center = values - jnp.mean(values, axis=-1, keepdims=True)
    inverse = lax.rsqrt(jnp.mean(center * center, axis=-1, keepdims=True) + EPS)
    return center * inverse, inverse


def norm_pull(grad, normal, inverse, gain):
    scaled = grad * gain
    return inverse * (
        scaled
        - jnp.mean(scaled, axis=-1, keepdims=True)
        - normal * jnp.mean(scaled * normal, axis=-1, keepdims=True)
    )


def loop(count, body, unroll=1):
    def step(index, carry):
        body(index)
        return carry

    lax.fori_loop(0, count, step, 0, unroll=unroll)


def tile(index, size):
    return pl.ds(pl.multiple_of(index * size, size), size)


def ffn_kernel(
    r1_ref,
    cot_ref,
    held_ref,
    w_ref,
    ln_ref,
    mixed_ref,
    dr1_ref,
    grads_ref,
    lngrad_ref,
    weights,
    held,
    held2,
    gates,
    ups,
    hid,
    dgate,
    dup,
    turned,
    turned2,
    total,
    g_tile,
    u_tile,
    send_a,
    recv_a,
    send_b,
    recv_b,
    send_c,
    recv_c,
    send_d,
    recv_d,
    load_sem,
    store_sem,
    *buffers,
):
    packs, share, width = r1_ref.shape
    rows = 4 * share
    fwd = buffers[:6]
    units = weights.shape[1] // 3
    col = 256
    n_width = width // col
    loads = [pltpu.make_async_copy(w_ref, weights, load_sem.at[packs - 1])]
    for pack in range(packs - 1):
        loads.append(pltpu.make_async_copy(held_ref.at[pack], held.at[pack], load_sem.at[pack]))
    for load in loads:
        load.start()
    _, core, row, mate, across = places()
    greet(mate, across)
    gather_one = Gather(held, send_a, recv_a, share)
    scatter_one = Scatter(*fwd, send_b, recv_b, share)
    gather_two = Gather(held2, send_c, recv_c, share)
    scatter_two = Scatter(*fwd, send_d, recv_d, share)
    gain1, shift1 = ln_ref[0:1, :], ln_ref[1:2, :]
    gain2, shift2 = ln_ref[2:3, :], ln_ref[3:4, :]
    lngrad_ref[...] = jnp.zeros_like(lngrad_ref)
    chunk = 32

    base = pl.multiple_of((core * 2 + row) * share, share)

    def first(index):
        normal, _ = norm_parts(r1_ref[packs - 1, tile(index, chunk), :])
        held[packs - 1, pl.ds(pl.multiple_of(base + index * chunk, chunk), chunk), :] = (
            normal * gain1 + shift1
        ).astype(BF16)

    loop(share // chunk, first, unroll=4)
    gather_one.start(packs - 1)
    loads[0].wait()

    def widen(pack):
        def ff(index):
            first = pl.multiple_of(index * share, share)
            x = held[pack, pl.ds(first, share), :]
            g_tile[...] = dot_nn(x, weights[:, pl.ds(0, units)])
            u_tile[...] = dot_nn(x, weights[:, pl.ds(units, units)])

            def act(part):
                rws = tile(part, ROWS)
                gate, up = g_tile[rws, :], u_tile[rws, :]
                out = pl.ds(pl.multiple_of(first + part * ROWS, ROWS), ROWS)
                cumulative = 0.5 * (1.0 + lax.erf(gate * ROOT_HALF))
                hid[out, :] = (gate * cumulative * up).astype(BF16)
                gates[pack, out, :] = gate.astype(BF16)
                ups[pack, out, :] = up.astype(BF16)

            loop(share // ROWS, act, unroll=2)

        loop(4, ff)

    def narrow(pack):
        for which in range(2):
            base = scatter_one.half(which)

            def down(index, base=base, which=which):
                rws = pl.ds(pl.multiple_of(base + index * share, share), share)
                value = dot_nt(hid[rws, :], weights[:, pl.ds(2 * units, units)])
                if which:
                    scatter_one.part[tile(index, share), :] = value
                else:
                    scatter_one.give[pack, tile(index, share), :] = value.astype(BF16)

            loop(2, down)
            if not which:
                scatter_one.start(pack)
        scatter_one.middle(pack)

    def turn(pack):
        scatter_one.finish(pack)
        gather_two_base = pl.multiple_of((core * 2 + row) * share, share)

        def second(index):
            rws = tile(index, chunk)
            normal, _ = norm_parts(r1_ref[pack, rws, :])
            ffn = scatter_one.own[pack, rws, :] + scatter_one.reach[pack, rws, :].astype(F32)
            normal2, inverse2 = norm_parts(normal * gain1 + shift1 + ffn)
            mixed_ref[pack, rws, :] = (normal2 * gain2 + shift2).astype(BF16)
            grad = cot_ref[pack, rws, :].astype(F32)
            value = norm_pull(grad, normal2, inverse2, gain2)
            dr1_ref[pack, rws, :] = value
            held2[pack, pl.ds(pl.multiple_of(gather_two_base + index * chunk, chunk), chunk), :] = value.astype(BF16)
            lngrad_ref[2:3, :] += jnp.sum(grad * normal2, axis=0, keepdims=True)
            lngrad_ref[3:4, :] += jnp.sum(grad, axis=0, keepdims=True)

        loop(share // chunk, second, unroll=4)
        scatter_one.drain(pack)
        gather_two.start(pack)

    def backward(pack):
        gather_two.finish(pack)
        for which in range(2):
            base = scatter_two.half(which)

            def bf(index, base=base):
                first = pl.multiple_of(base + index * share, share)
                g_tile[...] = dot_nn(held2[pack, pl.ds(first, share), :], weights[:, pl.ds(2 * units, units)])

                def act(part):
                    rws = tile(part, ROWS)
                    out = pl.ds(pl.multiple_of(first + part * ROWS, ROWS), ROWS)
                    dhid = g_tile[rws, :]
                    gate = gates[pack, out, :].astype(F32)
                    up = ups[pack, out, :].astype(F32)
                    cumulative = 0.5 * (1.0 + lax.erf(gate * ROOT_HALF))
                    density = jnp.exp(-0.5 * gate * gate) * DENSITY_SCALE
                    value = gate * cumulative
                    hid[out, :] = (value * up).astype(BF16)
                    dgate[out, :] = (dhid * up * (cumulative + gate * density)).astype(BF16)
                    dup[out, :] = (dhid * value).astype(BF16)

                loop(share // ROWS, act, unroll=2)

            loop(2, bf)

            def back(index, base=base, which=which):
                rws = pl.ds(pl.multiple_of(base + index * share, share), share)
                value = dot_nt(dgate[rws, :], weights[:, pl.ds(0, units)]) + dot_nt(
                    dup[rws, :], weights[:, pl.ds(units, units)]
                )
                if which:
                    scatter_two.part[tile(index, share), :] = value
                else:
                    scatter_two.give[pack, tile(index, share), :] = value.astype(BF16)

            loop(2, back)
            if not which:
                scatter_two.start(pack)
        scatter_two.middle(pack)

    def weight_grads(pack):
        def flip(index):
            rws = tile(index, 256)
            turned[:, rws] = held[pack, rws, :].T
            turned2[:, rws] = held2[pack, rws, :].T

        loop(rows // 256, flip)

        def add(index):
            rws = tile(index, col)
            a = turned[rws, :]
            b = turned2[rws, :]
            parts = (dot_nn(a, dgate[...]), dot_nn(a, dup[...]), dot_nn(b, hid[...]))
            for place, value in enumerate(parts):
                cols = pl.ds(place * units, units)
                if pack == 0:
                    total[rws, cols] = value
                else:
                    value = total[rws, cols] + value
                    if pack < packs - 1:
                        total[rws, cols] = value
                    else:
                        gates[place, rws, :] = value.astype(BF16)

        loop(n_width, add)

    def last(pack):
        scatter_two.finish(pack)

        def third(index):
            rws = tile(index, chunk)
            normal, inverse = norm_parts(r1_ref[pack, rws, :])
            grad = dr1_ref[pack, rws, :] + (
                scatter_two.own[pack, rws, :] + scatter_two.reach[pack, rws, :].astype(F32)
            )
            dr1_ref[pack, rws, :] = norm_pull(grad, normal, inverse, gain1)
            lngrad_ref[0:1, :] += jnp.sum(grad * normal, axis=0, keepdims=True)
            lngrad_ref[1:2, :] += jnp.sum(grad, axis=0, keepdims=True)

        loop(share // chunk, third, unroll=4)

    for pack in range(packs):
        if pack < packs - 1:
            loads[pack + 1].wait()
        else:
            gather_one.finish(pack)
        widen(pack)
        narrow(pack)
        if pack:
            turn(pack - 1)
    for pack in range(packs):
        backward(pack)
        weight_grads(pack)
        if pack == 0:
            turn(packs - 1)
        else:
            last(pack - 1)
    outs = [
        pltpu.make_async_copy(
            gates.at[place, pl.ds(0, width)],
            grads_ref.at[:, pl.ds(place * units, units)],
            store_sem.at[place],
        )
        for place in range(3)
    ]
    for out in outs:
        out.start()
    last(packs - 1)
    for out in outs:
        out.wait()
    gather_one.drain(packs - 1)
    for pack in range(packs):
        gather_two.drain(pack)
        scatter_two.drain(pack)


def ffn_call(r1, cot, held, weights, ln_params):
    packs, share, width = r1.shape
    rows = 4 * share
    units = weights.shape[1] // 3
    vm = pl.BlockSpec(memory_space=pltpu.VMEM)
    hb = pl.BlockSpec(memory_space=pl.ANY)
    dma = pltpu.SemaphoreType.DMA
    return pl.pallas_call(
        ffn_kernel,
        out_shape=(
            jax.ShapeDtypeStruct((packs, share, width), BF16),
            jax.ShapeDtypeStruct((packs, share, width), F32),
            jax.ShapeDtypeStruct((width, 3 * units), BF16),
            jax.ShapeDtypeStruct((8, width), F32),
        ),
        in_specs=[vm, vm, hb, hb, vm],
        out_specs=(vm, vm, hb, vm),
        scratch_shapes=[
            pltpu.VMEM((width, 3 * units), BF16),
            pltpu.VMEM((packs, rows, width), BF16),
            pltpu.VMEM((packs, rows, width), BF16),
            pltpu.VMEM((packs, rows, units), BF16),
            pltpu.VMEM((packs, rows, units), BF16),
            pltpu.VMEM((rows, units), BF16),
            pltpu.VMEM((rows, units), BF16),
            pltpu.VMEM((rows, units), BF16),
            pltpu.VMEM((width, rows), BF16),
            pltpu.VMEM((width, rows), BF16),
            pltpu.VMEM((width, 3 * units), F32),
            pltpu.VMEM((share, units), F32),
            pltpu.VMEM((share, units), F32),
            dma((packs, 3)),
            dma((packs, 3)),
            dma((packs, 2)),
            dma((packs, 2)),
            dma((packs, 3)),
            dma((packs, 3)),
            dma((packs, 2)),
            dma((packs, 2)),
            dma((packs,)),
            dma((3,)),
            *scatter_scratch(packs, share, width),
        ],
        compiler_params=pltpu.CompilerParams(
            collective_id=1, has_side_effects=True, vmem_limit_bytes=VMEM_LIMIT
        ),
        cost_estimate=pl.CostEstimate(flops=int(70e9), bytes_accessed=4 * 10**7, transcendentals=10**7),
        name="ffn",
    )(r1, cot, held, weights, ln_params)


class Runs:
    def __init__(self, offsets, pack):
        names = [offsets[pack, place] for place in range(8)]
        start = jnp.int32(4)
        for place in range(3, -1, -1):
            start = lax.select(names[place] == names[place + 3], jnp.int32(place), start)
        self.start = start
        self.names = [lax.select(start > place, names[place], names[place + 4]) for place in range(4)]

    def masks(self, index):
        own = self.names[0]
        for place in range(1, 4):
            own = lax.select(index == place, self.names[place], own)
        return [lax.select(own == name, jnp.float32(0.0), jnp.float32(NEG)) for name in self.names]

    def arrange(self, plain, order):
        for place in range(4):
            value = plain[held_run(place), :]
            for start in range(1, 5):
                value = lax.select(self.start == start, plain[held_run(place + start), :], value)
            order(pl.ds(place * UNIT, UNIT), value)
            value = lax.select(self.start > place, plain[held_run(place), :], plain[held_run(place + 4), :])
            order(pl.ds((place + 4) * UNIT, UNIT), value)

    def restore(self, order, plain):
        for run in range(8):
            first = max(0, run - 3)
            value = order[pl.ds((run - first) * UNIT, UNIT), :]
            for start in range(first + 1, min(run, 4) + 1):
                value = lax.select(self.start == start, order[pl.ds((run - start) * UNIT, UNIT), :], value)
            if run < 4:
                value = lax.select(self.start > run, order[pl.ds((run + 4) * UNIT, UNIT), :], value)
            else:
                value = lax.select(self.start <= run - 4, order[pl.ds(run * UNIT, UNIT), :], value)
            plain(held_run(run), value)


def held_run(run):
    half, part = divmod(run, 2)
    return pl.ds(((half % 2) * 2 + half // 2) * 2 * UNIT + part * UNIT, UNIT)


def writer(ref, *at):
    def write(rows, value):
        ref[(*at, rows, slice(None))] = value

    return write


def fill_bias(bias, slopes, wide):
    heads, size, _ = bias.shape

    def fill(index):
        rws = tile(index, UNIT)
        down = lax.broadcasted_iota(jnp.int32, (UNIT, size), 0) + index * UNIT
        along = lax.broadcasted_iota(jnp.int32, (UNIT, size), 1)
        distance = jnp.abs(down - along).astype(F32)
        for head in range(heads):
            bias[head, rws, :] = -slopes[wide * heads + head] * distance

    loop(size // UNIT, fill)


def split_weights(packed, w_qkv, w_out):
    width, each = packed.shape[0], packed.shape[1] // 4
    wide = w_out.shape[1]

    def part(index):
        rws = tile(index, 128)
        zeros = jnp.zeros((128, wide - each), BF16)
        for place in range(4):
            value = jnp.concatenate([packed[rws, pl.ds(place * each, each)], zeros], axis=1)
            if place < 3:
                w_qkv[rws, pl.ds(place * wide, wide)] = value
            else:
                w_out[rws, :] = value

    loop(width // 128, part)


def mask_row(runs, index):
    return jnp.concatenate([jnp.full((1, UNIT), part, F32) for part in runs.masks(index)], axis=1)


def split_heads(value, low):
    none = jnp.zeros_like(value)
    return jnp.concatenate([jnp.where(low, value, none), jnp.where(low, none, value)], axis=0)


def head_lanes():
    lane = lax.broadcasted_iota(jnp.int32, (1, 128), 1)
    return lane < HD


def attn_kernel(
    gathering,
    offsets_ref,
    slopes_ref,
    slots_ref,
    x_ref,
    w_ref,
    ln_ref,
    r1_ref,
    normed_ref,
    held_ref,
    qkv_ref,
    ctx_ref,
    w_qkv_ref,
    w_out_ref,
    *rest,
):
    w_ffn_ref, rest = (rest[0], rest[1:]) if gathering else (None, rest)
    (
        packed,
        w_qkv,
        w_out,
        bias,
        held,
        normed,
        plain,
        qkv,
        ctx_order,
        ctx,
        send_a,
        recv_a,
        send_b,
        recv_b,
        send_c,
        recv_c,
        load_sem,
        store_sem,
        *buffers,
    ) = rest
    packs, share, width = x_ref.shape
    rows = 4 * share
    lanes = w_out.shape[1]
    group = rows // 2
    wide, core, row, mate, across = places()
    if gathering:
        slab, near, near_send, near_recv, far, far_send, far_recv, ordered, *buffers = buffers
        load = pltpu.make_async_copy(w_ref, slab, load_sem)
        load.start()
        owners = OwnerGather(near, near_send, near_recv, slab.shape[0])
        others = OwnerGather(far, far_send, far_recv, slab.shape[0])
        holders = near.shape[1] // slab.shape[0]
        greet_all((("seq", holders), ("wide", 4)))
        load.wait()
        cut = near.shape[2]
        for part in range(owners.groups):
            value = slab[:, part * cut : (part + 1) * cut]
            near[part, owners.rows(owners.seq), :] = value.astype(BF16)
        owners.start()
        cut = far.shape[2]
        for part in range(others.groups):
            value = slab[:, width + part * cut : width + (part + 1) * cut]
            far[part, others.rows(others.seq), :] = value.astype(BF16)
    else:
        load = pltpu.make_async_copy(w_ref.at[:, pl.ds(0, packed.shape[1])], packed, load_sem)
        load.start()
        greet(mate, across)
    gather = Gather(held, send_a, recv_a, share)
    scatter = Scatter(*buffers, send_b, recv_b, share)
    spread = Gather(normed, send_c, recv_c, share)
    gain, shift = ln_ref[0:1, :], ln_ref[1:2, :]
    base = pl.multiple_of((core * 2 + row) * share, share)
    for pack in range(packs):
        held[pack, pl.ds(base, share), :] = x_ref[pack]
        gather.start(pack)
    fill_bias(bias, slopes_ref, wide)
    stores = []
    todo = []

    def pump(count):
        for _ in range(min(count, len(todo))):
            todo.pop(0)()

    if gathering:
        for step in owners.steps():
            step()
        others.start()
        todo = others.steps()
        cut = near.shape[2]
        for part in range(owners.groups):
            owners.finish(part)
            order_slabs(slots_ref, near, part, packed, pl.ds(part * cut, cut), holders)

        def settled(part):
            others.finish(part)
            cut = far.shape[2]
            cols = pl.ds(part * cut, cut)
            order_slabs(slots_ref, far, part, ordered, cols, holders)
            copy = pltpu.make_async_copy(
                ordered.at[:, cols], w_ffn_ref.at[:, cols], store_sem.at[packs + 1, part]
            )
            copy.start()
            stores.append(copy)

        todo += [functools.partial(settled, part) for part in range(others.groups)]
    else:
        load.wait()
    split_weights(packed, w_qkv, w_out)
    low = head_lanes()
    scale = jnp.asarray(HD ** (-0.5), BF16)
    for place, (source, target) in enumerate(((w_qkv, w_qkv_ref), (w_out, w_out_ref))):
        copy = pltpu.make_async_copy(source, target, store_sem.at[packs, place])
        copy.start()
        stores.append(copy)

    def attend(pack):
        runs = Runs(offsets_ref, pack)
        gather.finish(pack)

        def project(index):
            rws = tile(index, 256)
            value = dot_nn(held[pack, rws, :], w_qkv[...])
            plain[rws, pl.ds(0, lanes)] = (value[:, :lanes].astype(BF16) * scale).astype(BF16)
            plain[rws, pl.ds(lanes, 2 * lanes)] = value[:, lanes:].astype(BF16)

        loop(rows // 256, project)
        runs.arrange(plain, writer(qkv, pack))
        for side in range(2):
            keys = pl.ds(side * group, group)

            def weigh(part, queries, offset, side=side, keys=keys, pack=pack):
                scores = dot_nt(queries, qkv[pack, keys, pl.ds(lanes + part * 128, 128)]) + offset
                powers = jnp.exp(scores - jnp.max(scores, axis=-1, keepdims=True))
                total = jnp.sum(powers, axis=-1, keepdims=True)
                return dot_nn(powers.astype(BF16), qkv[pack, keys, pl.ds(2 * lanes + part * 128, 128)]) / total

            def pair(index, side=side, pack=pack):
                rws = pl.ds(pl.multiple_of(side * group + index * UNIT, UNIT), UNIT)
                offset = jnp.concatenate([bias[head, tile(index, UNIT), :] for head in range(2)], axis=0)
                if side:
                    offset = offset + mask_row(runs, index)
                out = weigh(0, split_heads(qkv[pack, rws, pl.ds(0, 128)], low), offset)
                ctx_order[rws, pl.ds(0, 128)] = jnp.where(low, out[:UNIT], out[UNIT:]).astype(BF16)

            def single(index, side=side, pack=pack):
                rws = pl.ds(pl.multiple_of(side * group + index * 2 * UNIT, 2 * UNIT), 2 * UNIT)
                offset = bias[2, tile(index, 2 * UNIT), :]
                if side:
                    offset = jnp.concatenate(
                        [
                            offset[half * UNIT : (half + 1) * UNIT] + mask_row(runs, 2 * index + half)
                            for half in range(2)
                        ],
                        axis=0,
                    )
                out = weigh(1, qkv[pack, rws, pl.ds(128, 128)], offset)
                ctx_order[rws, pl.ds(128, 128)] = out.astype(BF16)

            loop(4, pair, unroll=PAIRS)
            loop(2, single, unroll=SINGLES)
            pump(((0, 0), (2, 1), (1, 1))[pack][side])
        runs.restore(ctx_order, writer(ctx, pack))
        for which in range(2):
            big = pl.ds(scatter.half(which), 2 * share)

            def out(index, which=which, big=big):
                cols = tile(index, 256)
                value = dot_nt(ctx[pack, big, :], w_out[cols, :])
                if which:
                    scatter.part[:, cols] = value
                else:
                    scatter.give[pack, :, cols] = value.astype(BF16)

            loop(width // 256, out)
            if not which:
                scatter.start(pack)
        scatter.middle(pack)
        pump((1, 0, 0)[pack])
        for place, (source, target) in enumerate(((held, held_ref), (qkv, qkv_ref), (ctx, ctx_ref))):
            copy = pltpu.make_async_copy(source.at[pack], target.at[pack], store_sem.at[pack, place])
            copy.start()
            stores.append(copy)

    def settle(pack):
        scatter.finish(pack)

        last = pack == packs - 1

        def add(index):
            rws = tile(index, 32)
            attn = scatter.own[pack, rws, :] + scatter.reach[pack, rws, :].astype(F32)
            value = x_ref[pack, rws, :].astype(F32) + attn
            r1_ref[pack, rws, :] = value
            if not last:
                normal, _ = norm_parts(value)
                out = pl.ds(pl.multiple_of(base + index * 32, 32), 32)
                normed[pack, out, :] = (normal * gain + shift).astype(BF16)

        loop(share // 32, add, unroll=4)
        if not last:
            spread.start(pack)

    def hand_on(pack):
        spread.finish(pack)
        copy = pltpu.make_async_copy(normed.at[pack], normed_ref.at[pack], store_sem.at[packs + 2, pack])
        copy.start()
        stores.append(copy)

    for pack in range(packs):
        attend(pack)
        if pack:
            settle(pack - 1)
        if pack > 1:
            hand_on(pack - 2)
    pump(1)
    settle(packs - 1)
    pump(len(todo))
    hand_on(packs - 2)
    for copy in stores:
        copy.wait()
    for pack in range(packs):
        gather.drain(pack)
        scatter.drain(pack)
        if pack < packs - 1:
            spread.drain(pack)
    if gathering:
        owners.drain()
        others.drain()


def back_kernel(
    summing,
    offsets_ref,
    slopes_ref,
    dr1_ref,
    w_qkv_ref,
    w_out_ref,
    x_ref,
    qkv_ref,
    ctx_ref,
    *rest,
):
    padded_ref, rest = (rest[0], rest[1:]) if summing else (None, rest)
    grad_ref, grads_ref, *rest = rest
    owned_ref, rest = (rest[0], rest[1:]) if summing else (None, rest)
    (
        w_qkv,
        w_out,
        bias,
        held,
        x_all,
        qkv,
        ctx,
        plain,
        dctx,
        dorder,
        dplain,
        sum_k,
        sum_v,
        turned,
        total,
        total_out,
        send_a,
        recv_a,
        send_b,
        recv_b,
        load_sem,
        fetch_sem,
        *buffers,
    ) = rest
    if summing:
        owners = OwnerSum(padded_ref, *buffers[6:])

        def put(rws, cols, value):
            owned_ref[rws, cols] = value.astype(BF16)

        todo = owners.steps(put)
    else:
        todo = []

    def pump(count):
        for _ in range(min(count, len(todo))):
            todo.pop(0)()

    packs, share, width = dr1_ref.shape
    rows = 4 * share
    lanes = w_out.shape[1]
    group = rows // 2
    loads = [
        pltpu.make_async_copy(source, target, load_sem.at[place])
        for place, (source, target) in enumerate(((w_qkv_ref, w_qkv), (w_out_ref, w_out)))
    ]
    for copy in loads:
        copy.start()
    fetches = []
    for pack in range(packs):
        for place, (source, target) in enumerate(((x_ref, x_all), (qkv_ref, qkv), (ctx_ref, ctx))):
            copy = pltpu.make_async_copy(source.at[pack], target.at[pack], fetch_sem.at[pack, place])
            copy.start()
            fetches.append(copy)
    wide, core, row, mate, across = places()
    if summing:
        greet_all((("seq", padded_ref.shape[0]), ("wide", 4)))
    else:
        greet(mate, across)
    gather = Gather(held, send_a, recv_a, share)
    scatter = Scatter(*buffers[:6], send_b, recv_b, share)
    base = pl.multiple_of((core * 2 + row) * share, share)
    if summing:
        owners.start(0, 2)
    for pack in range(packs):
        held[pack, pl.ds(base, share), :] = dr1_ref[pack].astype(BF16)
        gather.start(pack)
    fill_bias(bias, slopes_ref, wide)
    for copy in loads:
        copy.wait()
    low = head_lanes()
    scale = HD ** (-0.5)

    def pull(pack):
        runs = Runs(offsets_ref, pack)
        gather.finish(pack)

        def project(index):
            rws = tile(index, 256)
            plain[rws, :] = dot_nn(held[pack, rws, :], w_out[...]).astype(BF16)

        loop(rows // 256, project)
        runs.arrange(plain, writer(dctx))
        for copy in fetches[3 * pack : 3 * pack + 3]:
            copy.wait()
        for side in range(2):
            keys = pl.ds(side * group, group)
            sum_k[...] = jnp.zeros_like(sum_k)
            sum_v[...] = jnp.zeros_like(sum_v)

            def masked(offset, index):
                return jnp.concatenate(
                    [offset[t * UNIT : (t + 1) * UNIT] + value for t, value in enumerate(runs.masks(index))],
                    axis=0,
                )

            def pull_back(part, queries, dout, offset, keys=keys, pack=pack):
                block = pl.ds(part * 128, 128)
                k_all = qkv[pack, keys, pl.ds(lanes + part * 128, 128)]
                v_all = qkv[pack, keys, pl.ds(2 * lanes + part * 128, 128)]
                scores = dot_nt(k_all, queries) + offset
                powers = jnp.exp(scores - jnp.max(scores, axis=0, keepdims=True))
                probs = powers * (1.0 / jnp.sum(powers, axis=0, keepdims=True))
                dprobs = dot_nt(v_all, dout)
                delta = jnp.sum(probs * dprobs, axis=0, keepdims=True)
                dscores = (probs * (dprobs - delta)).astype(BF16)
                sum_v[:, block] += dot_nn(probs.astype(BF16), dout)
                sum_k[:, block] += dot_nn(dscores, queries)
                return dot_tn(dscores, k_all) * scale

            def pair(index, side=side, pack=pack):
                rws = pl.ds(pl.multiple_of(side * group + index * UNIT, UNIT), UNIT)
                block = pl.ds(0, 128)
                offsets = [bias[head, :, tile(index, UNIT)] for head in range(2)]
                if side:
                    offsets = [masked(offset, index) for offset in offsets]
                dq = pull_back(
                    0,
                    split_heads(qkv[pack, rws, block], low),
                    split_heads(dctx[rws, block], low),
                    jnp.concatenate(offsets, axis=1),
                )
                dorder[rws, block] = jnp.where(low, dq[:UNIT], dq[UNIT:]).astype(BF16)

            def single(index, side=side, pack=pack):
                rws = pl.ds(pl.multiple_of(side * group + index * 2 * UNIT, 2 * UNIT), 2 * UNIT)
                block = pl.ds(128, 128)
                offset = bias[2, :, tile(index, 2 * UNIT)]
                if side:
                    offset = jnp.concatenate(
                        [
                            masked(offset[:, half * UNIT : (half + 1) * UNIT], 2 * index + half)
                            for half in range(2)
                        ],
                        axis=1,
                    )
                dorder[rws, block] = pull_back(1, qkv[pack, rws, block], dctx[rws, block], offset).astype(BF16)

            loop(4, pair, unroll=PAIRS)
            loop(2, single, unroll=SINGLES)
            pump(((4, 2), (1, 0), (2, 2))[pack][side])
            dorder[keys, pl.ds(lanes, lanes)] = sum_k[...].astype(BF16)
            dorder[keys, pl.ds(2 * lanes, lanes)] = sum_v[...].astype(BF16)
        runs.restore(dorder, writer(dplain))
        for which in range(2):
            big = pl.ds(scatter.half(which), 2 * share)

            def out(index, which=which, big=big):
                cols = tile(index, 256)
                value = dot_nt(dplain[big, :], w_qkv[cols, :])
                if which:
                    scatter.part[:, cols] = value
                else:
                    scatter.give[pack, :, cols] = value.astype(BF16)

            loop(width // 256, out)
            if not which:
                scatter.start(pack)
        scatter.middle(pack)
        pump((2, 1, 1)[pack])

    def weight_grads(pack):
        for source, result, target in ((x_all, dplain, total), (held, ctx.at[pack], total_out)):

            def flip(index, source=source):
                rws = tile(index, 256)
                turned[:, rws] = source[pack, rws, :].T

            loop(rows // 256, flip)

            def add(index, result=result, target=target):
                rws = tile(index, 256)
                value = dot_nn(turned[rws, :], result[...])
                if pack:
                    value = value + target[rws, :]
                target[rws, :] = value

            loop(width // 256, add)

    def settle(pack):
        scatter.finish(pack)

        def add(index):
            rws = tile(index, 64)
            grad_ref[pack, rws, :] = dr1_ref[pack, rws, :] + (
                scatter.own[pack, rws, :] + scatter.reach[pack, rws, :].astype(F32)
            )

        loop(share // 64, add)

    for pack in range(packs):
        pull(pack)
        weight_grads(pack)
        pump((1, 0, 1)[pack])
        if pack:
            settle(pack - 1)
    each = width // 4

    def pack_up(index):
        rws = tile(index, 128)
        pieces = [total[rws, pl.ds(place * lanes, each)] for place in range(3)]
        pieces.append(total_out[rws, pl.ds(0, each)])
        grads_ref[rws, :] = jnp.concatenate([piece.astype(BF16) for piece in pieces], axis=1)

    loop(width // 128, pack_up)
    settle(packs - 1)

    pump(len(todo))
    if summing:
        owners.drain()
    for pack in range(packs):
        gather.drain(pack)
        scatter.drain(pack)


def attn_call(x, weights, ln_params, slots, offsets, slopes, seq_count):
    packs, share, width = x.shape
    rows = 4 * share
    lanes = 256
    vm = pl.BlockSpec(memory_space=pltpu.VMEM)
    hb = pl.BlockSpec(memory_space=pl.ANY)
    sm = pl.BlockSpec(memory_space=pltpu.SMEM)
    dma = pltpu.SemaphoreType.DMA
    more, more_out = [], []
    if seq_count:
        slab, units = weights.shape[0], weights.shape[1] - width
        groups = len(GATHER_ORDERS)
        more = [
            pltpu.VMEM(weights.shape, F32),
            *gather_scratch(seq_count * slab, width, groups),
            *gather_scratch(seq_count * slab, units, groups),
            pltpu.VMEM((width, units), BF16),
        ]
        more_out = [jax.ShapeDtypeStruct((width, units), BF16)]
    return pl.pallas_call(
        functools.partial(attn_kernel, bool(seq_count)),
        out_shape=(
            jax.ShapeDtypeStruct((packs, share, width), F32),
            jax.ShapeDtypeStruct((packs - 1, rows, width), BF16),
            jax.ShapeDtypeStruct((packs, rows, width), BF16),
            jax.ShapeDtypeStruct((packs, rows, 3 * lanes), BF16),
            jax.ShapeDtypeStruct((packs, rows, lanes), BF16),
            jax.ShapeDtypeStruct((width, 3 * lanes), BF16),
            jax.ShapeDtypeStruct((width, lanes), BF16),
            *more_out,
        ),
        in_specs=[sm, sm, sm, vm, hb, vm],
        out_specs=(vm, *[hb] * (6 + len(more_out))),
        scratch_shapes=[
            pltpu.VMEM((width, width), BF16),
            pltpu.VMEM((width, 3 * lanes), BF16),
            pltpu.VMEM((width, lanes), BF16),
            pltpu.VMEM((3, rows // 2, rows // 2), F32),
            pltpu.VMEM((packs, rows, width), BF16),
            pltpu.VMEM((packs - 1, rows, width), BF16),
            pltpu.VMEM((rows, 3 * lanes), BF16),
            pltpu.VMEM((packs, rows, 3 * lanes), BF16),
            pltpu.VMEM((rows, lanes), BF16),
            pltpu.VMEM((packs, rows, lanes), BF16),
            dma((packs, 3)),
            dma((packs, 3)),
            dma((packs, 2)),
            dma((packs, 2)),
            dma((packs, 3)),
            dma((packs, 3)),
            dma(()),
            dma((packs + 3, 3)),
            *more,
            *scatter_scratch(packs, share, width),
        ],
        compiler_params=pltpu.CompilerParams(
            collective_id=2, has_side_effects=True, vmem_limit_bytes=VMEM_LIMIT
        ),
        cost_estimate=pl.CostEstimate(flops=int(14e9), bytes_accessed=4 * 10**7, transcendentals=10**7),
        name="attn",
    )(offsets, slopes, slots, x, weights, ln_params)


def back_call(dr1, w_qkv, w_out, x_all, qkv, ctx, padded, offsets, slopes, seq_count):
    packs, share, width = dr1.shape
    rows = 4 * share
    lanes = 256
    summing = padded is not None
    more_in, more_out, more_scratch = [], [], []
    if summing:
        slab, cols = padded.shape[0] // seq_count, padded.shape[1]
        more_in = [padded.reshape(seq_count, slab, cols)]
        more_out = [jax.ShapeDtypeStruct((slab, cols), BF16)]
        more_scratch = owner_scratch(slab, cols, len(SUM_ORDERS))
    vm = pl.BlockSpec(memory_space=pltpu.VMEM)
    hb = pl.BlockSpec(memory_space=pl.ANY)
    sm = pl.BlockSpec(memory_space=pltpu.SMEM)
    dma = pltpu.SemaphoreType.DMA
    return pl.pallas_call(
        functools.partial(back_kernel, summing),
        out_shape=(
            jax.ShapeDtypeStruct((packs, share, width), F32),
            jax.ShapeDtypeStruct((width, width), BF16),
            *more_out,
        ),
        in_specs=[sm, sm, vm, hb, hb, hb, hb, hb] + [hb] * len(more_in),
        out_specs=(vm, vm, *[vm] * len(more_out)),
        scratch_shapes=[
            pltpu.VMEM((width, 3 * lanes), BF16),
            pltpu.VMEM((width, lanes), BF16),
            pltpu.VMEM((3, rows // 2, rows // 2), F32),
            pltpu.VMEM((packs, rows, width), BF16),
            pltpu.VMEM((packs, rows, width), BF16),
            pltpu.VMEM((packs, rows, 3 * lanes), BF16),
            pltpu.VMEM((packs, rows, lanes), BF16),
            pltpu.VMEM((rows, lanes), BF16),
            pltpu.VMEM((rows, lanes), BF16),
            pltpu.VMEM((rows, 3 * lanes), BF16),
            pltpu.VMEM((rows, 3 * lanes), BF16),
            pltpu.VMEM((rows // 2, lanes), F32),
            pltpu.VMEM((rows // 2, lanes), F32),
            pltpu.VMEM((width, rows), BF16),
            pltpu.VMEM((width, 3 * lanes), F32),
            pltpu.VMEM((width, lanes), F32),
            dma((packs, 3)),
            dma((packs, 3)),
            dma((packs, 2)),
            dma((packs, 2)),
            dma((2,)),
            dma((packs, 3)),
            *scatter_scratch(packs, share, width),
            *more_scratch,
        ],
        compiler_params=pltpu.CompilerParams(
            collective_id=3, has_side_effects=True, vmem_limit_bytes=VMEM_LIMIT
        ),
        cost_estimate=pl.CostEstimate(flops=int(40e9), bytes_accessed=4 * 10**7, transcendentals=10**7),
        name="back",
    )(offsets, slopes, dr1, w_qkv, w_out, x_all, qkv, ctx, *more_in)


def flip_bits(place, *bits):
    for bit in bits:
        place = place + bit - 2 * bit * lax.rem(place // bit, 2)
    return place


GATHER_ORDERS = ((4, 2, 1), (4, 2, 1), (4, 1, 2))
SUM_ORDERS = ((1, 2, 4), (1, 2, 4), (2, 1, 4))


class OwnerGather:
    PEERS = (0, 1, 2, 1, 2, 2, 2)
    SLABS = ((), (), (), (0,), (0,), (1,), (0, 1))

    def __init__(self, held, send, recv, slab):
        self.held, self.send, self.recv, self.slab = held, send, recv, slab
        self.groups = held.shape[0]
        self.seq = lax.axis_index("seq")

    def rows(self, owner):
        return pl.ds(pl.multiple_of(owner * self.slab, self.slab), self.slab)

    def copy(self, group, leg, incoming=False):
        order = GATHER_ORDERS[group]
        bits = [order[place] for place in self.SLABS[leg]]
        if incoming:
            bits.append(order[self.PEERS[leg]])
        block = self.held.at[group, self.rows(flip_bits(self.seq, *bits))]
        peer = flip_bits(self.seq, order[self.PEERS[leg]])
        return remote(block, block, self.send.at[group, leg], self.recv.at[group, leg], peer, "seq")

    def start(self):
        for group in range(self.groups):
            for leg in range(3):
                self.copy(group, leg).start()

    def steps(self):
        found = []
        passed = {0: (3, 4), 1: (5,), 3: (6,)}
        for group, first in ((0, 0), (0, 1), (2, 1), (1, 0), (1, 1), (2, 0), (0, 3), (1, 3), (2, 3)):

            def step(group=group, first=first):
                self.copy(group, first, True).wait_recv()
                for leg in passed[first]:
                    self.copy(group, leg).start()

            found.append(step)
        return found

    def finish(self, group):
        for leg in (2, 4, 5, 6):
            self.copy(group, leg, True).wait_recv()

    def drain(self):
        for group in range(self.groups):
            for leg in range(7):
                self.copy(group, leg).wait_send()


def gather_scratch(rows, cols, groups):
    dma = pltpu.SemaphoreType.DMA
    return [pltpu.VMEM((groups, rows, cols // groups), BF16), dma((groups, 7)), dma((groups, 7))]


def order_slabs(slots, slabs, group, target, cols, owners):
    blocks, rows, slab = slots.shape[0], target.shape[0], slabs.shape[1] // owners
    block, step = rows // blocks, 8
    for first in range(0, blocks, step):
        last = first + step - 1
        low = first // CAP
        high = max(o for o in range(owners) if max(o, blocks - CAP * (owners - o)) <= last)
        count = (high - low + 1) * slab
        lines = []
        for place in range(first, first + step):
            down = lax.broadcasted_iota(jnp.int32, (block, count), 0)
            along = lax.broadcasted_iota(jnp.int32, (block, count), 1)
            hit = along - down == slots[place] * block - low * slab
            lines.append(jnp.where(hit, 1.0, 0.0).astype(BF16))
        lines = jnp.concatenate(lines, axis=0)
        for part in range(0, cols.size, 256):
            value = dot_nn(lines, slabs[group, pl.ds(low * slab, count), pl.ds(part, 256)])
            target[pl.ds(first * block, step * block), pl.ds(cols.start + part, 256)] = value.astype(BF16)


class OwnerSum:
    KEPT = ((1, 2), (1,), (2,), ())

    def __init__(self, source, own, first, second, third, load, send, recv):
        self.source, self.own, self.first, self.second, self.third = source, own, first, second, third
        self.load, self.send, self.recv = load, send, recv
        self.groups, self.slab, self.size = own.shape[0], own.shape[2], own.shape[3]
        self.seq = lax.axis_index("seq")

    def block(self, group, step, *more):
        order = SUM_ORDERS[group]
        owner = flip_bits(self.seq, *[order[place] for place in self.KEPT[step]], *more)
        return self.source.at[owner, :, pl.ds(group * self.size, self.size)]

    def fetch(self, group, step):
        return pltpu.make_async_copy(
            self.block(group, step), self.own.at[group, step], self.load.at[group, step]
        )

    def copy(self, group, leg):
        order = SUM_ORDERS[group]
        if leg < 4:
            source, target, bit = self.block(group, leg, order[0]), self.first.at[group, leg], order[0]
        elif leg < 6:
            source, target, bit = self.own.at[group, leg - 4], self.second.at[group, leg - 4], order[1]
        else:
            source, target, bit = self.own.at[group, 2], self.third.at[group], order[2]
        return remote(
            source, target, self.send.at[group, leg], self.recv.at[group, leg], flip_bits(self.seq, bit), "seq"
        )

    def start(self, *groups):
        for group in groups:
            for step in range(4):
                self.copy(group, step).start()
                self.fetch(group, step).start()

    def into(self, group, step, *others):
        def part(row):
            rws = tile(row, 32)
            value = self.own[group, step, rws, :].astype(F32)
            for other in others:
                value = value + other[rws, :].astype(F32)
            self.own[group, step, rws, :] = value.astype(BF16)

        loop(self.slab // 32, part, unroll=3)

    def add(self, group, step):
        self.fetch(group, step).wait()
        self.copy(group, step).wait_recv()
        if step < 2:
            self.into(group, step, self.first.at[group, step])
            self.copy(group, 4 + step).start()
        if group == 2 and step == 1:
            self.start(1)

    def pair(self, group):
        self.copy(group, 4).wait_recv()
        self.into(group, 2, self.first.at[group, 2], self.second.at[group, 0])
        self.copy(group, 6).start()

    def finish(self, group, target):
        self.copy(group, 5).wait_recv()
        self.copy(group, 6).wait_recv()

        def part(row):
            rws = tile(row, 32)
            value = self.own[group, 3, rws, :].astype(F32)
            for other in (self.first.at[group, 3], self.second.at[group, 1], self.third.at[group]):
                value = value + other[rws, :].astype(F32)
            target(rws, pl.ds(group * self.size, self.size), value)

        loop(self.slab // 32, part)

    def steps(self, target):
        add, pair, finish = self.add, self.pair, self.finish
        found = [functools.partial(add, group, step) for step in range(4) for group in (0, 2)]
        found += [functools.partial(pair, 0), functools.partial(pair, 2)]
        found += [functools.partial(add, 1, 0), functools.partial(add, 1, 1)]
        found += [functools.partial(finish, 0, target), functools.partial(finish, 2, target)]
        found += [functools.partial(add, 1, 2), functools.partial(pair, 1), functools.partial(add, 1, 3)]
        found.append(functools.partial(finish, 1, target))
        return found

    def drain(self):
        for group in range(self.groups):
            for leg in range(7):
                self.copy(group, leg).wait_send()


def owner_scratch(slab, width, groups):
    dma = pltpu.SemaphoreType.DMA
    size = width // groups
    return [
        pltpu.VMEM((groups, 4, slab, size), BF16),
        pltpu.VMEM((groups, 4, slab, size), BF16),
        pltpu.VMEM((groups, 2, slab, size), BF16),
        pltpu.VMEM((groups, slab, size), BF16),
        dma((groups, 4)),
        dma((groups, 7)),
        dma((groups, 7)),
    ]


class Total:
    def __init__(self, axis, slots, send, recv):
        self.axis, self.slots, self.send, self.recv = axis, slots, send, recv
        self.count = slots.shape[0]
        self.place = lax.axis_index(axis)

    def copy(self, step):
        mine = self.slots.at[self.place]
        return remote(
            mine, mine, self.send.at[step - 1], self.recv.at[self.place], self.peer(step), self.axis
        )

    def peer(self, step):
        return lax.rem(self.place + step, self.count)

    def start(self, value):
        self.slots[self.place] = value
        for step in range(1, self.count):
            self.copy(step).start()

    def finish(self):
        for step in range(1, self.count):
            other = self.peer(step)
            slot = self.slots.at[other]
            remote(
                slot, slot, self.send.at[step - 1], self.recv.at[other], other, self.axis
            ).wait_recv()
        value = self.slots[0]
        for place in range(1, self.count):
            value = value + self.slots[place]
        return value

    def drain(self):
        for step in range(1, self.count):
            self.copy(step).wait_send()


def total_scratch(count, shape):
    dma = pltpu.SemaphoreType.DMA
    return [pltpu.VMEM((count, *shape), F32), dma((count - 1,)), dma((count,))]


def greet_all(axes):
    barrier = pltpu.get_barrier_semaphore()
    sent = 0
    for axis, count in axes:
        place = lax.axis_index(axis)
        for step in range(1, count):
            peer = lax.rem(place + step, count)
            pl.semaphore_signal(barrier, inc=1, device_id={axis: peer}, device_id_type=MESH)
            sent += 1
    pl.semaphore_wait(barrier, sent)


def close_kernel(
    seq_count,
    wide_count,
    kept_ref,
    grads_ref,
    ffn_ref,
    ln_ref,
    owned_ref,
    ln_out_ref,
    square_ref,
    *scratch,
):
    greet_all((("seq", seq_count), ("wide", wide_count)))
    sums, scratch = scratch[:7], scratch[7:]
    owners = OwnerSum(grads_ref, *sums)
    norms = [Total("wide", *scratch[0:3]), Total("seq", *scratch[3:6])]
    squares = [Total("wide", *scratch[6:9]), Total("seq", *scratch[9:12])]
    acc = scratch[12]
    slab = owned_ref.shape[0]
    width = grads_ref.shape[2]
    owners.start(0, 2)
    norms[0].start(ln_ref[...])
    acc[...] = jnp.zeros_like(acc)

    def keep(rws, value):
        row = lax.broadcasted_iota(jnp.int32, value.shape, 0) + rws.start
        return jnp.where(row < kept_ref[0], value, 0.0)

    def note(value):
        square = value * value
        rows = sum(square[row : row + 8] for row in range(0, value.shape[0], 8))
        acc[...] += sum(rows[:, place : place + 128] for place in range(0, value.shape[1], 128))

    def put(rws, cols, value):
        value = keep(rws, value)
        owned_ref[rws, cols] = value
        note(value)

    def from_ffn(index):
        rws = tile(index, 16)
        value = keep(rws, ffn_ref[rws, :].astype(F32))
        owned_ref[rws, pl.ds(width, ffn_ref.shape[1])] = value
        note(value)

    steps = owners.steps(put)
    for step in steps[:10]:
        step()
    norms[1].start(norms[0].finish())
    for step in steps[10:14]:
        step()
    loop(slab // 16, from_ffn)
    for step in steps[14:]:
        step()
    squares[0].start(acc[...])
    squares[1].start(squares[0].finish())
    ln_out_ref[...] = norms[1].finish()
    square_ref[...] = squares[1].finish()
    owners.drain()
    for part in (*norms, *squares):
        part.drain()


def close_call(kept, grads, ffn_owned, ln_rows, seq_count, wide_count):
    slab = ffn_owned.shape[0]
    width = grads.shape[1]
    vm = pl.BlockSpec(memory_space=pltpu.VMEM)
    sm = pl.BlockSpec(memory_space=pltpu.SMEM)
    return pl.pallas_call(
        functools.partial(close_kernel, seq_count, wide_count),
        out_shape=(
            jax.ShapeDtypeStruct((slab, width + ffn_owned.shape[1]), F32),
            jax.ShapeDtypeStruct(ln_rows.shape, F32),
            jax.ShapeDtypeStruct((8, 128), F32),
        ),
        in_specs=[sm, pl.BlockSpec(memory_space=pl.ANY), vm, vm],
        out_specs=(vm, vm, vm),
        scratch_shapes=[
            *owner_scratch(slab, width, len(SUM_ORDERS)),
            *total_scratch(wide_count, ln_rows.shape),
            *total_scratch(seq_count, ln_rows.shape),
            *total_scratch(wide_count, (8, 128)),
            *total_scratch(seq_count, (8, 128)),
            pltpu.VMEM((8, 128), F32),
        ],
        compiler_params=pltpu.CompilerParams(
            collective_id=4, has_side_effects=True, vmem_limit_bytes=VMEM_LIMIT
        ),
        name="close",
    )(kept, grads.reshape(seq_count, slab, width), ffn_owned, ln_rows)


def adam_kernel(
    own_ref,
    owned_ref,
    master_ref,
    first_ref,
    second_ref,
    parts_ref,
    total_ref,
    params_ref,
    ln_first_ref,
    ln_second_ref,
    new_master_ref,
    new_first_ref,
    new_second_ref,
    norms_ref,
    norms_first_ref,
    norms_second_ref,
    norm_ref,
):
    rows = params_ref.shape[0]
    total = total_ref[0:rows, :]
    squares = jnp.sum(parts_ref[...], axis=(0, 1), keepdims=True)
    norm = jnp.sqrt(squares + jnp.sum(total * total, axis=(0, 1), keepdims=True))
    clip = jnp.minimum(1.0, 1.0 / (norm + 1e-06))
    norm_ref[...] = norm
    step = pl.program_id(0)
    size = owned_ref.shape[0]

    @pl.when(step == 0)
    def _():
        new = adamw(
            params_ref[...], total * clip, ln_first_ref[...], ln_second_ref[...], 0.0, NORM_RATE
        )
        for target, value in zip((norms_ref, norms_first_ref, norms_second_ref), new):
            target[...] = value

    def part(index):
        rws = tile(index, 8)
        new = adamw(
            master_ref[rws, :], owned_ref[rws, :] * clip, first_ref[rws, :], second_ref[rws, :], DECAY, RATE
        )
        row = lax.broadcasted_iota(jnp.int32, (8, owned_ref.shape[1]), 0) + step * size + index * 8
        for target, value in zip((new_master_ref, new_first_ref, new_second_ref), new):
            target[rws, :] = jnp.where(row < own_ref[0], value, 0.0)

    loop(size // 8, part)


def adam_call(own_rows, owned, master, first, second, parts, total, params, ln_first, ln_second):
    slab, cols = master.shape
    size = slab // 6
    big = pl.BlockSpec((size, cols), lambda step: (step, 0))
    small = lambda array: pl.BlockSpec(array.shape, lambda step: (0, 0))
    like = lambda array: jax.ShapeDtypeStruct(array.shape, F32)
    return pl.pallas_call(
        adam_kernel,
        grid=(6,),
        out_shape=(
            like(master),
            like(master),
            like(master),
            like(params),
            like(params),
            like(params),
            jax.ShapeDtypeStruct((1, 1), F32),
        ),
        in_specs=[
            pl.BlockSpec(memory_space=pltpu.SMEM),
            big,
            big,
            big,
            big,
            small(parts),
            small(total),
            small(params),
            small(params),
            small(params),
        ],
        out_specs=(
            big,
            big,
            big,
            small(params),
            small(params),
            small(params),
            pl.BlockSpec((1, 1), lambda step: (0, 0)),
        ),
        compiler_params=pltpu.CompilerParams(vmem_limit_bytes=VMEM_LIMIT),
        name="adam",
    )(own_rows, owned, master, first, second, parts, total, params, ln_first, ln_second)


def pick_kernel(block, places_ref, source_ref, target_ref, held, sems, sem):
    count = places_ref.shape[1]

    def copy(index):
        return pltpu.make_async_copy(
            source_ref.at[pl.ds(pl.multiple_of(places_ref[0, index] * block, block), block)],
            held.at[pl.ds(pl.multiple_of(index * block, block), block)],
            sems.at[index],
        )

    loop(count, lambda index: copy(index).start())
    loop(count, lambda index: copy(index).wait())
    out = pltpu.make_async_copy(held, target_ref, sem)
    out.start()
    out.wait()


def spread_kernel(block, places_ref, source_ref, target_ref, held, sems, sem):
    count = places_ref.shape[1]
    load = pltpu.make_async_copy(source_ref, held, sem)
    load.start()
    load.wait()

    def copy(index):
        return pltpu.make_async_copy(
            held.at[pl.ds(pl.multiple_of(index * block, block), block)],
            target_ref.at[pl.ds(pl.multiple_of(places_ref[1, index] * block, block), block)],
            sems.at[index],
        )

    loop(count, lambda index: copy(index).start())
    loop(count, lambda index: copy(index).wait())


def move_blocks(kernel, source, places, rows, block):
    hb = pl.BlockSpec(memory_space=pl.ANY)
    count = places.shape[1]
    return pl.pallas_call(
        functools.partial(kernel, block),
        out_shape=jax.ShapeDtypeStruct((rows, source.shape[1]), source.dtype),
        in_specs=[pl.BlockSpec(memory_space=pltpu.SMEM), hb],
        out_specs=hb,
        scratch_shapes=[
            pltpu.VMEM((count * block, source.shape[1]), source.dtype),
            pltpu.SemaphoreType.DMA((count,)),
            pltpu.SemaphoreType.DMA(()),
        ],
        compiler_params=pltpu.CompilerParams(vmem_limit_bytes=VMEM_LIMIT),
        name="move",
    )(places, source)


def per_device(
    hidden_in,
    cotangent,
    seq_offsets,
    owner_blocks,
    master,
    first_moment,
    second_moment,
    ln_params,
    ln_first,
    ln_second,
):
    width = hidden_in.shape[2]
    slab_rows = master.shape[0]
    block = slab_rows // CAP
    source, valid, target = owner_maps(owner_blocks, width, CAP, block)
    gathered_rows = slab_rows * lax.axis_size("seq")
    count = width // block
    fits = block % 16 == 0
    slots = target[::block] // block
    both = jnp.stack([slots, slots])

    def to_order(array):
        if fits:
            return move_blocks(pick_kernel, array, both, width, block)
        return jnp.take(array, target, axis=0)

    def to_owner(grads):
        if fits:
            return move_blocks(spread_kernel, grads, both, gathered_rows, block)
        return jnp.take(grads, source, axis=0)

    seq_count = lax.axis_size("seq")
    own_kernels = fits and seq_count == 8
    if own_kernels:
        weights = master
    else:
        low = master.astype(jnp.bfloat16)
        weights, w_ffn = (
            to_order(lax.all_gather(part, "seq", axis=0, tiled=True)) for part in (low[:, :width], low[:, width:])
        )
    slopes = jnp.exp2(-8.0 * (jnp.arange(H, dtype=jnp.float32) + 1.0) / H)
    x = jnp.transpose(hidden_in, (1, 0, 2))
    r1, normed, x_all, qkv, ctx, w_qkv, w_out, *more = attn_call(
        x, weights, ln_params, slots, seq_offsets, slopes, seq_count if own_kernels else 0
    )
    w_ffn = more[0] if own_kernels else w_ffn
    mixed_p, dr1_p, ffn_grads, ln_rows = ffn_call(
        r1, jnp.transpose(cotangent, (1, 0, 2)), normed, w_ffn, ln_params
    )
    mixed = jnp.transpose(mixed_p, (1, 0, 2))

    ffn_padded = to_owner(ffn_grads)
    grad_p, attn_grads, *more = back_call(
        dr1_p, w_qkv, w_out, x_all, qkv, ctx, ffn_padded if own_kernels else None, seq_offsets, slopes, seq_count
    )
    input_grad = jnp.transpose(grad_p, (1, 0, 2))
    attn_padded = to_owner(attn_grads)
    mine = jnp.arange(seq_count, dtype=jnp.int32) == lax.axis_index("seq")
    own_rows = jnp.sum(jnp.where(mine, owner_blocks, 0)) * block
    kept = (jnp.arange(slab_rows, dtype=jnp.int32) < own_rows)[:, None]
    if own_kernels:
        owned, ln_total, parts = close_call(
            own_rows[None], attn_padded, more[0], ln_rows, seq_count, lax.axis_size("wide")
        )
        *updated, grad_norm = adam_call(
            own_rows[None],
            owned,
            master,
            first_moment,
            second_moment,
            parts,
            ln_total,
            ln_params,
            ln_first,
            ln_second,
        )
        return (mixed, input_grad, *updated, grad_norm[0, 0])
    ffn_owned = lax.psum_scatter(ffn_padded, "seq", scatter_dimension=0, tiled=True)
    attn_owned = lax.psum_scatter(attn_padded, "seq", scatter_dimension=0, tiled=True)
    owned = jnp.concatenate([attn_owned, ffn_owned], axis=1).astype(jnp.float32)
    owned = jnp.where(kept, owned, 0.0)
    squares, ln_total = lax.psum((jnp.sum(owned * owned), ln_rows[:4]), ("seq", "wide"))
    grad_norm = jnp.sqrt(squares + jnp.sum(ln_total * ln_total))
    clip = jnp.minimum(1.0, 1.0 / (grad_norm + 1e-06))
    param_new, first_new, second_new = adamw(
        master, owned * clip, first_moment, second_moment, DECAY, RATE
    )
    norms_new, norms_first, norms_second = adamw(
        ln_params, ln_total * clip, ln_first, ln_second, 0.0, NORM_RATE
    )
    return (
        mixed,
        input_grad,
        jnp.where(kept, param_new, 0.0),
        jnp.where(kept, first_new, 0.0),
        jnp.where(kept, second_new, 0.0),
        norms_new,
        norms_first,
        norms_second,
        grad_norm,
    )


def solution(mesh):
    return jax.shard_map(
        per_device,
        mesh=mesh,
        in_specs=(
            P("wide", "seq", None),
            P("wide", "seq", None),
            P("seq", None),
            P(),
            P("seq", "wide"),
            P("seq", "wide"),
            P("seq", "wide"),
            P(),
            P(),
            P(),
        ),
        out_specs=(
            P("wide", "seq", None),
            P("wide", "seq", None),
            P("seq", "wide"),
            P("seq", "wide"),
            P("seq", "wide"),
            P(),
            P(),
            P(),
            P(),
        ),
        check_vma=False,
    )
```
